32 devices in a mesh: group: 2 (over y), seq: 4 (over x, core), dom: 4 (over z).
Axes of the slice: x: 2, y: 2, z: 4, core: 2. Of those that a mesh axis runs over, the one named last changes fastest.
Arguments:
- q_nope: bfloat16 [32, 128, 128], P(('group', 'dom'), 'seq'), parts along dimension 0, may hold values from -6 to 6
- q_rope: bfloat16 [32, 128, 64], P(('group', 'dom'), 'seq'), parts along dimension 0, may hold values from -8 to 8
- w_uk: bfloat16 [128, 128, 512], P('seq'), may hold values from -0.5 to 0.5
- w_uv: bfloat16 [128, 512, 128], P('seq'), may hold values from -1.5 to 1.5
- prefix: bfloat16 [32768, 576], P(('group', 'seq')), parts along dimension 0, may hold values from -8 to 8
- private_caches: bfloat16 [32, 256, 576], P(('group', 'dom'), 'seq'), parts along dimension 0, may hold values from -8 to 8
- new_latent: bfloat16 [32, 576], P(('group', 'dom')), parts along dimension 0, may hold values from -6 to 6
- ancestors: int32 [32], P(('group', 'dom')), parts along dimension 0, may hold values from 0 to 15
- lengths: int32 [32], P('group'), parts along dimension 0, may hold values from 1 to 255
Outputs:
- head_values: bfloat16 [32, 128, 128], P(('group', 'dom'), 'seq'), parts along dimension 0
- new_caches: bfloat16 [32, 256, 576], P(('group', 'dom'), 'seq'), parts along dimension 0
The draws below stay inside these ranges and needn't reach their ends.
There are 2 independent parts, one for each index of `group`. The reference program is written for one: setup_inputs(seed, part) draws one part's arguments, and reference() takes and returns one part's arrays. A program takes and returns all parts, laid end to end along the dimension named above; an argument that names none is the same for every part. Nothing has to cross between parts.
All inputs are finite; a program needn't handle non-finite values.
Results may differ from the reference program's by a relative error of at most 0.0085.
Values may be sent and summed in bfloat16 or wider, within the bound.
No kernel may reach another device: no remote copies, remote signals or barrier semaphores. Data moves between devices by JAX's collectives and lax.ppermute only.
A program may use at most 64 MiB of HBM per device.

```python
import jax
import jax.numpy as jnp
from jax import lax

KV_RANK = 512
ROPE = 64
NOPE = 128
VH = 128
HEADS = 128
PRE_DEV = 4096
SUF_DEV = 64
PARTICLES = 16
PRE = 16384
SUF = 256
LATENT = 576
N_SEQ = 4


def draw_prefix(key, part):
    values = jnp.clip(1.5 * jax.random.normal(jax.random.fold_in(key, 11), (PRE, KV_RANK + ROPE), jnp.float32), -8.0, 8.0)
    return values.astype(jnp.bfloat16)


def draw_q_rope(key, part):
    values = jnp.clip(jax.random.normal(jax.random.fold_in(key, 17), (PARTICLES, HEADS, ROPE), jnp.float32), -8.0, 8.0)
    return values.astype(jnp.bfloat16)


def set_ends(result, stream_key, least, high):
    longest = result.shape.index(max(result.shape))
    spots = []
    for shift in (0, 1):
        where = [jax.random.randint(jax.random.fold_in(stream_key, axis), (), 0, length) for axis, length in enumerate(result.shape)]
        where[longest] = (where[longest] + shift) % result.shape[longest]
        spots.append(tuple(where))
    return result.at[spots[0]].set(least).at[spots[1]].set(high)


def steps_of(stream_key, dims, cuts, smallest, top_value):
    def one(axis_at, shards_of):
        heights = jax.random.uniform(jax.random.fold_in(jax.random.fold_in(stream_key, 6), axis_at), (shards_of,), jnp.float32, smallest / len(cuts), top_value / len(cuts))
        return jnp.repeat(jnp.exp(heights), dims[axis_at] // shards_of).reshape((-1,) + (1,) * (len(dims) - axis_at - 1))

    loudness = one(*cuts[0])
    for cut in cuts[1:]:
        loudness = loudness * one(*cut)
    return loudness


def noise(key, shape, deviation, reach, shards=(), kind=jnp.bfloat16):
    values = jax.random.normal(key, shape, jnp.float32) * deviation
    if len(shards) > 0:
        values = steps_of(key, shape, shards, -0.22, 0.18) * values
    return jnp.clip(values, min=-reach, max=reach).astype(kind)


def setup_inputs(seed: int = 0, part: int = 0) -> dict:
    key_list = jax.random.split(jax.random.key(seed), 10)
    part_splits = jax.random.split(jax.random.fold_in(key_list[9], part), 10)
    return {
        "q_nope": noise(part_splits[0], (PARTICLES, HEADS, NOPE), 1.0, 6.0, ((0, 4), (1, 4))),
        "q_rope": draw_q_rope(jax.random.fold_in(jax.random.fold_in(key_list[9], part), 71), part),
        "w_uk": noise(key_list[2], (HEADS, NOPE, KV_RANK), NOPE ** -0.5, 0.5, ((0, 4),)),
        "w_uv": noise(key_list[3], (HEADS, KV_RANK, VH), (KV_RANK // 32) ** -0.5, 1.5, ((0, 4),)),
        "prefix": draw_prefix(jax.random.fold_in(jax.random.fold_in(key_list[9], part), 71), part),
        "private_caches": noise(part_splits[5], (PARTICLES, SUF, LATENT), 2.0, 8.0, ((0, 4), (1, 4))),
        "new_latent": noise(part_splits[6], (PARTICLES, LATENT), 1.0, 6.0, ((0, 4),)),
        "ancestors": set_ends(jax.random.randint(part_splits[7], (PARTICLES,), 0, PARTICLES), jax.random.fold_in(part_splits[7], 1), 0, PARTICLES - 1).astype(jnp.int32),
        "lengths": set_ends(jax.random.randint(part_splits[8], (PARTICLES,), 1, SUF), jax.random.fold_in(part_splits[8], 1), 1, SUF - 1).astype(jnp.int32),
    }


masked_score = -1e30


def merge_partials(left_part, right_part):
    left_max, left_sum, left_acc = left_part
    right_max, right_sum, right_acc = right_part
    largest = jnp.maximum(left_max, right_max)
    left_factor = jnp.exp(left_max - largest)
    right_factor = jnp.exp(right_max - largest)
    return (largest, left_sum * left_factor + right_sum * right_factor,
            left_acc * left_factor[..., None] + right_acc * right_factor[..., None])


def reference(q_nope, q_rope, w_uk, w_uv, prefix, private_caches, new_latent, ancestors, lengths):
    softmax_scale = (NOPE + ROPE) ** -0.5
    latent_width = KV_RANK + ROPE
    particle_total = ancestors.shape[0]
    owners = ancestors[:, None] == jnp.arange(particle_total, dtype=jnp.int32)[None, :]
    new_lengths = jnp.sum(jnp.where(owners, lengths[None, :], 0), axis=1).astype(jnp.int32)
    migrated = private_caches[ancestors]
    positions = jnp.arange(SUF, dtype=jnp.int32)
    writes = positions[None, :] == new_lengths[:, None]
    new_caches = jnp.where(writes[:, :, None], new_latent[:, None, :], migrated)
    query_latent = jnp.einsum("phn,hnc->phc", q_nope.astype(jnp.float32), w_uk.astype(jnp.float32)).astype(jnp.bfloat16)
    queries = jnp.concatenate([query_latent, q_rope], axis=2)
    row_total = particle_total * HEADS
    flat_queries = queries.reshape(row_total, latent_width)
    start_part = (jnp.full((row_total,), masked_score, jnp.float32),
                  jnp.zeros((row_total,), jnp.float32),
                  jnp.zeros((row_total, KV_RANK), jnp.float32))

    def prefix_block(carried, key_block):
        scores = jnp.dot(flat_queries, key_block.T, preferred_element_type=jnp.float32) * softmax_scale
        block_max = jnp.max(scores, axis=1)
        weights = jnp.exp(scores - block_max[:, None])
        block_sum = jnp.sum(weights, axis=1)
        block_acc = jnp.dot(weights.astype(jnp.bfloat16), key_block[:, :KV_RANK], preferred_element_type=jnp.float32)
        return merge_partials(carried, (block_max, block_sum, block_acc)), None

    combined, unused = lax.scan(prefix_block, start_part, prefix.reshape(N_SEQ, PRE_DEV, latent_width))
    wide_queries = queries.astype(jnp.float32)
    suffix_blocks = migrated.reshape(particle_total, N_SEQ, SUF_DEV, latent_width).transpose(1, 0, 2, 3)

    def suffix_block(carried, inputs):
        key_block, block_index = inputs
        block_positions = block_index * SUF_DEV + jnp.arange(SUF_DEV, dtype=jnp.int32)
        visible = (block_positions[None, :] < new_lengths[:, None])[:, None, :]
        scores = jnp.einsum("phc,pkc->phk", wide_queries, key_block.astype(jnp.float32)) * softmax_scale
        masked = jnp.where(visible, scores, masked_score)
        block_max = jnp.max(masked, axis=2)
        weights = jnp.where(visible, jnp.exp(masked - block_max[:, :, None]), 0.0)
        block_sum = jnp.sum(weights, axis=2)
        rounded = lax.optimization_barrier(weights.astype(jnp.bfloat16)).astype(jnp.float32)
        block_acc = jnp.einsum("phk,pkc->phc", rounded, key_block[:, :, :KV_RANK].astype(jnp.float32))
        return merge_partials(carried, (block_max.reshape(row_total), block_sum.reshape(row_total),
                                        block_acc.reshape(row_total, KV_RANK))), None

    combined, unused = lax.scan(suffix_block, combined, (suffix_blocks, jnp.arange(N_SEQ, dtype=jnp.int32)))
    latent_out = (combined[2] / combined[1][:, None]).astype(jnp.bfloat16).reshape(particle_total, HEADS, KV_RANK)
    head_values = jnp.einsum("phc,hcv->phv", latent_out.astype(jnp.float32), w_uv.astype(jnp.float32)).astype(jnp.bfloat16)
    return head_values, new_caches
```

```python
import functools
import math

import jax
import jax.numpy as jnp
from jax import lax
from jax.experimental import pallas as pl
from jax.experimental.pallas import tpu as pltpu
from jax.sharding import PartitionSpec as P

ROPE = 64
NOPE = 128
SCALE2 = (NOPE + ROPE) ** (-0.5) * math.log2(math.e)
HIDDEN = -1e30
LANES = 128
F32 = jnp.float32
BF16 = jnp.bfloat16
NT = (((1,), (1,)), ((), ()))

VMEM = pl.BlockSpec(memory_space=pltpu.VMEM)
SMEM = pl.BlockSpec(memory_space=pltpu.SMEM)
ANY = pl.BlockSpec(memory_space=pl.ANY)
PARAMS = pltpu.CompilerParams(vmem_limit_bytes=40 * 1024 * 1024)


def prefix_kernel(count, *refs):
    query_refs = refs[:count]
    prefix_hbm, acc_ref, max_ref, sum_ref, keys, sems = refs[count:]
    tiles, tile = keys.shape[0], keys.shape[1]
    rank = acc_ref.shape[1]

    def fetch(i):
        return pltpu.make_async_copy(
            prefix_hbm.at[pl.ds(i * tile, tile)], keys.at[i], sems.at[i]
        )

    for i in range(tiles):
        fetch(i).start()
    queries = jnp.concatenate([ref[...] for ref in query_refs], axis=0)
    for i in range(tiles):
        fetch(i).wait()
        scores = lax.dot_general(queries, keys[i], NT, preferred_element_type=F32) * SCALE2
        top = jnp.max(scores, axis=1, keepdims=True)
        if i > 0:
            top = jnp.maximum(top, largest)
        weights = jnp.exp2(scores - top)
        total = jnp.sum(weights, axis=1, keepdims=True)
        acc = jnp.dot(weights.astype(BF16), keys[i, :, :rank], preferred_element_type=F32)
        if i > 0:
            factor = jnp.exp2(largest - top)
            total = total + running * factor
            acc = acc + acc_ref[...] * factor
        largest, running = top, total
        acc_ref[...] = acc
    max_ref[...] = jnp.broadcast_to(largest, max_ref.shape)
    sum_ref[...] = jnp.broadcast_to(running, sum_ref.shape)


def prefix_attention(queries, prefix, rank, tiles=4):
    rows = sum(q.shape[0] for q in queries)
    tile = prefix.shape[0] // tiles
    stat = jax.ShapeDtypeStruct((rows, LANES), F32)
    return pl.pallas_call(
        functools.partial(prefix_kernel, len(queries)),
        out_shape=(jax.ShapeDtypeStruct((rows, rank), F32), stat, stat),
        in_specs=[VMEM] * len(queries) + [ANY],
        out_specs=(VMEM,) * 3,
        scratch_shapes=[
            pltpu.VMEM((tiles, tile, prefix.shape[1]), BF16),
            pltpu.SemaphoreType.DMA((tiles,)),
        ],
        compiler_params=PARAMS,
        name="prefix_attention",
    )(*queries, prefix)


def suffix_kernel(count, offsets, heads, *refs):
    anc, lens, place, fresh_ref = refs[:4]
    refs = refs[4:]
    query_refs, refs = refs[:count], refs[count:]
    stage_refs, refs = refs[: 3 * (count // 2)], refs[3 * (count // 2) :]
    block_refs, refs = refs[: len(offsets)], refs[len(offsets) :]
    cache_ref, refs = refs[0], refs[1:]
    out_refs, (moved, sems) = refs[:count], refs[count:]
    local, span, width = moved.shape
    rank = stage_refs[0].shape[1]

    for p in range(local):
        owner = lax.div(anc[p], local)
        slot = lax.rem(anc[p], local)
        for k, offset in enumerate(offsets):

            @pl.when(owner == place[1] + offset)
            def _():
                pltpu.make_async_copy(block_refs[k].at[slot], moved.at[p], sems.at[p]).start()

    for p in range(local):
        pltpu.make_async_copy(block_refs[0].at[0], moved.at[p], sems.at[p]).wait()

    start = place[0] * span
    ends = [lens[anc[p]] for p in range(local)]
    row_at = start + lax.broadcasted_iota(jnp.int32, (span, width), 0)
    for p in range(local):
        cache_ref[p] = jnp.where(row_at == ends[p], fresh_ref[pl.ds(p, 1), :], moved[p])

    keys = moved[...].reshape(local * span, width)
    half = 2 * heads * local
    shape = (half, local * span)
    row = lax.broadcasted_iota(jnp.int32, shape, 0)
    col = lax.broadcasted_iota(jnp.int32, shape, 1)
    row_of = lax.rem(lax.div(row, heads), local)
    at = start + lax.rem(col, span)
    col_of = lax.div(col, span)
    seen = jnp.zeros(shape, jnp.bool_)
    for p in range(local):
        seen = seen | ((row_of == p) & (col_of == p) & (at < ends[p]))
    lane = lax.broadcasted_iota(jnp.int32, (half, LANES), 1)
    for k in range(count // 2):
        queries = jnp.concatenate([query_refs[2 * k][...], query_refs[2 * k + 1][...]], axis=0)
        acc_ref, max_ref, sum_ref = stage_refs[3 * k : 3 * k + 3]
        scores = lax.dot_general(queries, keys, NT, preferred_element_type=F32) * SCALE2
        scores = jnp.where(seen, scores, HIDDEN)
        before = max_ref[:, 0:1]
        top = jnp.maximum(before, jnp.max(scores, axis=1, keepdims=True))
        weights = jnp.where(seen, jnp.exp2(scores - top), 0.0)
        factor = jnp.exp2(before - top)
        total = sum_ref[:, 0:1] * factor + jnp.sum(weights, axis=1, keepdims=True)
        acc = acc_ref[...] * factor + jnp.dot(
            weights.astype(BF16), keys[:, :rank], preferred_element_type=F32
        )
        level = top + jnp.log2(total)
        high = level.astype(BF16).astype(F32)
        middle = (level - high).astype(BF16).astype(F32)
        low = level - high - middle
        stats = jnp.where(lane == 0, high, jnp.where(lane == 1, middle, jnp.where(lane == 2, low, 0.0)))
        part = jnp.concatenate([(acc / total).astype(BF16), stats.astype(BF16)], axis=1)
        out_refs[2 * k][...] = part[: half // 2]
        out_refs[2 * k + 1][...] = part[half // 2 :]


def merge_kernel(count, *refs):
    part_refs, out_ref = refs[:count], refs[count]
    rank = out_ref.shape[1]
    levels = [jnp.sum(ref[:, rank:].astype(F32), axis=1, keepdims=True) for ref in part_refs]
    top = functools.reduce(jnp.maximum, levels)
    shares = [jnp.exp2(level - top) for level in levels]
    whole = functools.reduce(jnp.add, shares)
    acc = functools.reduce(
        jnp.add, [share * ref[:, :rank].astype(F32) for share, ref in zip(shares, part_refs)]
    )
    out_ref[...] = (acc / whole).astype(BF16)


def on_device(q_nope, q_rope, w_uk, w_uv, prefix, private_caches, new_latent, ancestors, lengths):
    local, heads = q_nope.shape[:2]
    span, width = private_caches.shape[1:]
    rank = w_uv.shape[1]
    seq_size, dom_size = lax.axis_size("seq"), lax.axis_size("dom")
    cores = 2 if seq_size % 2 == 0 else 1
    chips = seq_size // cores
    place = jnp.stack([lax.axis_index("seq"), lax.axis_index("dom")]).astype(jnp.int32)

    offsets, blocks = [0], [private_caches]
    left = right = private_caches
    for k in range(1, dom_size):
        right = lax.ppermute(right, "dom", [(i, i + 1) for i in range(k - 1, dom_size - 1)])
        left = lax.ppermute(left, "dom", [(i, i - 1) for i in range(1, dom_size - k + 1)])
        offsets += [-k, k]
        blocks += [right, left]

    query_latent = jnp.einsum("phn,hnc->phc", q_nope, w_uk, preferred_element_type=F32).astype(BF16)
    own = jnp.concatenate([query_latent, q_rope], axis=2).reshape(local * heads, width)

    def pairs(turn, flip):
        return [
            (x * cores + c, (x + turn) % chips * cores + (c ^ flip))
            for x in range(chips)
            for c in range(cores)
        ]

    routes = [(t, f) for t in range(chips) for f in range(cores)]
    queries = [own if r == (0, 0) else lax.ppermute(own, "seq", pairs(*r)) for r in routes]
    stages = []
    for k in range(0, len(routes), 2):
        stages += prefix_attention(queries[k : k + 2], prefix, rank)

    count = len(routes)
    rows = local * heads
    results = pl.pallas_call(
        functools.partial(suffix_kernel, count, tuple(offsets), heads),
        out_shape=(jax.ShapeDtypeStruct(private_caches.shape, BF16),)
        + (jax.ShapeDtypeStruct((rows, rank + LANES), BF16),) * count,
        in_specs=[SMEM] * 3 + [VMEM] * (1 + count + len(stages)) + [ANY] * len(blocks),
        out_specs=(VMEM,) * (1 + count),
        scratch_shapes=[
            pltpu.VMEM((local, span, width), BF16),
            pltpu.SemaphoreType.DMA((local,)),
        ],
        compiler_params=PARAMS,
        name="suffix_attention",
    )(ancestors, lengths, place, new_latent, *queries, *stages, *blocks)
    new_caches, parts = results[0], results[1:]

    parts = [
        part if r == (0, 0) else lax.ppermute(part, "seq", [(b, a) for a, b in pairs(*r)])
        for r, part in zip(routes, parts)
    ]
    latent_out = pl.pallas_call(
        functools.partial(merge_kernel, count),
        out_shape=jax.ShapeDtypeStruct((rows, rank), BF16),
        in_specs=[VMEM] * count,
        out_specs=VMEM,
        compiler_params=PARAMS,
        name="merge",
    )(*parts)
    head_values = jnp.einsum(
        "phc,hcv->phv", latent_out.reshape(local, heads, rank), w_uv, preferred_element_type=F32
    ).astype(BF16)
    return (head_values, new_caches)


def solution(mesh):
    placed = (
        P(("group", "dom"), "seq", None),
        P(("group", "dom"), "seq", None),
        P("seq", None, None),
        P("seq", None, None),
        P(("group", "seq"), None),
        P(("group", "dom"), "seq", None),
        P(("group", "dom"), None),
        P(("group", "dom")),
        P("group"),
    )
    return jax.shard_map(
        on_device,
        mesh=mesh,
        in_specs=placed,
        out_specs=(P(("group", "dom"), "seq", None), P(("group", "dom"), "seq", None)),
        check_vma=False,
    )
```

```python
import functools
import math

import jax
import jax.numpy as jnp
from jax import lax
from jax.experimental import pallas as pl
from jax.experimental.pallas import tpu as pltpu
from jax.sharding import PartitionSpec as P

ROPE = 64
NOPE = 128
SCALE2 = (NOPE + ROPE) ** (-0.5) * math.log2(math.e)
HIDDEN = -1e30
LANES = 128
F32 = jnp.float32
BF16 = jnp.bfloat16
NT = (((1,), (1,)), ((), ()))

VMEM = pl.BlockSpec(memory_space=pltpu.VMEM)
SMEM = pl.BlockSpec(memory_space=pltpu.SMEM)
ANY = pl.BlockSpec(memory_space=pl.ANY)
PARAMS = pltpu.CompilerParams(vmem_limit_bytes=24 * 1024 * 1024)


def prefix_kernel(count, tiles, *refs):
    query_refs = refs[:count]
    keys_ref, acc_ref, max_ref, sum_ref = refs[count:]
    rank = acc_ref.shape[1]
    tile = keys_ref.shape[1] // tiles
    queries = jnp.concatenate([ref[...] for ref in query_refs], axis=0)
    for i in range(tiles):
        part = pl.ds(i * tile, tile)
        scores = jnp.dot(queries, keys_ref[:, part], preferred_element_type=F32) * SCALE2
        top = jnp.max(scores, axis=1, keepdims=True)
        if i > 0:
            top = jnp.maximum(top, largest)
        weights = jnp.exp2(scores - top)
        total = jnp.sum(weights, axis=1, keepdims=True)
        acc = lax.dot_general(
            weights.astype(BF16), keys_ref[:rank, part], NT, preferred_element_type=F32
        )
        if i > 0:
            factor = jnp.exp2(largest - top)
            total = total + running * factor
            acc = acc + acc_ref[...] * factor
        largest, running = top, total
        acc_ref[...] = acc
    max_ref[...] = jnp.broadcast_to(largest, max_ref.shape)
    sum_ref[...] = jnp.broadcast_to(running, sum_ref.shape)


def prefix_attention(queries, keys, rank, tiles=4):
    rows = sum(q.shape[0] for q in queries)
    width, length = keys.shape
    stat = jax.ShapeDtypeStruct((rows, LANES), F32)
    return pl.pallas_call(
        functools.partial(prefix_kernel, len(queries), tiles),
        out_shape=(jax.ShapeDtypeStruct((rows, rank), F32), stat, stat),
        in_specs=[VMEM] * (len(queries) + 1),
        out_specs=(VMEM,) * 3,
        compiler_params=PARAMS,
        cost_estimate=pl.CostEstimate(
            flops=2 * rows * length * (width + rank),
            bytes_accessed=2 * width * length,
            transcendentals=rows * length,
        ),
        name="prefix_attention",
    )(*queries, keys)


def start_copies(count, block_refs, picks, out_ref, sems):
    for p, (which, slot) in enumerate(picks):
        for k in range(count):

            @pl.when(which == k)
            def _():
                pltpu.make_async_copy(block_refs[k].at[slot], out_ref.at[p], sems.at[p]).start()


def wait_copies(block_refs, out_ref, sems):
    for p in range(out_ref.shape[0]):
        pltpu.make_async_copy(block_refs[0].at[0], out_ref.at[p], sems.at[p]).wait()


def select_kernel(count, theirs, place, *refs):
    block_refs, (_, out_ref, sems) = refs[:count], refs[count:]
    local = out_ref.shape[0]
    picks = []
    for p in range(local):
        ancestor = theirs[p]
        picks.append((jnp.bitwise_xor(lax.div(ancestor, local), place[1]), lax.rem(ancestor, local)))
    start_copies(count, block_refs, picks, out_ref, sems)
    wait_copies(block_refs, out_ref, sems)


def suffix_kernel(count, sources, inner, heads, *refs):
    anc, lens, place, fresh_ref = refs[:4]
    refs = refs[4:]
    query_refs, refs = refs[:count], refs[count:]
    stage_refs, refs = refs[: 3 * (count // 2)], refs[3 * (count // 2) :]
    block_refs, refs = refs[:sources], refs[sources:]
    cache_ref, refs = refs[0], refs[1:]
    out_refs, (moved, sems) = refs[:count], refs[count:]
    local, span, width = moved.shape
    rank = stage_refs[0].shape[1]

    picks = []
    for p in range(local):
        owner = lax.div(anc[p], local)
        slot = lax.rem(anc[p], local)
        if inner:
            far = (place[1] == 0) | (place[1] == 3)
            far = far & (owner != place[1])
            which = jnp.where(far, sources - 1, jnp.bitwise_xor(owner, place[1]))
            slot = jnp.where(far, p, slot)
        else:
            which = lax.rem(place[1] - owner + sources, sources)
        picks.append((which, slot))
    start_copies(sources, block_refs, picks, moved, sems)

    cols, half = local * span, 2 * heads * local
    start = place[0] * span
    ends = [lens[anc[p]] for p in range(local)]
    col = lax.broadcasted_iota(jnp.int32, (1, cols), 1)
    row = lax.broadcasted_iota(jnp.int32, (half, 1), 0)
    col_of = jnp.zeros_like(col)
    row_of = jnp.zeros_like(row)
    limit = jnp.full_like(col, ends[0] - start)
    for p in range(1, local):
        col_of = col_of + (col >= p * span).astype(jnp.int32)
        limit = jnp.where(col >= p * span, ends[p] - start + p * span, limit)
    for k in range(2):
        for p in range(local):
            row_of = jnp.where(row >= (k * local + p) * heads, p, row_of)
    col_of = jnp.where(col < limit, col_of, -1)
    seen = row_of == col_of
    lane = lax.broadcasted_iota(jnp.int32, (half, LANES), 1)
    row_at = start + lax.broadcasted_iota(jnp.int32, (span, width), 0)

    wait_copies(block_refs, moved, sems)
    for p in range(local):
        cache_ref[p] = jnp.where(row_at == ends[p], fresh_ref[pl.ds(p, 1), :], moved[p])
    keys = moved[...].reshape(cols, width)
    for k in range(count // 2):
        queries = jnp.concatenate([query_refs[2 * k][...], query_refs[2 * k + 1][...]], axis=0)
        acc_ref, max_ref, sum_ref = stage_refs[3 * k : 3 * k + 3]
        scores = lax.dot_general(queries, keys, NT, preferred_element_type=F32) * SCALE2
        scores = jnp.where(seen, scores, HIDDEN)
        before = max_ref[:, 0:1]
        top = jnp.maximum(before, jnp.max(scores, axis=1, keepdims=True))
        weights = jnp.where(seen, jnp.exp2(scores - top), 0.0)
        factor = jnp.exp2(before - top)
        total = sum_ref[:, 0:1] * factor + jnp.sum(weights, axis=1, keepdims=True)
        acc = acc_ref[...] * factor + jnp.dot(
            weights.astype(BF16), keys[:, :rank], preferred_element_type=F32
        )
        level = top + jnp.log2(total)
        high = level.astype(BF16).astype(F32)
        middle = (level - high).astype(BF16).astype(F32)
        low = level - high - middle
        stats = jnp.where(lane == 0, high, jnp.where(lane == 1, middle, jnp.where(lane == 2, low, 0.0)))
        part = jnp.concatenate([(acc * (1.0 / total)).astype(BF16), stats.astype(BF16)], axis=1)
        out_refs[2 * k][...] = part[: half // 2]
        out_refs[2 * k + 1][...] = part[half // 2 :]


def merge_kernel(count, *refs):
    part_refs, out_ref = refs[:count], refs[count]
    rank = out_ref.shape[1]
    levels = [jnp.sum(ref[:, rank:].astype(F32), axis=1, keepdims=True) for ref in part_refs]
    top = functools.reduce(jnp.maximum, levels)
    shares = [jnp.exp2(level - top) for level in levels]
    whole = functools.reduce(jnp.add, shares)
    acc = functools.reduce(
        jnp.add, [share * ref[:, :rank].astype(F32) for share, ref in zip(shares, part_refs)]
    )
    out_ref[...] = (acc / whole).astype(BF16)


def on_device(q_nope, q_rope, w_uk, w_uv, prefix, private_caches, new_latent, ancestors, lengths):
    local, heads = q_nope.shape[:2]
    span, width = private_caches.shape[1:]
    rank = w_uv.shape[1]
    seq_size, dom_size = lax.axis_size("seq"), lax.axis_size("dom")
    cores = 2 if seq_size % 2 == 0 else 1
    chips = seq_size // cores
    place = jnp.stack([lax.axis_index("seq"), lax.axis_index("dom")]).astype(jnp.int32)

    inner = dom_size == 4
    if inner:
        far = lax.ppermute(private_caches, "dom", [(1, 2), (2, 1)])
        near = lax.ppermute(private_caches, "dom", [(0, 1), (3, 2)])
        middle = lax.ppermute(private_caches, "dom", [(0, 2), (3, 1)])
        theirs = lax.ppermute(ancestors, "dom", [(0, 1), (3, 2)])
        blocks = [private_caches, near, middle, far]
    else:
        blocks = [private_caches] + [
            lax.ppermute(private_caches, "dom", [(i, (i + k) % dom_size) for i in range(dom_size)])
            for k in range(1, dom_size)
        ]

    query_latent = jnp.einsum("phn,hnc->phc", q_nope, w_uk, preferred_element_type=F32).astype(BF16)
    own = jnp.concatenate([query_latent, q_rope], axis=2).reshape(local * heads, width)

    def pairs(turn, flip):
        return [
            (x * cores + c, (x + turn) % chips * cores + (c ^ flip))
            for x in range(chips)
            for c in range(cores)
        ]

    routes = [(t, f) for t in range(chips) for f in range(cores)]
    queries = [own if r == (0, 0) else lax.ppermute(own, "seq", pairs(*r)) for r in routes]
    keys = prefix.T
    stages = []
    for k in range(0, len(routes), 2):
        stages += prefix_attention(queries[k : k + 2], keys, rank)
        if inner and k == 0:
            chosen = pl.pallas_call(
                functools.partial(select_kernel, len(blocks)),
                out_shape=jax.ShapeDtypeStruct(private_caches.shape, BF16),
                in_specs=[SMEM] * 2 + [ANY] * (len(blocks) + 1),
                out_specs=ANY,
                scratch_shapes=[pltpu.SemaphoreType.DMA((local,))],
                compiler_params=PARAMS,
                name="select",
            )(theirs, place, *blocks, stages[1])
            blocks.append(lax.ppermute(chosen, "dom", [(1, 0), (2, 3)]))

    count = len(routes)
    rows = local * heads
    results = pl.pallas_call(
        functools.partial(suffix_kernel, count, len(blocks), inner, heads),
        out_shape=(jax.ShapeDtypeStruct(private_caches.shape, BF16),)
        + (jax.ShapeDtypeStruct((rows, rank + LANES), BF16),) * count,
        in_specs=[SMEM] * 3 + [VMEM] * (1 + count + len(stages)) + [ANY] * len(blocks),
        out_specs=(VMEM,) * (1 + count),
        scratch_shapes=[
            pltpu.VMEM((local, span, width), BF16),
            pltpu.SemaphoreType.DMA((local,)),
        ],
        compiler_params=PARAMS,
        name="suffix_attention",
    )(ancestors, lengths, place, new_latent, *queries, *stages, *blocks)
    new_caches, parts = results[0], results[1:]

    parts = [
        part if r == (0, 0) else lax.ppermute(part, "seq", [(b, a) for a, b in pairs(*r)])
        for r, part in zip(routes, parts)
    ]
    latent_out = pl.pallas_call(
        functools.partial(merge_kernel, count),
        out_shape=jax.ShapeDtypeStruct((rows, rank), BF16),
        in_specs=[VMEM] * count,
        out_specs=VMEM,
        compiler_params=PARAMS,
        name="merge",
    )(*parts)
    head_values = jnp.einsum(
        "phc,hcv->phv", latent_out.reshape(local, heads, rank), w_uv, preferred_element_type=F32
    ).astype(BF16)
    return (head_values, new_caches)


def solution(mesh):
    placed = (
        P(("group", "dom"), "seq", None),
        P(("group", "dom"), "seq", None),
        P("seq", None, None),
        P("seq", None, None),
        P(("group", "seq"), None),
        P(("group", "dom"), "seq", None),
        P(("group", "dom"), None),
        P(("group", "dom")),
        P("group"),
    )
    return jax.shard_map(
        on_device,
        mesh=mesh,
        in_specs=placed,
        out_specs=(P(("group", "dom"), "seq", None), P(("group", "dom"), "seq", None)),
        check_vma=False,
    )
```

```python
import functools
import math

import jax
import jax.numpy as jnp
from jax import lax
from jax.experimental import pallas as pl
from jax.experimental.pallas import tpu as pltpu
from jax.sharding import PartitionSpec as P

ROPE = 64
NOPE = 128
SCALE2 = (NOPE + ROPE) ** (-0.5) * math.log2(math.e)
HIDDEN = -1e30
LANES = 128
F32 = jnp.float32
BF16 = jnp.bfloat16
NT = (((1,), (1,)), ((), ()))

VMEM = pl.BlockSpec(memory_space=pltpu.VMEM)
SMEM = pl.BlockSpec(memory_space=pltpu.SMEM)
ANY = pl.BlockSpec(memory_space=pl.ANY)
PARAMS = pltpu.CompilerParams(vmem_limit_bytes=40 * 1024 * 1024)


def prefix_kernel(count, tiles, *refs):
    query_refs = refs[:count]
    keys_ref, acc_ref, max_ref, sum_ref = refs[count:]
    rank = acc_ref.shape[1]
    tile = keys_ref.shape[1] // tiles
    queries = jnp.concatenate([ref[...] for ref in query_refs], axis=0)
    for i in range(tiles):
        part = pl.ds(i * tile, tile)
        scores = jnp.dot(queries, keys_ref[:, part], preferred_element_type=F32) * SCALE2
        top = jnp.max(scores, axis=1, keepdims=True)
        if i > 0:
            top = jnp.maximum(top, largest)
        weights = jnp.exp2(scores - top)
        total = jnp.sum(weights, axis=1, keepdims=True)
        acc = lax.dot_general(
            weights.astype(BF16), keys_ref[:rank, part], NT, preferred_element_type=F32
        )
        if i > 0:
            factor = jnp.exp2(largest - top)
            total = total + running * factor
            acc = acc + acc_ref[...] * factor
        largest, running = top, total
        acc_ref[...] = acc
    max_ref[...] = jnp.broadcast_to(largest, max_ref.shape)
    sum_ref[...] = jnp.broadcast_to(running, sum_ref.shape)


def prefix_attention(queries, keys, rank, tiles=4):
    rows = sum(q.shape[0] for q in queries)
    width, length = keys.shape
    stat = jax.ShapeDtypeStruct((rows, LANES), F32)
    return pl.pallas_call(
        functools.partial(prefix_kernel, len(queries), tiles),
        out_shape=(jax.ShapeDtypeStruct((rows, rank), F32), stat, stat),
        in_specs=[VMEM] * (len(queries) + 1),
        out_specs=(VMEM,) * 3,
        compiler_params=PARAMS,
        cost_estimate=pl.CostEstimate(
            flops=2 * rows * length * (width + rank),
            bytes_accessed=2 * width * length,
            transcendentals=rows * length,
        ),
        name="prefix_attention",
    )(*queries, keys)


def start_copies(count, block_refs, picks, out_ref, sems):
    for p, (which, slot) in enumerate(picks):
        for k in range(count):

            @pl.when(which == k)
            def _():
                pltpu.make_async_copy(block_refs[k].at[slot], out_ref.at[p], sems.at[p]).start()


def wait_copies(block_refs, out_ref, sems):
    for p in range(out_ref.shape[0]):
        pltpu.make_async_copy(block_refs[0].at[0], out_ref.at[p], sems.at[p]).wait()


def suffix_kernel(count, sources, line, heads, *refs):
    anc, lens, place, fresh_ref = refs[:4]
    refs = refs[4:]
    query_refs, refs = refs[:count], refs[count:]
    stage_refs, refs = refs[: 3 * (count // 2)], refs[3 * (count // 2) :]
    block_refs, refs = refs[:sources], refs[sources:]
    cache_ref, refs = refs[0], refs[1:]
    keep_ref, give_ref, moved, sems = refs
    local, span, width = moved.shape
    rank = stage_refs[0].shape[1]

    picks = []
    for p in range(local):
        owner = lax.div(anc[p], local)
        slot = lax.rem(anc[p], local)
        if line:
            apart = jnp.bitwise_xor(owner, place[1])
            ends_line = (place[1] == 0) | (place[1] == 3)
            which = jnp.where(ends_line & (apart > 1), apart + 2, apart)
        else:
            which = lax.rem(place[1] - owner + sources, sources)
        picks.append((which, slot))
    start_copies(sources, block_refs, picks, moved, sems)

    cols, half = local * span, 2 * heads * local
    start = place[0] * span
    ends = [lens[anc[p]] for p in range(local)]
    col = lax.broadcasted_iota(jnp.int32, (1, cols), 1)
    row = lax.broadcasted_iota(jnp.int32, (half, 1), 0)
    col_of = jnp.zeros_like(col)
    row_of = jnp.zeros_like(row)
    limit = jnp.full_like(col, ends[0] - start)
    for p in range(1, local):
        col_of = col_of + (col >= p * span).astype(jnp.int32)
        limit = jnp.where(col >= p * span, ends[p] - start + p * span, limit)
    for k in range(2):
        for p in range(local):
            row_of = jnp.where(row >= (k * local + p) * heads, p, row_of)
    col_of = jnp.where(col < limit, col_of, -1)
    seen = row_of == col_of
    row_at = start + lax.broadcasted_iota(jnp.int32, (span, width), 0)

    wait_copies(block_refs, moved, sems)
    for p in range(local):
        cache_ref[p] = jnp.where(row_at == ends[p], fresh_ref[pl.ds(p, 1), :], moved[p])
    keys = moved[...].reshape(cols, width)
    for k in range(count // 2):
        queries = jnp.concatenate([query_refs[2 * k][...], query_refs[2 * k + 1][...]], axis=0)
        acc_ref, max_ref, sum_ref = stage_refs[3 * k : 3 * k + 3]
        scores = lax.dot_general(queries, keys, NT, preferred_element_type=F32) * SCALE2
        scores = jnp.where(seen, scores, HIDDEN)
        before = max_ref[:, 0:1]
        top = jnp.maximum(before, jnp.max(scores, axis=1, keepdims=True))
        weights = jnp.where(seen, jnp.exp2(scores - top), 0.0)
        factor = jnp.exp2(before - top)
        total = sum_ref[:, 0:1] * factor + jnp.sum(weights, axis=1, keepdims=True)
        acc = acc_ref[...] * factor + jnp.dot(
            weights.astype(BF16), keys[:, :rank], preferred_element_type=F32
        )
        level = top + jnp.log2(total)
        part = packed(acc * (1.0 / total), level)
        keep_ref[pl.ds(k * half // 2, half // 2)] = part[: half // 2]
        give_ref[pl.ds(k * half // 2, half // 2)] = part[half // 2 :]


def packed(values, level):
    rows = values.shape[0]
    lane = lax.broadcasted_iota(jnp.int32, (rows, LANES), 1)
    high = level.astype(BF16).astype(F32)
    middle = (level - high).astype(BF16).astype(F32)
    low = level - high - middle
    stats = jnp.where(lane == 0, high, jnp.where(lane == 1, middle, jnp.where(lane == 2, low, 0.0)))
    return jnp.concatenate([values.astype(BF16), stats.astype(BF16)], axis=1)


def merged(parts, rank):
    levels = [jnp.sum(part[:, rank:].astype(F32), axis=1, keepdims=True) for part in parts]
    top = functools.reduce(jnp.maximum, levels)
    shares = [jnp.exp2(level - top) for level in levels]
    whole = functools.reduce(jnp.add, shares)
    acc = functools.reduce(
        jnp.add, [share * part[:, :rank].astype(F32) for share, part in zip(shares, parts)]
    )
    return acc * (1.0 / whole), top + jnp.log2(whole)


def chip_kernel(chips, keep_ref, got_ref, *out_refs):
    rows, rank = out_refs[0].shape[0], out_refs[0].shape[1] - LANES
    for t in reversed(range(chips)):
        part = pl.ds(t * rows, rows)
        out_refs[t][...] = packed(*merged([keep_ref[part], got_ref[part]], rank))


def final_kernel(*refs):
    out_ref = refs[-1]
    values, _ = merged([ref[...] for ref in refs[:-1]], out_ref.shape[1])
    out_ref[...] = values.astype(BF16)


def on_device(q_nope, q_rope, w_uk, w_uv, prefix, private_caches, new_latent, ancestors, lengths):
    local, heads = q_nope.shape[:2]
    span, width = private_caches.shape[1:]
    rank = w_uv.shape[1]
    seq_size, dom_size = lax.axis_size("seq"), lax.axis_size("dom")
    cores = 2 if seq_size % 2 == 0 else 1
    chips = seq_size // cores
    place = jnp.stack([lax.axis_index("seq"), lax.axis_index("dom")]).astype(jnp.int32)

    line = dom_size == 4
    if line:
        near = lax.ppermute(private_caches, "dom", [(0, 1), (1, 0), (2, 3), (3, 2)])
        far = lax.ppermute(private_caches, "dom", [(1, 2), (2, 1)])
    else:
        blocks = [private_caches] + [
            lax.ppermute(private_caches, "dom", [(i, (i + k) % dom_size) for i in range(dom_size)])
            for k in range(1, dom_size)
        ]

    query_latent = jnp.einsum("phn,hnc->phc", q_nope, w_uk, preferred_element_type=F32).astype(BF16)
    own = jnp.concatenate([query_latent, q_rope], axis=2).reshape(local * heads, width)

    def pairs(turn, flip):
        return [
            (x * cores + c, (x + turn) % chips * cores + (c ^ flip))
            for x in range(chips)
            for c in range(cores)
        ]

    routes = [(t, f) for t in range(chips) for f in range(cores)]
    queries = [own if r == (0, 0) else lax.ppermute(own, "seq", pairs(*r)) for r in routes]
    keys = prefix.T
    if line:
        near, far, queries[1] = lax.optimization_barrier((near, far, queries[1]))
        inner_middle = lax.ppermute(near, "dom", [(1, 2), (2, 1)])
        outer_middle = lax.ppermute(far, "dom", [(1, 0), (2, 3)])
    stages = []
    for k in range(0, len(routes), 2):
        stages += prefix_attention(queries[k : k + 2], keys, rank)
        if line and k == 0:
            inner_middle, stages[1] = lax.optimization_barrier((inner_middle, stages[1]))
            outer_far = lax.ppermute(inner_middle, "dom", [(1, 0), (2, 3)])
    if line:
        blocks = [private_caches, near, inner_middle, far, outer_middle, outer_far]

    count = len(routes)
    rows = local * heads
    packed_rows = jax.ShapeDtypeStruct((chips * rows, rank + LANES), BF16)
    new_caches, keep, give = pl.pallas_call(
        functools.partial(suffix_kernel, count, len(blocks), line, heads),
        out_shape=(jax.ShapeDtypeStruct(private_caches.shape, BF16), packed_rows, packed_rows),
        in_specs=[SMEM] * 3 + [VMEM] * (1 + count + len(stages)) + [ANY] * len(blocks),
        out_specs=(VMEM,) * 3,
        scratch_shapes=[
            pltpu.VMEM((local, span, width), BF16),
            pltpu.SemaphoreType.DMA((local,)),
        ],
        compiler_params=PARAMS,
        name="suffix_attention",
    )(ancestors, lengths, place, new_latent, *queries, *stages, *blocks)

    got = lax.ppermute(give, "seq", pairs(0, 1))
    parts = pl.pallas_call(
        functools.partial(chip_kernel, chips),
        out_shape=[jax.ShapeDtypeStruct((rows, rank + LANES), BF16)] * chips,
        in_specs=[VMEM] * 2,
        out_specs=[VMEM] * chips,
        compiler_params=PARAMS,
        name="chip_merge",
    )(keep, got)
    parts = [parts[0]] + [
        lax.ppermute(parts[t], "seq", [(b, a) for a, b in pairs(t, 0)]) for t in range(1, chips)
    ]
    latent_out = pl.pallas_call(
        final_kernel,
        out_shape=jax.ShapeDtypeStruct((rows, rank), BF16),
        in_specs=[VMEM] * chips,
        out_specs=VMEM,
        compiler_params=PARAMS,
        name="merge",
    )(*parts)
    head_values = jnp.einsum(
        "phc,hcv->phv", latent_out.reshape(local, heads, rank), w_uv, preferred_element_type=F32
    ).astype(BF16)
    return (head_values, new_caches)


def solution(mesh):
    placed = (
        P(("group", "dom"), "seq", None),
        P(("group", "dom"), "seq", None),
        P("seq", None, None),
        P("seq", None, None),
        P(("group", "seq"), None),
        P(("group", "dom"), "seq", None),
        P(("group", "dom"), None),
        P(("group", "dom")),
        P("group"),
    )
    return jax.shard_map(
        on_device,
        mesh=mesh,
        in_specs=placed,
        out_specs=(P(("group", "dom"), "seq", None), P(("group", "dom"), "seq", None)),
        check_vma=False,
    )
```

```python
import functools
import math

import jax
import jax.numpy as jnp
from jax import lax
from jax.experimental import pallas as pl
from jax.experimental.pallas import tpu as pltpu
from jax.sharding import PartitionSpec as P

ROPE = 64
NOPE = 128
SCALE2 = (NOPE + ROPE) ** (-0.5) * math.log2(math.e)
HIDDEN = -1e30
LANES = 128
F32 = jnp.float32
BF16 = jnp.bfloat16
NT = (((1,), (1,)), ((), ()))

VMEM = pl.BlockSpec(memory_space=pltpu.VMEM)
SMEM = pl.BlockSpec(memory_space=pltpu.SMEM)
ANY = pl.BlockSpec(memory_space=pl.ANY)
HBM = pl.BlockSpec(memory_space=pltpu.HBM)
PARAMS = pltpu.CompilerParams(vmem_limit_bytes=40 * 1024 * 1024)
STREAM = pltpu.CompilerParams(vmem_limit_bytes=51 * 1024 * 1024)


def shape(dims, dtype=BF16):
    return jax.ShapeDtypeStruct(dims, dtype)


def pack_kernel(rank, cache_ref, out_ref):
    local, span, width = cache_ref.shape
    for p in range(local):
        out_ref[pl.ds(p * span, span)] = cache_ref[p, :, :rank]
    rope = jnp.concatenate([cache_ref[p, :, rank:] for p in range(local)], axis=1)
    tail = out_ref.shape[0] - local * span
    out_ref[pl.ds(local * span, tail)] = jnp.concatenate(
        [rope[i : i + tail] for i in range(0, span, tail)], axis=1
    )


def project_kernel(
    pieces, nope_ref, rope_ref, w_hbm, own_ref, nope, turned, w_ref, sems
):
    local, heads = nope_ref.shape[:2]
    rank = w_ref.shape[2]
    piece = heads // pieces
    fetches = [
        pltpu.make_async_copy(
            w_hbm.at[pl.ds(i * piece, piece)], w_ref.at[pl.ds(i * piece, piece)], sems.at[i]
        )
        for i in range(pieces)
    ]
    for fetch in fetches:
        fetch.start()
    for p in range(local):
        nope[pl.ds(p, heads, stride=local), :] = nope_ref[p].astype(F32)
        wide = rope_ref[p].astype(F32)
        wide = jnp.concatenate([wide, jnp.zeros((heads, LANES - wide.shape[1]), F32)], axis=1)
        turned[pl.ds(p, heads, stride=local), :] = wide
    width = nope.shape[1]
    first = lax.broadcasted_iota(jnp.int32, (2 * local, width), 0) < local

    def pair(h):
        two = nope[pl.ds(h * local, 2 * local), :]
        left = jnp.concatenate([jnp.where(first, two, 0.0), jnp.where(first, 0.0, two)], axis=1)
        weights = w_ref[pl.ds(h, 2)].reshape(2 * width, rank)
        return jnp.dot(left.astype(BF16), weights, preferred_element_type=F32)

    own_ref[:, rank:] = turned[:, : rope_ref.shape[2]].astype(BF16)
    for h in range(0, heads, 4):
        if h % piece == 0:
            fetches[h // piece].wait()
        own_ref[pl.ds(h * local, 4 * local), :rank] = jnp.concatenate(
            [pair(i) for i in (h, h + 2)], axis=0
        ).astype(BF16)


def prefix_kernel(count, tiles, *refs):
    query_refs = refs[:count]
    keys_hbm, acc_ref, max_ref, sum_ref, keys_ref, sems = refs[count:]
    rank = acc_ref.shape[1]
    tile = keys_ref.shape[1] // tiles

    def fetch(i):
        part = pl.ds(i * tile, tile)
        return pltpu.make_async_copy(keys_hbm.at[:, part], keys_ref.at[:, part], sems.at[i])

    for i in range(tiles):
        fetch(i).start()
    queries = jnp.concatenate([ref[...] for ref in query_refs], axis=0)
    for i in range(tiles):
        part = pl.ds(i * tile, tile)
        fetch(i).wait()
        scores = jnp.dot(queries, keys_ref[:, part], preferred_element_type=F32) * SCALE2
        top = jnp.max(scores, axis=1, keepdims=True)
        if i > 0:
            top = jnp.maximum(top, largest)
        weights = jnp.exp2(scores - top)
        total = jnp.sum(weights, axis=1, keepdims=True)
        acc = lax.dot_general(
            weights.astype(BF16), keys_ref[:rank, part], NT, preferred_element_type=F32
        )
        if i > 0:
            factor = jnp.exp2(largest - top)
            total = total + running * factor
            acc = acc + acc_ref[...] * factor
        largest, running = top, total
        acc_ref[...] = acc
    max_ref[...] = jnp.broadcast_to(largest, max_ref.shape)
    sum_ref[...] = jnp.broadcast_to(running, sum_ref.shape)


def prefix_attention(queries, keys, rank, tiles=4):
    rows = sum(q.shape[0] for q in queries)
    width, length = keys.shape
    stat = shape((rows, LANES), F32)
    return pl.pallas_call(
        functools.partial(prefix_kernel, len(queries), tiles),
        out_shape=(shape((rows, rank), F32), stat, stat),
        in_specs=[VMEM] * len(queries) + [HBM],
        out_specs=(VMEM,) * 3,
        scratch_shapes=[pltpu.VMEM(keys.shape, BF16), pltpu.SemaphoreType.DMA((tiles,))],
        compiler_params=STREAM,
        cost_estimate=pl.CostEstimate(
            flops=2 * rows * length * (width + rank),
            bytes_accessed=2 * width * length,
            transcendentals=rows * length,
        ),
        name="prefix_attention",
    )(*queries, keys)


def packed(values, level):
    rows = values.shape[0]
    lane = lax.broadcasted_iota(jnp.int32, (rows, LANES), 1)
    high = level.astype(BF16).astype(F32)
    middle = (level - high).astype(BF16).astype(F32)
    low = level - high - middle
    stats = jnp.where(lane == 0, high, jnp.where(lane == 1, middle, jnp.where(lane == 2, low, 0.0)))
    return jnp.concatenate([values.astype(BF16), stats.astype(BF16)], axis=1)


def merged(parts, rank):
    levels = [jnp.sum(part[:, rank:].astype(F32), axis=1, keepdims=True) for part in parts]
    top = functools.reduce(jnp.maximum, levels)
    shares = [jnp.exp2(level - top) for level in levels]
    whole = functools.reduce(jnp.add, shares)
    acc = functools.reduce(
        jnp.add, [share * part[:, :rank].astype(F32) for share, part in zip(shares, parts)]
    )
    return acc * (1.0 / whole), top + jnp.log2(whole)


def attend_suffix(refs, latents, ropes, ends, start, span, keep_ref, give_ref):
    local = len(ends)
    first_ref, second_ref, acc_ref, max_ref, sum_ref = refs
    rows, rank = acc_ref.shape
    half, cols = rows // 2, local * span
    col = lax.broadcasted_iota(jnp.int32, (1, cols), 1)
    col_of = jnp.zeros_like(col)
    limit = jnp.full_like(col, ends[0] - start)
    for p in range(1, local):
        col_of = col_of + (col >= p * span).astype(jnp.int32)
        limit = jnp.where(col >= p * span, ends[p] - start + p * span, limit)
    col_of = jnp.where(col < limit, col_of, -1)
    row_of = lax.rem(lax.broadcasted_iota(jnp.int32, (rows, 1), 0), local)
    seen = row_of == col_of

    queries = jnp.concatenate([first_ref[...], second_ref[...]], axis=0)
    scores = lax.dot_general(queries[:, :rank], latents, NT, preferred_element_type=F32)
    scores = scores + lax.dot_general(queries[:, rank:], ropes, NT, preferred_element_type=F32)
    scores = jnp.where(seen, scores * SCALE2, HIDDEN)
    before = max_ref[:, 0:1]
    top = jnp.maximum(before, jnp.max(scores, axis=1, keepdims=True))
    weights = jnp.where(seen, jnp.exp2(scores - top), 0.0)
    factor = jnp.exp2(before - top)
    total = sum_ref[:, 0:1] * factor + jnp.sum(weights, axis=1, keepdims=True)
    acc = acc_ref[...] * factor + jnp.dot(weights.astype(BF16), latents, preferred_element_type=F32)
    part = packed(acc * (1.0 / total), top + jnp.log2(total))
    keep_ref[...] = part[:half]
    give_ref[...] = part[half:]


def far_kernel(stages, sources, line, *refs):
    anc, lens, place = refs[:3]
    refs = refs[3:]
    stage_refs, refs = refs[: 5 * stages], refs[5 * stages :]
    block_refs, refs = refs[:sources], refs[sources:]
    moved_ref, rope_ref, refs = refs[0], refs[1], refs[2:]
    keep_refs, give_refs = refs[:stages], refs[stages : 2 * stages]
    folded, sems = refs[2 * stages :]
    local, tail, rank = folded.shape
    span = moved_ref.shape[0] // local
    rope = rope_ref.shape[1]

    def copies(p, k, slot):
        return (
            pltpu.make_async_copy(
                block_refs[k].at[pl.ds(pl.multiple_of(slot * span, span), span)],
                moved_ref.at[pl.ds(p * span, span)],
                sems.at[p],
            ),
            pltpu.make_async_copy(
                block_refs[k].at[pl.ds(local * span, tail)], folded.at[p], sems.at[local + p]
            ),
        )

    slots = []
    for p in range(local):
        owner = lax.div(anc[p], local)
        slots.append(lax.rem(anc[p], local))
        if line:
            apart = jnp.bitwise_xor(owner, place[1])
            at_end = (place[1] == 0) | (place[1] == 3)
            which = jnp.where(at_end & (apart > 1), apart + 2, apart)
        else:
            which = lax.rem(place[1] - owner + sources, sources)
        for k in range(sources):

            @pl.when(which == k)
            def _():
                for copy in copies(p, k, slots[p]):
                    copy.start()

    for p in range(local):
        for copy in copies(p, 0, 0):
            copy.wait()

    for p in range(local):
        for i in range(span // tail):
            from_slot = [
                folded[p, :, (i * local + q) * rope : (i * local + q + 1) * rope] for q in range(local)
            ]
            picked = from_slot[0]
            for q in range(1, local):
                picked = jnp.where(slots[p] == q, from_slot[q], picked)
            rope_ref[pl.ds(p * span + i * tail, tail)] = picked

    ends = [lens[anc[p]] for p in range(local)]
    for k in range(stages):
        attend_suffix(
            stage_refs[5 * k : 5 * k + 5],
            moved_ref[...],
            rope_ref[...],
            ends,
            place[0] * span,
            span,
            keep_refs[k],
            give_refs[k],
        )


def near_kernel(anc, lens, place, fresh_ref, *refs):
    stage_refs = refs[:5]
    moved_ref, rope_ref, cache_ref, keep_ref, give_ref = refs[5:]
    local, span, width = cache_ref.shape
    rank = moved_ref.shape[1]
    start = place[0] * span
    ends = [lens[anc[p]] for p in range(local)]
    attend_suffix(
        stage_refs, moved_ref[...], rope_ref[...], ends, start, span, keep_ref, give_ref
    )
    for p in range(local):
        at = start + lax.broadcasted_iota(jnp.int32, (span, 1), 0) == ends[p]
        part = pl.ds(p * span, span)
        cache_ref[p, :, :rank] = jnp.where(at, fresh_ref[pl.ds(p, 1), :rank], moved_ref[part])
        cache_ref[p, :, rank:] = jnp.where(at, fresh_ref[pl.ds(p, 1), rank:], rope_ref[part])


def chip_kernel(count, *refs):
    for k in range(count):
        out_ref = refs[2 * count + k]
        rank = out_ref.shape[1] - LANES
        out_ref[...] = packed(*merged([refs[k][...], refs[count + k][...]], rank))


def chip_merge(keep, got):
    return pl.pallas_call(
        functools.partial(chip_kernel, len(keep)),
        out_shape=[shape(k.shape) for k in keep],
        in_specs=[VMEM] * (2 * len(keep)),
        out_specs=[VMEM] * len(keep),
        compiler_params=PARAMS,
        name="chip_merge",
    )(*keep, *got)


def final_kernel(count, *refs):
    part_refs, (w_ref, out_ref, values) = refs[:count], refs[count:]
    heads, rank, reach = w_ref.shape
    local = out_ref.shape[0]
    latent = merged([ref[...] for ref in part_refs], rank)[0].astype(BF16)
    first = lax.broadcasted_iota(jnp.int32, (2 * local, reach), 0) < local
    for h in range(0, heads, 2):
        two = latent[h * local : (h + 2) * local]
        here = jnp.dot(two, w_ref[h], preferred_element_type=F32)
        there = jnp.dot(two, w_ref[h + 1], preferred_element_type=F32)
        values[pl.ds(h * local, 2 * local), :] = jnp.where(first, here, there)
    for p in range(local):
        out_ref[p] = values[pl.ds(p, heads, stride=local), :].astype(BF16)


def on_device(q_nope, q_rope, w_uk, w_uv, prefix, private_caches, new_latent, ancestors, lengths):
    local, heads, nope = q_nope.shape
    span, width = private_caches.shape[1:]
    rank, reach = w_uv.shape[1:]
    rope = width - rank
    rows = local * heads
    seq_size, dom_size = lax.axis_size("seq"), lax.axis_size("dom")
    cores = 2
    chips = seq_size // cores
    place = jnp.stack([lax.axis_index("seq"), lax.axis_index("dom")]).astype(jnp.int32)
    tail = span * local * rope // rank

    block = pl.pallas_call(
        functools.partial(pack_kernel, rank),
        out_shape=shape((local * span + tail, rank)),
        in_specs=[VMEM],
        out_specs=VMEM,
        compiler_params=PARAMS,
        name="pack",
    )(private_caches)
    line = dom_size == 4
    if line:
        near = lax.ppermute(block, "dom", [(0, 1), (1, 0), (2, 3), (3, 2)])
        far = lax.ppermute(block, "dom", [(1, 2), (2, 1)])
    else:
        blocks = [block] + [
            lax.ppermute(block, "dom", [(i, (i + k) % dom_size) for i in range(dom_size)])
            for k in range(1, dom_size)
        ]

    pieces = math.gcd(heads // 4, 4)
    own = pl.pallas_call(
        functools.partial(project_kernel, pieces),
        out_shape=shape((rows, width)),
        in_specs=[VMEM] * 2 + [HBM],
        out_specs=VMEM,
        scratch_shapes=[
            pltpu.VMEM((rows, nope), F32),
            pltpu.VMEM((rows, LANES), F32),
            pltpu.VMEM(w_uk.shape, BF16),
            pltpu.SemaphoreType.DMA((pieces,)),
        ],
        compiler_params=STREAM,
        name="project",
    )(q_nope, q_rope, w_uk)
    keys = prefix.T

    def pairs(turn, flip):
        return [
            (x * cores + c, (x + turn) % chips * cores + (c ^ flip))
            for x in range(chips)
            for c in range(cores)
        ]

    def back(turn, flip):
        return [(b, a) for a, b in pairs(turn, flip)]

    routes = [(t, f) for t in range(chips) for f in range(cores)]
    queries = [own if r == (0, 0) else lax.ppermute(own, "seq", pairs(*r)) for r in routes]
    if line:
        near, far, queries[1] = lax.optimization_barrier((near, far, queries[1]))
        inner_middle = lax.ppermute(near, "dom", [(1, 2), (2, 1)])
        outer_middle = lax.ppermute(far, "dom", [(1, 0), (2, 3)])
    stages = []
    for t in range(chips):
        stage = [*queries[2 * t : 2 * t + 2], *prefix_attention(queries[2 * t : 2 * t + 2], keys, rank)]
        stages.append(stage)
        if line and t == 0:
            inner_middle, stage[3] = lax.optimization_barrier((inner_middle, stage[3]))
            outer_far = lax.ppermute(inner_middle, "dom", [(1, 0), (2, 3)])
    if line:
        blocks = [block, near, inner_middle, far, outer_middle, outer_far]

    part = shape((rows, rank + LANES))
    others = chips - 1
    far_results = pl.pallas_call(
        functools.partial(far_kernel, others, len(blocks), line),
        out_shape=[shape((local * span, rank)), shape((local * span, rope))] + [part] * (2 * others),
        in_specs=[SMEM] * 3 + [VMEM] * (5 * others) + [ANY] * len(blocks),
        out_specs=[VMEM] * (2 + 2 * others),
        scratch_shapes=[
            pltpu.VMEM((local, tail, rank), BF16),
            pltpu.SemaphoreType.DMA((2 * local,)),
        ],
        compiler_params=PARAMS,
        name="suffix_far",
    )(ancestors, lengths, place, *[a for stage in stages[1:] for a in stage], *blocks)
    moved, moved_rope = far_results[:2]
    keep, give = far_results[2 : 2 + others], far_results[2 + others :]
    sums = chip_merge(keep, [lax.ppermute(g, "seq", pairs(0, 1)) for g in give])
    parts = [lax.ppermute(s, "seq", back(t, 0)) for t, s in enumerate(sums, 1)]

    new_caches, keep, give = pl.pallas_call(
        near_kernel,
        out_shape=[shape(private_caches.shape), part, part],
        in_specs=[SMEM] * 3 + [VMEM] * 8,
        out_specs=[VMEM] * 3,
        compiler_params=PARAMS,
        name="suffix_near",
    )(ancestors, lengths, place, new_latent, *stages[0], moved, moved_rope)
    parts += chip_merge([keep], [lax.ppermute(give, "seq", pairs(0, 1))])

    head_values = pl.pallas_call(
        functools.partial(final_kernel, chips),
        out_shape=shape((local, heads, reach)),
        in_specs=[VMEM] * (chips + 1),
        out_specs=VMEM,
        scratch_shapes=[pltpu.VMEM((rows, reach), F32)],
        compiler_params=PARAMS,
        name="final",
    )(*parts, w_uv)
    return (head_values, new_caches)


def solution(mesh):
    placed = (
        P(("group", "dom"), "seq", None),
        P(("group", "dom"), "seq", None),
        P("seq", None, None),
        P("seq", None, None),
        P(("group", "seq"), None),
        P(("group", "dom"), "seq", None),
        P(("group", "dom"), None),
        P(("group", "dom")),
        P("group"),
    )
    return jax.shard_map(
        on_device,
        mesh=mesh,
        in_specs=placed,
        out_specs=(P(("group", "dom"), "seq", None), P(("group", "dom"), "seq", None)),
        check_vma=False,
    )
```

```python
import functools
import math

import jax
import jax.numpy as jnp
from jax import lax
from jax.experimental import pallas as pl
from jax.experimental.pallas import tpu as pltpu
from jax.sharding import PartitionSpec as P

ROPE = 64
NOPE = 128
SCALE2 = (NOPE + ROPE) ** (-0.5) * math.log2(math.e)
HIDDEN = -1e30
LANES = 128
F32 = jnp.float32
BF16 = jnp.bfloat16
NT = (((1,), (1,)), ((), ()))

VMEM = pl.BlockSpec(memory_space=pltpu.VMEM)
SMEM = pl.BlockSpec(memory_space=pltpu.SMEM)
ANY = pl.BlockSpec(memory_space=pl.ANY)
HBM = pl.BlockSpec(memory_space=pltpu.HBM)
PARAMS = pltpu.CompilerParams(vmem_limit_bytes=40 * 1024 * 1024)
STREAM = pltpu.CompilerParams(vmem_limit_bytes=51 * 1024 * 1024)


def shape(dims, dtype=BF16):
    return jax.ShapeDtypeStruct(dims, dtype)


def pack_kernel(rank, cache_ref, out_ref):
    local, span, width = cache_ref.shape
    half = out_ref.shape[0] // 2
    some = span // 2
    tail = half - local * some
    rope = jnp.concatenate([cache_ref[p, :, rank:] for p in range(local)], axis=1)
    for h in range(2):
        for p in range(local):
            out_ref[pl.ds(h * half + p * some, some)] = cache_ref[p, pl.ds(h * some, some), :rank]
        out_ref[pl.ds(h * half + local * some, tail)] = jnp.concatenate(
            [rope[h * some + i : h * some + i + tail] for i in range(0, some, tail)], axis=1
        )


def project_kernel(pieces, local, nope_ref, rope_ref, w_hbm, own_ref, w_ref, sems):
    heads, _, rank = w_ref.shape
    piece = heads // pieces
    fetches = [
        pltpu.make_async_copy(
            w_hbm.at[pl.ds(i * piece, piece)], w_ref.at[pl.ds(i * piece, piece)], sems.at[i]
        )
        for i in range(pieces)
    ]
    for fetch in fetches[:2]:
        fetch.start()
    nope = nope_ref[...].astype(F32)
    width = nope.shape[1]
    first = lax.broadcasted_iota(jnp.int32, (2 * local, width), 0) < local

    def pair(h):
        two = nope[h * local : (h + 2) * local]
        left = jnp.concatenate([jnp.where(first, two, 0.0), jnp.where(first, 0.0, two)], axis=1)
        weights = w_ref[pl.ds(h, 2)].reshape(2 * width, rank)
        return jnp.dot(left.astype(BF16), weights, preferred_element_type=F32)

    own_ref[:, rank:] = rope_ref[...]
    for h in range(0, heads, 4):
        if h % piece == 0:
            at = h // piece
            fetches[at].wait()
            if at + 2 < pieces:
                fetches[at + 2].start()
        own_ref[pl.ds(h * local, 4 * local), :rank] = jnp.concatenate(
            [pair(i) for i in (h, h + 2)], axis=0
        ).astype(BF16)


def prefix_kernel(count, tiles, *refs):
    query_refs = refs[:count]
    keys_hbm, out_ref, max_ref, sum_ref, *give_ref, acc_ref, keys_ref, sems = refs[count:]
    rank = acc_ref.shape[1]
    parts = [pl.ds(begin, end - begin) for begin, end in zip(tiles, tiles[1:])]
    fetches = [
        pltpu.make_async_copy(keys_hbm.at[:, part], keys_ref.at[:, part], sems.at[i])
        for i, part in enumerate(parts)
    ]
    for fetch in fetches[:2]:
        fetch.start()
    queries = jnp.concatenate([ref[...] for ref in query_refs], axis=0)
    for i, part in enumerate(parts):
        fetches[i].wait()
        if i + 2 < len(parts):
            fetches[i + 2].start()
        scores = jnp.dot(queries, keys_ref[:, part], preferred_element_type=F32) * SCALE2
        top = jnp.max(scores, axis=1, keepdims=True)
        if i > 0:
            top = jnp.maximum(top, largest)
        weights = jnp.exp2(scores - top)
        total = jnp.sum(weights, axis=1, keepdims=True)
        acc = lax.dot_general(
            weights.astype(BF16), keys_ref[:rank, part], NT, preferred_element_type=F32
        )
        if i > 0:
            factor = jnp.exp2(largest - top)
            total = total + running * factor
            acc = acc + acc_ref[...] * factor
        largest, running = top, total
        if i < len(parts) - 1:
            acc_ref[...] = acc
    kept = out_ref.shape[0]
    out_ref[...] = acc[:kept]
    max_ref[...] = jnp.broadcast_to(largest[:kept], max_ref.shape)
    sum_ref[...] = jnp.broadcast_to(running[:kept], sum_ref.shape)
    if give_ref:
        level = largest[kept:] + jnp.log2(running[kept:])
        give_ref[0][...] = packed(acc[kept:] * (1.0 / running[kept:]), level)


def prefix_attention(queries, keys, rank, give):
    rows = sum(q.shape[0] for q in queries)
    kept = queries[0].shape[0] if give else rows
    width, length = keys.shape
    tiles = [0, length // 8] + [length * i // 4 for i in range(1, 5)]
    out = [shape((kept, rank), F32)] + [shape((kept, LANES), F32)] * 2
    if give:
        out.append(shape((rows - kept, rank + LANES)))
    return pl.pallas_call(
        functools.partial(prefix_kernel, len(queries), tiles),
        out_shape=out,
        in_specs=[VMEM] * len(queries) + [HBM],
        out_specs=[VMEM] * len(out),
        scratch_shapes=[
            pltpu.VMEM((rows, rank), F32),
            pltpu.VMEM(keys.shape, BF16),
            pltpu.SemaphoreType.DMA((len(tiles) - 1,)),
        ],
        compiler_params=STREAM,
        name="prefix_attention",
    )(*queries, keys)


def packed(values, level):
    rows = values.shape[0]
    lane = lax.broadcasted_iota(jnp.int32, (rows, LANES), 1)
    high = level.astype(BF16).astype(F32)
    middle = (level - high).astype(BF16).astype(F32)
    low = level - high - middle
    stats = jnp.where(lane == 0, high, jnp.where(lane == 1, middle, jnp.where(lane == 2, low, 0.0)))
    return jnp.concatenate([values.astype(BF16), stats.astype(BF16)], axis=1)


def merged(parts, rank):
    levels = [jnp.sum(part[:, rank:].astype(F32), axis=1, keepdims=True) for part in parts]
    top = functools.reduce(jnp.maximum, levels)
    shares = [jnp.exp2(level - top) for level in levels]
    whole = functools.reduce(jnp.add, shares)
    acc = functools.reduce(
        jnp.add, [share * part[:, :rank].astype(F32) for share, part in zip(shares, parts)]
    )
    return acc * (1.0 / whole), top + jnp.log2(whole)


def visible(rows, ends, starts, span):
    local = len(ends)
    cols = len(starts) * local * span
    col = lax.broadcasted_iota(jnp.int32, (1, cols), 1)
    col_of = jnp.zeros_like(col)
    limit = jnp.full_like(col, ends[0] - starts[0])
    for at in range(1, len(starts) * local):
        begin, p = at * span, at % local
        later = col >= begin
        col_of = jnp.where(later, p, col_of)
        limit = jnp.where(later, ends[p] - starts[at // local] + begin, limit)
    col_of = jnp.where(col < limit, col_of, -1)
    row_of = lax.rem(lax.broadcasted_iota(jnp.int32, (rows, 1), 0), local)
    return row_of == col_of


def attend(queries, keys, seen, rank, known):
    scores = lax.dot_general(queries, keys, NT, preferred_element_type=F32)
    scores = jnp.where(seen, scores * SCALE2, HIDDEN)
    top = jnp.max(scores, axis=1, keepdims=True)
    for level, _, _ in known:
        top = jnp.maximum(top, level)
    weights = jnp.where(seen, jnp.exp2(scores - top), 0.0)
    total = jnp.sum(weights, axis=1, keepdims=True)
    acc = jnp.dot(weights.astype(BF16), keys[:, :rank], preferred_element_type=F32)
    for level, mass, part in known:
        factor = jnp.exp2(level - top)
        total = total + mass * factor
        acc = acc + part * factor
    return packed(acc * (1.0 / total), top + jnp.log2(total))


def far_kernel(stages, sources, line, *refs):
    anc, lens, place = refs[:3]
    refs = refs[3:]
    stage_refs, refs = refs[: 5 * stages], refs[5 * stages :]
    count = max(ref for source in sources for ref, _ in source) + 1
    block_refs, refs = refs[:count], refs[count:]
    moved_ref, refs = refs[0], refs[1:]
    keep_refs, give_refs = refs[:stages], refs[stages : 2 * stages]
    folded, sems = refs[2 * stages :]
    local, _, tail, rank = folded.shape
    span = moved_ref.shape[0] // local
    some = span // 2
    rope = moved_ref.shape[1] - rank

    def copies(p, source, slot):
        found = []
        for h, (ref, base) in enumerate(source):
            at = pl.multiple_of(base + slot * some, 16)
            there = moved_ref.at[pl.ds(p * span + h * some, some), pl.ds(0, rank)]
            found.append((block_refs[ref].at[pl.ds(at, some)], there))
            found.append((block_refs[ref].at[pl.ds(base + local * some, tail)], folded.at[p, h]))
        return [pltpu.make_async_copy(a, b, sems.at[4 * p + i]) for i, (a, b) in enumerate(found)]

    slots = []
    for p in range(local):
        owner = lax.div(anc[p], local)
        slots.append(lax.rem(anc[p], local))
        if line:
            apart = jnp.bitwise_xor(owner, place[1])
            at_end = (place[1] == 0) | (place[1] == 3)
            which = jnp.where(at_end & (apart > 1), apart + 2, apart)
        else:
            which = lax.rem(place[1] - owner + len(sources), len(sources))
        for k, source in enumerate(sources):

            @pl.when(which == k)
            def _():
                for copy in copies(p, source, slots[p]):
                    copy.start()

    for p in range(local):
        for copy in copies(p, sources[0], 0):
            copy.wait()

    for p in range(local):
        for h in range(2):
            for i in range(some // tail):
                choices = [
                    folded[p, h, :, (i * local + q) * rope : (i * local + q + 1) * rope]
                    for q in range(local)
                ]
                picked = choices[0]
                for q in range(1, local):
                    picked = jnp.where(slots[p] == q, choices[q], picked)
                moved_ref[pl.ds(p * span + h * some + i * tail, tail), rank:] = picked

    ends = [lens[anc[p]] for p in range(local)]
    for k in range(stages):
        first_ref, second_ref, acc_ref, max_ref, sum_ref = stage_refs[5 * k : 5 * k + 5]
        queries = jnp.concatenate([first_ref[...], second_ref[...]], axis=0)
        seen = visible(queries.shape[0], ends, [place[0] * span], span)
        known = [(max_ref[:, 0:1], sum_ref[:, 0:1], acc_ref[...])]
        part = attend(queries, moved_ref[...], seen, rank, known)
        rows = first_ref.shape[0]
        keep_refs[k][...] = part[:rows]
        give_refs[k][...] = part[rows:]


def near_kernel(anc, lens, place, fresh_ref, *refs):
    query_ref, acc_ref, max_ref, sum_ref, got_ref, moved_ref, other_ref, cache_ref, part_ref = refs
    local, span, width = cache_ref.shape
    rank = acc_ref.shape[1]
    start, other = place[0] * span, jnp.bitwise_xor(place[0], 1) * span
    ends = [lens[anc[p]] for p in range(local)]
    keys = jnp.concatenate([moved_ref[...], other_ref[...]], axis=0)
    seen = visible(query_ref.shape[0], ends, [start, other], span)
    level = jnp.sum(got_ref[:, rank:].astype(F32), axis=1, keepdims=True)
    known = [
        (max_ref[:, 0:1], sum_ref[:, 0:1], acc_ref[...]),
        (level, 1.0, got_ref[:, :rank].astype(F32)),
    ]
    part_ref[...] = attend(query_ref[...], keys, seen, rank, known)
    for p in range(local):
        at = start + lax.broadcasted_iota(jnp.int32, (span, 1), 0) == ends[p]
        cache_ref[p] = jnp.where(at, fresh_ref[pl.ds(p, 1), :], moved_ref[pl.ds(p * span, span)])


def chip_kernel(count, *refs):
    for k in range(count):
        out_ref = refs[2 * count + k]
        rank = out_ref.shape[1] - LANES
        out_ref[...] = packed(*merged([refs[k][...], refs[count + k][...]], rank))


def chip_merge(keep, got):
    return pl.pallas_call(
        functools.partial(chip_kernel, len(keep)),
        out_shape=[shape(k.shape) for k in keep],
        in_specs=[VMEM] * (2 * len(keep)),
        out_specs=[VMEM] * len(keep),
        compiler_params=PARAMS,
        name="chip_merge",
    )(*keep, *got)


def final_kernel(count, *refs):
    part_refs, (w_ref, out_ref, values) = refs[:count], refs[count:]
    heads, rank, reach = w_ref.shape
    local = out_ref.shape[0]
    latent = merged([ref[...] for ref in part_refs], rank)[0].astype(BF16)
    first = lax.broadcasted_iota(jnp.int32, (2 * local, reach), 0) < local
    for h in range(0, heads, 2):
        two = latent[h * local : (h + 2) * local]
        here = jnp.dot(two, w_ref[h], preferred_element_type=F32)
        there = jnp.dot(two, w_ref[h + 1], preferred_element_type=F32)
        values[pl.ds(h * local, 2 * local), :] = jnp.where(first, here, there)
    for p in range(local):
        out_ref[p] = values[pl.ds(p, heads, stride=local), :].astype(BF16)


def after_kernel(_, value_ref, out_ref):
    out_ref[...] = value_ref[...]


def after(token, value):
    return pl.pallas_call(
        after_kernel,
        out_shape=shape(value.shape, value.dtype),
        in_specs=[ANY, VMEM],
        out_specs=VMEM,
        compiler_params=PARAMS,
        name="after",
    )(token, value)


def on_device(q_nope, q_rope, w_uk, w_uv, prefix, private_caches, new_latent, ancestors, lengths):
    local, heads, nope = q_nope.shape
    span, width = private_caches.shape[1:]
    rank, reach = w_uv.shape[1:]
    rope = width - rank
    rows = local * heads
    seq_size, dom_size = lax.axis_size("seq"), lax.axis_size("dom")
    cores = 2
    chips = seq_size // cores
    place = jnp.stack([lax.axis_index("seq"), lax.axis_index("dom")]).astype(jnp.int32)
    tail = span * local * rope // rank

    block = pl.pallas_call(
        functools.partial(pack_kernel, rank),
        out_shape=shape((local * span + tail, rank)),
        in_specs=[VMEM],
        out_specs=VMEM,
        compiler_params=PARAMS,
        name="pack",
    )(private_caches)
    nope_rows, rope_rows = (jnp.swapaxes(q, 0, 1).reshape(rows, -1) for q in (q_nope, q_rope))
    line = dom_size == 4
    if line:
        near = lax.ppermute(block, "dom", [(0, 1), (1, 0), (2, 3), (3, 2)])
        far = lax.ppermute(block, "dom", [(1, 2), (2, 1)])
    else:
        blocks = [block] + [
            lax.ppermute(block, "dom", [(i, (i + k) % dom_size) for i in range(dom_size)])
            for k in range(1, dom_size)
        ]

    pieces = math.gcd(heads // 4, 4)
    own = pl.pallas_call(
        functools.partial(project_kernel, pieces, local),
        out_shape=shape((rows, width)),
        in_specs=[VMEM] * 2 + [HBM],
        out_specs=VMEM,
        scratch_shapes=[pltpu.VMEM(w_uk.shape, BF16), pltpu.SemaphoreType.DMA((pieces,))],
        compiler_params=STREAM,
        name="project",
    )(nope_rows, rope_rows, w_uk)
    keys = prefix.T

    def pairs(turn, flip):
        return [
            (x * cores + c, (x + turn) % chips * cores + (c ^ flip))
            for x in range(chips)
            for c in range(cores)
        ]

    def back(turn, flip):
        return [(b, a) for a, b in pairs(turn, flip)]

    routes = [(t, f) for t in range(chips) for f in range(cores)]
    queries = [own if r == (0, 0) else lax.ppermute(own, "seq", pairs(*r)) for r in routes]
    stages = []
    half = block.shape[0] // 2
    for t in range(chips):
        asked = queries[2 * t : 2 * t + 2]
        stage = [*asked, *prefix_attention(asked, keys, rank, t == 0)]
        stages.append(stage)
        if line and t == 0:
            near, far, stage[3] = lax.optimization_barrier((near, far, stage[3]))
            outer = lax.ppermute(far, "dom", [(1, 0), (2, 3)])
            second = [
                lax.ppermute(piece, "dom", [(1, 2), (2, 1)])
                for piece in (near[: half + 16], near[half:])
            ]
        if t == 0:
            given = lax.ppermute(stage.pop(), "seq", pairs(0, 1))
    if line:
        third = []
        for piece in second:
            piece, stages[-1][3] = lax.optimization_barrier((piece, stages[-1][3]))
            third.append(lax.ppermute(piece, "dom", [(1, 0), (2, 3)]))
            stages[-1][3] = after(piece, stages[-1][3])
    if line:
        blocks = [block, near, far, outer, *second, *third]
        whole = [((i, 0), (i, half)) for i in range(4)]
        halves = [((i, 0), (i + 1, 0)) for i in (4, 6)]
        sources = (whole[0], whole[1], halves[0], whole[2], whole[3], halves[1])
    else:
        sources = tuple(((i, 0), (i, half)) for i in range(dom_size))

    part = shape((rows, rank + LANES))
    others = chips - 1
    far_results = pl.pallas_call(
        functools.partial(far_kernel, others, sources, line),
        out_shape=[shape((local * span, width))] + [part] * (2 * others),
        in_specs=[SMEM] * 3 + [VMEM] * (5 * others) + [ANY] * len(blocks),
        out_specs=[VMEM] * (1 + 2 * others),
        scratch_shapes=[
            pltpu.VMEM((local, 2, tail // 2, rank), BF16),
            pltpu.SemaphoreType.DMA((4 * local,)),
        ],
        compiler_params=PARAMS,
        name="suffix_far",
    )(ancestors, lengths, place, *[a for stage in stages[1:] for a in stage], *blocks)
    moved = far_results[0]
    keep, give = far_results[1 : 1 + others], far_results[1 + others :]
    sums = chip_merge(keep, [lax.ppermute(g, "seq", pairs(0, 1)) for g in give])
    parts = [lax.ppermute(s, "seq", back(t, 0)) for t, s in enumerate(sums, 1)]
    other = lax.ppermute(moved, "seq", pairs(0, 1))

    moved, _ = lax.optimization_barrier((moved, sums[0]))
    query, _, acc, level, mass = stages[0]
    new_caches, own_part = pl.pallas_call(
        near_kernel,
        out_shape=[shape(private_caches.shape), part],
        in_specs=[SMEM] * 3 + [VMEM] * 8,
        out_specs=[VMEM] * 2,
        compiler_params=PARAMS,
        name="suffix_near",
    )(ancestors, lengths, place, new_latent, query, acc, level, mass, given, moved, other)
    parts.append(own_part)

    head_values = pl.pallas_call(
        functools.partial(final_kernel, chips),
        out_shape=shape((local, heads, reach)),
        in_specs=[VMEM] * (chips + 1),
        out_specs=VMEM,
        scratch_shapes=[pltpu.VMEM((rows, reach), F32)],
        compiler_params=PARAMS,
        name="final",
    )(*parts, w_uv)
    return (head_values, new_caches)


def solution(mesh):
    placed = (
        P(("group", "dom"), "seq", None),
        P(("group", "dom"), "seq", None),
        P("seq", None, None),
        P("seq", None, None),
        P(("group", "seq"), None),
        P(("group", "dom"), "seq", None),
        P(("group", "dom"), None),
        P(("group", "dom")),
        P("group"),
    )
    return jax.shard_map(
        on_device,
        mesh=mesh,
        in_specs=placed,
        out_specs=(P(("group", "dom"), "seq", None), P(("group", "dom"), "seq", None)),
        check_vma=False,
    )
```

```python
import functools
import math

import jax
import jax.numpy as jnp
from jax import lax
from jax.experimental import pallas as pl
from jax.experimental.pallas import tpu as pltpu
from jax.sharding import PartitionSpec as P

ROPE = 64
NOPE = 128
SCALE2 = (NOPE + ROPE) ** (-0.5) * math.log2(math.e)
HIDDEN = -1e30
LANES = 128
F32 = jnp.float32
BF16 = jnp.bfloat16
NT = (((1,), (1,)), ((), ()))

VMEM = pl.BlockSpec(memory_space=pltpu.VMEM)
SMEM = pl.BlockSpec(memory_space=pltpu.SMEM)
ANY = pl.BlockSpec(memory_space=pl.ANY)
HBM = pl.BlockSpec(memory_space=pltpu.HBM)
PARAMS = pltpu.CompilerParams(vmem_limit_bytes=40 * 1024 * 1024)
STREAM = pltpu.CompilerParams(vmem_limit_bytes=51 * 1024 * 1024)


def shape(dims, dtype=BF16):
    return jax.ShapeDtypeStruct(dims, dtype)


def pack_kernel(rank, cache_ref, out_ref):
    local, span, width = cache_ref.shape
    for p in range(local):
        out_ref[pl.ds(p * span, span)] = cache_ref[p, :, :rank]
    rope = jnp.concatenate([cache_ref[p, :, rank:] for p in range(local)], axis=1)
    tail = out_ref.shape[0] - local * span
    out_ref[pl.ds(local * span, tail)] = jnp.concatenate(
        [rope[i : i + tail] for i in range(0, span, tail)], axis=1
    )


def project_kernel(
    pieces, local, nope_ref, rope_ref, w_hbm, own_ref, w_ref, sems
):
    heads, _, rank = w_ref.shape
    piece = heads // pieces
    fetches = [
        pltpu.make_async_copy(
            w_hbm.at[pl.ds(i * piece, piece)], w_ref.at[pl.ds(i * piece, piece)], sems.at[i]
        )
        for i in range(pieces)
    ]
    for fetch in fetches:
        fetch.start()
    nope = nope_ref[...].astype(F32)
    width = nope.shape[1]
    first = lax.broadcasted_iota(jnp.int32, (2 * local, width), 0) < local

    def pair(h):
        two = nope[h * local : (h + 2) * local]
        left = jnp.concatenate([jnp.where(first, two, 0.0), jnp.where(first, 0.0, two)], axis=1)
        weights = w_ref[pl.ds(h, 2)].reshape(2 * width, rank)
        return jnp.dot(left.astype(BF16), weights, preferred_element_type=F32)

    own_ref[:, rank:] = rope_ref[...]
    for h in range(0, heads, 4):
        if h % piece == 0:
            fetches[h // piece].wait()
        own_ref[pl.ds(h * local, 4 * local), :rank] = jnp.concatenate(
            [pair(i) for i in (h, h + 2)], axis=0
        ).astype(BF16)


def prefix_kernel(count, tiles, *refs):
    query_refs = refs[:count]
    keys_hbm, out_ref, max_ref, sum_ref, *give_ref, acc_ref, keys_ref, sems = refs[count:]
    rank = acc_ref.shape[1]
    tile = keys_ref.shape[1] // tiles
    parts = [pl.ds(i * tile, tile) for i in range(tiles)]
    fetches = [
        pltpu.make_async_copy(keys_hbm.at[:, part], keys_ref.at[:, part], sems.at[i])
        for i, part in enumerate(parts)
    ]
    for fetch in fetches:
        fetch.start()
    queries = jnp.concatenate([ref[...] for ref in query_refs], axis=0)

    def score(i):
        fetches[i].wait()
        return jnp.dot(queries, keys_ref[:, parts[i]], preferred_element_type=F32) * SCALE2

    ahead = score(0)
    for i in range(tiles):
        scores = ahead
        if i + 1 < tiles:
            ahead = score(i + 1)
        top = jnp.max(scores, axis=1, keepdims=True)
        if i > 0:
            top = jnp.maximum(top, largest)
        weights = jnp.exp2(scores - top)
        total = jnp.sum(weights, axis=1, keepdims=True)
        acc = lax.dot_general(
            weights.astype(BF16), keys_ref[:rank, parts[i]], NT, preferred_element_type=F32
        )
        if i > 0:
            factor = jnp.exp2(largest - top)
            total = total + running * factor
            acc = acc + acc_ref[...] * factor
        largest, running = top, total
        if i < tiles - 1:
            acc_ref[...] = acc
    kept = out_ref.shape[0]
    out_ref[...] = acc[:kept]
    max_ref[...] = jnp.broadcast_to(largest[:kept], max_ref.shape)
    sum_ref[...] = jnp.broadcast_to(running[:kept], sum_ref.shape)
    if give_ref:
        level = largest[kept:] + jnp.log2(running[kept:])
        give_ref[0][...] = packed(acc[kept:] * (1.0 / running[kept:]), level)


def prefix_attention(queries, keys, rank, give, tiles=4):
    rows = sum(q.shape[0] for q in queries)
    kept = queries[0].shape[0] if give else rows
    width, length = keys.shape
    out = [shape((kept, rank), F32)] + [shape((kept, LANES), F32)] * 2
    if give:
        out.append(shape((rows - kept, rank + LANES)))
    return pl.pallas_call(
        functools.partial(prefix_kernel, len(queries), tiles),
        out_shape=out,
        in_specs=[VMEM] * len(queries) + [HBM],
        out_specs=[VMEM] * len(out),
        scratch_shapes=[
            pltpu.VMEM((rows, rank), F32),
            pltpu.VMEM(keys.shape, BF16),
            pltpu.SemaphoreType.DMA((tiles,)),
        ],
        compiler_params=STREAM,
        cost_estimate=None if give else pl.CostEstimate(
            flops=2 * rows * length * (width + rank),
            bytes_accessed=2 * width * length,
            transcendentals=rows * length,
        ),
        name="prefix_attention",
    )(*queries, keys)


def packed(values, level):
    rows = values.shape[0]
    lane = lax.broadcasted_iota(jnp.int32, (rows, LANES), 1)
    high = level.astype(BF16).astype(F32)
    middle = (level - high).astype(BF16).astype(F32)
    low = level - high - middle
    stats = jnp.where(lane == 0, high, jnp.where(lane == 1, middle, jnp.where(lane == 2, low, 0.0)))
    return jnp.concatenate([values.astype(BF16), stats.astype(BF16)], axis=1)


def merged(parts, rank):
    levels = [jnp.sum(part[:, rank:].astype(F32), axis=1, keepdims=True) for part in parts]
    top = functools.reduce(jnp.maximum, levels)
    shares = [jnp.exp2(level - top) for level in levels]
    whole = functools.reduce(jnp.add, shares)
    acc = functools.reduce(
        jnp.add, [share * part[:, :rank].astype(F32) for share, part in zip(shares, parts)]
    )
    return acc * (1.0 / whole), top + jnp.log2(whole)


def visible(rows, ends, starts, span):
    local = len(ends)
    cols = len(starts) * local * span
    col = lax.broadcasted_iota(jnp.int32, (1, cols), 1)
    col_of = jnp.zeros_like(col)
    limit = jnp.full_like(col, ends[0] - starts[0])
    for at in range(1, len(starts) * local):
        begin, p = at * span, at % local
        later = col >= begin
        col_of = jnp.where(later, p, col_of)
        limit = jnp.where(later, ends[p] - starts[at // local] + begin, limit)
    col_of = jnp.where(col < limit, col_of, -1)
    row_of = lax.rem(lax.broadcasted_iota(jnp.int32, (rows, 1), 0), local)
    return row_of == col_of


def attend(queries, keys, seen, rank, known):
    scores = lax.dot_general(queries, keys, NT, preferred_element_type=F32)
    scores = jnp.where(seen, scores * SCALE2, HIDDEN)
    top = jnp.max(scores, axis=1, keepdims=True)
    for level, _, _ in known:
        top = jnp.maximum(top, level)
    weights = jnp.where(seen, jnp.exp2(scores - top), 0.0)
    total = jnp.sum(weights, axis=1, keepdims=True)
    acc = jnp.dot(weights.astype(BF16), keys[:, :rank], preferred_element_type=F32)
    for level, mass, part in known:
        factor = jnp.exp2(level - top)
        total = total + mass * factor
        acc = acc + part * factor
    return packed(acc * (1.0 / total), top + jnp.log2(total))


def far_kernel(stages, sources, line, *refs):
    anc, lens, place = refs[:3]
    refs = refs[3:]
    stage_refs, refs = refs[: 5 * stages], refs[5 * stages :]
    block_refs, refs = refs[:sources], refs[sources:]
    moved_ref, refs = refs[0], refs[1:]
    keep_refs, give_refs = refs[:stages], refs[stages : 2 * stages]
    folded, sems = refs[2 * stages :]
    local, tail, rank = folded.shape
    span = moved_ref.shape[0] // local
    rope = moved_ref.shape[1] - rank

    def copies(p, k, slot):
        at = pl.multiple_of(slot * span, span)
        there = moved_ref.at[pl.ds(p * span, span), pl.ds(0, rank)]
        return (
            pltpu.make_async_copy(block_refs[k].at[pl.ds(at, span)], there, sems.at[2 * p]),
            pltpu.make_async_copy(
                block_refs[k].at[pl.ds(local * span, tail)], folded.at[p], sems.at[2 * p + 1]
            ),
        )

    slots = []
    for p in range(local):
        owner = lax.div(anc[p], local)
        slots.append(lax.rem(anc[p], local))
        if line:
            apart = jnp.bitwise_xor(owner, place[1])
            at_end = (place[1] == 0) | (place[1] == 3)
            which = jnp.where(at_end & (apart > 1), apart + 2, apart)
        else:
            which = lax.rem(place[1] - owner + sources, sources)
        for k in range(sources):

            @pl.when(which == k)
            def _():
                for copy in copies(p, k, slots[p]):
                    copy.start()

    for p in range(local):
        for copy in copies(p, 0, 0):
            copy.wait()

    for p in range(local):
        for i in range(span // tail):
            choices = [
                folded[p, :, (i * local + q) * rope : (i * local + q + 1) * rope] for q in range(local)
            ]
            picked = choices[0]
            for q in range(1, local):
                picked = jnp.where(slots[p] == q, choices[q], picked)
            moved_ref[pl.ds(p * span + i * tail, tail), rank:] = picked

    ends = [lens[anc[p]] for p in range(local)]
    for k in range(stages):
        first_ref, second_ref, acc_ref, max_ref, sum_ref = stage_refs[5 * k : 5 * k + 5]
        queries = jnp.concatenate([first_ref[...], second_ref[...]], axis=0)
        seen = visible(queries.shape[0], ends, [place[0] * span], span)
        known = [(max_ref[:, 0:1], sum_ref[:, 0:1], acc_ref[...])]
        part = attend(queries, moved_ref[...], seen, rank, known)
        rows = first_ref.shape[0]
        keep_refs[k][...] = part[:rows]
        give_refs[k][...] = part[rows:]


def near_kernel(anc, lens, place, fresh_ref, *refs):
    query_ref, acc_ref, max_ref, sum_ref, got_ref, moved_ref, other_ref, cache_ref, part_ref = refs
    local, span, width = cache_ref.shape
    rank = acc_ref.shape[1]
    start, other = place[0] * span, jnp.bitwise_xor(place[0], 1) * span
    ends = [lens[anc[p]] for p in range(local)]
    keys = jnp.concatenate([moved_ref[...], other_ref[...]], axis=0)
    seen = visible(query_ref.shape[0], ends, [start, other], span)
    level = jnp.sum(got_ref[:, rank:].astype(F32), axis=1, keepdims=True)
    known = [
        (max_ref[:, 0:1], sum_ref[:, 0:1], acc_ref[...]),
        (level, 1.0, got_ref[:, :rank].astype(F32)),
    ]
    part_ref[...] = attend(query_ref[...], keys, seen, rank, known)
    for p in range(local):
        at = start + lax.broadcasted_iota(jnp.int32, (span, 1), 0) == ends[p]
        cache_ref[p] = jnp.where(at, fresh_ref[pl.ds(p, 1), :], moved_ref[pl.ds(p * span, span)])


def chip_kernel(count, *refs):
    for k in range(count):
        out_ref = refs[2 * count + k]
        rank = out_ref.shape[1] - LANES
        out_ref[...] = packed(*merged([refs[k][...], refs[count + k][...]], rank))


def chip_merge(keep, got):
    return pl.pallas_call(
        functools.partial(chip_kernel, len(keep)),
        out_shape=[shape(k.shape) for k in keep],
        in_specs=[VMEM] * (2 * len(keep)),
        out_specs=[VMEM] * len(keep),
        compiler_params=PARAMS,
        name="chip_merge",
    )(*keep, *got)


def final_kernel(count, *refs):
    part_refs, (w_ref, out_ref, values) = refs[:count], refs[count:]
    heads, rank, reach = w_ref.shape
    local = out_ref.shape[0]
    latent = merged([ref[...] for ref in part_refs], rank)[0].astype(BF16)
    first = lax.broadcasted_iota(jnp.int32, (2 * local, reach), 0) < local
    for h in range(0, heads, 2):
        two = latent[h * local : (h + 2) * local]
        weights = jnp.concatenate([w_ref[h], w_ref[h + 1]], axis=1)
        both = jnp.dot(two, weights, preferred_element_type=F32)
        values[pl.ds(h * local, 2 * local), :] = jnp.where(first, both[:, :reach], both[:, reach:])
    for p in range(local):
        out_ref[p] = values[pl.ds(p, heads, stride=local), :].astype(BF16)


def on_device(q_nope, q_rope, w_uk, w_uv, prefix, private_caches, new_latent, ancestors, lengths):
    local, heads, nope = q_nope.shape
    span, width = private_caches.shape[1:]
    rank, reach = w_uv.shape[1:]
    rope = width - rank
    rows = local * heads
    seq_size, dom_size = lax.axis_size("seq"), lax.axis_size("dom")
    cores = 2
    chips = seq_size // cores
    place = jnp.stack([lax.axis_index("seq"), lax.axis_index("dom")]).astype(jnp.int32)
    tail = span * local * rope // rank

    block = pl.pallas_call(
        functools.partial(pack_kernel, rank),
        out_shape=shape((local * span + tail, rank)),
        in_specs=[VMEM],
        out_specs=VMEM,
        compiler_params=PARAMS,
        name="pack",
    )(private_caches)
    nope_rows, rope_rows = (jnp.swapaxes(q, 0, 1).reshape(rows, -1) for q in (q_nope, q_rope))
    line = dom_size == 4
    if line:
        near = lax.ppermute(block, "dom", [(0, 1), (1, 0), (2, 3), (3, 2)])
        far = lax.ppermute(block, "dom", [(1, 2), (2, 1)])
    else:
        blocks = [block] + [
            lax.ppermute(block, "dom", [(i, (i + k) % dom_size) for i in range(dom_size)])
            for k in range(1, dom_size)
        ]

    pieces = math.gcd(heads // 4, 4)
    own = pl.pallas_call(
        functools.partial(project_kernel, pieces, local),
        out_shape=shape((rows, width)),
        in_specs=[VMEM] * 2 + [HBM],
        out_specs=VMEM,
        scratch_shapes=[pltpu.VMEM(w_uk.shape, BF16), pltpu.SemaphoreType.DMA((pieces,))],
        compiler_params=STREAM,
        name="project",
    )(nope_rows, rope_rows, w_uk)
    keys = prefix.T
    if line:
        sent, own = lax.optimization_barrier((block, own))
        inner_middle = lax.ppermute(sent, "dom", [(0, 2), (3, 1)])

    def pairs(turn, flip):
        return [
            (x * cores + c, (x + turn) % chips * cores + (c ^ flip))
            for x in range(chips)
            for c in range(cores)
        ]

    def back(turn, flip):
        return [(b, a) for a, b in pairs(turn, flip)]

    routes = [(t, f) for t in range(chips) for f in range(cores)]
    queries = [own if r == (0, 0) else lax.ppermute(own, "seq", pairs(*r)) for r in routes]
    if line:
        near, far, queries[1] = lax.optimization_barrier((near, far, queries[1]))
        outer_middle = lax.ppermute(far, "dom", [(1, 0), (2, 3)])
    stages = []
    for t in range(chips):
        asked = queries[2 * t : 2 * t + 2]
        stage = [*asked, *prefix_attention(asked, keys, rank, t == 0)]
        stages.append(stage)
        if t == 0:
            given = lax.ppermute(stage.pop(), "seq", pairs(0, 1))
        if line and t == 0:
            inner_middle, stage[3] = lax.optimization_barrier((inner_middle, stage[3]))
            outer_far = lax.ppermute(inner_middle, "dom", [(1, 0), (2, 3)])
    if line:
        blocks = [block, near, inner_middle, far, outer_middle, outer_far]

    part = shape((rows, rank + LANES))
    others = chips - 1
    far_results = pl.pallas_call(
        functools.partial(far_kernel, others, len(blocks), line),
        out_shape=[shape((local * span, width))] + [part] * (2 * others),
        in_specs=[SMEM] * 3 + [VMEM] * (5 * others) + [ANY] * len(blocks),
        out_specs=[VMEM] * (1 + 2 * others),
        scratch_shapes=[
            pltpu.VMEM((local, tail, rank), BF16),
            pltpu.SemaphoreType.DMA((2 * local,)),
        ],
        compiler_params=PARAMS,
        name="suffix_far",
    )(ancestors, lengths, place, *[a for stage in stages[1:] for a in stage], *blocks)
    moved = far_results[0]
    keep, give = far_results[1 : 1 + others], far_results[1 + others :]
    sums = chip_merge(keep, [lax.ppermute(g, "seq", pairs(0, 1)) for g in give])
    parts = [lax.ppermute(s, "seq", back(t, 0)) for t, s in enumerate(sums, 1)]
    other = lax.ppermute(moved, "seq", pairs(0, 1))

    moved, _ = lax.optimization_barrier((moved, sums[0]))
    query, _, acc, level, mass = stages[0]
    new_caches, own_part = pl.pallas_call(
        near_kernel,
        out_shape=[shape(private_caches.shape), part],
        in_specs=[SMEM] * 3 + [VMEM] * 8,
        out_specs=[VMEM] * 2,
        compiler_params=PARAMS,
        name="suffix_near",
    )(ancestors, lengths, place, new_latent, query, acc, level, mass, given, moved, other)
    parts.append(own_part)

    head_values = pl.pallas_call(
        functools.partial(final_kernel, chips),
        out_shape=shape((local, heads, reach)),
        in_specs=[VMEM] * (chips + 1),
        out_specs=VMEM,
        scratch_shapes=[pltpu.VMEM((rows, reach), F32)],
        compiler_params=PARAMS,
        name="final",
    )(*parts, w_uv)
    return (head_values, new_caches)


def solution(mesh):
    placed = (
        P(("group", "dom"), "seq", None),
        P(("group", "dom"), "seq", None),
        P("seq", None, None),
        P("seq", None, None),
        P(("group", "seq"), None),
        P(("group", "dom"), "seq", None),
        P(("group", "dom"), None),
        P(("group", "dom")),
        P("group"),
    )
    return jax.shard_map(
        on_device,
        mesh=mesh,
        in_specs=placed,
        out_specs=(P(("group", "dom"), "seq", None), P(("group", "dom"), "seq", None)),
        check_vma=False,
    )
```

```python
import functools
import math

import jax
import jax.numpy as jnp
from jax import lax
from jax.experimental import pallas as pl
from jax.experimental.pallas import tpu as pltpu
from jax.sharding import PartitionSpec as P

ROPE = 64
NOPE = 128
SCALE2 = (NOPE + ROPE) ** (-0.5) * math.log2(math.e)
HIDDEN = -1e30
LANES = 128
F32 = jnp.float32
BF16 = jnp.bfloat16
NT = (((1,), (1,)), ((), ()))

VMEM = pl.BlockSpec(memory_space=pltpu.VMEM)
SMEM = pl.BlockSpec(memory_space=pltpu.SMEM)
ANY = pl.BlockSpec(memory_space=pl.ANY)
HBM = pl.BlockSpec(memory_space=pltpu.HBM)
PARAMS = pltpu.CompilerParams(vmem_limit_bytes=40 * 1024 * 1024)
STREAM = pltpu.CompilerParams(vmem_limit_bytes=51 * 1024 * 1024)


def shape(dims, dtype=BF16):
    return jax.ShapeDtypeStruct(dims, dtype)


def pack_kernel(rank, anc, cache_ref, out_ref, ext_ref):
    local, span, width = cache_ref.shape
    for p in range(local):
        out_ref[pl.ds(p * span, span)] = cache_ref[p, :, :rank]
    rope = jnp.concatenate([cache_ref[p, :, rank:] for p in range(local)], axis=1)
    tail = out_ref.shape[0] - local * span
    out_ref[pl.ds(local * span, tail)] = jnp.concatenate(
        [rope[i : i + tail] for i in range(0, span, tail)], axis=1
    )
    whole = out_ref.shape[0]
    ext_ref[pl.ds(0, whole)] = out_ref[...]
    lane = lax.broadcasted_iota(jnp.int32, (ext_ref.shape[0] - whole, rank), 1)
    names = jnp.zeros(lane.shape, F32)
    for p in range(local):
        names = jnp.where(lane == p, anc[p].astype(F32), names)
    ext_ref[pl.ds(whole, ext_ref.shape[0] - whole)] = names.astype(BF16)


def project_kernel(
    pieces, local, nope_ref, rope_ref, w_hbm, own_ref, w_ref, sems
):
    heads, _, rank = w_ref.shape
    piece = heads // pieces
    fetches = [
        pltpu.make_async_copy(
            w_hbm.at[pl.ds(i * piece, piece)], w_ref.at[pl.ds(i * piece, piece)], sems.at[i]
        )
        for i in range(pieces)
    ]
    for fetch in fetches:
        fetch.start()
    nope = nope_ref[...].astype(F32)
    width = nope.shape[1]
    first = lax.broadcasted_iota(jnp.int32, (2 * local, width), 0) < local

    def pair(h):
        two = nope[h * local : (h + 2) * local]
        left = jnp.concatenate([jnp.where(first, two, 0.0), jnp.where(first, 0.0, two)], axis=1)
        weights = w_ref[pl.ds(h, 2)].reshape(2 * width, rank)
        return jnp.dot(left.astype(BF16), weights, preferred_element_type=F32)

    own_ref[:, rank:] = rope_ref[...]
    for h in range(0, heads, 4):
        if h % piece == 0:
            fetches[h // piece].wait()
        own_ref[pl.ds(h * local, 4 * local), :rank] = jnp.concatenate(
            [pair(i) for i in (h, h + 2)], axis=0
        ).astype(BF16)


def prefix_kernel(count, tiles, *refs):
    query_refs = refs[:count]
    keys_hbm, out_ref, max_ref, sum_ref, *give_ref, acc_ref, keys_ref, sems = refs[count:]
    rank = acc_ref.shape[1]
    tile = keys_ref.shape[1] // tiles
    parts = [pl.ds(i * tile, tile) for i in range(tiles)]
    fetches = [
        pltpu.make_async_copy(keys_hbm.at[:, part], keys_ref.at[:, part], sems.at[i])
        for i, part in enumerate(parts)
    ]
    for fetch in fetches:
        fetch.start()
    queries = jnp.concatenate([ref[...] for ref in query_refs], axis=0)

    def score(i):
        fetches[i].wait()
        return jnp.dot(queries, keys_ref[:, parts[i]], preferred_element_type=F32) * SCALE2

    ahead = score(0)
    for i in range(tiles):
        scores = ahead
        if i + 1 < tiles:
            ahead = score(i + 1)
        top = jnp.max(scores, axis=1, keepdims=True)
        if i > 0:
            top = jnp.maximum(top, largest)
        weights = jnp.exp2(scores - top)
        total = jnp.sum(weights, axis=1, keepdims=True)
        acc = lax.dot_general(
            weights.astype(BF16), keys_ref[:rank, parts[i]], NT, preferred_element_type=F32
        )
        if i > 0:
            factor = jnp.exp2(largest - top)
            total = total + running * factor
            acc = acc + acc_ref[...] * factor
        largest, running = top, total
        if i < tiles - 1:
            acc_ref[...] = acc
    kept = out_ref.shape[0]
    out_ref[...] = acc[:kept]
    max_ref[...] = jnp.broadcast_to(largest[:kept], max_ref.shape)
    sum_ref[...] = jnp.broadcast_to(running[:kept], sum_ref.shape)
    if give_ref:
        level = largest[kept:] + jnp.log2(running[kept:])
        give_ref[0][...] = packed(acc[kept:] * (1.0 / running[kept:]), level)


def prefix_attention(queries, keys, rank, give, tiles=4):
    rows = sum(q.shape[0] for q in queries)
    kept = queries[0].shape[0] if give else rows
    width, length = keys.shape
    out = [shape((kept, rank), F32)] + [shape((kept, LANES), F32)] * 2
    if give:
        out.append(shape((rows - kept, rank + LANES)))
    return pl.pallas_call(
        functools.partial(prefix_kernel, len(queries), tiles),
        out_shape=out,
        in_specs=[VMEM] * len(queries) + [HBM],
        out_specs=[VMEM] * len(out),
        scratch_shapes=[
            pltpu.VMEM((rows, rank), F32),
            pltpu.VMEM(keys.shape, BF16),
            pltpu.SemaphoreType.DMA((tiles,)),
        ],
        compiler_params=STREAM,
        cost_estimate=None if give else pl.CostEstimate(
            flops=2 * rows * length * (width + rank),
            bytes_accessed=2 * width * length,
            transcendentals=rows * length,
        ),
        name="prefix_attention",
    )(*queries, keys)


def packed(values, level):
    rows = values.shape[0]
    lane = lax.broadcasted_iota(jnp.int32, (rows, LANES), 1)
    high = level.astype(BF16).astype(F32)
    middle = (level - high).astype(BF16).astype(F32)
    low = level - high - middle
    stats = jnp.where(lane == 0, high, jnp.where(lane == 1, middle, jnp.where(lane == 2, low, 0.0)))
    return jnp.concatenate([values.astype(BF16), stats.astype(BF16)], axis=1)


def merged(parts, rank):
    levels = [jnp.sum(part[:, rank:].astype(F32), axis=1, keepdims=True) for part in parts]
    top = functools.reduce(jnp.maximum, levels)
    shares = [jnp.exp2(level - top) for level in levels]
    whole = functools.reduce(jnp.add, shares)
    acc = functools.reduce(
        jnp.add, [share * part[:, :rank].astype(F32) for share, part in zip(shares, parts)]
    )
    return acc * (1.0 / whole), top + jnp.log2(whole)


def visible(rows, ends, starts, span):
    local = len(ends)
    cols = len(starts) * local * span
    col = lax.broadcasted_iota(jnp.int32, (1, cols), 1)
    col_of = jnp.zeros_like(col)
    limit = jnp.full_like(col, ends[0] - starts[0])
    for at in range(1, len(starts) * local):
        begin, p = at * span, at % local
        later = col >= begin
        col_of = jnp.where(later, p, col_of)
        limit = jnp.where(later, ends[p] - starts[at // local] + begin, limit)
    col_of = jnp.where(col < limit, col_of, -1)
    row_of = lax.rem(lax.broadcasted_iota(jnp.int32, (rows, 1), 0), local)
    return row_of == col_of


def attend(queries, keys, seen, rank, known):
    scores = lax.dot_general(queries, keys, NT, preferred_element_type=F32)
    scores = jnp.where(seen, scores * SCALE2, HIDDEN)
    top = jnp.max(scores, axis=1, keepdims=True)
    for level, _, _ in known:
        top = jnp.maximum(top, level)
    weights = jnp.where(seen, jnp.exp2(scores - top), 0.0)
    total = jnp.sum(weights, axis=1, keepdims=True)
    acc = jnp.dot(weights.astype(BF16), keys[:, :rank], preferred_element_type=F32)
    for level, mass, part in known:
        factor = jnp.exp2(level - top)
        total = total + mass * factor
        acc = acc + part * factor
    return packed(acc * (1.0 / total), top + jnp.log2(total))


def gather_blocks(block_refs, picks, latents_ref, folded, sems):
    local, tail, rank = folded.shape
    span = latents_ref.shape[0] // local

    def copies(p, k, slot):
        at = pl.multiple_of(slot * span, span)
        return (
            pltpu.make_async_copy(
                block_refs[k].at[pl.ds(at, span)],
                latents_ref.at[pl.ds(p * span, span), pl.ds(0, rank)],
                sems.at[2 * p],
            ),
            pltpu.make_async_copy(
                block_refs[k].at[pl.ds(local * span, tail)], folded.at[p], sems.at[2 * p + 1]
            ),
        )

    for p, (which, slot) in enumerate(picks):
        for k in range(len(block_refs)):

            @pl.when(which == k)
            def _():
                for copy in copies(p, k, slot):
                    copy.start()

    for p in range(local):
        for copy in copies(p, 0, 0):
            copy.wait()


def rope_rows(folded, p, i, slot, rope):
    local = folded.shape[0]
    choices = [folded[p, :, (i * local + q) * rope : (i * local + q + 1) * rope] for q in range(local)]
    picked = choices[0]
    for q in range(1, local):
        picked = jnp.where(slot == q, choices[q], picked)
    return picked


def select_kernel(rope, theirs, place, *refs):
    block_refs, (_, out_ref, folded, sems) = refs[:-4], refs[-4:]
    local, tail, rank = folded.shape
    span = (out_ref.shape[0] - tail) // local
    picks = []
    for p in range(local):
        owner = lax.div(theirs[p], local)
        picks.append((jnp.bitwise_xor(owner, place[1]), lax.rem(theirs[p], local)))
    gather_blocks(block_refs, picks, out_ref.at[pl.ds(0, local * span)], folded, sems)
    rows = [
        rope_rows(folded, p, i, picks[p][1], rope) for i in range(span // tail) for p in range(local)
    ]
    out_ref[pl.ds(local * span, tail)] = jnp.concatenate(rows, axis=1)


def far_kernel(stages, sources, line, *refs):
    anc, lens, place = refs[:3]
    refs = refs[3:]
    stage_refs, refs = refs[: 5 * stages], refs[5 * stages :]
    block_refs, refs = refs[:sources], refs[sources:]
    moved_ref, refs = refs[0], refs[1:]
    keep_refs, give_refs = refs[:stages], refs[stages : 2 * stages]
    folded, sems = refs[2 * stages :]
    local, tail, rank = folded.shape
    span = moved_ref.shape[0] // local
    rope = moved_ref.shape[1] - rank

    picks = []
    for p in range(local):
        owner, slot = lax.div(anc[p], local), lax.rem(anc[p], local)
        if line:
            which = jnp.bitwise_xor(owner, place[1])
            chosen = ((place[1] == 0) | (place[1] == 3)) & (which != 0)
            which = jnp.where(chosen, sources - 1, which)
            slot = jnp.where(chosen, p, slot)
        else:
            which = lax.rem(place[1] - owner + sources, sources)
        picks.append((which, slot))
    gather_blocks(block_refs, picks, moved_ref, folded, sems)
    for p in range(local):
        for i in range(span // tail):
            moved_ref[pl.ds(p * span + i * tail, tail), rank:] = rope_rows(
                folded, p, i, picks[p][1], rope
            )

    ends = [lens[anc[p]] for p in range(local)]
    for k in range(stages):
        first_ref, second_ref, acc_ref, max_ref, sum_ref = stage_refs[5 * k : 5 * k + 5]
        queries = jnp.concatenate([first_ref[...], second_ref[...]], axis=0)
        seen = visible(queries.shape[0], ends, [place[0] * span], span)
        known = [(max_ref[:, 0:1], sum_ref[:, 0:1], acc_ref[...])]
        part = attend(queries, moved_ref[...], seen, rank, known)
        rows = first_ref.shape[0]
        keep_refs[k][...] = part[:rows]
        give_refs[k][...] = part[rows:]


def near_kernel(anc, lens, place, fresh_ref, *refs):
    query_ref, acc_ref, max_ref, sum_ref, got_ref, moved_ref, other_ref, cache_ref, part_ref = refs
    local, span, width = cache_ref.shape
    rank = acc_ref.shape[1]
    start, other = place[0] * span, jnp.bitwise_xor(place[0], 1) * span
    ends = [lens[anc[p]] for p in range(local)]
    keys = jnp.concatenate([moved_ref[...], other_ref[...]], axis=0)
    seen = visible(query_ref.shape[0], ends, [start, other], span)
    level = jnp.sum(got_ref[:, rank:].astype(F32), axis=1, keepdims=True)
    known = [
        (max_ref[:, 0:1], sum_ref[:, 0:1], acc_ref[...]),
        (level, 1.0, got_ref[:, :rank].astype(F32)),
    ]
    part_ref[...] = attend(query_ref[...], keys, seen, rank, known)
    for p in range(local):
        at = start + lax.broadcasted_iota(jnp.int32, (span, 1), 0) == ends[p]
        cache_ref[p] = jnp.where(at, fresh_ref[pl.ds(p, 1), :], moved_ref[pl.ds(p * span, span)])


def chip_kernel(count, *refs):
    for k in range(count):
        out_ref = refs[2 * count + k]
        rank = out_ref.shape[1] - LANES
        out_ref[...] = packed(*merged([refs[k][...], refs[count + k][...]], rank))


def chip_merge(keep, got):
    return pl.pallas_call(
        functools.partial(chip_kernel, len(keep)),
        out_shape=[shape(k.shape) for k in keep],
        in_specs=[VMEM] * (2 * len(keep)),
        out_specs=[VMEM] * len(keep),
        compiler_params=PARAMS,
        name="chip_merge",
    )(*keep, *got)


def final_kernel(count, *refs):
    part_refs, (w_ref, out_ref, values) = refs[:count], refs[count:]
    heads, rank, reach = w_ref.shape
    local = out_ref.shape[0]
    latent = merged([ref[...] for ref in part_refs], rank)[0].astype(BF16)
    first = lax.broadcasted_iota(jnp.int32, (2 * local, reach), 0) < local
    for h in range(0, heads, 2):
        two = latent[h * local : (h + 2) * local]
        weights = jnp.concatenate([w_ref[h], w_ref[h + 1]], axis=1)
        both = jnp.dot(two, weights, preferred_element_type=F32)
        values[pl.ds(h * local, 2 * local), :] = jnp.where(first, both[:, :reach], both[:, reach:])
    for p in range(local):
        out_ref[p] = values[pl.ds(p, heads, stride=local), :].astype(BF16)


def on_device(q_nope, q_rope, w_uk, w_uv, prefix, private_caches, new_latent, ancestors, lengths):
    local, heads, nope = q_nope.shape
    span, width = private_caches.shape[1:]
    rank, reach = w_uv.shape[1:]
    rope = width - rank
    rows = local * heads
    seq_size, dom_size = lax.axis_size("seq"), lax.axis_size("dom")
    cores = 2
    chips = seq_size // cores
    place = jnp.stack([lax.axis_index("seq"), lax.axis_index("dom")]).astype(jnp.int32)
    tail = span * local * rope // rank

    whole = local * span + tail
    block, extended = pl.pallas_call(
        functools.partial(pack_kernel, rank),
        out_shape=(shape((whole, rank)), shape((whole + 16, rank))),
        in_specs=[SMEM, VMEM],
        out_specs=(VMEM,) * 2,
        compiler_params=PARAMS,
        name="pack",
    )(ancestors, private_caches)
    nope_rows, rope_rows = (jnp.swapaxes(q, 0, 1).reshape(rows, -1) for q in (q_nope, q_rope))
    line = dom_size == 4
    if line:
        far = lax.ppermute(block, "dom", [(1, 2), (2, 1)])
        near = lax.ppermute(extended, "dom", [(0, 1), (3, 2)])
    else:
        blocks = [block] + [
            lax.ppermute(block, "dom", [(i, (i + k) % dom_size) for i in range(dom_size)])
            for k in range(1, dom_size)
        ]

    pieces = math.gcd(heads // 4, 4)
    own = pl.pallas_call(
        functools.partial(project_kernel, pieces, local),
        out_shape=shape((rows, width)),
        in_specs=[VMEM] * 2 + [HBM],
        out_specs=VMEM,
        scratch_shapes=[pltpu.VMEM(w_uk.shape, BF16), pltpu.SemaphoreType.DMA((pieces,))],
        compiler_params=STREAM,
        name="project",
    )(nope_rows, rope_rows, w_uk)
    keys = prefix.T
    if line:
        sent, own = lax.optimization_barrier((block, own))
        middle = lax.ppermute(sent, "dom", [(0, 2), (3, 1)])

    def pairs(turn, flip):
        return [
            (x * cores + c, (x + turn) % chips * cores + (c ^ flip))
            for x in range(chips)
            for c in range(cores)
        ]

    def back(turn, flip):
        return [(b, a) for a, b in pairs(turn, flip)]

    routes = [(t, f) for t in range(chips) for f in range(cores)]
    queries = [own if r == (0, 0) else lax.ppermute(own, "seq", pairs(*r)) for r in routes]
    if line:
        far, queries[1] = lax.optimization_barrier((far, queries[1]))
    stages = []
    for t in range(chips):
        asked = queries[2 * t : 2 * t + 2]
        stage = [*asked, *prefix_attention(asked, keys, rank, t == 0)]
        stages.append(stage)
        if t == 0:
            given = lax.ppermute(stage.pop(), "seq", pairs(0, 1))
        if line and t == 0:
            blocks = [block, near, middle, far]
            theirs = near[whole, :local].astype(F32).astype(jnp.int32)
            chosen = pl.pallas_call(
                functools.partial(select_kernel, rope),
                out_shape=shape((whole, rank)),
                in_specs=[SMEM] * 2 + [ANY] * 5,
                out_specs=VMEM,
                scratch_shapes=[
                    pltpu.VMEM((local, tail, rank), BF16),
                    pltpu.SemaphoreType.DMA((2 * local,)),
                ],
                compiler_params=PARAMS,
                name="select",
            )(theirs, place, *blocks, stage[3])
            blocks.append(lax.ppermute(chosen, "dom", [(1, 0), (2, 3)]))

    part = shape((rows, rank + LANES))
    others = chips - 1
    far_results = pl.pallas_call(
        functools.partial(far_kernel, others, len(blocks), line),
        out_shape=[shape((local * span, width))] + [part] * (2 * others),
        in_specs=[SMEM] * 3 + [VMEM] * (5 * others) + [ANY] * len(blocks),
        out_specs=[VMEM] * (1 + 2 * others),
        scratch_shapes=[
            pltpu.VMEM((local, tail, rank), BF16),
            pltpu.SemaphoreType.DMA((2 * local,)),
        ],
        compiler_params=PARAMS,
        name="suffix_far",
    )(ancestors, lengths, place, *[a for stage in stages[1:] for a in stage], *blocks)
    moved = far_results[0]
    keep, give = far_results[1 : 1 + others], far_results[1 + others :]
    sums = chip_merge(keep, [lax.ppermute(g, "seq", pairs(0, 1)) for g in give])
    parts = [lax.ppermute(s, "seq", back(t, 0)) for t, s in enumerate(sums, 1)]
    other = lax.ppermute(moved, "seq", pairs(0, 1))

    moved, _ = lax.optimization_barrier((moved, sums[0]))
    query, _, acc, level, mass = stages[0]
    new_caches, own_part = pl.pallas_call(
        near_kernel,
        out_shape=[shape(private_caches.shape), part],
        in_specs=[SMEM] * 3 + [VMEM] * 8,
        out_specs=[VMEM] * 2,
        compiler_params=PARAMS,
        name="suffix_near",
    )(ancestors, lengths, place, new_latent, query, acc, level, mass, given, moved, other)
    parts.append(own_part)

    head_values = pl.pallas_call(
        functools.partial(final_kernel, chips),
        out_shape=shape((local, heads, reach)),
        in_specs=[VMEM] * (chips + 1),
        out_specs=VMEM,
        scratch_shapes=[pltpu.VMEM((rows, reach), F32)],
        compiler_params=PARAMS,
        name="final",
    )(*parts, w_uv)
    return (head_values, new_caches)


def solution(mesh):
    placed = (
        P(("group", "dom"), "seq", None),
        P(("group", "dom"), "seq", None),
        P("seq", None, None),
        P("seq", None, None),
        P(("group", "seq"), None),
        P(("group", "dom"), "seq", None),
        P(("group", "dom"), None),
        P(("group", "dom")),
        P("group"),
    )
    return jax.shard_map(
        on_device,
        mesh=mesh,
        in_specs=placed,
        out_specs=(P(("group", "dom"), "seq", None), P(("group", "dom"), "seq", None)),
        check_vma=False,
    )
```

```python
import functools
import math

import jax
import jax.numpy as jnp
from jax import lax
from jax.experimental import pallas as pl
from jax.experimental.pallas import tpu as pltpu
from jax.sharding import PartitionSpec as P

ROPE = 64
NOPE = 128
SCALE2 = (NOPE + ROPE) ** (-0.5) * math.log2(math.e)
HIDDEN = -1e30
LANES = 128
F32 = jnp.float32
BF16 = jnp.bfloat16
NT = (((1,), (1,)), ((), ()))

VMEM = pl.BlockSpec(memory_space=pltpu.VMEM)
SMEM = pl.BlockSpec(memory_space=pltpu.SMEM)
ANY = pl.BlockSpec(memory_space=pl.ANY)
HBM = pl.BlockSpec(memory_space=pltpu.HBM)
PARAMS = pltpu.CompilerParams(vmem_limit_bytes=40 * 1024 * 1024)
STREAM = pltpu.CompilerParams(vmem_limit_bytes=51 * 1024 * 1024)


def shape(dims, dtype=BF16):
    return jax.ShapeDtypeStruct(dims, dtype)


def pack_kernel(rank, cache_ref, out_ref):
    local, span, _ = cache_ref.shape
    some = span // 2
    for p in range(local):
        part = pl.ds(p * some, some)
        first, second = cache_ref[p, :some], cache_ref[p, some:]
        out_ref[part, :rank] = first[:, :rank]
        out_ref[part, rank : 2 * rank] = second[:, :rank]
        out_ref[part, 2 * rank :] = jnp.concatenate([first[:, rank:], second[:, rank:]], axis=1)


def project_kernel(
    pieces, local, nope_ref, rope_ref, w_hbm, own_ref, w_ref, sems
):
    heads, _, rank = w_ref.shape
    piece = heads // pieces
    fetches = [
        pltpu.make_async_copy(
            w_hbm.at[pl.ds(i * piece, piece)], w_ref.at[pl.ds(i * piece, piece)], sems.at[i]
        )
        for i in range(pieces)
    ]
    for fetch in fetches:
        fetch.start()
    nope = nope_ref[...].astype(F32)
    width = nope.shape[1]
    first = lax.broadcasted_iota(jnp.int32, (2 * local, width), 0) < local

    def pair(h):
        two = nope[h * local : (h + 2) * local]
        left = jnp.concatenate([jnp.where(first, two, 0.0), jnp.where(first, 0.0, two)], axis=1)
        weights = w_ref[pl.ds(h, 2)].reshape(2 * width, rank)
        return jnp.dot(left.astype(BF16), weights, preferred_element_type=F32)

    own_ref[:, rank:] = rope_ref[...]
    for h in range(0, heads, 4):
        if h % piece == 0:
            fetches[h // piece].wait()
        own_ref[pl.ds(h * local, 4 * local), :rank] = jnp.concatenate(
            [pair(i) for i in (h, h + 2)], axis=0
        ).astype(BF16)


def prefix_kernel(count, tiles, *refs):
    query_refs = refs[:count]
    keys_hbm, out_ref, max_ref, sum_ref, *give_ref, acc_ref, keys_ref, sems = refs[count:]
    rank = acc_ref.shape[1]
    tile = keys_ref.shape[1] // tiles
    parts = [pl.ds(i * tile, tile) for i in range(tiles)]
    fetches = [
        pltpu.make_async_copy(keys_hbm.at[:, part], keys_ref.at[:, part], sems.at[i])
        for i, part in enumerate(parts)
    ]
    for fetch in fetches:
        fetch.start()
    queries = jnp.concatenate([ref[...] for ref in query_refs], axis=0)

    def score(i):
        fetches[i].wait()
        return jnp.dot(queries, keys_ref[:, parts[i]], preferred_element_type=F32) * SCALE2

    ahead = score(0)
    for i in range(tiles):
        scores = ahead
        if i + 1 < tiles:
            ahead = score(i + 1)
        top = jnp.max(scores, axis=1, keepdims=True)
        if i > 0:
            top = jnp.maximum(top, largest)
        weights = jnp.exp2(scores - top)
        total = jnp.sum(weights, axis=1, keepdims=True)
        acc = lax.dot_general(
            weights.astype(BF16), keys_ref[:rank, parts[i]], NT, preferred_element_type=F32
        )
        if i > 0:
            factor = jnp.exp2(largest - top)
            total = total + running * factor
            acc = acc + acc_ref[...] * factor
        largest, running = top, total
        if i < tiles - 1:
            acc_ref[...] = acc
    kept = out_ref.shape[0]
    out_ref[...] = acc[:kept]
    max_ref[...] = jnp.broadcast_to(largest[:kept], max_ref.shape)
    sum_ref[...] = jnp.broadcast_to(running[:kept], sum_ref.shape)
    if give_ref:
        level = largest[kept:] + jnp.log2(running[kept:])
        give_ref[0][...] = packed(acc[kept:] * (1.0 / running[kept:]), level)


def prefix_attention(queries, keys, rank, give, tiles=4):
    rows = sum(q.shape[0] for q in queries)
    kept = queries[0].shape[0] if give else rows
    width, length = keys.shape
    out = [shape((kept, rank), F32)] + [shape((kept, LANES), F32)] * 2
    if give:
        out.append(shape((rows - kept, rank + LANES)))
    return pl.pallas_call(
        functools.partial(prefix_kernel, len(queries), tiles),
        out_shape=out,
        in_specs=[VMEM] * len(queries) + [HBM],
        out_specs=[VMEM] * len(out),
        scratch_shapes=[
            pltpu.VMEM((rows, rank), F32),
            pltpu.VMEM(keys.shape, BF16),
            pltpu.SemaphoreType.DMA((tiles,)),
        ],
        compiler_params=STREAM,
        cost_estimate=None if give else pl.CostEstimate(
            flops=2 * rows * length * (width + rank),
            bytes_accessed=2 * width * length,
            transcendentals=rows * length,
        ),
        name="prefix_attention",
    )(*queries, keys)


def packed(values, level):
    rows = values.shape[0]
    lane = lax.broadcasted_iota(jnp.int32, (rows, LANES), 1)
    high = level.astype(BF16).astype(F32)
    middle = (level - high).astype(BF16).astype(F32)
    low = level - high - middle
    stats = jnp.where(lane == 0, high, jnp.where(lane == 1, middle, jnp.where(lane == 2, low, 0.0)))
    return jnp.concatenate([values.astype(BF16), stats.astype(BF16)], axis=1)


def merged(parts, rank):
    levels = [jnp.sum(part[:, rank:].astype(F32), axis=1, keepdims=True) for part in parts]
    top = functools.reduce(jnp.maximum, levels)
    shares = [jnp.exp2(level - top) for level in levels]
    whole = functools.reduce(jnp.add, shares)
    acc = functools.reduce(
        jnp.add, [share * part[:, :rank].astype(F32) for share, part in zip(shares, parts)]
    )
    return acc * (1.0 / whole), top + jnp.log2(whole)


def visible(rows, ends, starts, span):
    local = len(ends)
    cols = len(starts) * local * span
    col = lax.broadcasted_iota(jnp.int32, (1, cols), 1)
    col_of = jnp.zeros_like(col)
    limit = jnp.full_like(col, ends[0] - starts[0])
    for at in range(1, len(starts) * local):
        begin, p = at * span, at % local
        later = col >= begin
        col_of = jnp.where(later, p, col_of)
        limit = jnp.where(later, ends[p] - starts[at // local] + begin, limit)
    col_of = jnp.where(col < limit, col_of, -1)
    row_of = lax.rem(lax.broadcasted_iota(jnp.int32, (rows, 1), 0), local)
    return row_of == col_of


def attend(queries, keys, seen, rank, known):
    scores = lax.dot_general(queries, keys, NT, preferred_element_type=F32)
    scores = jnp.where(seen, scores * SCALE2, HIDDEN)
    top = jnp.max(scores, axis=1, keepdims=True)
    for level, _, _ in known:
        top = jnp.maximum(top, level)
    weights = jnp.where(seen, jnp.exp2(scores - top), 0.0)
    total = jnp.sum(weights, axis=1, keepdims=True)
    acc = jnp.dot(weights.astype(BF16), keys[:, :rank], preferred_element_type=F32)
    for level, mass, part in known:
        factor = jnp.exp2(level - top)
        total = total + mass * factor
        acc = acc + part * factor
    return packed(acc * (1.0 / total), top + jnp.log2(total))


def gather_blocks(block_refs, picks, out_ref, sems):
    some = out_ref.shape[0] // len(picks)

    def copy(p, k, slot):
        return pltpu.make_async_copy(
            block_refs[k].at[pl.ds(pl.multiple_of(slot * some, some), some)],
            out_ref.at[pl.ds(p * some, some)],
            sems.at[p],
        )

    for p, (which, slot) in enumerate(picks):
        for k in range(len(block_refs)):

            @pl.when(which == k)
            def _():
                copy(p, k, slot).start()

    for p in range(len(picks)):
        copy(p, 0, 0).wait()


def at_end(place):
    return (place[1] == 0) | (place[1] == 3)


def select_kernel(theirs, place, *refs):
    block_refs, (_, out_ref, sems) = refs[:-3], refs[-3:]
    local = sems.shape[0]
    picks = []
    for p in range(local):
        apart = jnp.bitwise_xor(lax.div(theirs[p], local), place[1])
        which = jnp.where(at_end(place), 0, jnp.maximum(apart - 1, 0))
        picks.append((which, jnp.where(at_end(place), p, lax.rem(theirs[p], local))))
    gather_blocks(block_refs, picks, out_ref, sems)


def far_kernel(stages, sources, line, *refs):
    anc, lens, place = refs[:3]
    refs = refs[3:]
    stage_refs, refs = refs[: 5 * stages], refs[5 * stages :]
    block_refs, refs = refs[:sources], refs[sources:]
    moved_ref, refs = refs[0], refs[1:]
    keep_refs, give_refs = refs[:stages], refs[stages : 2 * stages]
    raw, sems = refs[2 * stages :]
    local = sems.shape[0]
    some = raw.shape[0] // local
    span, width = 2 * some, moved_ref.shape[1]
    rank = stage_refs[2].shape[1]

    picks = []
    for p in range(local):
        owner, slot = lax.div(anc[p], local), lax.rem(anc[p], local)
        if line:
            which = jnp.bitwise_xor(owner, place[1])
            chosen = at_end(place) & (which != 0)
            which = jnp.where(chosen, 1, which)
            slot = jnp.where(chosen, p, slot)
        else:
            which = lax.rem(place[1] - owner + sources, sources)
        picks.append((which, slot))
    gather_blocks(block_refs, picks, raw, sems)
    for p in range(local):
        for h in range(2):
            part, rows = pl.ds(p * some, some), pl.ds(p * span + h * some, some)
            rope = 2 * rank + h * (width - rank)
            moved_ref[rows, :rank] = raw[part, h * rank : (h + 1) * rank]
            moved_ref[rows, rank:] = raw[part, rope : rope + width - rank]

    ends = [lens[anc[p]] for p in range(local)]
    for k in range(stages):
        first_ref, second_ref, acc_ref, max_ref, sum_ref = stage_refs[5 * k : 5 * k + 5]
        queries = jnp.concatenate([first_ref[...], second_ref[...]], axis=0)
        seen = visible(queries.shape[0], ends, [place[0] * span], span)
        known = [(max_ref[:, 0:1], sum_ref[:, 0:1], acc_ref[...])]
        part = attend(queries, moved_ref[...], seen, rank, known)
        rows = first_ref.shape[0]
        keep_refs[k][...] = part[:rows]
        give_refs[k][...] = part[rows:]


def near_kernel(anc, lens, place, fresh_ref, *refs):
    query_ref, acc_ref, max_ref, sum_ref, got_ref, moved_ref, other_ref, cache_ref, part_ref = refs
    local, span, width = cache_ref.shape
    rank = acc_ref.shape[1]
    start, other = place[0] * span, jnp.bitwise_xor(place[0], 1) * span
    ends = [lens[anc[p]] for p in range(local)]
    keys = jnp.concatenate([moved_ref[...], other_ref[...]], axis=0)
    seen = visible(query_ref.shape[0], ends, [start, other], span)
    level = jnp.sum(got_ref[:, rank:].astype(F32), axis=1, keepdims=True)
    known = [
        (max_ref[:, 0:1], sum_ref[:, 0:1], acc_ref[...]),
        (level, 1.0, got_ref[:, :rank].astype(F32)),
    ]
    part_ref[...] = attend(query_ref[...], keys, seen, rank, known)
    for p in range(local):
        at = start + lax.broadcasted_iota(jnp.int32, (span, 1), 0) == ends[p]
        cache_ref[p] = jnp.where(at, fresh_ref[pl.ds(p, 1), :], moved_ref[pl.ds(p * span, span)])


def chip_kernel(count, *refs):
    for k in range(count):
        out_ref = refs[2 * count + k]
        rank = out_ref.shape[1] - LANES
        out_ref[...] = packed(*merged([refs[k][...], refs[count + k][...]], rank))


def chip_merge(keep, got):
    return pl.pallas_call(
        functools.partial(chip_kernel, len(keep)),
        out_shape=[shape(k.shape) for k in keep],
        in_specs=[VMEM] * (2 * len(keep)),
        out_specs=[VMEM] * len(keep),
        compiler_params=PARAMS,
        name="chip_merge",
    )(*keep, *got)


def final_kernel(count, *refs):
    part_refs, (w_ref, out_ref, values) = refs[:count], refs[count:]
    heads, rank, reach = w_ref.shape
    local = out_ref.shape[0]
    latent = merged([ref[...] for ref in part_refs], rank)[0].astype(BF16)
    first = lax.broadcasted_iota(jnp.int32, (2 * local, reach), 0) < local
    for h in range(0, heads, 2):
        two = latent[h * local : (h + 2) * local]
        weights = jnp.concatenate([w_ref[h], w_ref[h + 1]], axis=1)
        both = jnp.dot(two, weights, preferred_element_type=F32)
        values[pl.ds(h * local, 2 * local), :] = jnp.where(first, both[:, :reach], both[:, reach:])
    for p in range(local):
        out_ref[p] = values[pl.ds(p, heads, stride=local), :].astype(BF16)


def on_device(q_nope, q_rope, w_uk, w_uv, prefix, private_caches, new_latent, ancestors, lengths):
    local, heads, nope = q_nope.shape
    span, width = private_caches.shape[1:]
    rank, reach = w_uv.shape[1:]
    rows = local * heads
    seq_size, dom_size = lax.axis_size("seq"), lax.axis_size("dom")
    cores = 2
    chips = seq_size // cores
    place = jnp.stack([lax.axis_index("seq"), lax.axis_index("dom")]).astype(jnp.int32)
    block = pl.pallas_call(
        functools.partial(pack_kernel, rank),
        out_shape=shape((local * span // 2, 2 * width)),
        in_specs=[VMEM],
        out_specs=VMEM,
        compiler_params=PARAMS,
        name="pack",
    )(private_caches)
    nope_rows, rope_rows = (jnp.swapaxes(q, 0, 1).reshape(rows, -1) for q in (q_nope, q_rope))
    line = dom_size == 4
    if line:
        far = lax.ppermute(block, "dom", [(1, 2), (2, 1)])
        swap = [(0, 1), (1, 0), (2, 3), (3, 2)]
        theirs = lax.ppermute(ancestors, "dom", swap)
    else:
        blocks = [block] + [
            lax.ppermute(block, "dom", [(i, (i + k) % dom_size) for i in range(dom_size)])
            for k in range(1, dom_size)
        ]

    if line:
        theirs, nope_rows = lax.optimization_barrier((theirs, nope_rows))
    pieces = math.gcd(heads // 4, 4)
    own = pl.pallas_call(
        functools.partial(project_kernel, pieces, local),
        out_shape=shape((rows, width)),
        in_specs=[VMEM] * 2 + [HBM],
        out_specs=VMEM,
        scratch_shapes=[pltpu.VMEM(w_uk.shape, BF16), pltpu.SemaphoreType.DMA((pieces,))],
        compiler_params=STREAM,
        name="project",
    )(nope_rows, rope_rows, w_uk)
    keys = prefix.T
    if line:
        sent, own = lax.optimization_barrier((block, own))
        middle = lax.ppermute(sent, "dom", [(0, 2), (3, 1)])

    def pairs(turn, flip):
        return [
            (x * cores + c, (x + turn) % chips * cores + (c ^ flip))
            for x in range(chips)
            for c in range(cores)
        ]

    def back(turn, flip):
        return [(b, a) for a, b in pairs(turn, flip)]

    routes = [(t, f) for t in range(chips) for f in range(cores)]
    queries = [own if r == (0, 0) else lax.ppermute(own, "seq", pairs(*r)) for r in routes]
    if line:
        far, queries[1] = lax.optimization_barrier((far, queries[1]))
    stages = []
    for t in range(chips):
        asked = queries[2 * t : 2 * t + 2]
        stage = [*asked, *prefix_attention(asked, keys, rank, t == 0)]
        stages.append(stage)
        if t == 0:
            given = lax.ppermute(stage.pop(), "seq", pairs(0, 1))
        if line and t == 0:
            chosen = pl.pallas_call(
                select_kernel,
                out_shape=shape(block.shape),
                in_specs=[SMEM] * 2 + [ANY] * 4,
                out_specs=VMEM,
                scratch_shapes=[pltpu.SemaphoreType.DMA((local,))],
                compiler_params=PARAMS,
                cost_estimate=pl.CostEstimate(flops=0, bytes_accessed=0, transcendentals=0),
                name="select",
            )(theirs, place, block, middle, far, stage[3])
            blocks = [block, lax.ppermute(chosen, "dom", swap), middle, far]

    part = shape((rows, rank + LANES))
    others = chips - 1
    far_results = pl.pallas_call(
        functools.partial(far_kernel, others, len(blocks), line),
        out_shape=[shape((local * span, width))] + [part] * (2 * others),
        in_specs=[SMEM] * 3 + [VMEM] * (5 * others) + [ANY] * len(blocks),
        out_specs=[VMEM] * (1 + 2 * others),
        scratch_shapes=[
            pltpu.VMEM(block.shape, BF16),
            pltpu.SemaphoreType.DMA((local,)),
        ],
        compiler_params=PARAMS,
        name="suffix_far",
    )(ancestors, lengths, place, *[a for stage in stages[1:] for a in stage], *blocks)
    moved = far_results[0]
    keep, give = far_results[1 : 1 + others], far_results[1 + others :]
    sums = chip_merge(keep, [lax.ppermute(g, "seq", pairs(0, 1)) for g in give])
    parts = [lax.ppermute(s, "seq", back(t, 0)) for t, s in enumerate(sums, 1)]
    other = lax.ppermute(moved, "seq", pairs(0, 1))

    moved, _ = lax.optimization_barrier((moved, sums[0]))
    query, _, acc, level, mass = stages[0]
    new_caches, own_part = pl.pallas_call(
        near_kernel,
        out_shape=[shape(private_caches.shape), part],
        in_specs=[SMEM] * 3 + [VMEM] * 8,
        out_specs=[VMEM] * 2,
        compiler_params=PARAMS,
        name="suffix_near",
    )(ancestors, lengths, place, new_latent, query, acc, level, mass, given, moved, other)
    parts.append(own_part)

    head_values = pl.pallas_call(
        functools.partial(final_kernel, chips),
        out_shape=shape((local, heads, reach)),
        in_specs=[VMEM] * (chips + 1),
        out_specs=VMEM,
        scratch_shapes=[pltpu.VMEM((rows, reach), F32)],
        compiler_params=PARAMS,
        name="final",
    )(*parts, w_uv)
    return (head_values, new_caches)


def solution(mesh):
    placed = (
        P(("group", "dom"), "seq", None),
        P(("group", "dom"), "seq", None),
        P("seq", None, None),
        P("seq", None, None),
        P(("group", "seq"), None),
        P(("group", "dom"), "seq", None),
        P(("group", "dom"), None),
        P(("group", "dom")),
        P("group"),
    )
    return jax.shard_map(
        on_device,
        mesh=mesh,
        in_specs=placed,
        out_specs=(P(("group", "dom"), "seq", None), P(("group", "dom"), "seq", None)),
        check_vma=False,
    )
```

```python
import functools
import math

import jax
import jax.numpy as jnp
from jax import lax
from jax.experimental import pallas as pl
from jax.experimental.pallas import tpu as pltpu
from jax.sharding import PartitionSpec as P

ROPE = 64
NOPE = 128
SCALE2 = (NOPE + ROPE) ** (-0.5) * math.log2(math.e)
HIDDEN = -1e30
LANES = 128
F32 = jnp.float32
BF16 = jnp.bfloat16
NT = (((1,), (1,)), ((), ()))

VMEM = pl.BlockSpec(memory_space=pltpu.VMEM)
SMEM = pl.BlockSpec(memory_space=pltpu.SMEM)
ANY = pl.BlockSpec(memory_space=pl.ANY)
HBM = pl.BlockSpec(memory_space=pltpu.HBM)
PARAMS = pltpu.CompilerParams(vmem_limit_bytes=40 * 1024 * 1024)
STREAM = pltpu.CompilerParams(vmem_limit_bytes=51 * 1024 * 1024)


def shape(dims, dtype=BF16):
    return jax.ShapeDtypeStruct(dims, dtype)


def pack_kernel(rank, cache_ref, out_ref):
    local, span, _ = cache_ref.shape
    some = span // 2
    for p in range(local):
        part = pl.ds(p * some, some)
        first, second = cache_ref[p, :some], cache_ref[p, some:]
        out_ref[part, :rank] = first[:, :rank]
        out_ref[part, rank : 2 * rank] = second[:, :rank]
        out_ref[part, 2 * rank :] = jnp.concatenate([first[:, rank:], second[:, rank:]], axis=1)


def project_kernel(
    pieces, local, nope_ref, rope_ref, w_hbm, own_ref, w_ref, sems
):
    heads, _, rank = w_ref.shape
    piece = heads // pieces
    fetches = [
        pltpu.make_async_copy(
            w_hbm.at[pl.ds(i * piece, piece)], w_ref.at[pl.ds(i * piece, piece)], sems.at[i]
        )
        for i in range(pieces)
    ]
    for fetch in fetches:
        fetch.start()
    nope = nope_ref[...].astype(F32)
    width = nope.shape[1]
    first = lax.broadcasted_iota(jnp.int32, (2 * local, width), 0) < local

    def pair(h):
        two = nope[h * local : (h + 2) * local]
        left = jnp.concatenate([jnp.where(first, two, 0.0), jnp.where(first, 0.0, two)], axis=1)
        weights = w_ref[pl.ds(h, 2)].reshape(2 * width, rank)
        return jnp.dot(left.astype(BF16), weights, preferred_element_type=F32)

    own_ref[:, rank:] = rope_ref[...]
    for h in range(0, heads, 4):
        if h % piece == 0:
            fetches[h // piece].wait()
        own_ref[pl.ds(h * local, 4 * local), :rank] = jnp.concatenate(
            [pair(i) for i in (h, h + 2)], axis=0
        ).astype(BF16)


def prefix_kernel(count, tiles, *refs):
    query_refs = refs[:count]
    keys_hbm, out_ref, max_ref, sum_ref, *give_ref, acc_ref, keys_ref, sems = refs[count:]
    rank = acc_ref.shape[1]
    tile = keys_ref.shape[1] // tiles
    parts = [pl.ds(i * tile, tile) for i in range(tiles)]
    fetches = [
        pltpu.make_async_copy(keys_hbm.at[:, part], keys_ref.at[:, part], sems.at[i])
        for i, part in enumerate(parts)
    ]
    for fetch in fetches:
        fetch.start()
    queries = jnp.concatenate([ref[...] for ref in query_refs], axis=0)

    def score(i):
        fetches[i].wait()
        return jnp.dot(queries, keys_ref[:, parts[i]], preferred_element_type=F32) * SCALE2

    ahead = score(0)
    for i in range(tiles):
        scores = ahead
        if i + 1 < tiles:
            ahead = score(i + 1)
        top = jnp.max(scores, axis=1, keepdims=True)
        if i > 0:
            top = jnp.maximum(top, largest)
        weights = jnp.exp2(scores - top)
        total = jnp.sum(weights, axis=1, keepdims=True)
        acc = lax.dot_general(
            weights.astype(BF16), keys_ref[:rank, parts[i]], NT, preferred_element_type=F32
        )
        if i > 0:
            factor = jnp.exp2(largest - top)
            total = total + running * factor
            acc = acc + acc_ref[...] * factor
        largest, running = top, total
        if i < tiles - 1:
            acc_ref[...] = acc
    kept = out_ref.shape[0]
    out_ref[...] = acc[:kept]
    max_ref[...] = jnp.broadcast_to(largest[:kept], max_ref.shape)
    sum_ref[...] = jnp.broadcast_to(running[:kept], sum_ref.shape)
    if give_ref:
        level = largest[kept:] + jnp.log2(running[kept:])
        give_ref[0][...] = packed(acc[kept:] * (1.0 / running[kept:]), level)


def prefix_attention(queries, keys, rank, give, tiles=4):
    rows = sum(q.shape[0] for q in queries)
    kept = queries[0].shape[0] if give else rows
    width, length = keys.shape
    out = [shape((kept, rank), F32)] + [shape((kept, LANES), F32)] * 2
    if give:
        out.append(shape((rows - kept, rank + LANES)))
    return pl.pallas_call(
        functools.partial(prefix_kernel, len(queries), tiles),
        out_shape=out,
        in_specs=[VMEM] * len(queries) + [HBM],
        out_specs=[VMEM] * len(out),
        scratch_shapes=[
            pltpu.VMEM((rows, rank), F32),
            pltpu.VMEM(keys.shape, BF16),
            pltpu.SemaphoreType.DMA((tiles,)),
        ],
        compiler_params=STREAM,
        cost_estimate=None if give else pl.CostEstimate(
            flops=2 * rows * length * (width + rank),
            bytes_accessed=2 * width * length,
            transcendentals=rows * length,
        ),
        name="prefix_attention",
    )(*queries, keys)


def packed(values, level):
    rows = values.shape[0]
    lane = lax.broadcasted_iota(jnp.int32, (rows, LANES), 1)
    high = level.astype(BF16).astype(F32)
    middle = (level - high).astype(BF16).astype(F32)
    low = level - high - middle
    stats = jnp.where(lane == 0, high, jnp.where(lane == 1, middle, jnp.where(lane == 2, low, 0.0)))
    return jnp.concatenate([values.astype(BF16), stats.astype(BF16)], axis=1)


def merged(parts, rank):
    levels = [jnp.sum(part[:, rank:].astype(F32), axis=1, keepdims=True) for part in parts]
    top = functools.reduce(jnp.maximum, levels)
    shares = [jnp.exp2(level - top) for level in levels]
    whole = functools.reduce(jnp.add, shares)
    acc = functools.reduce(
        jnp.add, [share * part[:, :rank].astype(F32) for share, part in zip(shares, parts)]
    )
    return acc * (1.0 / whole), top + jnp.log2(whole)


def visible(rows, ends, starts, span):
    local = len(ends)
    cols = len(starts) * local * span
    col = lax.broadcasted_iota(jnp.int32, (1, cols), 1)
    col_of = jnp.zeros_like(col)
    limit = jnp.full_like(col, ends[0] - starts[0])
    for at in range(1, len(starts) * local):
        begin, p = at * span, at % local
        later = col >= begin
        col_of = jnp.where(later, p, col_of)
        limit = jnp.where(later, ends[p] - starts[at // local] + begin, limit)
    col_of = jnp.where(col < limit, col_of, -1)
    row_of = lax.rem(lax.broadcasted_iota(jnp.int32, (rows, 1), 0), local)
    return row_of == col_of


def attend(queries, keys, seen, rank, known):
    scores = lax.dot_general(queries, keys, NT, preferred_element_type=F32)
    scores = jnp.where(seen, scores * SCALE2, HIDDEN)
    top = jnp.max(scores, axis=1, keepdims=True)
    for level, _, _ in known:
        top = jnp.maximum(top, level)
    weights = jnp.where(seen, jnp.exp2(scores - top), 0.0)
    total = jnp.sum(weights, axis=1, keepdims=True)
    acc = jnp.dot(weights.astype(BF16), keys[:, :rank], preferred_element_type=F32)
    for level, mass, part in known:
        factor = jnp.exp2(level - top)
        total = total + mass * factor
        acc = acc + part * factor
    return packed(acc * (1.0 / total), top + jnp.log2(total))


def gather_blocks(block_refs, picks, out_ref, sems):
    some = out_ref.shape[0] // len(picks)

    def copy(p, k, slot):
        return pltpu.make_async_copy(
            block_refs[k].at[pl.ds(pl.multiple_of(slot * some, some), some)],
            out_ref.at[pl.ds(p * some, some)],
            sems.at[p],
        )

    for p, (which, slot) in enumerate(picks):
        for k in range(len(block_refs)):

            @pl.when(which == k)
            def _():
                copy(p, k, slot).start()

    for p in range(len(picks)):
        copy(p, 0, 0).wait()


def at_end(place):
    return (place[1] == 0) | (place[1] == 3)


def select_kernel(theirs, place, *refs):
    block_refs, (_, out_ref, sems) = refs[:-3], refs[-3:]
    local = sems.shape[0]
    picks = []
    for p in range(local):
        apart = jnp.bitwise_xor(lax.div(theirs[p], local), place[1])
        which = jnp.where(at_end(place), 0, jnp.maximum(apart - 1, 0))
        picks.append((which, jnp.where(at_end(place), p, lax.rem(theirs[p], local))))
    gather_blocks(block_refs, picks, out_ref, sems)


def far_kernel(stages, sources, line, *refs):
    anc, lens, place = refs[:3]
    refs = refs[3:]
    stage_refs, refs = refs[: 5 * stages], refs[5 * stages :]
    block_refs, refs = refs[:sources], refs[sources:]
    moved_ref, refs = refs[0], refs[1:]
    keep_refs, give_refs = refs[:stages], refs[stages : 2 * stages]
    raw, sems = refs[2 * stages :]
    local = sems.shape[0]
    some = raw.shape[0] // local
    span, width = 2 * some, moved_ref.shape[1]
    rank = stage_refs[2].shape[1]

    picks = []
    for p in range(local):
        owner, slot = lax.div(anc[p], local), lax.rem(anc[p], local)
        if line:
            which = jnp.bitwise_xor(owner, place[1])
            chosen = at_end(place) & (which != 0)
            which = jnp.where(chosen, 1, which)
            slot = jnp.where(chosen, p, slot)
        else:
            which = lax.rem(place[1] - owner + sources, sources)
        picks.append((which, slot))
    gather_blocks(block_refs, picks, raw, sems)
    for p in range(local):
        for h in range(2):
            part, rows = pl.ds(p * some, some), pl.ds(p * span + h * some, some)
            rope = 2 * rank + h * (width - rank)
            moved_ref[rows, :rank] = raw[part, h * rank : (h + 1) * rank]
            moved_ref[rows, rank:] = raw[part, rope : rope + width - rank]

    ends = [lens[anc[p]] for p in range(local)]
    for k in range(stages):
        first_ref, second_ref, acc_ref, max_ref, sum_ref = stage_refs[5 * k : 5 * k + 5]
        queries = jnp.concatenate([first_ref[...], second_ref[...]], axis=0)
        seen = visible(queries.shape[0], ends, [place[0] * span], span)
        known = [(max_ref[:, 0:1], sum_ref[:, 0:1], acc_ref[...])]
        part = attend(queries, moved_ref[...], seen, rank, known)
        rows = first_ref.shape[0]
        keep_refs[k][...] = part[:rows]
        give_refs[k][...] = part[rows:]


def near_kernel(anc, lens, place, fresh_ref, *refs):
    query_ref, acc_ref, max_ref, sum_ref, got_ref, moved_ref, other_ref, cache_ref, part_ref = refs
    local, span, width = cache_ref.shape
    rank = acc_ref.shape[1]
    start, other = place[0] * span, jnp.bitwise_xor(place[0], 1) * span
    ends = [lens[anc[p]] for p in range(local)]
    keys = jnp.concatenate([moved_ref[...], other_ref[...]], axis=0)
    seen = visible(query_ref.shape[0], ends, [start, other], span)
    level = jnp.sum(got_ref[:, rank:].astype(F32), axis=1, keepdims=True)
    known = [
        (max_ref[:, 0:1], sum_ref[:, 0:1], acc_ref[...]),
        (level, 1.0, got_ref[:, :rank].astype(F32)),
    ]
    part_ref[...] = attend(query_ref[...], keys, seen, rank, known)
    for p in range(local):
        at = start + lax.broadcasted_iota(jnp.int32, (span, 1), 0) == ends[p]
        cache_ref[p] = jnp.where(at, fresh_ref[pl.ds(p, 1), :], moved_ref[pl.ds(p * span, span)])


def chip_kernel(count, *refs):
    for k in range(count):
        out_ref = refs[2 * count + k]
        rank = out_ref.shape[1] - LANES
        out_ref[...] = packed(*merged([refs[k][...], refs[count + k][...]], rank))


def chip_merge(keep, got):
    return pl.pallas_call(
        functools.partial(chip_kernel, len(keep)),
        out_shape=[shape(k.shape) for k in keep],
        in_specs=[VMEM] * (2 * len(keep)),
        out_specs=[VMEM] * len(keep),
        compiler_params=PARAMS,
        name="chip_merge",
    )(*keep, *got)


def final_kernel(count, *refs):
    part_refs, (w_ref, out_ref, values) = refs[:count], refs[count:]
    heads, rank, reach = w_ref.shape
    local = out_ref.shape[0]
    latent = merged([ref[...] for ref in part_refs], rank)[0].astype(BF16)
    first = lax.broadcasted_iota(jnp.int32, (2 * local, reach), 0) < local
    for h in range(0, heads, 2):
        two = latent[h * local : (h + 2) * local]
        weights = jnp.concatenate([w_ref[h], w_ref[h + 1]], axis=1)
        both = jnp.dot(two, weights, preferred_element_type=F32)
        values[pl.ds(h * local, 2 * local), :] = jnp.where(first, both[:, :reach], both[:, reach:])
    for p in range(local):
        out_ref[p] = values[pl.ds(p, heads, stride=local), :].astype(BF16)


def on_device(q_nope, q_rope, w_uk, w_uv, prefix, private_caches, new_latent, ancestors, lengths):
    local, heads, nope = q_nope.shape
    span, width = private_caches.shape[1:]
    rank, reach = w_uv.shape[1:]
    rows = local * heads
    seq_size, dom_size = lax.axis_size("seq"), lax.axis_size("dom")
    cores = 2
    chips = seq_size // cores
    place = jnp.stack([lax.axis_index("seq"), lax.axis_index("dom")]).astype(jnp.int32)
    block = pl.pallas_call(
        functools.partial(pack_kernel, rank),
        out_shape=shape((local * span // 2, 2 * width)),
        in_specs=[VMEM],
        out_specs=VMEM,
        compiler_params=PARAMS,
        name="pack",
    )(private_caches)
    nope_rows, rope_rows = (jnp.swapaxes(q, 0, 1).reshape(rows, -1) for q in (q_nope, q_rope))
    line = dom_size == 4
    if line:
        far = lax.ppermute(block, "dom", [(1, 2), (2, 1)])
        swap = [(0, 1), (1, 0), (2, 3), (3, 2)]
        block, named = lax.optimization_barrier((block, ancestors))
        theirs = lax.ppermute(named, "dom", swap)
    else:
        blocks = [block] + [
            lax.ppermute(block, "dom", [(i, (i + k) % dom_size) for i in range(dom_size)])
            for k in range(1, dom_size)
        ]

    if line:
        theirs, nope_rows = lax.optimization_barrier((theirs, nope_rows))
    pieces = math.gcd(heads // 4, 4)
    own = pl.pallas_call(
        functools.partial(project_kernel, pieces, local),
        out_shape=shape((rows, width)),
        in_specs=[VMEM] * 2 + [HBM],
        out_specs=VMEM,
        scratch_shapes=[pltpu.VMEM(w_uk.shape, BF16), pltpu.SemaphoreType.DMA((pieces,))],
        compiler_params=STREAM,
        name="project",
    )(nope_rows, rope_rows, w_uk)
    keys = prefix.T
    if line:
        sent, own = lax.optimization_barrier((block, own))
        middle = lax.ppermute(sent, "dom", [(0, 2), (3, 1)])

    def pairs(turn, flip):
        return [
            (x * cores + c, (x + turn) % chips * cores + (c ^ flip))
            for x in range(chips)
            for c in range(cores)
        ]

    def back(turn, flip):
        return [(b, a) for a, b in pairs(turn, flip)]

    routes = [(t, f) for t in range(chips) for f in range(cores)]
    queries = [own if r == (0, 0) else lax.ppermute(own, "seq", pairs(*r)) for r in routes]
    if line:
        far, queries[1] = lax.optimization_barrier((far, queries[1]))
    stages = []
    for t in range(chips):
        asked = queries[2 * t : 2 * t + 2]
        stage = [*asked, *prefix_attention(asked, keys, rank, t == 0)]
        stages.append(stage)
        if t == 0:
            given = lax.ppermute(stage.pop(), "seq", pairs(0, 1))
        if line and t == 0:
            chosen = pl.pallas_call(
                select_kernel,
                out_shape=shape(block.shape),
                in_specs=[SMEM] * 2 + [ANY] * 4,
                out_specs=VMEM,
                scratch_shapes=[pltpu.SemaphoreType.DMA((local,))],
                compiler_params=PARAMS,
                cost_estimate=pl.CostEstimate(flops=0, bytes_accessed=0, transcendentals=0),
                name="select",
            )(theirs, place, block, middle, far, stage[3])
            blocks = [block, lax.ppermute(chosen, "dom", swap), middle, far]

    part = shape((rows, rank + LANES))
    others = chips - 1
    far_results = pl.pallas_call(
        functools.partial(far_kernel, others, len(blocks), line),
        out_shape=[shape((local * span, width))] + [part] * (2 * others),
        in_specs=[SMEM] * 3 + [VMEM] * (5 * others) + [ANY] * len(blocks),
        out_specs=[VMEM] * (1 + 2 * others),
        scratch_shapes=[
            pltpu.VMEM(block.shape, BF16),
            pltpu.SemaphoreType.DMA((local,)),
        ],
        compiler_params=PARAMS,
        name="suffix_far",
    )(ancestors, lengths, place, *[a for stage in stages[1:] for a in stage], *blocks)
    moved = far_results[0]
    keep, give = far_results[1 : 1 + others], far_results[1 + others :]
    sums = chip_merge(keep, [lax.ppermute(g, "seq", pairs(0, 1)) for g in give])
    parts = [lax.ppermute(s, "seq", back(t, 0)) for t, s in enumerate(sums, 1)]
    other = lax.ppermute(moved, "seq", pairs(0, 1))

    moved, _ = lax.optimization_barrier((moved, sums[0]))
    query, _, acc, level, mass = stages[0]
    new_caches, own_part = pl.pallas_call(
        near_kernel,
        out_shape=[shape(private_caches.shape), part],
        in_specs=[SMEM] * 3 + [VMEM] * 8,
        out_specs=[VMEM] * 2,
        compiler_params=PARAMS,
        name="suffix_near",
    )(ancestors, lengths, place, new_latent, query, acc, level, mass, given, moved, other)
    parts.append(own_part)

    head_values = pl.pallas_call(
        functools.partial(final_kernel, chips),
        out_shape=shape((local, heads, reach)),
        in_specs=[VMEM] * (chips + 1),
        out_specs=VMEM,
        scratch_shapes=[pltpu.VMEM((rows, reach), F32)],
        compiler_params=PARAMS,
        name="final",
    )(*parts, w_uv)
    return (head_values, new_caches)


def solution(mesh):
    placed = (
        P(("group", "dom"), "seq", None),
        P(("group", "dom"), "seq", None),
        P("seq", None, None),
        P("seq", None, None),
        P(("group", "seq"), None),
        P(("group", "dom"), "seq", None),
        P(("group", "dom"), None),
        P(("group", "dom")),
        P("group"),
    )
    return jax.shard_map(
        on_device,
        mesh=mesh,
        in_specs=placed,
        out_specs=(P(("group", "dom"), "seq", None), P(("group", "dom"), "seq", None)),
        check_vma=False,
    )
```

```python
import functools
import math

import jax
import jax.numpy as jnp
from jax import lax
from jax.experimental import pallas as pl
from jax.experimental.pallas import tpu as pltpu
from jax.sharding import PartitionSpec as P

ROPE = 64
NOPE = 128
SCALE2 = (NOPE + ROPE) ** (-0.5) * math.log2(math.e)
HIDDEN = -1e30
LANES = 128
F32 = jnp.float32
BF16 = jnp.bfloat16
NT = (((1,), (1,)), ((), ()))

VMEM = pl.BlockSpec(memory_space=pltpu.VMEM)
SMEM = pl.BlockSpec(memory_space=pltpu.SMEM)
ANY = pl.BlockSpec(memory_space=pl.ANY)
HBM = pl.BlockSpec(memory_space=pltpu.HBM)
PARAMS = pltpu.CompilerParams(vmem_limit_bytes=40 * 1024 * 1024)
STREAM = pltpu.CompilerParams(vmem_limit_bytes=51 * 1024 * 1024)


def shape(dims, dtype=BF16):
    return jax.ShapeDtypeStruct(dims, dtype)


def pack_kernel(rank, cache_ref, out_ref):
    local, span, _ = cache_ref.shape
    some = span // 2
    for p in range(local):
        part = pl.ds(p * some, some)
        first, second = cache_ref[p, :some], cache_ref[p, some:]
        out_ref[part, :rank] = first[:, :rank]
        out_ref[part, rank : 2 * rank] = second[:, :rank]
        out_ref[part, 2 * rank :] = jnp.concatenate([first[:, rank:], second[:, rank:]], axis=1)


def project_kernel(
    pieces, local, nope_ref, rope_ref, w_hbm, own_ref, w_ref, sems
):
    heads, _, rank = w_ref.shape
    piece = heads // pieces
    fetches = [
        pltpu.make_async_copy(
            w_hbm.at[pl.ds(i * piece, piece)], w_ref.at[pl.ds(i * piece, piece)], sems.at[i]
        )
        for i in range(pieces)
    ]
    for fetch in fetches:
        fetch.start()
    nope = nope_ref[...].astype(F32)
    width = nope.shape[1]
    first = lax.broadcasted_iota(jnp.int32, (2 * local, width), 0) < local

    def pair(h):
        two = nope[h * local : (h + 2) * local]
        left = jnp.concatenate([jnp.where(first, two, 0.0), jnp.where(first, 0.0, two)], axis=1)
        weights = w_ref[pl.ds(h, 2)].reshape(2 * width, rank)
        return jnp.dot(left.astype(BF16), weights, preferred_element_type=F32)

    own_ref[:, rank:] = rope_ref[...]
    for h in range(0, heads, 4):
        if h % piece == 0:
            fetches[h // piece].wait()
        own_ref[pl.ds(h * local, 4 * local), :rank] = jnp.concatenate(
            [pair(i) for i in (h, h + 2)], axis=0
        ).astype(BF16)


def prefix_kernel(count, tiles, *refs):
    query_refs = refs[:count]
    keys_hbm, out_ref, max_ref, sum_ref, *give_ref, acc_ref, keys_ref, sems = refs[count:]
    rank = acc_ref.shape[1]
    tile = keys_ref.shape[1] // tiles
    parts = [pl.ds(i * tile, tile) for i in range(tiles)]
    fetches = [
        pltpu.make_async_copy(keys_hbm.at[:, part], keys_ref.at[:, part], sems.at[i])
        for i, part in enumerate(parts)
    ]
    for fetch in fetches:
        fetch.start()
    queries = jnp.concatenate([ref[...] for ref in query_refs], axis=0)

    def score(i):
        fetches[i].wait()
        return jnp.dot(queries, keys_ref[:, parts[i]], preferred_element_type=F32) * SCALE2

    ahead = score(0)
    for i in range(tiles):
        scores = ahead
        if i + 1 < tiles:
            ahead = score(i + 1)
        top = jnp.max(scores, axis=1, keepdims=True)
        if i > 0:
            top = jnp.maximum(top, largest)
        weights = jnp.exp2(scores - top)
        total = jnp.sum(weights, axis=1, keepdims=True)
        acc = lax.dot_general(
            weights.astype(BF16), keys_ref[:rank, parts[i]], NT, preferred_element_type=F32
        )
        if i > 0:
            factor = jnp.exp2(largest - top)
            total = total + running * factor
            acc = acc + acc_ref[...] * factor
        largest, running = top, total
        if i < tiles - 1:
            acc_ref[...] = acc
    kept = out_ref.shape[0]
    out_ref[...] = acc[:kept]
    max_ref[...] = jnp.broadcast_to(largest[:kept], max_ref.shape)
    sum_ref[...] = jnp.broadcast_to(running[:kept], sum_ref.shape)
    if give_ref:
        level = largest[kept:] + jnp.log2(running[kept:])
        give_ref[0][...] = packed(acc[kept:] * (1.0 / running[kept:]), level)


def prefix_attention(queries, keys, rank, give, tiles=4):
    rows = sum(q.shape[0] for q in queries)
    kept = queries[0].shape[0] if give else rows
    width, length = keys.shape
    out = [shape((kept, rank), F32)] + [shape((kept, LANES), F32)] * 2
    if give:
        out.append(shape((rows - kept, rank + LANES)))
    return pl.pallas_call(
        functools.partial(prefix_kernel, len(queries), tiles),
        out_shape=out,
        in_specs=[VMEM] * len(queries) + [HBM],
        out_specs=[VMEM] * len(out),
        scratch_shapes=[
            pltpu.VMEM((rows, rank), F32),
            pltpu.VMEM(keys.shape, BF16),
            pltpu.SemaphoreType.DMA((tiles,)),
        ],
        compiler_params=STREAM,
        cost_estimate=pl.CostEstimate(
            flops=0 if give else 2 * rows * length * (width + rank),
            bytes_accessed=0 if give else 2 * width * length,
            transcendentals=0 if give else rows * length,
        ),
        name="prefix_attention",
    )(*queries, keys)


def packed(values, level):
    rows = values.shape[0]
    lane = lax.broadcasted_iota(jnp.int32, (rows, LANES), 1)
    high = level.astype(BF16).astype(F32)
    middle = (level - high).astype(BF16).astype(F32)
    low = level - high - middle
    stats = jnp.where(lane == 0, high, jnp.where(lane == 1, middle, jnp.where(lane == 2, low, 0.0)))
    return jnp.concatenate([values.astype(BF16), stats.astype(BF16)], axis=1)


def merged(parts, rank):
    levels = [jnp.sum(part[:, rank:].astype(F32), axis=1, keepdims=True) for part in parts]
    top = functools.reduce(jnp.maximum, levels)
    shares = [jnp.exp2(level - top) for level in levels]
    whole = functools.reduce(jnp.add, shares)
    acc = functools.reduce(
        jnp.add, [share * part[:, :rank].astype(F32) for share, part in zip(shares, parts)]
    )
    return acc * (1.0 / whole), top + jnp.log2(whole)


def visible(rows, ends, starts, span):
    local = len(ends)
    cols = len(starts) * local * span
    col = lax.broadcasted_iota(jnp.int32, (1, cols), 1)
    col_of = jnp.zeros_like(col)
    limit = jnp.full_like(col, ends[0] - starts[0])
    for at in range(1, len(starts) * local):
        begin, p = at * span, at % local
        later = col >= begin
        col_of = jnp.where(later, p, col_of)
        limit = jnp.where(later, ends[p] - starts[at // local] + begin, limit)
    col_of = jnp.where(col < limit, col_of, -1)
    row_of = lax.rem(lax.broadcasted_iota(jnp.int32, (rows, 1), 0), local)
    return row_of == col_of


def attend(queries, keys, seen, rank, known):
    scores = lax.dot_general(queries, keys, NT, preferred_element_type=F32)
    scores = jnp.where(seen, scores * SCALE2, HIDDEN)
    top = jnp.max(scores, axis=1, keepdims=True)
    for level, _, _ in known:
        top = jnp.maximum(top, level)
    weights = jnp.where(seen, jnp.exp2(scores - top), 0.0)
    total = jnp.sum(weights, axis=1, keepdims=True)
    acc = jnp.dot(weights.astype(BF16), keys[:, :rank], preferred_element_type=F32)
    for level, mass, part in known:
        factor = jnp.exp2(level - top)
        total = total + mass * factor
        acc = acc + part * factor
    return packed(acc * (1.0 / total), top + jnp.log2(total))


def gather_blocks(block_refs, picks, out_ref, sems):
    some = out_ref.shape[0] // len(picks)

    def copy(p, k, slot):
        return pltpu.make_async_copy(
            block_refs[k].at[pl.ds(pl.multiple_of(slot * some, some), some)],
            out_ref.at[pl.ds(p * some, some)],
            sems.at[p],
        )

    for p, (which, slot) in enumerate(picks):
        for k in range(len(block_refs)):

            @pl.when(which == k)
            def _():
                copy(p, k, slot).start()

    for p in range(len(picks)):
        copy(p, 0, 0).wait()


def at_end(place):
    return (place[1] == 0) | (place[1] == 3)


def select_kernel(theirs, place, *refs):
    block_refs, (_, out_ref, sems) = refs[:-3], refs[-3:]
    local = sems.shape[0]
    picks = []
    for p in range(local):
        apart = jnp.bitwise_xor(lax.div(theirs[p], local), place[1])
        which = jnp.where(at_end(place), 0, jnp.maximum(apart - 1, 0))
        picks.append((which, jnp.where(at_end(place), p, lax.rem(theirs[p], local))))
    gather_blocks(block_refs, picks, out_ref, sems)


def far_kernel(stages, sources, line, *refs):
    anc, lens, place = refs[:3]
    refs = refs[3:]
    stage_refs, refs = refs[: 5 * stages], refs[5 * stages :]
    block_refs, refs = refs[:sources], refs[sources:]
    moved_ref, refs = refs[0], refs[1:]
    keep_refs, give_refs = refs[:stages], refs[stages : 2 * stages]
    raw, sems = refs[2 * stages :]
    local = sems.shape[0]
    some = raw.shape[0] // local
    span, width = 2 * some, moved_ref.shape[1]
    rank = stage_refs[2].shape[1]

    picks = []
    for p in range(local):
        owner, slot = lax.div(anc[p], local), lax.rem(anc[p], local)
        if line:
            which = jnp.bitwise_xor(owner, place[1])
            chosen = at_end(place) & (which != 0)
            which = jnp.where(chosen, 1, which)
            slot = jnp.where(chosen, p, slot)
        else:
            which = lax.rem(place[1] - owner + sources, sources)
        picks.append((which, slot))
    gather_blocks(block_refs, picks, raw, sems)
    for p in range(local):
        for h in range(2):
            part, rows = pl.ds(p * some, some), pl.ds(p * span + h * some, some)
            rope = 2 * rank + h * (width - rank)
            moved_ref[rows, :rank] = raw[part, h * rank : (h + 1) * rank]
            moved_ref[rows, rank:] = raw[part, rope : rope + width - rank]

    ends = [lens[anc[p]] for p in range(local)]
    for k in range(stages):
        first_ref, second_ref, acc_ref, max_ref, sum_ref = stage_refs[5 * k : 5 * k + 5]
        queries = jnp.concatenate([first_ref[...], second_ref[...]], axis=0)
        seen = visible(queries.shape[0], ends, [place[0] * span], span)
        known = [(max_ref[:, 0:1], sum_ref[:, 0:1], acc_ref[...])]
        part = attend(queries, moved_ref[...], seen, rank, known)
        rows = first_ref.shape[0]
        keep_refs[k][...] = part[:rows]
        give_refs[k][...] = part[rows:]


def near_kernel(anc, lens, place, fresh_ref, *refs):
    query_ref, acc_ref, max_ref, sum_ref, got_ref, moved_ref, other_ref, cache_ref, part_ref = refs
    local, span, width = cache_ref.shape
    rank = acc_ref.shape[1]
    start, other = place[0] * span, jnp.bitwise_xor(place[0], 1) * span
    ends = [lens[anc[p]] for p in range(local)]
    keys = jnp.concatenate([moved_ref[...], other_ref[...]], axis=0)
    seen = visible(query_ref.shape[0], ends, [start, other], span)
    level = jnp.sum(got_ref[:, rank:].astype(F32), axis=1, keepdims=True)
    known = [
        (max_ref[:, 0:1], sum_ref[:, 0:1], acc_ref[...]),
        (level, 1.0, got_ref[:, :rank].astype(F32)),
    ]
    part_ref[...] = attend(query_ref[...], keys, seen, rank, known)
    for p in range(local):
        at = start + lax.broadcasted_iota(jnp.int32, (span, 1), 0) == ends[p]
        cache_ref[p] = jnp.where(at, fresh_ref[pl.ds(p, 1), :], moved_ref[pl.ds(p * span, span)])


def chip_kernel(count, *refs):
    for k in range(count):
        out_ref = refs[2 * count + k]
        rank = out_ref.shape[1] - LANES
        out_ref[...] = packed(*merged([refs[k][...], refs[count + k][...]], rank))


def chip_merge(keep, got):
    return pl.pallas_call(
        functools.partial(chip_kernel, len(keep)),
        out_shape=[shape(k.shape) for k in keep],
        in_specs=[VMEM] * (2 * len(keep)),
        out_specs=[VMEM] * len(keep),
        compiler_params=PARAMS,
        name="chip_merge",
    )(*keep, *got)


def final_kernel(count, *refs):
    part_refs, (w_ref, out_ref, values) = refs[:count], refs[count:]
    heads, rank, reach = w_ref.shape
    local = out_ref.shape[0]
    latent = merged([ref[...] for ref in part_refs], rank)[0].astype(BF16)
    first = lax.broadcasted_iota(jnp.int32, (2 * local, reach), 0) < local
    for h in range(0, heads, 2):
        two = latent[h * local : (h + 2) * local]
        weights = jnp.concatenate([w_ref[h], w_ref[h + 1]], axis=1)
        both = jnp.dot(two, weights, preferred_element_type=F32)
        values[pl.ds(h * local, 2 * local), :] = jnp.where(first, both[:, :reach], both[:, reach:])
    for p in range(local):
        out_ref[p] = values[pl.ds(p, heads, stride=local), :].astype(BF16)


def on_device(q_nope, q_rope, w_uk, w_uv, prefix, private_caches, new_latent, ancestors, lengths):
    local, heads, nope = q_nope.shape
    span, width = private_caches.shape[1:]
    rank, reach = w_uv.shape[1:]
    rows = local * heads
    seq_size, dom_size = lax.axis_size("seq"), lax.axis_size("dom")
    cores = 2
    chips = seq_size // cores
    place = jnp.stack([lax.axis_index("seq"), lax.axis_index("dom")]).astype(jnp.int32)
    block = pl.pallas_call(
        functools.partial(pack_kernel, rank),
        out_shape=shape((local * span // 2, 2 * width)),
        in_specs=[VMEM],
        out_specs=VMEM,
        compiler_params=PARAMS,
        name="pack",
    )(private_caches)
    nope_rows, rope_rows = (jnp.swapaxes(q, 0, 1).reshape(rows, -1) for q in (q_nope, q_rope))
    line = dom_size == 4
    if line:
        far = lax.ppermute(block, "dom", [(1, 2), (2, 1)])
        swap = [(0, 1), (1, 0), (2, 3), (3, 2)]
        middle = lax.ppermute(block, "dom", [(0, 2), (3, 1)])
        theirs = lax.ppermute(ancestors, "dom", [(0, 1), (3, 2)])
    else:
        blocks = [block] + [
            lax.ppermute(block, "dom", [(i, (i + k) % dom_size) for i in range(dom_size)])
            for k in range(1, dom_size)
        ]

    pieces = math.gcd(heads // 4, 4)
    own = pl.pallas_call(
        functools.partial(project_kernel, pieces, local),
        out_shape=shape((rows, width)),
        in_specs=[VMEM] * 2 + [HBM],
        out_specs=VMEM,
        scratch_shapes=[pltpu.VMEM(w_uk.shape, BF16), pltpu.SemaphoreType.DMA((pieces,))],
        compiler_params=STREAM,
        name="project",
    )(nope_rows, rope_rows, w_uk)
    keys = prefix.T

    def pairs(turn, flip):
        return [
            (x * cores + c, (x + turn) % chips * cores + (c ^ flip))
            for x in range(chips)
            for c in range(cores)
        ]

    def back(turn, flip):
        return [(b, a) for a, b in pairs(turn, flip)]

    routes = [(t, f) for t in range(chips) for f in range(cores)]
    queries = [own if r == (0, 0) else lax.ppermute(own, "seq", pairs(*r)) for r in routes]
    if line:
        far, queries[1] = lax.optimization_barrier((far, queries[1]))
    stages = []
    for t in range(chips):
        asked = queries[2 * t : 2 * t + 2]
        stage = [*asked, *prefix_attention(asked, keys, rank, t == 0)]
        stages.append(stage)
        if t == 0:
            given = lax.ppermute(stage.pop(), "seq", pairs(0, 1))
        if line and t == 0:
            chosen = pl.pallas_call(
                select_kernel,
                out_shape=shape(block.shape),
                in_specs=[SMEM] * 2 + [ANY] * 4,
                out_specs=VMEM,
                scratch_shapes=[pltpu.SemaphoreType.DMA((local,))],
                compiler_params=PARAMS,
                cost_estimate=pl.CostEstimate(flops=0, bytes_accessed=0, transcendentals=0),
                name="select",
            )(theirs, place, block, middle, far, stage[3])
            blocks = [block, lax.ppermute(chosen, "dom", swap), middle, far]

    part = shape((rows, rank + LANES))
    others = chips - 1
    far_results = pl.pallas_call(
        functools.partial(far_kernel, others, len(blocks), line),
        out_shape=[shape((local * span, width))] + [part] * (2 * others),
        in_specs=[SMEM] * 3 + [VMEM] * (5 * others) + [ANY] * len(blocks),
        out_specs=[VMEM] * (1 + 2 * others),
        scratch_shapes=[
            pltpu.VMEM(block.shape, BF16),
            pltpu.SemaphoreType.DMA((local,)),
        ],
        compiler_params=PARAMS,
        name="suffix_far",
    )(ancestors, lengths, place, *[a for stage in stages[1:] for a in stage], *blocks)
    moved = far_results[0]
    keep, give = far_results[1 : 1 + others], far_results[1 + others :]
    sums = chip_merge(keep, [lax.ppermute(g, "seq", pairs(0, 1)) for g in give])
    parts = [lax.ppermute(s, "seq", back(t, 0)) for t, s in enumerate(sums, 1)]
    other = lax.ppermute(moved, "seq", pairs(0, 1))

    moved, _ = lax.optimization_barrier((moved, sums[0]))
    query, _, acc, level, mass = stages[0]
    new_caches, own_part = pl.pallas_call(
        near_kernel,
        out_shape=[shape(private_caches.shape), part],
        in_specs=[SMEM] * 3 + [VMEM] * 8,
        out_specs=[VMEM] * 2,
        compiler_params=PARAMS,
        name="suffix_near",
    )(ancestors, lengths, place, new_latent, query, acc, level, mass, given, moved, other)
    parts.append(own_part)

    head_values = pl.pallas_call(
        functools.partial(final_kernel, chips),
        out_shape=shape((local, heads, reach)),
        in_specs=[VMEM] * (chips + 1),
        out_specs=VMEM,
        scratch_shapes=[pltpu.VMEM((rows, reach), F32)],
        compiler_params=PARAMS,
        name="final",
    )(*parts, w_uv)
    return (head_values, new_caches)


def solution(mesh):
    placed = (
        P(("group", "dom"), "seq", None),
        P(("group", "dom"), "seq", None),
        P("seq", None, None),
        P("seq", None, None),
        P(("group", "seq"), None),
        P(("group", "dom"), "seq", None),
        P(("group", "dom"), None),
        P(("group", "dom")),
        P("group"),
    )
    return jax.shard_map(
        on_device,
        mesh=mesh,
        in_specs=placed,
        out_specs=(P(("group", "dom"), "seq", None), P(("group", "dom"), "seq", None)),
        check_vma=False,
    )
```

```python
import functools
import math

import jax
import jax.numpy as jnp
from jax import lax
from jax.experimental import pallas as pl
from jax.experimental.pallas import tpu as pltpu
from jax.sharding import PartitionSpec as P

ROPE = 64
NOPE = 128
SCALE2 = (NOPE + ROPE) ** (-0.5) * math.log2(math.e)
HIDDEN = -1e30
LANES = 128
F32 = jnp.float32
BF16 = jnp.bfloat16
NT = (((1,), (1,)), ((), ()))

VMEM = pl.BlockSpec(memory_space=pltpu.VMEM)
SMEM = pl.BlockSpec(memory_space=pltpu.SMEM)
ANY = pl.BlockSpec(memory_space=pl.ANY)
HBM = pl.BlockSpec(memory_space=pltpu.HBM)
PARAMS = pltpu.CompilerParams(vmem_limit_bytes=40 * 1024 * 1024)
STREAM = pltpu.CompilerParams(vmem_limit_bytes=51 * 1024 * 1024)


def shape(dims, dtype=BF16):
    return jax.ShapeDtypeStruct(dims, dtype)


def pack_kernel(rank, cache_ref, out_ref):
    local, span, _ = cache_ref.shape
    some = span // 2
    for p in range(local):
        part = pl.ds(p * some, some)
        first, second = cache_ref[p, :some], cache_ref[p, some:]
        out_ref[part, :rank] = first[:, :rank]
        out_ref[part, rank : 2 * rank] = second[:, :rank]
        out_ref[part, 2 * rank :] = jnp.concatenate([first[:, rank:], second[:, rank:]], axis=1)


def project_kernel(
    pieces, local, nope_ref, rope_ref, w_hbm, own_ref, w_ref, sems
):
    heads, _, rank = w_ref.shape
    piece = heads // pieces
    fetches = [
        pltpu.make_async_copy(
            w_hbm.at[pl.ds(i * piece, piece)], w_ref.at[pl.ds(i * piece, piece)], sems.at[i]
        )
        for i in range(pieces)
    ]
    for fetch in fetches:
        fetch.start()
    nope = nope_ref[...].astype(F32)
    width = nope.shape[1]
    first = lax.broadcasted_iota(jnp.int32, (2 * local, width), 0) < local

    def pair(h):
        two = nope[h * local : (h + 2) * local]
        left = jnp.concatenate([jnp.where(first, two, 0.0), jnp.where(first, 0.0, two)], axis=1)
        weights = w_ref[pl.ds(h, 2)].reshape(2 * width, rank)
        return jnp.dot(left.astype(BF16), weights, preferred_element_type=F32)

    own_ref[:, rank:] = rope_ref[...]
    for h in range(0, heads, 4):
        if h % piece == 0:
            fetches[h // piece].wait()
        own_ref[pl.ds(h * local, 4 * local), :rank] = jnp.concatenate(
            [pair(i) for i in (h, h + 2)], axis=0
        ).astype(BF16)


def prefix_kernel(count, tiles, *refs):
    query_refs = refs[:count]
    keys_hbm, out_ref, max_ref, sum_ref, *give_ref, acc_ref, keys_ref, sems = refs[count:]
    rank = acc_ref.shape[1]
    tile = keys_ref.shape[1] // tiles
    parts = [pl.ds(i * tile, tile) for i in range(tiles)]
    fetches = [
        pltpu.make_async_copy(keys_hbm.at[:, part], keys_ref.at[:, part], sems.at[i])
        for i, part in enumerate(parts)
    ]
    for fetch in fetches:
        fetch.start()
    queries = jnp.concatenate([ref[...] for ref in query_refs], axis=0)

    def score(i):
        fetches[i].wait()
        return jnp.dot(queries, keys_ref[:, parts[i]], preferred_element_type=F32) * SCALE2

    ahead = score(0)
    for i in range(tiles):
        scores = ahead
        if i + 1 < tiles:
            ahead = score(i + 1)
        top = jnp.max(scores, axis=1, keepdims=True)
        if i > 0:
            top = jnp.maximum(top, largest)
        weights = jnp.exp2(scores - top)
        total = jnp.sum(weights, axis=1, keepdims=True)
        acc = lax.dot_general(
            weights.astype(BF16), keys_ref[:rank, parts[i]], NT, preferred_element_type=F32
        )
        if i > 0:
            factor = jnp.exp2(largest - top)
            total = total + running * factor
            acc = acc + acc_ref[...] * factor
        largest, running = top, total
        if i < tiles - 1:
            acc_ref[...] = acc
    kept = out_ref.shape[0]
    out_ref[...] = acc[:kept]
    max_ref[...] = jnp.broadcast_to(largest[:kept], max_ref.shape)
    sum_ref[...] = jnp.broadcast_to(running[:kept], sum_ref.shape)
    if give_ref:
        level = largest[kept:] + jnp.log2(running[kept:])
        give_ref[0][...] = packed(acc[kept:] * (1.0 / running[kept:]), level)


def prefix_attention(queries, keys, rank, give, tiles=4):
    rows = sum(q.shape[0] for q in queries)
    kept = queries[0].shape[0] if give else rows
    width, length = keys.shape
    out = [shape((kept, rank), F32)] + [shape((kept, LANES), F32)] * 2
    if give:
        out.append(shape((rows - kept, rank + LANES)))
    return pl.pallas_call(
        functools.partial(prefix_kernel, len(queries), tiles),
        out_shape=out,
        in_specs=[VMEM] * len(queries) + [HBM],
        out_specs=[VMEM] * len(out),
        scratch_shapes=[
            pltpu.VMEM((rows, rank), F32),
            pltpu.VMEM(keys.shape, BF16),
            pltpu.SemaphoreType.DMA((tiles,)),
        ],
        compiler_params=STREAM,
        cost_estimate=pl.CostEstimate(
            flops=0 if give else 2 * rows * length * (width + rank),
            bytes_accessed=0 if give else 2 * width * length,
            transcendentals=0 if give else rows * length,
        ),
        name="prefix_attention",
    )(*queries, keys)


def packed(values, level):
    rows = values.shape[0]
    lane = lax.broadcasted_iota(jnp.int32, (rows, LANES), 1)
    high = level.astype(BF16).astype(F32)
    middle = (level - high).astype(BF16).astype(F32)
    low = level - high - middle
    stats = jnp.where(lane == 0, high, jnp.where(lane == 1, middle, jnp.where(lane == 2, low, 0.0)))
    return jnp.concatenate([values.astype(BF16), stats.astype(BF16)], axis=1)


def merged(parts, rank):
    levels = [jnp.sum(part[:, rank:].astype(F32), axis=1, keepdims=True) for part in parts]
    top = functools.reduce(jnp.maximum, levels)
    shares = [jnp.exp2(level - top) for level in levels]
    whole = functools.reduce(jnp.add, shares)
    acc = functools.reduce(
        jnp.add, [share * part[:, :rank].astype(F32) for share, part in zip(shares, parts)]
    )
    return acc * (1.0 / whole), top + jnp.log2(whole)


def visible(rows, ends, starts, span):
    local = len(ends)
    cols = len(starts) * local * span
    col = lax.broadcasted_iota(jnp.int32, (1, cols), 1)
    col_of = jnp.zeros_like(col)
    limit = jnp.full_like(col, ends[0] - starts[0])
    for at in range(1, len(starts) * local):
        begin, p = at * span, at % local
        later = col >= begin
        col_of = jnp.where(later, p, col_of)
        limit = jnp.where(later, ends[p] - starts[at // local] + begin, limit)
    col_of = jnp.where(col < limit, col_of, -1)
    row_of = lax.rem(lax.broadcasted_iota(jnp.int32, (rows, 1), 0), local)
    return row_of == col_of


def attend(queries, keys, seen, rank, known):
    scores = lax.dot_general(queries, keys, NT, preferred_element_type=F32)
    scores = jnp.where(seen, scores * SCALE2, HIDDEN)
    top = jnp.max(scores, axis=1, keepdims=True)
    for level, _, _ in known:
        top = jnp.maximum(top, level)
    weights = jnp.where(seen, jnp.exp2(scores - top), 0.0)
    total = jnp.sum(weights, axis=1, keepdims=True)
    acc = jnp.dot(weights.astype(BF16), keys[:, :rank], preferred_element_type=F32)
    for level, mass, part in known:
        factor = jnp.exp2(level - top)
        total = total + mass * factor
        acc = acc + part * factor
    return packed(acc * (1.0 / total), top + jnp.log2(total))


def gather_blocks(block_refs, picks, out_ref, sems):
    some = out_ref.shape[0] // len(picks)

    def copy(p, k, slot):
        return pltpu.make_async_copy(
            block_refs[k].at[pl.ds(pl.multiple_of(slot * some, some), some)],
            out_ref.at[pl.ds(p * some, some)],
            sems.at[p],
        )

    for p, (which, slot) in enumerate(picks):
        for k in range(len(block_refs)):

            @pl.when(which == k)
            def _():
                copy(p, k, slot).start()

    for p in range(len(picks)):
        copy(p, 0, 0).wait()


def at_end(place):
    return (place[1] == 0) | (place[1] == 3)


def select_kernel(theirs, place, *refs):
    block_refs, (_, out_ref, sems) = refs[:-3], refs[-3:]
    local = sems.shape[0]
    picks = []
    for p in range(local):
        apart = jnp.bitwise_xor(lax.div(theirs[p], local), place[1])
        which = jnp.where(at_end(place), 0, jnp.maximum(apart - 1, 0))
        picks.append((which, jnp.where(at_end(place), p, lax.rem(theirs[p], local))))
    gather_blocks(block_refs, picks, out_ref, sems)


def far_kernel(stages, sources, line, *refs):
    anc, lens, place = refs[:3]
    refs = refs[3:]
    stage_refs, refs = refs[: 5 * stages], refs[5 * stages :]
    block_refs, refs = refs[:sources], refs[sources:]
    moved_ref, refs = refs[0], refs[1:]
    keep_refs, give_refs = refs[:stages], refs[stages : 2 * stages]
    raw, sems = refs[2 * stages :]
    local = sems.shape[0]
    some = raw.shape[0] // local
    span, width = 2 * some, moved_ref.shape[1]
    rank = stage_refs[2].shape[1]

    picks = []
    for p in range(local):
        owner, slot = lax.div(anc[p], local), lax.rem(anc[p], local)
        if line:
            which = jnp.bitwise_xor(owner, place[1])
            chosen = at_end(place) & (which != 0)
            which = jnp.where(chosen, 1, which)
            slot = jnp.where(chosen, p, slot)
        else:
            which = lax.rem(place[1] - owner + sources, sources)
        picks.append((which, slot))
    gather_blocks(block_refs, picks, raw, sems)
    for p in range(local):
        for h in range(2):
            part, rows = pl.ds(p * some, some), pl.ds(p * span + h * some, some)
            rope = 2 * rank + h * (width - rank)
            moved_ref[rows, :rank] = raw[part, h * rank : (h + 1) * rank]
            moved_ref[rows, rank:] = raw[part, rope : rope + width - rank]

    ends = [lens[anc[p]] for p in range(local)]
    for k in range(stages):
        first_ref, second_ref, acc_ref, max_ref, sum_ref = stage_refs[5 * k : 5 * k + 5]
        queries = jnp.concatenate([first_ref[...], second_ref[...]], axis=0)
        seen = visible(queries.shape[0], ends, [place[0] * span], span)
        known = [(max_ref[:, 0:1], sum_ref[:, 0:1], acc_ref[...])]
        part = attend(queries, moved_ref[...], seen, rank, known)
        rows = first_ref.shape[0]
        keep_refs[k][...] = part[:rows]
        give_refs[k][...] = part[rows:]


def near_kernel(anc, lens, place, fresh_ref, *refs):
    query_ref, acc_ref, max_ref, sum_ref, got_ref, moved_ref, other_ref, cache_ref, part_ref = refs
    local, span, width = cache_ref.shape
    rank = acc_ref.shape[1]
    start, other = place[0] * span, jnp.bitwise_xor(place[0], 1) * span
    ends = [lens[anc[p]] for p in range(local)]
    keys = jnp.concatenate([moved_ref[...], other_ref[...]], axis=0)
    seen = visible(query_ref.shape[0], ends, [start, other], span)
    level = jnp.sum(got_ref[:, rank:].astype(F32), axis=1, keepdims=True)
    known = [
        (max_ref[:, 0:1], sum_ref[:, 0:1], acc_ref[...]),
        (level, 1.0, got_ref[:, :rank].astype(F32)),
    ]
    part_ref[...] = attend(query_ref[...], keys, seen, rank, known)
    for p in range(local):
        at = start + lax.broadcasted_iota(jnp.int32, (span, 1), 0) == ends[p]
        cache_ref[p] = jnp.where(at, fresh_ref[pl.ds(p, 1), :], moved_ref[pl.ds(p * span, span)])


def chip_kernel(count, *refs):
    for k in range(count):
        out_ref = refs[2 * count + k]
        rank = out_ref.shape[1] - LANES
        out_ref[...] = packed(*merged([refs[k][...], refs[count + k][...]], rank))


def chip_merge(keep, got):
    return pl.pallas_call(
        functools.partial(chip_kernel, len(keep)),
        out_shape=[shape(k.shape) for k in keep],
        in_specs=[VMEM] * (2 * len(keep)),
        out_specs=[VMEM] * len(keep),
        compiler_params=PARAMS,
        name="chip_merge",
    )(*keep, *got)


def final_kernel(count, *refs):
    part_refs, (w_ref, out_ref, values) = refs[:count], refs[count:]
    heads, rank, reach = w_ref.shape
    local = out_ref.shape[0]
    latent = merged([ref[...] for ref in part_refs], rank)[0].astype(BF16)
    first = lax.broadcasted_iota(jnp.int32, (2 * local, reach), 0) < local
    for h in range(0, heads, 2):
        two = latent[h * local : (h + 2) * local]
        weights = jnp.concatenate([w_ref[h], w_ref[h + 1]], axis=1)
        both = jnp.dot(two, weights, preferred_element_type=F32)
        values[pl.ds(h * local, 2 * local), :] = jnp.where(first, both[:, :reach], both[:, reach:])
    for p in range(local):
        out_ref[p] = values[pl.ds(p, heads, stride=local), :].astype(BF16)


def on_device(q_nope, q_rope, w_uk, w_uv, prefix, private_caches, new_latent, ancestors, lengths):
    local, heads, nope = q_nope.shape
    span, width = private_caches.shape[1:]
    rank, reach = w_uv.shape[1:]
    rows = local * heads
    seq_size, dom_size = lax.axis_size("seq"), lax.axis_size("dom")
    cores = 2
    chips = seq_size // cores
    place = jnp.stack([lax.axis_index("seq"), lax.axis_index("dom")]).astype(jnp.int32)
    block = pl.pallas_call(
        functools.partial(pack_kernel, rank),
        out_shape=shape((local * span // 2, 2 * width)),
        in_specs=[VMEM],
        out_specs=VMEM,
        compiler_params=PARAMS,
        name="pack",
    )(private_caches)
    nope_rows, rope_rows = (jnp.swapaxes(q, 0, 1).reshape(rows, -1) for q in (q_nope, q_rope))
    line = dom_size == 4
    if line:
        far = lax.ppermute(block, "dom", [(1, 2), (2, 1)])
        swap = [(0, 1), (1, 0), (2, 3), (3, 2)]
        middle = lax.ppermute(block, "dom", [(0, 2), (3, 1)])
        theirs = lax.ppermute(ancestors, "dom", [(0, 1), (3, 2)])
    else:
        blocks = [block] + [
            lax.ppermute(block, "dom", [(i, (i + k) % dom_size) for i in range(dom_size)])
            for k in range(1, dom_size)
        ]

    pieces = math.gcd(heads // 4, 4)
    own = pl.pallas_call(
        functools.partial(project_kernel, pieces, local),
        out_shape=shape((rows, width)),
        in_specs=[VMEM] * 2 + [HBM],
        out_specs=VMEM,
        scratch_shapes=[pltpu.VMEM(w_uk.shape, BF16), pltpu.SemaphoreType.DMA((pieces,))],
        compiler_params=STREAM,
        name="project",
    )(nope_rows, rope_rows, w_uk)
    keys = prefix.T

    def pairs(turn, flip):
        return [
            (x * cores + c, (x + turn) % chips * cores + (c ^ flip))
            for x in range(chips)
            for c in range(cores)
        ]

    def back(turn, flip):
        return [(b, a) for a, b in pairs(turn, flip)]

    routes = [(t, f) for t in range(chips) for f in range(cores)]
    queries = [own if r == (0, 0) else lax.ppermute(own, "seq", pairs(*r)) for r in routes]
    stages = []
    for t in range(chips):
        asked = queries[2 * t : 2 * t + 2]
        stage = [*asked, *prefix_attention(asked, keys, rank, t == 0)]
        stages.append(stage)
        if t == 0:
            given = lax.ppermute(stage.pop(), "seq", pairs(0, 1))
        if line and t == 0:
            chosen = pl.pallas_call(
                select_kernel,
                out_shape=shape(block.shape),
                in_specs=[SMEM] * 2 + [ANY] * 4,
                out_specs=VMEM,
                scratch_shapes=[pltpu.SemaphoreType.DMA((local,))],
                compiler_params=PARAMS,
                cost_estimate=pl.CostEstimate(flops=0, bytes_accessed=0, transcendentals=0),
                name="select",
            )(theirs, place, block, middle, far, stage[3])
            blocks = [block, lax.ppermute(chosen, "dom", swap), middle, far]

    part = shape((rows, rank + LANES))
    others = chips - 1
    far_results = pl.pallas_call(
        functools.partial(far_kernel, others, len(blocks), line),
        out_shape=[shape((local * span, width))] + [part] * (2 * others),
        in_specs=[SMEM] * 3 + [VMEM] * (5 * others) + [ANY] * len(blocks),
        out_specs=[VMEM] * (1 + 2 * others),
        scratch_shapes=[
            pltpu.VMEM(block.shape, BF16),
            pltpu.SemaphoreType.DMA((local,)),
        ],
        compiler_params=PARAMS,
        name="suffix_far",
    )(ancestors, lengths, place, *[a for stage in stages[1:] for a in stage], *blocks)
    moved = far_results[0]
    keep, give = far_results[1 : 1 + others], far_results[1 + others :]
    sums = chip_merge(keep, [lax.ppermute(g, "seq", pairs(0, 1)) for g in give])
    parts = [lax.ppermute(s, "seq", back(t, 0)) for t, s in enumerate(sums, 1)]
    other = lax.ppermute(moved, "seq", pairs(0, 1))

    moved, _ = lax.optimization_barrier((moved, sums[0]))
    query, _, acc, level, mass = stages[0]
    new_caches, own_part = pl.pallas_call(
        near_kernel,
        out_shape=[shape(private_caches.shape), part],
        in_specs=[SMEM] * 3 + [VMEM] * 8,
        out_specs=[VMEM] * 2,
        compiler_params=PARAMS,
        name="suffix_near",
    )(ancestors, lengths, place, new_latent, query, acc, level, mass, given, moved, other)
    parts.append(own_part)

    head_values = pl.pallas_call(
        functools.partial(final_kernel, chips),
        out_shape=shape((local, heads, reach)),
        in_specs=[VMEM] * (chips + 1),
        out_specs=VMEM,
        scratch_shapes=[pltpu.VMEM((rows, reach), F32)],
        compiler_params=PARAMS,
        name="final",
    )(*parts, w_uv)
    return (head_values, new_caches)


def solution(mesh):
    placed = (
        P(("group", "dom"), "seq", None),
        P(("group", "dom"), "seq", None),
        P("seq", None, None),
        P("seq", None, None),
        P(("group", "seq"), None),
        P(("group", "dom"), "seq", None),
        P(("group", "dom"), None),
        P(("group", "dom")),
        P("group"),
    )
    return jax.shard_map(
        on_device,
        mesh=mesh,
        in_specs=placed,
        out_specs=(P(("group", "dom"), "seq", None), P(("group", "dom"), "seq", None)),
        check_vma=False,
    )
```

```python
import functools
import math

import jax
import jax.numpy as jnp
from jax import lax
from jax.experimental import pallas as pl
from jax.experimental.pallas import tpu as pltpu
from jax.sharding import PartitionSpec as P

ROPE = 64
NOPE = 128
SCALE2 = (NOPE + ROPE) ** (-0.5) * math.log2(math.e)
HIDDEN = -1e30
LANES = 128
F32 = jnp.float32
BF16 = jnp.bfloat16
NT = (((1,), (1,)), ((), ()))

VMEM = pl.BlockSpec(memory_space=pltpu.VMEM)
SMEM = pl.BlockSpec(memory_space=pltpu.SMEM)
ANY = pl.BlockSpec(memory_space=pl.ANY)
HBM = pl.BlockSpec(memory_space=pltpu.HBM)
PARAMS = pltpu.CompilerParams(vmem_limit_bytes=40 * 1024 * 1024)
STREAM = pltpu.CompilerParams(vmem_limit_bytes=51 * 1024 * 1024)


def shape(dims, dtype=BF16):
    return jax.ShapeDtypeStruct(dims, dtype)


def pack_kernel(rank, cache_ref, out_ref):
    local, span, _ = cache_ref.shape
    some = span // 2
    for p in range(local):
        part = pl.ds(p * some, some)
        first, second = cache_ref[p, :some], cache_ref[p, some:]
        out_ref[part, :rank] = first[:, :rank]
        out_ref[part, rank : 2 * rank] = second[:, :rank]
        out_ref[part, 2 * rank :] = jnp.concatenate([first[:, rank:], second[:, rank:]], axis=1)


def project_kernel(pieces, local, asked_ref, w_hbm, own_ref, w_ref, sems):
    heads, _, rank = w_ref.shape
    piece = heads // pieces
    fetches = [
        pltpu.make_async_copy(
            w_hbm.at[pl.ds(i * piece, piece)], w_ref.at[pl.ds(i * piece, piece)], sems.at[i]
        )
        for i in range(pieces)
    ]
    for fetch in fetches:
        fetch.start()
    width = w_ref.shape[1]
    nope = asked_ref[:, :width].astype(F32)
    first = lax.broadcasted_iota(jnp.int32, (2 * local, width), 0) < local

    def pair(h):
        two = nope[h * local : (h + 2) * local]
        left = jnp.concatenate([jnp.where(first, two, 0.0), jnp.where(first, 0.0, two)], axis=1)
        weights = w_ref[pl.ds(h, 2)].reshape(2 * width, rank)
        return jnp.dot(left.astype(BF16), weights, preferred_element_type=F32)

    own_ref[:, rank:] = asked_ref[:, width:]
    for h in range(0, heads, 4):
        if h % piece == 0:
            fetches[h // piece].wait()
        own_ref[pl.ds(h * local, 4 * local), :rank] = jnp.concatenate(
            [pair(i) for i in (h, h + 2)], axis=0
        ).astype(BF16)


def prefix_kernel(count, tiles, *refs):
    query_refs = refs[:count]
    keys_hbm, out_ref, max_ref, sum_ref, *give_ref, acc_ref, keys_ref, sems = refs[count:]
    rank = acc_ref.shape[1]
    tile = keys_ref.shape[1] // tiles
    parts = [pl.ds(i * tile, tile) for i in range(tiles)]
    fetches = [
        pltpu.make_async_copy(keys_hbm.at[:, part], keys_ref.at[:, part], sems.at[i])
        for i, part in enumerate(parts)
    ]
    for fetch in fetches:
        fetch.start()
    queries = jnp.concatenate([ref[...] for ref in query_refs], axis=0)

    def score(i):
        fetches[i].wait()
        return jnp.dot(queries, keys_ref[:, parts[i]], preferred_element_type=F32) * SCALE2

    ahead = score(0)
    for i in range(tiles):
        scores = ahead
        if i + 1 < tiles:
            ahead = score(i + 1)
        top = jnp.max(scores, axis=1, keepdims=True)
        if i > 0:
            top = jnp.maximum(top, largest)
        weights = jnp.exp2(scores - top)
        total = jnp.sum(weights, axis=1, keepdims=True)
        acc = lax.dot_general(
            weights.astype(BF16), keys_ref[:rank, parts[i]], NT, preferred_element_type=F32
        )
        if i > 0:
            factor = jnp.exp2(largest - top)
            total = total + running * factor
            acc = acc + acc_ref[...] * factor
        largest, running = top, total
        if i < tiles - 1:
            acc_ref[...] = acc
    kept = out_ref.shape[0]
    out_ref[...] = acc[:kept]
    max_ref[...] = jnp.broadcast_to(largest[:kept], max_ref.shape)
    sum_ref[...] = jnp.broadcast_to(running[:kept], sum_ref.shape)
    if give_ref:
        level = largest[kept:] + jnp.log2(running[kept:])
        give_ref[0][...] = packed(acc[kept:] * (1.0 / running[kept:]), level)


def prefix_attention(queries, keys, rank, give, tiles=4):
    rows = sum(q.shape[0] for q in queries)
    kept = queries[0].shape[0] if give else rows
    width, length = keys.shape
    out = [shape((kept, rank), F32)] + [shape((kept, LANES), F32)] * 2
    if give:
        out.append(shape((rows - kept, rank + LANES)))
    return pl.pallas_call(
        functools.partial(prefix_kernel, len(queries), tiles),
        out_shape=out,
        in_specs=[VMEM] * len(queries) + [HBM],
        out_specs=[VMEM] * len(out),
        scratch_shapes=[
            pltpu.VMEM((rows, rank), F32),
            pltpu.VMEM(keys.shape, BF16),
            pltpu.SemaphoreType.DMA((tiles,)),
        ],
        compiler_params=STREAM,
        cost_estimate=pl.CostEstimate(
            flops=0 if give else 2 * rows * length * (width + rank),
            bytes_accessed=0 if give else 2 * width * length,
            transcendentals=0 if give else rows * length,
        ),
        name="prefix_attention",
    )(*queries, keys)


def packed(values, level):
    rows = values.shape[0]
    lane = lax.broadcasted_iota(jnp.int32, (rows, LANES), 1)
    high = level.astype(BF16).astype(F32)
    middle = (level - high).astype(BF16).astype(F32)
    low = level - high - middle
    stats = jnp.where(lane == 0, high, jnp.where(lane == 1, middle, jnp.where(lane == 2, low, 0.0)))
    return jnp.concatenate([values.astype(BF16), stats.astype(BF16)], axis=1)


def merged(parts, rank):
    levels = [jnp.sum(part[:, rank:].astype(F32), axis=1, keepdims=True) for part in parts]
    top = functools.reduce(jnp.maximum, levels)
    shares = [jnp.exp2(level - top) for level in levels]
    whole = functools.reduce(jnp.add, shares)
    acc = functools.reduce(
        jnp.add, [share * part[:, :rank].astype(F32) for share, part in zip(shares, parts)]
    )
    return acc * (1.0 / whole), top + jnp.log2(whole)


def visible(rows, ends, starts, span):
    local = len(ends)
    cols = len(starts) * local * span
    col = lax.broadcasted_iota(jnp.int32, (1, cols), 1)
    col_of = jnp.zeros_like(col)
    limit = jnp.full_like(col, ends[0] - starts[0])
    for at in range(1, len(starts) * local):
        begin, p = at * span, at % local
        later = col >= begin
        col_of = jnp.where(later, p, col_of)
        limit = jnp.where(later, ends[p] - starts[at // local] + begin, limit)
    col_of = jnp.where(col < limit, col_of, -1)
    row_of = lax.rem(lax.broadcasted_iota(jnp.int32, (rows, 1), 0), local)
    return row_of == col_of


def attend(queries, keys, seen, rank, known):
    scores = lax.dot_general(queries, keys, NT, preferred_element_type=F32)
    scores = jnp.where(seen, scores * SCALE2, HIDDEN)
    top = jnp.max(scores, axis=1, keepdims=True)
    for level, _, _ in known:
        top = jnp.maximum(top, level)
    weights = jnp.where(seen, jnp.exp2(scores - top), 0.0)
    total = jnp.sum(weights, axis=1, keepdims=True)
    acc = jnp.dot(weights.astype(BF16), keys[:, :rank], preferred_element_type=F32)
    for level, mass, part in known:
        factor = jnp.exp2(level - top)
        total = total + mass * factor
        acc = acc + part * factor
    return packed(acc * (1.0 / total), top + jnp.log2(total))


def gather_blocks(block_refs, picks, out_ref, sems):
    some = out_ref.shape[0] // len(picks)

    def copy(p, k, slot):
        return pltpu.make_async_copy(
            block_refs[k].at[pl.ds(pl.multiple_of(slot * some, some), some)],
            out_ref.at[pl.ds(p * some, some)],
            sems.at[p],
        )

    for p, (which, slot) in enumerate(picks):
        for k in range(len(block_refs)):

            @pl.when(which == k)
            def _():
                copy(p, k, slot).start()

    for p in range(len(picks)):
        copy(p, 0, 0).wait()


def at_end(place):
    return (place[1] == 0) | (place[1] == 3)


def select_kernel(theirs, place, *refs):
    block_refs, (_, out_ref, sems) = refs[:-3], refs[-3:]
    local = sems.shape[0]
    picks = []
    for p in range(local):
        apart = jnp.bitwise_xor(lax.div(theirs[p], local), place[1])
        which = jnp.where(at_end(place) | (apart < 2), 0, 4 - apart)
        picks.append((which, jnp.where(at_end(place), p, lax.rem(theirs[p], local))))
    gather_blocks(block_refs, picks, out_ref, sems)


def far_kernel(stages, sources, line, *refs):
    anc, lens, place = refs[:3]
    refs = refs[3:]
    stage_refs, refs = refs[: 5 * stages], refs[5 * stages :]
    block_refs, refs = refs[:sources], refs[sources:]
    moved_ref, refs = refs[0], refs[1:]
    keep_refs, give_refs = refs[:stages], refs[stages : 2 * stages]
    raw, sems = refs[2 * stages :]
    local = sems.shape[0]
    some = raw.shape[0] // local
    span, width = 2 * some, moved_ref.shape[1]
    rank = stage_refs[2].shape[1]

    picks = []
    for p in range(local):
        owner, slot = lax.div(anc[p], local), lax.rem(anc[p], local)
        if line:
            which = jnp.bitwise_xor(owner, place[1])
            chosen = at_end(place) & (which != 0)
            which = jnp.where(chosen, 1, which)
            slot = jnp.where(chosen, p, slot)
        else:
            which = lax.rem(place[1] - owner + sources, sources)
        picks.append((which, slot))
    gather_blocks(block_refs, picks, raw, sems)
    for p in range(local):
        for h in range(2):
            part, rows = pl.ds(p * some, some), pl.ds(p * span + h * some, some)
            rope = 2 * rank + h * (width - rank)
            moved_ref[rows, :rank] = raw[part, h * rank : (h + 1) * rank]
            moved_ref[rows, rank:] = raw[part, rope : rope + width - rank]

    ends = [lens[anc[p]] for p in range(local)]
    for k in range(stages):
        first_ref, second_ref, acc_ref, max_ref, sum_ref = stage_refs[5 * k : 5 * k + 5]
        queries = jnp.concatenate([first_ref[...], second_ref[...]], axis=0)
        seen = visible(queries.shape[0], ends, [place[0] * span], span)
        known = [(max_ref[:, 0:1], sum_ref[:, 0:1], acc_ref[...])]
        part = attend(queries, moved_ref[...], seen, rank, known)
        rows = first_ref.shape[0]
        keep_refs[k][...] = part[:rows]
        give_refs[k][...] = part[rows:]


def near_kernel(anc, lens, place, fresh_ref, *refs):
    query_ref, acc_ref, max_ref, sum_ref, got_ref, moved_ref, other_ref, cache_ref, part_ref = refs
    local, span, width = cache_ref.shape
    rank = acc_ref.shape[1]
    start, other = place[0] * span, jnp.bitwise_xor(place[0], 1) * span
    ends = [lens[anc[p]] for p in range(local)]
    keys = jnp.concatenate([moved_ref[...], other_ref[...]], axis=0)
    seen = visible(query_ref.shape[0], ends, [start, other], span)
    level = jnp.sum(got_ref[:, rank:].astype(F32), axis=1, keepdims=True)
    known = [
        (max_ref[:, 0:1], sum_ref[:, 0:1], acc_ref[...]),
        (level, 1.0, got_ref[:, :rank].astype(F32)),
    ]
    part_ref[...] = attend(query_ref[...], keys, seen, rank, known)
    for p in range(local):
        at = start + lax.broadcasted_iota(jnp.int32, (span, 1), 0) == ends[p]
        cache_ref[p] = jnp.where(at, fresh_ref[pl.ds(p, 1), :], moved_ref[pl.ds(p * span, span)])


def chip_kernel(count, *refs):
    for k in range(count):
        out_ref = refs[2 * count + k]
        rank = out_ref.shape[1] - LANES
        out_ref[...] = packed(*merged([refs[k][...], refs[count + k][...]], rank))


def chip_merge(keep, got):
    return pl.pallas_call(
        functools.partial(chip_kernel, len(keep)),
        out_shape=[shape(k.shape) for k in keep],
        in_specs=[VMEM] * (2 * len(keep)),
        out_specs=[VMEM] * len(keep),
        compiler_params=PARAMS,
        name="chip_merge",
    )(*keep, *got)


def final_kernel(count, *refs):
    part_refs, (w_ref, out_ref, values) = refs[:count], refs[count:]
    heads, rank, reach = w_ref.shape
    local = out_ref.shape[0]
    latent = merged([ref[...] for ref in part_refs], rank)[0].astype(BF16)
    first = lax.broadcasted_iota(jnp.int32, (2 * local, reach), 0) < local
    for h in range(0, heads, 2):
        two = latent[h * local : (h + 2) * local]
        weights = jnp.concatenate([w_ref[h], w_ref[h + 1]], axis=1)
        both = jnp.dot(two, weights, preferred_element_type=F32)
        values[pl.ds(h * local, 2 * local), :] = jnp.where(first, both[:, :reach], both[:, reach:])
    for p in range(local):
        out_ref[p] = values[pl.ds(p, heads, stride=local), :].astype(BF16)


def on_device(q_nope, q_rope, w_uk, w_uv, prefix, private_caches, new_latent, ancestors, lengths):
    local, heads, nope = q_nope.shape
    span, width = private_caches.shape[1:]
    rank, reach = w_uv.shape[1:]
    rows = local * heads
    seq_size, dom_size = lax.axis_size("seq"), lax.axis_size("dom")
    cores = 2
    chips = seq_size // cores
    place = jnp.stack([lax.axis_index("seq"), lax.axis_index("dom")]).astype(jnp.int32)
    block = pl.pallas_call(
        functools.partial(pack_kernel, rank),
        out_shape=shape((local * span // 2, 2 * width)),
        in_specs=[VMEM],
        out_specs=VMEM,
        compiler_params=PARAMS,
        name="pack",
    )(private_caches)
    asked_rows = jnp.swapaxes(jnp.concatenate([q_nope, q_rope], axis=2), 0, 1).reshape(rows, -1)
    line = dom_size == 4
    if line:
        swap = [(0, 1), (1, 0), (2, 3), (3, 2)]
        middle = lax.ppermute(block, "dom", [(0, 2), (3, 1)])
        far = lax.ppermute(block, "dom", [(1, 2), (2, 1)])
        theirs = lax.ppermute(ancestors, "dom", [(0, 1), (3, 2)])
    else:
        blocks = [block] + [
            lax.ppermute(block, "dom", [(i, (i + k) % dom_size) for i in range(dom_size)])
            for k in range(1, dom_size)
        ]

    pieces = math.gcd(heads // 4, 4)
    own = pl.pallas_call(
        functools.partial(project_kernel, pieces, local),
        out_shape=shape((rows, width)),
        in_specs=[VMEM, HBM],
        out_specs=VMEM,
        scratch_shapes=[pltpu.VMEM(w_uk.shape, BF16), pltpu.SemaphoreType.DMA((pieces,))],
        compiler_params=STREAM,
        name="project",
    )(asked_rows, w_uk)
    keys = prefix.T

    def pairs(turn, flip):
        return [
            (x * cores + c, (x + turn) % chips * cores + (c ^ flip))
            for x in range(chips)
            for c in range(cores)
        ]

    def back(turn, flip):
        return [(b, a) for a, b in pairs(turn, flip)]

    routes = [(t, f) for t in range(chips) for f in range(cores)]
    queries = [own if r == (0, 0) else lax.ppermute(own, "seq", pairs(*r)) for r in routes]
    stages = []
    for t in range(chips):
        asked = queries[2 * t : 2 * t + 2]
        stage = [*asked, *prefix_attention(asked, keys, rank, t == 0)]
        stages.append(stage)
        if t == 0:
            given = lax.ppermute(stage.pop(), "seq", pairs(0, 1))
        if line and t == 0:
            chosen = pl.pallas_call(
                select_kernel,
                out_shape=shape(block.shape),
                in_specs=[SMEM] * 2 + [ANY] * 4,
                out_specs=VMEM,
                scratch_shapes=[pltpu.SemaphoreType.DMA((local,))],
                compiler_params=PARAMS,
                cost_estimate=pl.CostEstimate(flops=0, bytes_accessed=0, transcendentals=0),
                name="select",
            )(theirs, place, block, far, middle, stage[3])
            blocks = [block, lax.ppermute(chosen, "dom", swap), middle, far]

    part = shape((rows, rank + LANES))
    others = chips - 1
    far_results = pl.pallas_call(
        functools.partial(far_kernel, others, len(blocks), line),
        out_shape=[shape((local * span, width))] + [part] * (2 * others),
        in_specs=[SMEM] * 3 + [VMEM] * (5 * others) + [ANY] * len(blocks),
        out_specs=[VMEM] * (1 + 2 * others),
        scratch_shapes=[
            pltpu.VMEM(block.shape, BF16),
            pltpu.SemaphoreType.DMA((local,)),
        ],
        compiler_params=PARAMS,
        name="suffix_far",
    )(ancestors, lengths, place, *[a for stage in stages[1:] for a in stage], *blocks)
    moved = far_results[0]
    keep, give = far_results[1 : 1 + others], far_results[1 + others :]
    sums = chip_merge(keep, [lax.ppermute(g, "seq", pairs(0, 1)) for g in give])
    parts = [lax.ppermute(s, "seq", back(t, 0)) for t, s in enumerate(sums, 1)]
    other = lax.ppermute(moved, "seq", pairs(0, 1))

    moved, _ = lax.optimization_barrier((moved, sums[0]))
    query, _, acc, level, mass = stages[0]
    new_caches, own_part = pl.pallas_call(
        near_kernel,
        out_shape=[shape(private_caches.shape), part],
        in_specs=[SMEM] * 3 + [VMEM] * 8,
        out_specs=[VMEM] * 2,
        compiler_params=PARAMS,
        name="suffix_near",
    )(ancestors, lengths, place, new_latent, query, acc, level, mass, given, moved, other)
    parts.append(own_part)

    head_values = pl.pallas_call(
        functools.partial(final_kernel, chips),
        out_shape=shape((local, heads, reach)),
        in_specs=[VMEM] * (chips + 1),
        out_specs=VMEM,
        scratch_shapes=[pltpu.VMEM((rows, reach), F32)],
        compiler_params=PARAMS,
        name="final",
    )(*parts, w_uv)
    return (head_values, new_caches)


def solution(mesh):
    placed = (
        P(("group", "dom"), "seq", None),
        P(("group", "dom"), "seq", None),
        P("seq", None, None),
        P("seq", None, None),
        P(("group", "seq"), None),
        P(("group", "dom"), "seq", None),
        P(("group", "dom"), None),
        P(("group", "dom")),
        P("group"),
    )
    return jax.shard_map(
        on_device,
        mesh=mesh,
        in_specs=placed,
        out_specs=(P(("group", "dom"), "seq", None), P(("group", "dom"), "seq", None)),
        check_vma=False,
    )
```

```python
import functools
import math

import jax
import jax.numpy as jnp
from jax import lax
from jax.experimental import pallas as pl
from jax.experimental.pallas import tpu as pltpu
from jax.sharding import PartitionSpec as P

ROPE = 64
NOPE = 128
SCALE2 = (NOPE + ROPE) ** (-0.5) * math.log2(math.e)
HIDDEN = -1e30
LANES = 128
F32 = jnp.float32
BF16 = jnp.bfloat16
NT = (((1,), (1,)), ((), ()))

VMEM = pl.BlockSpec(memory_space=pltpu.VMEM)
SMEM = pl.BlockSpec(memory_space=pltpu.SMEM)
ANY = pl.BlockSpec(memory_space=pl.ANY)
HBM = pl.BlockSpec(memory_space=pltpu.HBM)
PARAMS = pltpu.CompilerParams(vmem_limit_bytes=40 * 1024 * 1024)
STREAM = pltpu.CompilerParams(vmem_limit_bytes=51 * 1024 * 1024)


def shape(dims, dtype=BF16):
    return jax.ShapeDtypeStruct(dims, dtype)


def pack_kernel(rank, cache_ref, out_ref):
    local, span, _ = cache_ref.shape
    some = span // 2
    for p in range(local):
        part = pl.ds(p * some, some)
        first, second = cache_ref[p, :some], cache_ref[p, some:]
        out_ref[part, :rank] = first[:, :rank]
        out_ref[part, rank : 2 * rank] = second[:, :rank]
        out_ref[part, 2 * rank :] = jnp.concatenate([first[:, rank:], second[:, rank:]], axis=1)


def project_kernel(pieces, local, asked_ref, w_hbm, own_ref, w_ref, sems):
    heads, _, rank = w_ref.shape
    piece = heads // pieces
    fetches = [
        pltpu.make_async_copy(
            w_hbm.at[pl.ds(i * piece, piece)], w_ref.at[pl.ds(i * piece, piece)], sems.at[i]
        )
        for i in range(pieces)
    ]
    for fetch in fetches:
        fetch.start()
    width = w_ref.shape[1]
    nope = asked_ref[:, :width].astype(F32)
    first = lax.broadcasted_iota(jnp.int32, (2 * local, width), 0) < local

    def pair(h):
        two = nope[h * local : (h + 2) * local]
        left = jnp.concatenate([jnp.where(first, two, 0.0), jnp.where(first, 0.0, two)], axis=1)
        weights = w_ref[pl.ds(h, 2)].reshape(2 * width, rank)
        return jnp.dot(left.astype(BF16), weights, preferred_element_type=F32)

    own_ref[:, rank:] = asked_ref[:, width:]
    for h in range(0, heads, 4):
        if h % piece == 0:
            fetches[h // piece].wait()
        own_ref[pl.ds(h * local, 4 * local), :rank] = jnp.concatenate(
            [pair(i) for i in (h, h + 2)], axis=0
        ).astype(BF16)


def prefix_kernel(count, tiles, *refs):
    query_refs = refs[:count]
    keys_hbm, out_ref, max_ref, sum_ref, *give_ref, acc_ref, keys_ref, sems = refs[count:]
    rank = acc_ref.shape[1]
    tile = keys_ref.shape[1] // tiles
    parts = [pl.ds(i * tile, tile) for i in range(tiles)]
    fetches = [
        pltpu.make_async_copy(keys_hbm.at[:, part], keys_ref.at[:, part], sems.at[i])
        for i, part in enumerate(parts)
    ]
    for fetch in fetches:
        fetch.start()
    queries = jnp.concatenate([ref[...] for ref in query_refs], axis=0)

    def score(i):
        fetches[i].wait()
        return jnp.dot(queries, keys_ref[:, parts[i]], preferred_element_type=F32) * SCALE2

    ahead = score(0)
    for i in range(tiles):
        scores = ahead
        if i + 1 < tiles:
            ahead = score(i + 1)
        top = jnp.max(scores, axis=1, keepdims=True)
        if i > 0:
            top = jnp.maximum(top, largest)
        weights = jnp.exp2(scores - top)
        total = jnp.sum(weights, axis=1, keepdims=True)
        acc = lax.dot_general(
            weights.astype(BF16), keys_ref[:rank, parts[i]], NT, preferred_element_type=F32
        )
        if i > 0:
            factor = jnp.exp2(largest - top)
            total = total + running * factor
            acc = acc + acc_ref[...] * factor
        largest, running = top, total
        if i < tiles - 1:
            acc_ref[...] = acc
    kept = out_ref.shape[0]
    out_ref[...] = acc[:kept]
    max_ref[...] = jnp.broadcast_to(largest[:kept], max_ref.shape)
    sum_ref[...] = jnp.broadcast_to(running[:kept], sum_ref.shape)
    if give_ref:
        level = largest[kept:] + jnp.log2(running[kept:])
        give_ref[0][...] = packed(acc[kept:] * (1.0 / running[kept:]), level)


def prefix_attention(queries, keys, rank, give, tiles=4):
    rows = sum(q.shape[0] for q in queries)
    kept = queries[0].shape[0] if give else rows
    width, length = keys.shape
    out = [shape((kept, rank), F32)] + [shape((kept, LANES), F32)] * 2
    if give:
        out.append(shape((rows - kept, rank + LANES)))
    return pl.pallas_call(
        functools.partial(prefix_kernel, len(queries), tiles),
        out_shape=out,
        in_specs=[VMEM] * len(queries) + [HBM],
        out_specs=[VMEM] * len(out),
        scratch_shapes=[
            pltpu.VMEM((rows, rank), F32),
            pltpu.VMEM(keys.shape, BF16),
            pltpu.SemaphoreType.DMA((tiles,)),
        ],
        compiler_params=STREAM,
        cost_estimate=pl.CostEstimate(
            flops=0 if give else 2 * rows * length * (width + rank),
            bytes_accessed=0 if give else 2 * width * length,
            transcendentals=0 if give else rows * length,
        ),
        name="prefix_attention",
    )(*queries, keys)


def packed(values, level):
    rows = values.shape[0]
    lane = lax.broadcasted_iota(jnp.int32, (rows, LANES), 1)
    high = level.astype(BF16).astype(F32)
    middle = (level - high).astype(BF16).astype(F32)
    low = level - high - middle
    stats = jnp.where(lane == 0, high, jnp.where(lane == 1, middle, jnp.where(lane == 2, low, 0.0)))
    return jnp.concatenate([values.astype(BF16), stats.astype(BF16)], axis=1)


def merged(parts, rank):
    levels = [jnp.sum(part[:, rank:].astype(F32), axis=1, keepdims=True) for part in parts]
    top = functools.reduce(jnp.maximum, levels)
    shares = [jnp.exp2(level - top) for level in levels]
    whole = functools.reduce(jnp.add, shares)
    acc = functools.reduce(
        jnp.add, [share * part[:, :rank].astype(F32) for share, part in zip(shares, parts)]
    )
    return acc * (1.0 / whole), top + jnp.log2(whole)


def visible(rows, ends, starts, span):
    local = len(ends)
    cols = len(starts) * local * span
    col = lax.broadcasted_iota(jnp.int32, (1, cols), 1)
    col_of = jnp.zeros_like(col)
    limit = jnp.full_like(col, ends[0] - starts[0])
    for at in range(1, len(starts) * local):
        begin, p = at * span, at % local
        later = col >= begin
        col_of = jnp.where(later, p, col_of)
        limit = jnp.where(later, ends[p] - starts[at // local] + begin, limit)
    col_of = jnp.where(col < limit, col_of, -1)
    row_of = lax.rem(lax.broadcasted_iota(jnp.int32, (rows, 1), 0), local)
    return row_of == col_of


def attend(queries, keys, seen, rank, known):
    scores = lax.dot_general(queries, keys, NT, preferred_element_type=F32)
    scores = jnp.where(seen, scores * SCALE2, HIDDEN)
    top = jnp.max(scores, axis=1, keepdims=True)
    for level, _, _ in known:
        top = jnp.maximum(top, level)
    weights = jnp.where(seen, jnp.exp2(scores - top), 0.0)
    total = jnp.sum(weights, axis=1, keepdims=True)
    acc = jnp.dot(weights.astype(BF16), keys[:, :rank], preferred_element_type=F32)
    for level, mass, part in known:
        factor = jnp.exp2(level - top)
        total = total + mass * factor
        acc = acc + part * factor
    return packed(acc * (1.0 / total), top + jnp.log2(total))


def gather_blocks(block_refs, picks, out_ref, sems):
    some = out_ref.shape[0] // len(picks)

    def copy(p, k, slot):
        return pltpu.make_async_copy(
            block_refs[k].at[pl.ds(pl.multiple_of(slot * some, some), some)],
            out_ref.at[pl.ds(p * some, some)],
            sems.at[p],
        )

    for p, (which, slot) in enumerate(picks):
        for k in range(len(block_refs)):

            @pl.when(which == k)
            def _():
                copy(p, k, slot).start()

    for p in range(len(picks)):
        copy(p, 0, 0).wait()


def at_end(place):
    return (place[1] == 0) | (place[1] == 3)


def select_kernel(theirs, place, *refs):
    block_refs, (_, out_ref, sems) = refs[:-3], refs[-3:]
    local = sems.shape[0]
    picks = []
    for p in range(local):
        apart = jnp.bitwise_xor(lax.div(theirs[p], local), place[1])
        which = jnp.where(at_end(place) | (apart < 2), 0, 4 - apart)
        picks.append((which, jnp.where(at_end(place), p, lax.rem(theirs[p], local))))
    gather_blocks(block_refs, picks, out_ref, sems)


def far_kernel(stages, sources, line, *refs):
    anc, lens, place = refs[:3]
    refs = refs[3:]
    stage_refs, refs = refs[: 5 * stages], refs[5 * stages :]
    block_refs, refs = refs[:sources], refs[sources:]
    moved_ref, refs = refs[0], refs[1:]
    keep_refs, give_refs = refs[:stages], refs[stages : 2 * stages]
    raw, sems = refs[2 * stages :]
    local = sems.shape[0]
    some = raw.shape[0] // local
    span, width = 2 * some, moved_ref.shape[1]
    rank = stage_refs[2].shape[1]

    picks = []
    for p in range(local):
        owner, slot = lax.div(anc[p], local), lax.rem(anc[p], local)
        if line:
            which = jnp.bitwise_xor(owner, place[1])
            chosen = at_end(place) & (which != 0)
            which = jnp.where(chosen, 1, which)
            slot = jnp.where(chosen, p, slot)
        else:
            which = lax.rem(place[1] - owner + sources, sources)
        picks.append((which, slot))
    gather_blocks(block_refs, picks, raw, sems)
    for p in range(local):
        for h in range(2):
            part, rows = pl.ds(p * some, some), pl.ds(p * span + h * some, some)
            rope = 2 * rank + h * (width - rank)
            moved_ref[rows, :rank] = raw[part, h * rank : (h + 1) * rank]
            moved_ref[rows, rank:] = raw[part, rope : rope + width - rank]

    ends = [lens[anc[p]] for p in range(local)]
    for k in range(stages):
        first_ref, second_ref, acc_ref, max_ref, sum_ref = stage_refs[5 * k : 5 * k + 5]
        queries = jnp.concatenate([first_ref[...], second_ref[...]], axis=0)
        seen = visible(queries.shape[0], ends, [place[0] * span], span)
        known = [(max_ref[:, 0:1], sum_ref[:, 0:1], acc_ref[...])]
        part = attend(queries, moved_ref[...], seen, rank, known)
        rows = first_ref.shape[0]
        keep_refs[k][...] = part[:rows]
        give_refs[k][...] = part[rows:]


def near_kernel(anc, lens, place, fresh_ref, *refs):
    query_ref, acc_ref, max_ref, sum_ref, got_ref, moved_ref, other_ref, cache_ref, part_ref = refs
    local, span, width = cache_ref.shape
    rank = acc_ref.shape[1]
    start, other = place[0] * span, jnp.bitwise_xor(place[0], 1) * span
    ends = [lens[anc[p]] for p in range(local)]
    keys = jnp.concatenate([moved_ref[...], other_ref[...]], axis=0)
    seen = visible(query_ref.shape[0], ends, [start, other], span)
    level = jnp.sum(got_ref[:, rank:].astype(F32), axis=1, keepdims=True)
    known = [
        (max_ref[:, 0:1], sum_ref[:, 0:1], acc_ref[...]),
        (level, 1.0, got_ref[:, :rank].astype(F32)),
    ]
    part_ref[...] = attend(query_ref[...], keys, seen, rank, known)
    for p in range(local):
        at = start + lax.broadcasted_iota(jnp.int32, (span, 1), 0) == ends[p]
        cache_ref[p] = jnp.where(at, fresh_ref[pl.ds(p, 1), :], moved_ref[pl.ds(p * span, span)])


def chip_kernel(count, *refs):
    for k in range(count):
        out_ref = refs[2 * count + k]
        rank = out_ref.shape[1] - LANES
        out_ref[...] = packed(*merged([refs[k][...], refs[count + k][...]], rank))


def chip_merge(keep, got):
    return pl.pallas_call(
        functools.partial(chip_kernel, len(keep)),
        out_shape=[shape(k.shape) for k in keep],
        in_specs=[VMEM] * (2 * len(keep)),
        out_specs=[VMEM] * len(keep),
        compiler_params=PARAMS,
        name="chip_merge",
    )(*keep, *got)


def final_kernel(count, *refs):
    part_refs, (w_ref, out_ref, values) = refs[:count], refs[count:]
    heads, rank, reach = w_ref.shape
    local = out_ref.shape[0]
    latent = merged([ref[...] for ref in part_refs], rank)[0].astype(BF16)
    first = lax.broadcasted_iota(jnp.int32, (2 * local, reach), 0) < local
    for h in range(0, heads, 2):
        two = latent[h * local : (h + 2) * local]
        weights = jnp.concatenate([w_ref[h], w_ref[h + 1]], axis=1)
        both = jnp.dot(two, weights, preferred_element_type=F32)
        values[pl.ds(h * local, 2 * local), :] = jnp.where(first, both[:, :reach], both[:, reach:])
    for p in range(local):
        out_ref[p] = values[pl.ds(p, heads, stride=local), :].astype(BF16)


def on_device(q_nope, q_rope, w_uk, w_uv, prefix, private_caches, new_latent, ancestors, lengths):
    local, heads, nope = q_nope.shape
    span, width = private_caches.shape[1:]
    rank, reach = w_uv.shape[1:]
    rows = local * heads
    seq_size, dom_size = lax.axis_size("seq"), lax.axis_size("dom")
    cores = 2
    chips = seq_size // cores
    place = jnp.stack([lax.axis_index("seq"), lax.axis_index("dom")]).astype(jnp.int32)
    block = pl.pallas_call(
        functools.partial(pack_kernel, rank),
        out_shape=shape((local * span // 2, 2 * width)),
        in_specs=[VMEM],
        out_specs=VMEM,
        compiler_params=PARAMS,
        name="pack",
    )(private_caches)
    asked_rows = jnp.swapaxes(jnp.concatenate([q_nope, q_rope], axis=2), 0, 1).reshape(rows, -1)
    line = dom_size == 4
    if line:
        swap = [(0, 1), (1, 0), (2, 3), (3, 2)]
        middle = lax.ppermute(block, "dom", [(0, 2), (3, 1)])
        far = lax.ppermute(block, "dom", [(1, 2), (2, 1)])
    else:
        blocks = [block] + [
            lax.ppermute(block, "dom", [(i, (i + k) % dom_size) for i in range(dom_size)])
            for k in range(1, dom_size)
        ]

    pieces = math.gcd(heads // 4, 4)
    own = pl.pallas_call(
        functools.partial(project_kernel, pieces, local),
        out_shape=shape((rows, width)),
        in_specs=[VMEM, HBM],
        out_specs=VMEM,
        scratch_shapes=[pltpu.VMEM(w_uk.shape, BF16), pltpu.SemaphoreType.DMA((pieces,))],
        compiler_params=STREAM,
        name="project",
    )(asked_rows, w_uk)
    keys = prefix.T

    def pairs(turn, flip):
        return [
            (x * cores + c, (x + turn) % chips * cores + (c ^ flip))
            for x in range(chips)
            for c in range(cores)
        ]

    def back(turn, flip):
        return [(b, a) for a, b in pairs(turn, flip)]

    routes = [(t, f) for t in range(chips) for f in range(cores)]
    queries = [own if r == (0, 0) else lax.ppermute(own, "seq", pairs(*r)) for r in routes]
    stages = []
    for t in range(chips):
        asked = queries[2 * t : 2 * t + 2]
        stage = [*asked, *prefix_attention(asked, keys, rank, t == 0)]
        stages.append(stage)
        if t == 0:
            given = lax.ppermute(stage.pop(), "seq", pairs(0, 1))
        if line and t == 0:
            named, stage[3] = lax.optimization_barrier((ancestors, stage[3]))
            theirs = lax.ppermute(named, "dom", [(0, 1), (3, 2)])
            chosen = pl.pallas_call(
                select_kernel,
                out_shape=shape(block.shape),
                in_specs=[SMEM] * 2 + [ANY] * 4,
                out_specs=VMEM,
                scratch_shapes=[pltpu.SemaphoreType.DMA((local,))],
                compiler_params=PARAMS,
                cost_estimate=pl.CostEstimate(flops=0, bytes_accessed=0, transcendentals=0),
                name="select",
            )(theirs, place, block, far, middle, stage[3])
            blocks = [block, lax.ppermute(chosen, "dom", swap), middle, far]

    part = shape((rows, rank + LANES))
    others = chips - 1
    far_results = pl.pallas_call(
        functools.partial(far_kernel, others, len(blocks), line),
        out_shape=[shape((local * span, width))] + [part] * (2 * others),
        in_specs=[SMEM] * 3 + [VMEM] * (5 * others) + [ANY] * len(blocks),
        out_specs=[VMEM] * (1 + 2 * others),
        scratch_shapes=[
            pltpu.VMEM(block.shape, BF16),
            pltpu.SemaphoreType.DMA((local,)),
        ],
        compiler_params=PARAMS,
        name="suffix_far",
    )(ancestors, lengths, place, *[a for stage in stages[1:] for a in stage], *blocks)
    moved = far_results[0]
    keep, give = far_results[1 : 1 + others], far_results[1 + others :]
    sums = chip_merge(keep, [lax.ppermute(g, "seq", pairs(0, 1)) for g in give])
    parts = [lax.ppermute(s, "seq", back(t, 0)) for t, s in enumerate(sums, 1)]
    other = lax.ppermute(moved, "seq", pairs(0, 1))

    moved, _ = lax.optimization_barrier((moved, sums[0]))
    query, _, acc, level, mass = stages[0]
    new_caches, own_part = pl.pallas_call(
        near_kernel,
        out_shape=[shape(private_caches.shape), part],
        in_specs=[SMEM] * 3 + [VMEM] * 8,
        out_specs=[VMEM] * 2,
        compiler_params=PARAMS,
        name="suffix_near",
    )(ancestors, lengths, place, new_latent, query, acc, level, mass, given, moved, other)
    parts.append(own_part)

    head_values = pl.pallas_call(
        functools.partial(final_kernel, chips),
        out_shape=shape((local, heads, reach)),
        in_specs=[VMEM] * (chips + 1),
        out_specs=VMEM,
        scratch_shapes=[pltpu.VMEM((rows, reach), F32)],
        compiler_params=PARAMS,
        name="final",
    )(*parts, w_uv)
    return (head_values, new_caches)


def solution(mesh):
    placed = (
        P(("group", "dom"), "seq", None),
        P(("group", "dom"), "seq", None),
        P("seq", None, None),
        P("seq", None, None),
        P(("group", "seq"), None),
        P(("group", "dom"), "seq", None),
        P(("group", "dom"), None),
        P(("group", "dom")),
        P("group"),
    )
    return jax.shard_map(
        on_device,
        mesh=mesh,
        in_specs=placed,
        out_specs=(P(("group", "dom"), "seq", None), P(("group", "dom"), "seq", None)),
        check_vma=False,
    )
```

```python
import functools
import math

import jax
import jax.numpy as jnp
from jax import lax
from jax.experimental import pallas as pl
from jax.experimental.pallas import tpu as pltpu
from jax.sharding import PartitionSpec as P

ROPE = 64
NOPE = 128
SCALE2 = (NOPE + ROPE) ** (-0.5) * math.log2(math.e)
HIDDEN = -1e30
LANES = 128
F32 = jnp.float32
BF16 = jnp.bfloat16
NT = (((1,), (1,)), ((), ()))

VMEM = pl.BlockSpec(memory_space=pltpu.VMEM)
SMEM = pl.BlockSpec(memory_space=pltpu.SMEM)
ANY = pl.BlockSpec(memory_space=pl.ANY)
HBM = pl.BlockSpec(memory_space=pltpu.HBM)
PARAMS = pltpu.CompilerParams(vmem_limit_bytes=40 * 1024 * 1024)
PACK = 8_000_000_000
PROJECT = 8_000_000_000


def shape(dims, dtype=BF16):
    return jax.ShapeDtypeStruct(dims, dtype)


def pack_kernel(rank, cache_ref, out_ref):
    local, span, _ = cache_ref.shape
    some = span // 2
    for p in range(local):
        part = pl.ds(p * some, some)
        first, second = cache_ref[p, :some], cache_ref[p, some:]
        out_ref[part, :rank] = first[:, :rank]
        out_ref[part, rank : 2 * rank] = second[:, :rank]
        out_ref[part, 2 * rank :] = jnp.concatenate([first[:, rank:], second[:, rank:]], axis=1)


def project_kernel(local, asked_ref, w_ref, own_ref):
    heads, _, rank = w_ref.shape
    width = w_ref.shape[1]
    nope = asked_ref[:, :width].astype(F32)
    first = lax.broadcasted_iota(jnp.int32, (2 * local, width), 0) < local

    def pair(h):
        two = nope[h * local : (h + 2) * local]
        left = jnp.concatenate([jnp.where(first, two, 0.0), jnp.where(first, 0.0, two)], axis=1)
        weights = w_ref[pl.ds(h, 2)].reshape(2 * width, rank)
        return jnp.dot(left.astype(BF16), weights, preferred_element_type=F32)

    own_ref[:, rank:] = asked_ref[:, width:]
    for h in range(0, heads, 4):
        own_ref[pl.ds(h * local, 4 * local), :rank] = jnp.concatenate(
            [pair(i) for i in (h, h + 2)], axis=0
        ).astype(BF16)


def prefix_kernel(count, tiles, *refs):
    query_refs = refs[:count]
    keys_ref, out_ref, max_ref, sum_ref, *give_ref, acc_ref = refs[count:]
    rank = acc_ref.shape[1]
    tile = keys_ref.shape[1] // tiles
    parts = [pl.ds(i * tile, tile) for i in range(tiles)]
    queries = jnp.concatenate([ref[...] for ref in query_refs], axis=0)

    def score(i):
        return jnp.dot(queries, keys_ref[:, parts[i]], preferred_element_type=F32) * SCALE2

    ahead = score(0)
    for i in range(tiles):
        scores = ahead
        if i + 1 < tiles:
            ahead = score(i + 1)
        top = jnp.max(scores, axis=1, keepdims=True)
        if i > 0:
            top = jnp.maximum(top, largest)
        weights = jnp.exp2(scores - top)
        total = jnp.sum(weights, axis=1, keepdims=True)
        acc = lax.dot_general(
            weights.astype(BF16), keys_ref[:rank, parts[i]], NT, preferred_element_type=F32
        )
        if i > 0:
            factor = jnp.exp2(largest - top)
            total = total + running * factor
            acc = acc + acc_ref[...] * factor
        largest, running = top, total
        if i < tiles - 1:
            acc_ref[...] = acc
    kept = out_ref.shape[0]
    out_ref[...] = acc[:kept]
    max_ref[...] = jnp.broadcast_to(largest[:kept], max_ref.shape)
    sum_ref[...] = jnp.broadcast_to(running[:kept], sum_ref.shape)
    if give_ref:
        level = largest[kept:] + jnp.log2(running[kept:])
        give_ref[0][...] = packed(acc[kept:] * (1.0 / running[kept:]), level)


def prefix_attention(queries, keys, rank, give, tiles=4):
    rows = sum(q.shape[0] for q in queries)
    kept = queries[0].shape[0] if give else rows
    width, length = keys.shape
    out = [shape((kept, rank), F32)] + [shape((kept, LANES), F32)] * 2
    if give:
        out.append(shape((rows - kept, rank + LANES)))
    return pl.pallas_call(
        functools.partial(prefix_kernel, len(queries), tiles),
        out_shape=out,
        in_specs=[VMEM] * (len(queries) + 1),
        out_specs=[VMEM] * len(out),
        scratch_shapes=[pltpu.VMEM((rows, rank), F32)],
        compiler_params=PARAMS,
        cost_estimate=pl.CostEstimate(
            flops=0 if give else 2 * rows * length * (width + rank),
            bytes_accessed=0 if give else 2 * width * length,
            transcendentals=0 if give else rows * length,
        ),
        name="prefix_attention",
    )(*queries, keys)


def packed(values, level):
    rows = values.shape[0]
    lane = lax.broadcasted_iota(jnp.int32, (rows, LANES), 1)
    high = level.astype(BF16).astype(F32)
    middle = (level - high).astype(BF16).astype(F32)
    low = level - high - middle
    stats = jnp.where(lane == 0, high, jnp.where(lane == 1, middle, jnp.where(lane == 2, low, 0.0)))
    return jnp.concatenate([values.astype(BF16), stats.astype(BF16)], axis=1)


def merged(parts, rank):
    levels = [jnp.sum(part[:, rank:].astype(F32), axis=1, keepdims=True) for part in parts]
    top = functools.reduce(jnp.maximum, levels)
    shares = [jnp.exp2(level - top) for level in levels]
    whole = functools.reduce(jnp.add, shares)
    acc = functools.reduce(
        jnp.add, [share * part[:, :rank].astype(F32) for share, part in zip(shares, parts)]
    )
    return acc * (1.0 / whole), top + jnp.log2(whole)


def visible(rows, ends, starts, span):
    local = len(ends)
    cols = len(starts) * local * span
    col = lax.broadcasted_iota(jnp.int32, (1, cols), 1)
    col_of = jnp.zeros_like(col)
    limit = jnp.full_like(col, ends[0] - starts[0])
    for at in range(1, len(starts) * local):
        begin, p = at * span, at % local
        later = col >= begin
        col_of = jnp.where(later, p, col_of)
        limit = jnp.where(later, ends[p] - starts[at // local] + begin, limit)
    col_of = jnp.where(col < limit, col_of, -1)
    row_of = lax.rem(lax.broadcasted_iota(jnp.int32, (rows, 1), 0), local)
    return row_of == col_of


def attend(queries, keys, seen, rank, known):
    scores = lax.dot_general(queries, keys, NT, preferred_element_type=F32)
    scores = jnp.where(seen, scores * SCALE2, HIDDEN)
    top = jnp.max(scores, axis=1, keepdims=True)
    for level, _, _ in known:
        top = jnp.maximum(top, level)
    weights = jnp.where(seen, jnp.exp2(scores - top), 0.0)
    total = jnp.sum(weights, axis=1, keepdims=True)
    acc = jnp.dot(weights.astype(BF16), keys[:, :rank], preferred_element_type=F32)
    for level, mass, part in known:
        factor = jnp.exp2(level - top)
        total = total + mass * factor
        acc = acc + part * factor
    return packed(acc * (1.0 / total), top + jnp.log2(total))


def gather_blocks(block_refs, picks, out_ref, sems):
    some = out_ref.shape[0] // len(picks)

    def copy(p, k, slot):
        return pltpu.make_async_copy(
            block_refs[k].at[pl.ds(pl.multiple_of(slot * some, some), some)],
            out_ref.at[pl.ds(p * some, some)],
            sems.at[p],
        )

    for p, (which, slot) in enumerate(picks):
        for k in range(len(block_refs)):

            @pl.when(which == k)
            def _():
                copy(p, k, slot).start()

    for p in range(len(picks)):
        copy(p, 0, 0).wait()


def at_end(place):
    return (place[1] == 0) | (place[1] == 3)


def select_kernel(theirs, place, *refs):
    block_refs, (_, out_ref, sems) = refs[:-3], refs[-3:]
    local = sems.shape[0]
    picks = []
    for p in range(local):
        apart = jnp.bitwise_xor(lax.div(theirs[p], local), place[1])
        which = jnp.where(at_end(place) | (apart < 2), 0, 4 - apart)
        picks.append((which, jnp.where(at_end(place), p, lax.rem(theirs[p], local))))
    gather_blocks(block_refs, picks, out_ref, sems)


def far_kernel(stages, sources, line, *refs):
    anc, lens, place = refs[:3]
    refs = refs[3:]
    stage_refs, refs = refs[: 5 * stages], refs[5 * stages :]
    block_refs, refs = refs[:sources], refs[sources:]
    moved_ref, refs = refs[0], refs[1:]
    keep_refs, give_refs = refs[:stages], refs[stages : 2 * stages]
    raw, sems = refs[2 * stages :]
    local = sems.shape[0]
    some = raw.shape[0] // local
    span, width = 2 * some, moved_ref.shape[1]
    rank = stage_refs[2].shape[1]

    picks = []
    for p in range(local):
        owner, slot = lax.div(anc[p], local), lax.rem(anc[p], local)
        if line:
            which = jnp.bitwise_xor(owner, place[1])
            chosen = at_end(place) & (which != 0)
            which = jnp.where(chosen, 1, which)
            slot = jnp.where(chosen, p, slot)
        else:
            which = lax.rem(place[1] - owner + sources, sources)
        picks.append((which, slot))
    gather_blocks(block_refs, picks, raw, sems)
    for p in range(local):
        for h in range(2):
            part, rows = pl.ds(p * some, some), pl.ds(p * span + h * some, some)
            rope = 2 * rank + h * (width - rank)
            moved_ref[rows, :rank] = raw[part, h * rank : (h + 1) * rank]
            moved_ref[rows, rank:] = raw[part, rope : rope + width - rank]

    ends = [lens[anc[p]] for p in range(local)]
    for k in range(stages):
        first_ref, second_ref, acc_ref, max_ref, sum_ref = stage_refs[5 * k : 5 * k + 5]
        queries = jnp.concatenate([first_ref[...], second_ref[...]], axis=0)
        seen = visible(queries.shape[0], ends, [place[0] * span], span)
        known = [(max_ref[:, 0:1], sum_ref[:, 0:1], acc_ref[...])]
        part = attend(queries, moved_ref[...], seen, rank, known)
        rows = first_ref.shape[0]
        keep_refs[k][...] = part[:rows]
        give_refs[k][...] = part[rows:]


def near_kernel(anc, lens, place, fresh_ref, *refs):
    query_ref, acc_ref, max_ref, sum_ref, got_ref, moved_ref, other_ref, cache_ref, part_ref = refs
    local, span, width = cache_ref.shape
    rank = acc_ref.shape[1]
    start, other = place[0] * span, jnp.bitwise_xor(place[0], 1) * span
    ends = [lens[anc[p]] for p in range(local)]
    keys = jnp.concatenate([moved_ref[...], other_ref[...]], axis=0)
    seen = visible(query_ref.shape[0], ends, [start, other], span)
    level = jnp.sum(got_ref[:, rank:].astype(F32), axis=1, keepdims=True)
    known = [
        (max_ref[:, 0:1], sum_ref[:, 0:1], acc_ref[...]),
        (level, 1.0, got_ref[:, :rank].astype(F32)),
    ]
    part_ref[...] = attend(query_ref[...], keys, seen, rank, known)
    for p in range(local):
        at = start + lax.broadcasted_iota(jnp.int32, (span, 1), 0) == ends[p]
        cache_ref[p] = jnp.where(at, fresh_ref[pl.ds(p, 1), :], moved_ref[pl.ds(p * span, span)])


def chip_kernel(count, *refs):
    for k in range(count):
        out_ref = refs[2 * count + k]
        rank = out_ref.shape[1] - LANES
        out_ref[...] = packed(*merged([refs[k][...], refs[count + k][...]], rank))


def chip_merge(keep, got):
    return pl.pallas_call(
        functools.partial(chip_kernel, len(keep)),
        out_shape=[shape(k.shape) for k in keep],
        in_specs=[VMEM] * (2 * len(keep)),
        out_specs=[VMEM] * len(keep),
        compiler_params=PARAMS,
        name="chip_merge",
    )(*keep, *got)


def final_kernel(count, *refs):
    part_refs, (w_ref, out_ref, values) = refs[:count], refs[count:]
    heads, rank, reach = w_ref.shape
    local = out_ref.shape[0]
    latent = merged([ref[...] for ref in part_refs], rank)[0].astype(BF16)
    first = lax.broadcasted_iota(jnp.int32, (2 * local, reach), 0) < local
    for h in range(0, heads, 2):
        two = latent[h * local : (h + 2) * local]
        weights = jnp.concatenate([w_ref[h], w_ref[h + 1]], axis=1)
        both = jnp.dot(two, weights, preferred_element_type=F32)
        values[pl.ds(h * local, 2 * local), :] = jnp.where(first, both[:, :reach], both[:, reach:])
    for p in range(local):
        out_ref[p] = values[pl.ds(p, heads, stride=local), :].astype(BF16)


def on_device(q_nope, q_rope, w_uk, w_uv, prefix, private_caches, new_latent, ancestors, lengths):
    local, heads, nope = q_nope.shape
    span, width = private_caches.shape[1:]
    rank, reach = w_uv.shape[1:]
    rows = local * heads
    seq_size, dom_size = lax.axis_size("seq"), lax.axis_size("dom")
    cores = 2
    chips = seq_size // cores
    place = jnp.stack([lax.axis_index("seq"), lax.axis_index("dom")]).astype(jnp.int32)
    block = pl.pallas_call(
        functools.partial(pack_kernel, rank),
        out_shape=shape((local * span // 2, 2 * width)),
        in_specs=[VMEM],
        out_specs=VMEM,
        compiler_params=PARAMS,
        cost_estimate=pl.CostEstimate(flops=PACK, bytes_accessed=0, transcendentals=0),
        name="pack",
    )(private_caches)
    asked_rows = jnp.swapaxes(jnp.concatenate([q_nope, q_rope], axis=2), 0, 1).reshape(rows, -1)
    line = dom_size == 4
    if line:
        swap = [(0, 1), (1, 0), (2, 3), (3, 2)]
        middle = lax.ppermute(block, "dom", [(0, 2), (3, 1)])
        far = lax.ppermute(block, "dom", [(1, 2), (2, 1)])
        theirs = lax.ppermute(ancestors, "dom", [(0, 1), (3, 2)])
    else:
        blocks = [block] + [
            lax.ppermute(block, "dom", [(i, (i + k) % dom_size) for i in range(dom_size)])
            for k in range(1, dom_size)
        ]

    own = pl.pallas_call(
        functools.partial(project_kernel, local),
        out_shape=shape((rows, width)),
        in_specs=[VMEM] * 2,
        out_specs=VMEM,
        compiler_params=PARAMS,
        cost_estimate=pl.CostEstimate(flops=PROJECT, bytes_accessed=0, transcendentals=0),
        name="project",
    )(asked_rows, w_uk)
    keys = prefix.T

    def pairs(turn, flip):
        return [
            (x * cores + c, (x + turn) % chips * cores + (c ^ flip))
            for x in range(chips)
            for c in range(cores)
        ]

    def back(turn, flip):
        return [(b, a) for a, b in pairs(turn, flip)]

    routes = [(t, f) for t in range(chips) for f in range(cores)]
    queries = [own if r == (0, 0) else lax.ppermute(own, "seq", pairs(*r)) for r in routes]
    stages = []
    for t in range(chips):
        asked = queries[2 * t : 2 * t + 2]
        stage = [*asked, *prefix_attention(asked, keys, rank, t == 0)]
        stages.append(stage)
        if t == 0:
            given = lax.ppermute(stage.pop(), "seq", pairs(0, 1))
        if line and t == 0:
            chosen = pl.pallas_call(
                select_kernel,
                out_shape=shape(block.shape),
                in_specs=[SMEM] * 2 + [ANY] * 4,
                out_specs=VMEM,
                scratch_shapes=[pltpu.SemaphoreType.DMA((local,))],
                compiler_params=PARAMS,
                cost_estimate=pl.CostEstimate(flops=0, bytes_accessed=0, transcendentals=0),
                name="select",
            )(theirs, place, block, far, middle, stage[3])
            blocks = [block, lax.ppermute(chosen, "dom", swap), middle, far]

    part = shape((rows, rank + LANES))
    others = chips - 1
    far_results = pl.pallas_call(
        functools.partial(far_kernel, others, len(blocks), line),
        out_shape=[shape((local * span, width))] + [part] * (2 * others),
        in_specs=[SMEM] * 3 + [VMEM] * (5 * others) + [ANY] * len(blocks),
        out_specs=[VMEM] * (1 + 2 * others),
        scratch_shapes=[
            pltpu.VMEM(block.shape, BF16),
            pltpu.SemaphoreType.DMA((local,)),
        ],
        compiler_params=PARAMS,
        name="suffix_far",
    )(ancestors, lengths, place, *[a for stage in stages[1:] for a in stage], *blocks)
    moved = far_results[0]
    keep, give = far_results[1 : 1 + others], far_results[1 + others :]
    sums = chip_merge(keep, [lax.ppermute(g, "seq", pairs(0, 1)) for g in give])
    parts = [lax.ppermute(s, "seq", back(t, 0)) for t, s in enumerate(sums, 1)]
    other = lax.ppermute(moved, "seq", pairs(0, 1))

    moved, _ = lax.optimization_barrier((moved, sums[0]))
    query, _, acc, level, mass = stages[0]
    new_caches, own_part = pl.pallas_call(
        near_kernel,
        out_shape=[shape(private_caches.shape), part],
        in_specs=[SMEM] * 3 + [VMEM] * 8,
        out_specs=[VMEM] * 2,
        compiler_params=PARAMS,
        name="suffix_near",
    )(ancestors, lengths, place, new_latent, query, acc, level, mass, given, moved, other)
    parts.append(own_part)

    head_values = pl.pallas_call(
        functools.partial(final_kernel, chips),
        out_shape=shape((local, heads, reach)),
        in_specs=[VMEM] * (chips + 1),
        out_specs=VMEM,
        scratch_shapes=[pltpu.VMEM((rows, reach), F32)],
        compiler_params=PARAMS,
        name="final",
    )(*parts, w_uv)
    return (head_values, new_caches)


def solution(mesh):
    placed = (
        P(("group", "dom"), "seq", None),
        P(("group", "dom"), "seq", None),
        P("seq", None, None),
        P("seq", None, None),
        P(("group", "seq"), None),
        P(("group", "dom"), "seq", None),
        P(("group", "dom"), None),
        P(("group", "dom")),
        P("group"),
    )
    return jax.shard_map(
        on_device,
        mesh=mesh,
        in_specs=placed,
        out_specs=(P(("group", "dom"), "seq", None), P(("group", "dom"), "seq", None)),
        check_vma=False,
    )
```

```python
import functools
import math

import jax
import jax.numpy as jnp
from jax import lax
from jax.experimental import pallas as pl
from jax.experimental.pallas import tpu as pltpu
from jax.sharding import PartitionSpec as P

ROPE = 64
NOPE = 128
SCALE2 = (NOPE + ROPE) ** (-0.5) * math.log2(math.e)
HIDDEN = -1e30
LANES = 128
F32 = jnp.float32
BF16 = jnp.bfloat16
NT = (((1,), (1,)), ((), ()))

VMEM = pl.BlockSpec(memory_space=pltpu.VMEM)
SMEM = pl.BlockSpec(memory_space=pltpu.SMEM)
ANY = pl.BlockSpec(memory_space=pl.ANY)
HBM = pl.BlockSpec(memory_space=pltpu.HBM)
PARAMS = pltpu.CompilerParams(vmem_limit_bytes=40 * 1024 * 1024)
PACK = 8_000_000_000
PROJECT = 8_000_000_000


def shape(dims, dtype=BF16):
    return jax.ShapeDtypeStruct(dims, dtype)


def pack_kernel(rank, cache_ref, out_ref):
    local, span, _ = cache_ref.shape
    some = span // 2
    for p in range(local):
        part = pl.ds(p * some, some)
        first, second = cache_ref[p, :some], cache_ref[p, some:]
        out_ref[part, :rank] = first[:, :rank]
        out_ref[part, rank : 2 * rank] = second[:, :rank]
        out_ref[part, 2 * rank :] = jnp.concatenate([first[:, rank:], second[:, rank:]], axis=1)


def project_kernel(local, nope_ref, rope_ref, w_ref, own_ref):
    heads, _, rank = w_ref.shape
    nope = nope_ref[...].astype(F32)
    width = nope.shape[1]
    first = lax.broadcasted_iota(jnp.int32, (2 * local, width), 0) < local

    def pair(h):
        two = nope[h * local : (h + 2) * local]
        left = jnp.concatenate([jnp.where(first, two, 0.0), jnp.where(first, 0.0, two)], axis=1)
        weights = w_ref[pl.ds(h, 2)].reshape(2 * width, rank)
        return jnp.dot(left.astype(BF16), weights, preferred_element_type=F32)

    own_ref[:, rank:] = rope_ref[...]
    for h in range(0, heads, 4):
        own_ref[pl.ds(h * local, 4 * local), :rank] = jnp.concatenate(
            [pair(i) for i in (h, h + 2)], axis=0
        ).astype(BF16)


def prefix_kernel(count, tiles, *refs):
    query_refs = refs[:count]
    keys_ref, out_ref, max_ref, sum_ref, *give_ref, acc_ref = refs[count:]
    rank = acc_ref.shape[1]
    tile = keys_ref.shape[1] // tiles
    parts = [pl.ds(i * tile, tile) for i in range(tiles)]
    queries = jnp.concatenate([ref[...] for ref in query_refs], axis=0)

    def score(i):
        return jnp.dot(queries, keys_ref[:, parts[i]], preferred_element_type=F32) * SCALE2

    ahead = score(0)
    for i in range(tiles):
        scores = ahead
        if i + 1 < tiles:
            ahead = score(i + 1)
        top = jnp.max(scores, axis=1, keepdims=True)
        if i > 0:
            top = jnp.maximum(top, largest)
        weights = jnp.exp2(scores - top)
        total = jnp.sum(weights, axis=1, keepdims=True)
        acc = lax.dot_general(
            weights.astype(BF16), keys_ref[:rank, parts[i]], NT, preferred_element_type=F32
        )
        if i > 0:
            factor = jnp.exp2(largest - top)
            total = total + running * factor
            acc = acc + acc_ref[...] * factor
        largest, running = top, total
        if i < tiles - 1:
            acc_ref[...] = acc
    kept = out_ref.shape[0]
    out_ref[...] = acc[:kept]
    max_ref[...] = jnp.broadcast_to(largest[:kept], max_ref.shape)
    sum_ref[...] = jnp.broadcast_to(running[:kept], sum_ref.shape)
    if give_ref:
        level = largest[kept:] + jnp.log2(running[kept:])
        give_ref[0][...] = packed(acc[kept:] * (1.0 / running[kept:]), level)


def prefix_attention(queries, keys, rank, give, tiles=4):
    rows = sum(q.shape[0] for q in queries)
    kept = queries[0].shape[0] if give else rows
    width, length = keys.shape
    out = [shape((kept, rank), F32)] + [shape((kept, LANES), F32)] * 2
    if give:
        out.append(shape((rows - kept, rank + LANES)))
    return pl.pallas_call(
        functools.partial(prefix_kernel, len(queries), tiles),
        out_shape=out,
        in_specs=[VMEM] * (len(queries) + 1),
        out_specs=[VMEM] * len(out),
        scratch_shapes=[pltpu.VMEM((rows, rank), F32)],
        compiler_params=PARAMS,
        cost_estimate=pl.CostEstimate(
            flops=0 if give else 2 * rows * length * (width + rank),
            bytes_accessed=0 if give else 2 * width * length,
            transcendentals=0 if give else rows * length,
        ),
        name="prefix_attention",
    )(*queries, keys)


def packed(values, level):
    rows = values.shape[0]
    lane = lax.broadcasted_iota(jnp.int32, (rows, LANES), 1)
    high = level.astype(BF16).astype(F32)
    middle = (level - high).astype(BF16).astype(F32)
    low = level - high - middle
    stats = jnp.where(lane == 0, high, jnp.where(lane == 1, middle, jnp.where(lane == 2, low, 0.0)))
    return jnp.concatenate([values.astype(BF16), stats.astype(BF16)], axis=1)


def merged(parts, rank):
    levels = [jnp.sum(part[:, rank:].astype(F32), axis=1, keepdims=True) for part in parts]
    top = functools.reduce(jnp.maximum, levels)
    shares = [jnp.exp2(level - top) for level in levels]
    whole = functools.reduce(jnp.add, shares)
    acc = functools.reduce(
        jnp.add, [share * part[:, :rank].astype(F32) for share, part in zip(shares, parts)]
    )
    return acc * (1.0 / whole), top + jnp.log2(whole)


def visible(rows, ends, starts, span):
    local = len(ends)
    cols = len(starts) * local * span
    col = lax.broadcasted_iota(jnp.int32, (1, cols), 1)
    col_of = jnp.zeros_like(col)
    limit = jnp.full_like(col, ends[0] - starts[0])
    for at in range(1, len(starts) * local):
        begin, p = at * span, at % local
        later = col >= begin
        col_of = jnp.where(later, p, col_of)
        limit = jnp.where(later, ends[p] - starts[at // local] + begin, limit)
    col_of = jnp.where(col < limit, col_of, -1)
    row_of = lax.rem(lax.broadcasted_iota(jnp.int32, (rows, 1), 0), local)
    return row_of == col_of


def attend(queries, keys, seen, rank, known):
    scores = lax.dot_general(queries, keys, NT, preferred_element_type=F32)
    scores = jnp.where(seen, scores * SCALE2, HIDDEN)
    top = jnp.max(scores, axis=1, keepdims=True)
    for level, _, _ in known:
        top = jnp.maximum(top, level)
    weights = jnp.where(seen, jnp.exp2(scores - top), 0.0)
    total = jnp.sum(weights, axis=1, keepdims=True)
    acc = jnp.dot(weights.astype(BF16), keys[:, :rank], preferred_element_type=F32)
    for level, mass, part in known:
        factor = jnp.exp2(level - top)
        total = total + mass * factor
        acc = acc + part * factor
    return packed(acc * (1.0 / total), top + jnp.log2(total))


def gather_blocks(block_refs, picks, out_ref, sems):
    some = out_ref.shape[0] // len(picks)

    def copy(p, k, slot):
        return pltpu.make_async_copy(
            block_refs[k].at[pl.ds(pl.multiple_of(slot * some, some), some)],
            out_ref.at[pl.ds(p * some, some)],
            sems.at[p],
        )

    for p, (which, slot) in enumerate(picks):
        for k in range(len(block_refs)):

            @pl.when(which == k)
            def _():
                copy(p, k, slot).start()

    for p in range(len(picks)):
        copy(p, 0, 0).wait()


def at_end(dom):
    return (dom == 0) | (dom == 3)


def select_kernel(theirs, *refs):
    dom = lax.axis_index("dom")
    block_refs, (_, out_ref, sems) = refs[:-3], refs[-3:]
    local = sems.shape[0]
    picks = []
    for p in range(local):
        apart = jnp.bitwise_xor(lax.div(theirs[p], local), dom)
        which = jnp.where(at_end(dom), 0, jnp.maximum(apart - 1, 0))
        picks.append((which, jnp.where(at_end(dom), p, lax.rem(theirs[p], local))))
    gather_blocks(block_refs, picks, out_ref, sems)


def far_kernel(stages, sources, line, *refs):
    anc, lens = refs[:2]
    refs = refs[2:]
    seq, dom = lax.axis_index("seq"), lax.axis_index("dom")
    stage_refs, refs = refs[: 5 * stages], refs[5 * stages :]
    block_refs, refs = refs[:sources], refs[sources:]
    moved_ref, refs = refs[0], refs[1:]
    keep_refs, give_refs = refs[:stages], refs[stages : 2 * stages]
    raw, sems = refs[2 * stages :]
    local = sems.shape[0]
    some = raw.shape[0] // local
    span, width = 2 * some, moved_ref.shape[1]
    rank = stage_refs[2].shape[1]

    picks = []
    for p in range(local):
        owner, slot = lax.div(anc[p], local), lax.rem(anc[p], local)
        if line:
            which = jnp.bitwise_xor(owner, dom)
            chosen = at_end(dom) & (which != 0)
            which = jnp.where(chosen, 1, which)
            slot = jnp.where(chosen, p, slot)
        else:
            which = lax.rem(dom - owner + sources, sources)
        picks.append((which, slot))
    gather_blocks(block_refs, picks, raw, sems)
    for p in range(local):
        for h in range(2):
            part, rows = pl.ds(p * some, some), pl.ds(p * span + h * some, some)
            rope = 2 * rank + h * (width - rank)
            moved_ref[rows, :rank] = raw[part, h * rank : (h + 1) * rank]
            moved_ref[rows, rank:] = raw[part, rope : rope + width - rank]

    ends = [lens[anc[p]] for p in range(local)]
    for k in range(stages):
        first_ref, second_ref, acc_ref, max_ref, sum_ref = stage_refs[5 * k : 5 * k + 5]
        queries = jnp.concatenate([first_ref[...], second_ref[...]], axis=0)
        seen = visible(queries.shape[0], ends, [seq * span], span)
        known = [(max_ref[:, 0:1], sum_ref[:, 0:1], acc_ref[...])]
        part = attend(queries, moved_ref[...], seen, rank, known)
        rows = first_ref.shape[0]
        keep_refs[k][...] = part[:rows]
        give_refs[k][...] = part[rows:]


def near_kernel(anc, lens, fresh_ref, *refs):
    seq = lax.axis_index("seq")
    query_ref, acc_ref, max_ref, sum_ref, got_ref, moved_ref, other_ref, cache_ref, part_ref = refs
    local, span, width = cache_ref.shape
    rank = acc_ref.shape[1]
    start, other = seq * span, jnp.bitwise_xor(seq, 1) * span
    ends = [lens[anc[p]] for p in range(local)]
    keys = jnp.concatenate([moved_ref[...], other_ref[...]], axis=0)
    seen = visible(query_ref.shape[0], ends, [start, other], span)
    level = jnp.sum(got_ref[:, rank:].astype(F32), axis=1, keepdims=True)
    known = [
        (max_ref[:, 0:1], sum_ref[:, 0:1], acc_ref[...]),
        (level, 1.0, got_ref[:, :rank].astype(F32)),
    ]
    part_ref[...] = attend(query_ref[...], keys, seen, rank, known)
    for p in range(local):
        at = start + lax.broadcasted_iota(jnp.int32, (span, 1), 0) == ends[p]
        cache_ref[p] = jnp.where(at, fresh_ref[pl.ds(p, 1), :], moved_ref[pl.ds(p * span, span)])


def chip_kernel(count, *refs):
    for k in range(count):
        out_ref = refs[2 * count + k]
        rank = out_ref.shape[1] - LANES
        out_ref[...] = packed(*merged([refs[k][...], refs[count + k][...]], rank))


def chip_merge(keep, got):
    return pl.pallas_call(
        functools.partial(chip_kernel, len(keep)),
        out_shape=[shape(k.shape) for k in keep],
        in_specs=[VMEM] * (2 * len(keep)),
        out_specs=[VMEM] * len(keep),
        compiler_params=PARAMS,
        name="chip_merge",
    )(*keep, *got)


def final_kernel(count, *refs):
    part_refs, (w_ref, out_ref, values) = refs[:count], refs[count:]
    heads, rank, reach = w_ref.shape
    local = out_ref.shape[0]
    latent = merged([ref[...] for ref in part_refs], rank)[0].astype(BF16)
    first = lax.broadcasted_iota(jnp.int32, (2 * local, reach), 0) < local
    for h in range(0, heads, 2):
        two = latent[h * local : (h + 2) * local]
        weights = jnp.concatenate([w_ref[h], w_ref[h + 1]], axis=1)
        both = jnp.dot(two, weights, preferred_element_type=F32)
        values[pl.ds(h * local, 2 * local), :] = jnp.where(first, both[:, :reach], both[:, reach:])
    for p in range(local):
        out_ref[p] = values[pl.ds(p, heads, stride=local), :].astype(BF16)


def on_device(q_nope, q_rope, w_uk, w_uv, prefix, private_caches, new_latent, ancestors, lengths):
    local, heads, nope = q_nope.shape
    span, width = private_caches.shape[1:]
    rank, reach = w_uv.shape[1:]
    rows = local * heads
    seq_size, dom_size = lax.axis_size("seq"), lax.axis_size("dom")
    cores = 2
    chips = seq_size // cores
    block = pl.pallas_call(
        functools.partial(pack_kernel, rank),
        out_shape=shape((local * span // 2, 2 * width)),
        in_specs=[VMEM],
        out_specs=VMEM,
        compiler_params=PARAMS,
        cost_estimate=pl.CostEstimate(flops=PACK, bytes_accessed=0, transcendentals=0),
        name="pack",
    )(private_caches)
    nope_rows, rope_rows = (jnp.swapaxes(q, 0, 1).reshape(rows, -1) for q in (q_nope, q_rope))
    line = dom_size == 4
    if line:
        swap = [(0, 1), (1, 0), (2, 3), (3, 2)]
        middle = lax.ppermute(block, "dom", [(0, 2), (3, 1)])
        far = lax.ppermute(block, "dom", [(1, 2), (2, 1)])
        theirs = lax.ppermute(ancestors, "dom", [(0, 1), (3, 2)])
    else:
        blocks = [block] + [
            lax.ppermute(block, "dom", [(i, (i + k) % dom_size) for i in range(dom_size)])
            for k in range(1, dom_size)
        ]

    own = pl.pallas_call(
        functools.partial(project_kernel, local),
        out_shape=shape((rows, width)),
        in_specs=[VMEM] * 3,
        out_specs=VMEM,
        compiler_params=PARAMS,
        cost_estimate=pl.CostEstimate(flops=PROJECT, bytes_accessed=0, transcendentals=0),
        name="project",
    )(nope_rows, rope_rows, w_uk)
    keys = prefix.T

    def pairs(turn, flip):
        return [
            (x * cores + c, (x + turn) % chips * cores + (c ^ flip))
            for x in range(chips)
            for c in range(cores)
        ]

    def back(turn, flip):
        return [(b, a) for a, b in pairs(turn, flip)]

    routes = [(t, f) for t in range(chips) for f in range(cores)]
    queries = [own if r == (0, 0) else lax.ppermute(own, "seq", pairs(*r)) for r in routes]
    stages = []
    for t in range(chips):
        asked = queries[2 * t : 2 * t + 2]
        stage = [*asked, *prefix_attention(asked, keys, rank, t == 0)]
        stages.append(stage)
        if t == 0:
            given = lax.ppermute(stage.pop(), "seq", pairs(0, 1))
        if line and t == 0:
            chosen = pl.pallas_call(
                select_kernel,
                out_shape=shape(block.shape),
                in_specs=[SMEM] + [ANY] * 4,
                out_specs=VMEM,
                scratch_shapes=[pltpu.SemaphoreType.DMA((local,))],
                compiler_params=PARAMS,
                cost_estimate=pl.CostEstimate(flops=0, bytes_accessed=0, transcendentals=0),
                name="select",
            )(theirs, block, middle, far, stage[3])
            blocks = [block, lax.ppermute(chosen, "dom", swap), middle, far]

    part = shape((rows, rank + LANES))
    others = chips - 1
    far_results = pl.pallas_call(
        functools.partial(far_kernel, others, len(blocks), line),
        out_shape=[shape((local * span, width))] + [part] * (2 * others),
        in_specs=[SMEM] * 2 + [VMEM] * (5 * others) + [ANY] * len(blocks),
        out_specs=[VMEM] * (1 + 2 * others),
        scratch_shapes=[
            pltpu.VMEM(block.shape, BF16),
            pltpu.SemaphoreType.DMA((local,)),
        ],
        compiler_params=PARAMS,
        name="suffix_far",
    )(ancestors, lengths, *[a for stage in stages[1:] for a in stage], *blocks)
    moved = far_results[0]
    keep, give = far_results[1 : 1 + others], far_results[1 + others :]
    sums = chip_merge(keep, [lax.ppermute(g, "seq", pairs(0, 1)) for g in give])
    parts = [lax.ppermute(s, "seq", back(t, 0)) for t, s in enumerate(sums, 1)]
    other = lax.ppermute(moved, "seq", pairs(0, 1))

    moved, _ = lax.optimization_barrier((moved, sums[0]))
    query, _, acc, level, mass = stages[0]
    new_caches, own_part = pl.pallas_call(
        near_kernel,
        out_shape=[shape(private_caches.shape), part],
        in_specs=[SMEM] * 2 + [VMEM] * 8,
        out_specs=[VMEM] * 2,
        compiler_params=PARAMS,
        name="suffix_near",
    )(ancestors, lengths, new_latent, query, acc, level, mass, given, moved, other)
    parts.append(own_part)

    head_values = pl.pallas_call(
        functools.partial(final_kernel, chips),
        out_shape=shape((local, heads, reach)),
        in_specs=[VMEM] * (chips + 1),
        out_specs=VMEM,
        scratch_shapes=[pltpu.VMEM((rows, reach), F32)],
        compiler_params=PARAMS,
        name="final",
    )(*parts, w_uv)
    return (head_values, new_caches)


def solution(mesh):
    placed = (
        P(("group", "dom"), "seq", None),
        P(("group", "dom"), "seq", None),
        P("seq", None, None),
        P("seq", None, None),
        P(("group", "seq"), None),
        P(("group", "dom"), "seq", None),
        P(("group", "dom"), None),
        P(("group", "dom")),
        P("group"),
    )
    return jax.shard_map(
        on_device,
        mesh=mesh,
        in_specs=placed,
        out_specs=(P(("group", "dom"), "seq", None), P(("group", "dom"), "seq", None)),
        check_vma=False,
    )
```

```python
import functools
import math

import jax
import jax.numpy as jnp
from jax import lax
from jax.experimental import pallas as pl
from jax.experimental.pallas import tpu as pltpu
from jax.sharding import PartitionSpec as P

ROPE = 64
NOPE = 128
SCALE2 = (NOPE + ROPE) ** (-0.5) * math.log2(math.e)
HIDDEN = -1e30
LANES = 128
F32 = jnp.float32
BF16 = jnp.bfloat16
NT = (((1,), (1,)), ((), ()))

VMEM = pl.BlockSpec(memory_space=pltpu.VMEM)
SMEM = pl.BlockSpec(memory_space=pltpu.SMEM)
ANY = pl.BlockSpec(memory_space=pl.ANY)
HBM = pl.BlockSpec(memory_space=pltpu.HBM)
PARAMS = pltpu.CompilerParams(vmem_limit_bytes=40 * 1024 * 1024)
NO_COST = pl.CostEstimate(flops=0, bytes_accessed=0, transcendentals=0)
PACK = 8_000_000_000
PROJECT = 8_000_000_000


def shape(dims, dtype=BF16):
    return jax.ShapeDtypeStruct(dims, dtype)


def pack_kernel(rank, cache_ref, out_ref):
    local, span, _ = cache_ref.shape
    some = span // 2
    for p in range(local):
        part = pl.ds(p * some, some)
        first, second = cache_ref[p, :some], cache_ref[p, some:]
        out_ref[part, :rank] = first[:, :rank]
        out_ref[part, rank : 2 * rank] = second[:, :rank]
        out_ref[part, 2 * rank :] = jnp.concatenate([first[:, rank:], second[:, rank:]], axis=1)


def project_kernel(local, nope_ref, rope_ref, w_ref, own_ref):
    heads, _, rank = w_ref.shape
    nope = nope_ref[...].astype(F32)
    width = nope.shape[1]
    first = lax.broadcasted_iota(jnp.int32, (2 * local, width), 0) < local

    def pair(h):
        two = nope[h * local : (h + 2) * local]
        left = jnp.concatenate([jnp.where(first, two, 0.0), jnp.where(first, 0.0, two)], axis=1)
        weights = w_ref[pl.ds(h, 2)].reshape(2 * width, rank)
        return jnp.dot(left.astype(BF16), weights, preferred_element_type=F32)

    own_ref[:, rank:] = rope_ref[...]
    for h in range(0, heads, 4):
        own_ref[pl.ds(h * local, 4 * local), :rank] = jnp.concatenate(
            [pair(i) for i in (h, h + 2)], axis=0
        ).astype(BF16)


def prefix_kernel(count, tiles, *refs):
    query_refs = refs[:count]
    keys_ref, out_ref, max_ref, sum_ref, *give_ref, acc_ref = refs[count:]
    rank = acc_ref.shape[1]
    tile = keys_ref.shape[1] // tiles
    parts = [pl.ds(i * tile, tile) for i in range(tiles)]
    queries = jnp.concatenate([ref[...] for ref in query_refs], axis=0)

    def score(i):
        return jnp.dot(queries, keys_ref[:, parts[i]], preferred_element_type=F32) * SCALE2

    ahead = score(0)
    for i in range(tiles):
        scores = ahead
        if i + 1 < tiles:
            ahead = score(i + 1)
        top = jnp.max(scores, axis=1, keepdims=True)
        if i > 0:
            top = jnp.maximum(top, largest)
        weights = jnp.exp2(scores - top)
        total = jnp.sum(weights, axis=1, keepdims=True)
        acc = lax.dot_general(
            weights.astype(BF16), keys_ref[:rank, parts[i]], NT, preferred_element_type=F32
        )
        if i > 0:
            factor = jnp.exp2(largest - top)
            total = total + running * factor
            acc = acc + acc_ref[...] * factor
        largest, running = top, total
        if i < tiles - 1:
            acc_ref[...] = acc
    kept = out_ref.shape[0]
    out_ref[...] = acc[:kept]
    max_ref[...] = jnp.broadcast_to(largest[:kept], max_ref.shape)
    sum_ref[...] = jnp.broadcast_to(running[:kept], sum_ref.shape)
    if give_ref:
        level = largest[kept:] + jnp.log2(running[kept:])
        give_ref[0][...] = packed(acc[kept:] * (1.0 / running[kept:]), level)


def prefix_attention(queries, keys, rank, give, tiles=4):
    rows = sum(q.shape[0] for q in queries)
    kept = queries[0].shape[0] if give else rows
    width, length = keys.shape
    out = [shape((kept, rank), F32)] + [shape((kept, LANES), F32)] * 2
    if give:
        out.append(shape((rows - kept, rank + LANES)))
    return pl.pallas_call(
        functools.partial(prefix_kernel, len(queries), tiles),
        out_shape=out,
        in_specs=[VMEM] * (len(queries) + 1),
        out_specs=[VMEM] * len(out),
        scratch_shapes=[pltpu.VMEM((rows, rank), F32)],
        compiler_params=PARAMS,
        cost_estimate=pl.CostEstimate(
            flops=0 if give else 2 * rows * length * (width + rank),
            bytes_accessed=0 if give else 2 * width * length,
            transcendentals=0 if give else rows * length,
        ),
        name="prefix_attention",
    )(*queries, keys)


def packed(values, level):
    rows = values.shape[0]
    lane = lax.broadcasted_iota(jnp.int32, (rows, LANES), 1)
    high = level.astype(BF16).astype(F32)
    middle = (level - high).astype(BF16).astype(F32)
    low = level - high - middle
    stats = jnp.where(lane == 0, high, jnp.where(lane == 1, middle, jnp.where(lane == 2, low, 0.0)))
    return jnp.concatenate([values.astype(BF16), stats.astype(BF16)], axis=1)


def merged(parts, rank):
    levels = [jnp.sum(part[:, rank:].astype(F32), axis=1, keepdims=True) for part in parts]
    top = functools.reduce(jnp.maximum, levels)
    shares = [jnp.exp2(level - top) for level in levels]
    whole = functools.reduce(jnp.add, shares)
    acc = functools.reduce(
        jnp.add, [share * part[:, :rank].astype(F32) for share, part in zip(shares, parts)]
    )
    return acc * (1.0 / whole), top + jnp.log2(whole)


def visible(rows, ends, starts, span):
    local = len(ends)
    cols = len(starts) * local * span
    col = lax.broadcasted_iota(jnp.int32, (1, cols), 1)
    col_of = jnp.zeros_like(col)
    limit = jnp.full_like(col, ends[0] - starts[0])
    for at in range(1, len(starts) * local):
        begin, p = at * span, at % local
        later = col >= begin
        col_of = jnp.where(later, p, col_of)
        limit = jnp.where(later, ends[p] - starts[at // local] + begin, limit)
    col_of = jnp.where(col < limit, col_of, -1)
    row_of = lax.rem(lax.broadcasted_iota(jnp.int32, (rows, 1), 0), local)
    return row_of == col_of


def attend(queries, keys, seen, rank, known):
    scores = lax.dot_general(queries, keys, NT, preferred_element_type=F32)
    scores = jnp.where(seen, scores * SCALE2, HIDDEN)
    top = jnp.max(scores, axis=1, keepdims=True)
    for level, _, _ in known:
        top = jnp.maximum(top, level)
    weights = jnp.where(seen, jnp.exp2(scores - top), 0.0)
    total = jnp.sum(weights, axis=1, keepdims=True)
    acc = jnp.dot(weights.astype(BF16), keys[:, :rank], preferred_element_type=F32)
    for level, mass, part in known:
        factor = jnp.exp2(level - top)
        total = total + mass * factor
        acc = acc + part * factor
    return packed(acc * (1.0 / total), top + jnp.log2(total))


def at_end(dom):
    return (dom == 0) | (dom == 3)


def gather_kernel(line, chosen, names, *refs):
    block_refs, out_ref = refs[:-1], refs[-1]
    if chosen:
        block_refs = block_refs[:-1]
    dom = lax.axis_index("dom")
    local = names.shape[0]
    some = out_ref.shape[0] // local
    for p in range(local):
        owner, slot = lax.div(names[p], local), lax.rem(names[p], local)
        if line:
            apart = jnp.bitwise_xor(owner, dom)
            which = jnp.where(at_end(dom), 0, jnp.maximum(apart - 1, 0))
            if chosen:
                slot = jnp.where(at_end(dom), p, slot)
        else:
            which = lax.rem(dom - owner + len(block_refs), len(block_refs))
        rows = pl.ds(pl.multiple_of(slot * some, some), some)
        for k, block_ref in enumerate(block_refs):

            @pl.when(which == k)
            def _():
                out_ref[pl.ds(p * some, some)] = block_ref[rows]


def gathered(names, blocks, line, token=None):
    token = [] if token is None else [token]
    return pl.pallas_call(
        functools.partial(gather_kernel, line, bool(token)),
        out_shape=shape(blocks[0].shape),
        in_specs=[SMEM] + [VMEM] * len(blocks) + [ANY] * len(token),
        out_specs=VMEM,
        compiler_params=PARAMS,
        cost_estimate=NO_COST,
        name="gather",
    )(names, *blocks, *token)


def far_part(anc, lens, query_ref, stage_refs, part, keys):
    acc_ref, max_ref, sum_ref = stage_refs
    local = anc.shape[0]
    span, rank = keys.shape[0] // local, acc_ref.shape[1]
    ends = [lens[anc[p]] for p in range(local)]
    seen = visible(query_ref.shape[0], ends, [lax.axis_index("seq") * span], span)
    known = [(max_ref[part, 0:1], sum_ref[part, 0:1], acc_ref[part])]
    return attend(query_ref[...], keys, seen, rank, known)


def give_kernel(stages, line, anc, lens, *refs):
    stage_refs, refs = refs[: 4 * stages], refs[4 * stages :]
    early_ref, late_ref, moved_ref, give_refs = refs[0], refs[1], refs[2], refs[3:]
    dom = lax.axis_index("dom")
    local = anc.shape[0]
    some = early_ref.shape[0] // local
    span, width = 2 * some, moved_ref.shape[1]
    rank = stage_refs[1].shape[1]

    def place(p, value):
        for h in range(2):
            rows, rope = pl.ds(p * span + h * some, some), 2 * rank + h * (width - rank)
            moved_ref[rows, :rank] = value[:, h * rank : (h + 1) * rank]
            moved_ref[rows, rank:] = value[:, rope : rope + width - rank]

    for p in range(local):
        if line:
            owner, slot = lax.div(anc[p], local), lax.rem(anc[p], local)
            apart = jnp.bitwise_xor(owner, dom)
            late = jnp.where(at_end(dom), apart != 0, apart == 1)
            slot = jnp.where(at_end(dom), p, slot)
            rows = pl.ds(pl.multiple_of(slot * some, some), some)

            @pl.when(late)
            def _():
                place(p, late_ref[rows])

            @pl.when(jnp.logical_not(late))
            def _():
                place(p, early_ref[pl.ds(p * some, some)])

        else:
            place(p, early_ref[pl.ds(p * some, some)])

    for k in range(stages):
        query_ref, *partial = stage_refs[4 * k : 4 * k + 4]
        rows = query_ref.shape[0]
        give_refs[k][...] = far_part(anc, lens, query_ref, partial, pl.ds(rows, rows), moved_ref[...])


def keep_kernel(stages, anc, lens, *refs):
    stage_refs, refs = refs[: 4 * stages], refs[4 * stages :]
    moved_ref, keep_refs = refs[0], refs[1:]
    for k in range(stages):
        query_ref, *partial = stage_refs[4 * k : 4 * k + 4]
        rows = query_ref.shape[0]
        keep_refs[k][...] = far_part(anc, lens, query_ref, partial, pl.ds(0, rows), moved_ref[...])


def near_kernel(anc, lens, fresh_ref, *refs):
    seq = lax.axis_index("seq")
    query_ref, acc_ref, max_ref, sum_ref, got_ref, moved_ref, other_ref, cache_ref, part_ref = refs
    local, span, width = cache_ref.shape
    rank = acc_ref.shape[1]
    start, other = seq * span, jnp.bitwise_xor(seq, 1) * span
    ends = [lens[anc[p]] for p in range(local)]
    keys = jnp.concatenate([moved_ref[...], other_ref[...]], axis=0)
    seen = visible(query_ref.shape[0], ends, [start, other], span)
    level = jnp.sum(got_ref[:, rank:].astype(F32), axis=1, keepdims=True)
    known = [
        (max_ref[:, 0:1], sum_ref[:, 0:1], acc_ref[...]),
        (level, 1.0, got_ref[:, :rank].astype(F32)),
    ]
    part_ref[...] = attend(query_ref[...], keys, seen, rank, known)
    for p in range(local):
        at = start + lax.broadcasted_iota(jnp.int32, (span, 1), 0) == ends[p]
        cache_ref[p] = jnp.where(at, fresh_ref[pl.ds(p, 1), :], moved_ref[pl.ds(p * span, span)])


def chip_kernel(count, *refs):
    for k in range(count):
        out_ref = refs[2 * count + k]
        rank = out_ref.shape[1] - LANES
        out_ref[...] = packed(*merged([refs[k][...], refs[count + k][...]], rank))


def chip_merge(keep, got):
    return pl.pallas_call(
        functools.partial(chip_kernel, len(keep)),
        out_shape=[shape(k.shape) for k in keep],
        in_specs=[VMEM] * (2 * len(keep)),
        out_specs=[VMEM] * len(keep),
        compiler_params=PARAMS,
        name="chip_merge",
    )(*keep, *got)


def final_kernel(count, *refs):
    part_refs, (w_ref, out_ref, values) = refs[:count], refs[count:]
    heads, rank, reach = w_ref.shape
    local = out_ref.shape[0]
    latent = merged([ref[...] for ref in part_refs], rank)[0].astype(BF16)
    first = lax.broadcasted_iota(jnp.int32, (2 * local, reach), 0) < local
    for h in range(0, heads, 2):
        two = latent[h * local : (h + 2) * local]
        weights = jnp.concatenate([w_ref[h], w_ref[h + 1]], axis=1)
        both = jnp.dot(two, weights, preferred_element_type=F32)
        values[pl.ds(h * local, 2 * local), :] = jnp.where(first, both[:, :reach], both[:, reach:])
    for p in range(local):
        out_ref[p] = values[pl.ds(p, heads, stride=local), :].astype(BF16)


def on_device(q_nope, q_rope, w_uk, w_uv, prefix, private_caches, new_latent, ancestors, lengths):
    local, heads, nope = q_nope.shape
    span, width = private_caches.shape[1:]
    rank, reach = w_uv.shape[1:]
    rows = local * heads
    seq_size, dom_size = lax.axis_size("seq"), lax.axis_size("dom")
    cores = 2
    chips = seq_size // cores
    block = pl.pallas_call(
        functools.partial(pack_kernel, rank),
        out_shape=shape((local * span // 2, 2 * width)),
        in_specs=[VMEM],
        out_specs=VMEM,
        compiler_params=PARAMS,
        cost_estimate=pl.CostEstimate(flops=PACK, bytes_accessed=0, transcendentals=0),
        name="pack",
    )(private_caches)
    nope_rows, rope_rows = (jnp.swapaxes(q, 0, 1).reshape(rows, -1) for q in (q_nope, q_rope))
    line = dom_size == 4
    if line:
        swap = [(0, 1), (1, 0), (2, 3), (3, 2)]
        middle = lax.ppermute(block, "dom", [(0, 2), (3, 1)])
        far = lax.ppermute(block, "dom", [(1, 2), (2, 1)])
        theirs = lax.ppermute(ancestors, "dom", [(0, 1), (3, 2)])
    else:
        blocks = [block] + [
            lax.ppermute(block, "dom", [(i, (i + k) % dom_size) for i in range(dom_size)])
            for k in range(1, dom_size)
        ]

    own = pl.pallas_call(
        functools.partial(project_kernel, local),
        out_shape=shape((rows, width)),
        in_specs=[VMEM] * 3,
        out_specs=VMEM,
        compiler_params=PARAMS,
        cost_estimate=pl.CostEstimate(flops=PROJECT, bytes_accessed=0, transcendentals=0),
        name="project",
    )(nope_rows, rope_rows, w_uk)
    keys = prefix.T

    def pairs(turn, flip):
        return [
            (x * cores + c, (x + turn) % chips * cores + (c ^ flip))
            for x in range(chips)
            for c in range(cores)
        ]

    def back(turn, flip):
        return [(b, a) for a, b in pairs(turn, flip)]

    routes = [(t, f) for t in range(chips) for f in range(cores)]
    queries = [own if r == (0, 0) else lax.ppermute(own, "seq", pairs(*r)) for r in routes]
    stages = []
    for t in range(chips):
        asked = queries[2 * t : 2 * t + 2]
        stage = [*asked, *prefix_attention(asked, keys, rank, t == 0)]
        stages.append(stage)
        if t == 0:
            given = lax.ppermute(stage.pop(), "seq", pairs(0, 1))
        if line and t == 0:
            chosen = gathered(theirs, [block, middle, far], line, stage[3])
            late = lax.ppermute(chosen, "dom", swap)
            early = gathered(ancestors, [block, middle, far], line)
    if not line:
        early = late = gathered(ancestors, blocks, line)

    part = shape((rows, rank + LANES))
    others = chips - 1
    giving = [a for stage in stages[1:] for a in stage[1:]]
    keeping = [a for stage in stages[1:] for a in (stage[0], *stage[2:])]
    moved, *give = pl.pallas_call(
        functools.partial(give_kernel, others, line),
        out_shape=[shape((local * span, width))] + [part] * others,
        in_specs=[SMEM] * 2 + [VMEM] * (len(giving) + 2),
        out_specs=[VMEM] * (1 + others),
        compiler_params=PARAMS,
        name="suffix_give",
    )(ancestors, lengths, *giving, early, late)
    keep = pl.pallas_call(
        functools.partial(keep_kernel, others),
        out_shape=[part] * others,
        in_specs=[SMEM] * 2 + [VMEM] * (len(keeping) + 1),
        out_specs=[VMEM] * others,
        compiler_params=PARAMS,
        name="suffix_keep",
    )(ancestors, lengths, *keeping, moved)
    sums = chip_merge(keep, [lax.ppermute(g, "seq", pairs(0, 1)) for g in give])
    parts = [lax.ppermute(s, "seq", back(t, 0)) for t, s in enumerate(sums, 1)]
    other = lax.ppermute(moved, "seq", pairs(0, 1))

    moved, _ = lax.optimization_barrier((moved, sums[0]))
    query, _, acc, level, mass = stages[0]
    new_caches, own_part = pl.pallas_call(
        near_kernel,
        out_shape=[shape(private_caches.shape), part],
        in_specs=[SMEM] * 2 + [VMEM] * 8,
        out_specs=[VMEM] * 2,
        compiler_params=PARAMS,
        name="suffix_near",
    )(ancestors, lengths, new_latent, query, acc, level, mass, given, moved, other)
    parts.append(own_part)

    head_values = pl.pallas_call(
        functools.partial(final_kernel, chips),
        out_shape=shape((local, heads, reach)),
        in_specs=[VMEM] * (chips + 1),
        out_specs=VMEM,
        scratch_shapes=[pltpu.VMEM((rows, reach), F32)],
        compiler_params=PARAMS,
        name="final",
    )(*parts, w_uv)
    return (head_values, new_caches)


def solution(mesh):
    placed = (
        P(("group", "dom"), "seq", None),
        P(("group", "dom"), "seq", None),
        P("seq", None, None),
        P("seq", None, None),
        P(("group", "seq"), None),
        P(("group", "dom"), "seq", None),
        P(("group", "dom"), None),
        P(("group", "dom")),
        P("group"),
    )
    return jax.shard_map(
        on_device,
        mesh=mesh,
        in_specs=placed,
        out_specs=(P(("group", "dom"), "seq", None), P(("group", "dom"), "seq", None)),
        check_vma=False,
    )
```

```python
import functools
import math

import jax
import jax.numpy as jnp
from jax import lax
from jax.experimental import pallas as pl
from jax.experimental.pallas import tpu as pltpu
from jax.sharding import PartitionSpec as P

ROPE = 64
NOPE = 128
SCALE2 = (NOPE + ROPE) ** (-0.5) * math.log2(math.e)
HIDDEN = -1e30
LANES = 128
F32 = jnp.float32
BF16 = jnp.bfloat16
NT = (((1,), (1,)), ((), ()))

VMEM = pl.BlockSpec(memory_space=pltpu.VMEM)
SMEM = pl.BlockSpec(memory_space=pltpu.SMEM)
ANY = pl.BlockSpec(memory_space=pl.ANY)
HBM = pl.BlockSpec(memory_space=pltpu.HBM)
PARAMS = pltpu.CompilerParams(vmem_limit_bytes=40 * 1024 * 1024)
NO_COST = pl.CostEstimate(flops=0, bytes_accessed=0, transcendentals=0)
PACK = 8_000_000_000
PROJECT = 8_000_000_000


def shape(dims, dtype=BF16):
    return jax.ShapeDtypeStruct(dims, dtype)


def pack_kernel(rank, cache_ref, out_ref):
    local, span, _ = cache_ref.shape
    some = span // 2
    for p in range(local):
        part = pl.ds(p * some, some)
        first, second = cache_ref[p, :some], cache_ref[p, some:]
        out_ref[part, :rank] = first[:, :rank]
        out_ref[part, rank : 2 * rank] = second[:, :rank]
        out_ref[part, 2 * rank :] = jnp.concatenate([first[:, rank:], second[:, rank:]], axis=1)


def project_kernel(local, nope_ref, rope_ref, w_ref, own_ref):
    heads, _, rank = w_ref.shape
    nope = nope_ref[...].astype(F32)
    width = nope.shape[1]
    first = lax.broadcasted_iota(jnp.int32, (2 * local, width), 0) < local

    def pair(h):
        two = nope[h * local : (h + 2) * local]
        left = jnp.concatenate([jnp.where(first, two, 0.0), jnp.where(first, 0.0, two)], axis=1)
        weights = w_ref[pl.ds(h, 2)].reshape(2 * width, rank)
        return jnp.dot(left.astype(BF16), weights, preferred_element_type=F32)

    own_ref[:, rank:] = rope_ref[...]
    for h in range(0, heads, 4):
        own_ref[pl.ds(h * local, 4 * local), :rank] = jnp.concatenate(
            [pair(i) for i in (h, h + 2)], axis=0
        ).astype(BF16)


def prefix_kernel(count, tiles, *refs):
    query_refs = refs[:count]
    keys_ref, out_ref, max_ref, sum_ref, *give_ref, acc_ref = refs[count:]
    rank = acc_ref.shape[1]
    tile = keys_ref.shape[1] // tiles
    parts = [pl.ds(i * tile, tile) for i in range(tiles)]
    queries = jnp.concatenate([ref[...] for ref in query_refs], axis=0)

    def score(i):
        return jnp.dot(queries, keys_ref[:, parts[i]], preferred_element_type=F32) * SCALE2

    ahead = score(0)
    for i in range(tiles):
        scores = ahead
        if i + 1 < tiles:
            ahead = score(i + 1)
        top = jnp.max(scores, axis=1, keepdims=True)
        if i > 0:
            top = jnp.maximum(top, largest)
        weights = jnp.exp2(scores - top)
        total = jnp.sum(weights, axis=1, keepdims=True)
        acc = lax.dot_general(
            weights.astype(BF16), keys_ref[:rank, parts[i]], NT, preferred_element_type=F32
        )
        if i > 0:
            factor = jnp.exp2(largest - top)
            total = total + running * factor
            acc = acc + acc_ref[...] * factor
        largest, running = top, total
        if i < tiles - 1:
            acc_ref[...] = acc
    kept = out_ref.shape[0]
    out_ref[...] = acc[:kept]
    max_ref[...] = jnp.broadcast_to(largest[:kept], max_ref.shape)
    sum_ref[...] = jnp.broadcast_to(running[:kept], sum_ref.shape)
    if give_ref:
        level = largest[kept:] + jnp.log2(running[kept:])
        give_ref[0][...] = packed(acc[kept:] * (1.0 / running[kept:]), level)


def prefix_attention(queries, keys, rank, give, tiles=4):
    rows = sum(q.shape[0] for q in queries)
    kept = queries[0].shape[0] if give else rows
    width, length = keys.shape
    out = [shape((kept, rank), F32)] + [shape((kept, LANES), F32)] * 2
    if give:
        out.append(shape((rows - kept, rank + LANES)))
    return pl.pallas_call(
        functools.partial(prefix_kernel, len(queries), tiles),
        out_shape=out,
        in_specs=[VMEM] * (len(queries) + 1),
        out_specs=[VMEM] * len(out),
        scratch_shapes=[pltpu.VMEM((rows, rank), F32)],
        compiler_params=PARAMS,
        cost_estimate=pl.CostEstimate(
            flops=0 if give else 2 * rows * length * (width + rank),
            bytes_accessed=0 if give else 2 * width * length,
            transcendentals=0 if give else rows * length,
        ),
        name="prefix_attention",
    )(*queries, keys)


def packed(values, level):
    rows = values.shape[0]
    lane = lax.broadcasted_iota(jnp.int32, (rows, LANES), 1)
    high = level.astype(BF16).astype(F32)
    middle = (level - high).astype(BF16).astype(F32)
    low = level - high - middle
    stats = jnp.where(lane == 0, high, jnp.where(lane == 1, middle, jnp.where(lane == 2, low, 0.0)))
    return jnp.concatenate([values.astype(BF16), stats.astype(BF16)], axis=1)


def unpacked(part):
    rank = part.shape[1] - LANES
    return part[:, :rank].astype(F32), jnp.sum(part[:, rank:].astype(F32), axis=1, keepdims=True)


def merged(parts):
    levels = [level for _, level in parts]
    top = functools.reduce(jnp.maximum, levels)
    shares = [jnp.exp2(level - top) for level in levels]
    whole = functools.reduce(jnp.add, shares)
    acc = functools.reduce(jnp.add, [share * values for share, (values, _) in zip(shares, parts)])
    return acc * (1.0 / whole), top + jnp.log2(whole)


def diagonal(rows, lanes):
    row = lax.broadcasted_iota(jnp.int32, (rows, lanes), 0)
    return row == lax.broadcasted_iota(jnp.int32, (rows, lanes), 1)


def visible(rows, ends, starts, span):
    local = len(ends)
    cols = len(starts) * local * span
    col = lax.broadcasted_iota(jnp.int32, (1, cols), 1)
    col_of = jnp.zeros_like(col)
    limit = jnp.full_like(col, ends[0] - starts[0])
    for at in range(1, len(starts) * local):
        begin, p = at * span, at % local
        later = col >= begin
        col_of = jnp.where(later, p, col_of)
        limit = jnp.where(later, ends[p] - starts[at // local] + begin, limit)
    col_of = jnp.where(col < limit, col_of, -1)
    row_of = lax.rem(lax.broadcasted_iota(jnp.int32, (rows, 1), 0), local)
    return row_of == col_of


def attend(queries, keys, seen, rank, known):
    scores = lax.dot_general(queries, keys, NT, preferred_element_type=F32)
    scores = jnp.where(seen, scores * SCALE2, HIDDEN)
    top = jnp.max(scores, axis=1, keepdims=True)
    for level, _, _ in known:
        top = jnp.maximum(top, level)
    weights = jnp.where(seen, jnp.exp2(scores - top), 0.0)
    total = jnp.sum(weights, axis=1, keepdims=True)
    acc = jnp.dot(weights.astype(BF16), keys[:, :rank], preferred_element_type=F32)
    for level, mass, part in known:
        factor = jnp.exp2(level - top)
        total = total + mass * factor
        acc = acc + part * factor
    return acc * (1.0 / total), top + jnp.log2(total)


def at_end(dom):
    return (dom == 0) | (dom == 3)


def gather_kernel(line, chosen, names, *refs):
    block_refs, out_ref = refs[:-1], refs[-1]
    if chosen:
        block_refs = block_refs[:-1]
    dom = lax.axis_index("dom")
    local = names.shape[0]
    some = out_ref.shape[0] // local
    for p in range(local):
        owner, slot = lax.div(names[p], local), lax.rem(names[p], local)
        if line:
            apart = jnp.bitwise_xor(owner, dom)
            which = jnp.where(at_end(dom), 0, jnp.maximum(apart - 1, 0))
            if chosen:
                slot = jnp.where(at_end(dom), p, slot)
        else:
            which = lax.rem(dom - owner + len(block_refs), len(block_refs))
        rows = pl.ds(pl.multiple_of(slot * some, some), some)
        for k, block_ref in enumerate(block_refs):

            @pl.when(which == k)
            def _():
                out_ref[pl.ds(p * some, some)] = block_ref[rows]


def gathered(names, blocks, line, token=None):
    token = [] if token is None else [token]
    return pl.pallas_call(
        functools.partial(gather_kernel, line, bool(token)),
        out_shape=shape(blocks[0].shape),
        in_specs=[SMEM] + [VMEM] * len(blocks) + [ANY] * len(token),
        out_specs=VMEM,
        compiler_params=PARAMS,
        cost_estimate=NO_COST,
        name="gather",
    )(names, *blocks, *token)


def far_part(anc, lens, query_ref, stage_refs, part, keys):
    acc_ref, max_ref, sum_ref = stage_refs
    local = anc.shape[0]
    span, rank = keys.shape[0] // local, acc_ref.shape[1]
    ends = [lens[anc[p]] for p in range(local)]
    seen = visible(query_ref.shape[0], ends, [lax.axis_index("seq") * span], span)
    known = [(max_ref[part, 0:1], sum_ref[part, 0:1], acc_ref[part])]
    return packed(*attend(query_ref[...], keys, seen, rank, known))


def give_kernel(stages, line, anc, lens, *refs):
    stage_refs, refs = refs[: 4 * stages], refs[4 * stages :]
    early_ref, late_ref, moved_ref, give_refs = refs[0], refs[1], refs[2], refs[3:]
    dom = lax.axis_index("dom")
    local = anc.shape[0]
    some = early_ref.shape[0] // local
    span, width = 2 * some, moved_ref.shape[1]
    rank = stage_refs[1].shape[1]

    def place(p, value):
        for h in range(2):
            rows, rope = pl.ds(p * span + h * some, some), 2 * rank + h * (width - rank)
            moved_ref[rows, :rank] = value[:, h * rank : (h + 1) * rank]
            moved_ref[rows, rank:] = value[:, rope : rope + width - rank]

    for p in range(local):
        if line:
            owner, slot = lax.div(anc[p], local), lax.rem(anc[p], local)
            apart = jnp.bitwise_xor(owner, dom)
            late = jnp.where(at_end(dom), apart != 0, apart == 1)
            slot = jnp.where(at_end(dom), p, slot)
            rows = pl.ds(pl.multiple_of(slot * some, some), some)

            @pl.when(late)
            def _():
                place(p, late_ref[rows])

            @pl.when(jnp.logical_not(late))
            def _():
                place(p, early_ref[pl.ds(p * some, some)])

        else:
            place(p, early_ref[pl.ds(p * some, some)])

    for k in range(stages):
        query_ref, *partial = stage_refs[4 * k : 4 * k + 4]
        rows = query_ref.shape[0]
        give_refs[k][...] = far_part(anc, lens, query_ref, partial, pl.ds(rows, rows), moved_ref[...])


def keep_kernel(stages, anc, lens, *refs):
    stage_refs, refs = refs[: 4 * stages], refs[4 * stages :]
    moved_ref, keep_refs = refs[0], refs[1:]
    for k in range(stages):
        query_ref, *partial = stage_refs[4 * k : 4 * k + 4]
        rows = query_ref.shape[0]
        keep_refs[k][...] = far_part(anc, lens, query_ref, partial, pl.ds(0, rows), moved_ref[...])


def near_kernel(anc, lens, fresh_ref, *refs):
    seq = lax.axis_index("seq")
    query_ref, acc_ref, max_ref, sum_ref, got_ref, moved_ref, other_ref, cache_ref, value_ref, level_ref = refs
    local, span, width = cache_ref.shape
    rank = acc_ref.shape[1]
    start, other = seq * span, jnp.bitwise_xor(seq, 1) * span
    ends = [lens[anc[p]] for p in range(local)]
    keys = jnp.concatenate([moved_ref[...], other_ref[...]], axis=0)
    seen = visible(query_ref.shape[0], ends, [start, other], span)
    level = jnp.sum(got_ref[:, rank:].astype(F32), axis=1, keepdims=True)
    known = [
        (max_ref[:, 0:1], sum_ref[:, 0:1], acc_ref[...]),
        (level, 1.0, got_ref[:, :rank].astype(F32)),
    ]
    values, level = attend(query_ref[...], keys, seen, rank, known)
    value_ref[...] = values
    level_ref[...] = jnp.broadcast_to(level, level_ref.shape)
    for p in range(local):
        at = start + lax.broadcasted_iota(jnp.int32, (span, 1), 0) == ends[p]
        cache_ref[p] = jnp.where(at, fresh_ref[pl.ds(p, 1), :], moved_ref[pl.ds(p * span, span)])


def chip_kernel(count, *refs):
    for k in range(count):
        value_ref, level_ref = refs[2 * count + 2 * k : 2 * count + 2 * k + 2]
        values, level = merged([unpacked(refs[k][...]), unpacked(refs[count + k][...])])
        value_ref[...] = values.astype(BF16)
        kept = jnp.where(diagonal(values.shape[0], level_ref.shape[1]), level, 0.0)
        level_ref[...] = jnp.broadcast_to(jnp.sum(kept, axis=0, keepdims=True), level_ref.shape)


def chip_merge(keep, got):
    rows, rank = keep[0].shape[0], keep[0].shape[1] - LANES
    return pl.pallas_call(
        functools.partial(chip_kernel, len(keep)),
        out_shape=[shape((rows, rank)), shape((8, max(rows, LANES)), F32)] * len(keep),
        in_specs=[VMEM] * (2 * len(keep)),
        out_specs=[VMEM] * (2 * len(keep)),
        compiler_params=PARAMS,
        name="chip_merge",
    )(*keep, *got)


def final_kernel(count, *refs):
    part_refs, (value_ref, level_ref, w_ref, out_ref, values) = refs[: 2 * count], refs[2 * count :]
    heads, rank, reach = w_ref.shape
    local = out_ref.shape[0]
    parts = [(value_ref[...], level_ref[:, 0:1])]
    for k in range(count):
        row = part_refs[2 * k + 1][0:1]
        kept = jnp.where(diagonal(value_ref.shape[0], row.shape[1]), row, 0.0)
        parts.append((part_refs[2 * k][...].astype(F32), jnp.sum(kept, axis=1, keepdims=True)))
    latent = merged(parts)[0].astype(BF16)
    first = lax.broadcasted_iota(jnp.int32, (2 * local, reach), 0) < local
    for h in range(0, heads, 2):
        two = latent[h * local : (h + 2) * local]
        weights = jnp.concatenate([w_ref[h], w_ref[h + 1]], axis=1)
        both = jnp.dot(two, weights, preferred_element_type=F32)
        values[pl.ds(h * local, 2 * local), :] = jnp.where(first, both[:, :reach], both[:, reach:])
    for p in range(local):
        out_ref[p] = values[pl.ds(p, heads, stride=local), :].astype(BF16)


def on_device(q_nope, q_rope, w_uk, w_uv, prefix, private_caches, new_latent, ancestors, lengths):
    local, heads, nope = q_nope.shape
    span, width = private_caches.shape[1:]
    rank, reach = w_uv.shape[1:]
    rows = local * heads
    seq_size, dom_size = lax.axis_size("seq"), lax.axis_size("dom")
    cores = 2
    chips = seq_size // cores
    block = pl.pallas_call(
        functools.partial(pack_kernel, rank),
        out_shape=shape((local * span // 2, 2 * width)),
        in_specs=[VMEM],
        out_specs=VMEM,
        compiler_params=PARAMS,
        cost_estimate=pl.CostEstimate(flops=PACK, bytes_accessed=0, transcendentals=0),
        name="pack",
    )(private_caches)
    nope_rows, rope_rows = (jnp.swapaxes(q, 0, 1).reshape(rows, -1) for q in (q_nope, q_rope))
    line = dom_size == 4
    if line:
        swap = [(0, 1), (1, 0), (2, 3), (3, 2)]
        middle = lax.ppermute(block, "dom", [(0, 2), (3, 1)])
        far = lax.ppermute(block, "dom", [(1, 2), (2, 1)])
        theirs = lax.ppermute(ancestors, "dom", [(0, 1), (3, 2)])
    else:
        blocks = [block] + [
            lax.ppermute(block, "dom", [(i, (i + k) % dom_size) for i in range(dom_size)])
            for k in range(1, dom_size)
        ]

    own = pl.pallas_call(
        functools.partial(project_kernel, local),
        out_shape=shape((rows, width)),
        in_specs=[VMEM] * 3,
        out_specs=VMEM,
        compiler_params=PARAMS,
        cost_estimate=pl.CostEstimate(flops=PROJECT, bytes_accessed=0, transcendentals=0),
        name="project",
    )(nope_rows, rope_rows, w_uk)
    keys = prefix.T

    def pairs(turn, flip):
        return [
            (x * cores + c, (x + turn) % chips * cores + (c ^ flip))
            for x in range(chips)
            for c in range(cores)
        ]

    def back(turn, flip):
        return [(b, a) for a, b in pairs(turn, flip)]

    routes = [(t, f) for t in range(chips) for f in range(cores)]
    queries = [own if r == (0, 0) else lax.ppermute(own, "seq", pairs(*r)) for r in routes]
    stages = []
    for t in range(chips):
        asked = queries[2 * t : 2 * t + 2]
        stage = [*asked, *prefix_attention(asked, keys, rank, t == 0)]
        stages.append(stage)
        if t == 0:
            given = lax.ppermute(stage.pop(), "seq", pairs(0, 1))
        if line and t == 0:
            chosen = gathered(theirs, [block, middle, far], line, stage[3])
            late = lax.ppermute(chosen, "dom", swap)
            early = gathered(ancestors, [block, middle, far], line)
    if not line:
        early = late = gathered(ancestors, blocks, line)

    part = shape((rows, rank + LANES))
    others = chips - 1
    giving = [a for stage in stages[1:] for a in stage[1:]]
    keeping = [a for stage in stages[1:] for a in (stage[0], *stage[2:])]
    moved, *give = pl.pallas_call(
        functools.partial(give_kernel, others, line),
        out_shape=[shape((local * span, width))] + [part] * others,
        in_specs=[SMEM] * 2 + [VMEM] * (len(giving) + 2),
        out_specs=[VMEM] * (1 + others),
        compiler_params=PARAMS,
        name="suffix_give",
    )(ancestors, lengths, *giving, early, late)
    keep = pl.pallas_call(
        functools.partial(keep_kernel, others),
        out_shape=[part] * others,
        in_specs=[SMEM] * 2 + [VMEM] * (len(keeping) + 1),
        out_specs=[VMEM] * others,
        compiler_params=PARAMS,
        name="suffix_keep",
    )(ancestors, lengths, *keeping, moved)
    sums = chip_merge(keep, [lax.ppermute(g, "seq", pairs(0, 1)) for g in give])
    parts = [lax.ppermute(s, "seq", back(1 + i // 2, 0)) for i, s in enumerate(sums)]
    other = lax.ppermute(moved, "seq", pairs(0, 1))

    moved, _ = lax.optimization_barrier((moved, sums[0]))
    query, _, acc, level, mass = stages[0]
    new_caches, *own_part = pl.pallas_call(
        near_kernel,
        out_shape=[shape(private_caches.shape), shape((rows, rank), F32), shape((rows, LANES), F32)],
        in_specs=[SMEM] * 2 + [VMEM] * 8,
        out_specs=[VMEM] * 3,
        compiler_params=PARAMS,
        name="suffix_near",
    )(ancestors, lengths, new_latent, query, acc, level, mass, given, moved, other)
    parts += own_part

    head_values = pl.pallas_call(
        functools.partial(final_kernel, others),
        out_shape=shape((local, heads, reach)),
        in_specs=[VMEM] * (2 * chips + 1),
        out_specs=VMEM,
        scratch_shapes=[pltpu.VMEM((rows, reach), F32)],
        compiler_params=PARAMS,
        name="final",
    )(*parts, w_uv)
    return (head_values, new_caches)


def solution(mesh):
    placed = (
        P(("group", "dom"), "seq", None),
        P(("group", "dom"), "seq", None),
        P("seq", None, None),
        P("seq", None, None),
        P(("group", "seq"), None),
        P(("group", "dom"), "seq", None),
        P(("group", "dom"), None),
        P(("group", "dom")),
        P("group"),
    )
    return jax.shard_map(
        on_device,
        mesh=mesh,
        in_specs=placed,
        out_specs=(P(("group", "dom"), "seq", None), P(("group", "dom"), "seq", None)),
        check_vma=False,
    )
```

```python
import functools
import math

import jax
import jax.numpy as jnp
from jax import lax
from jax.experimental import pallas as pl
from jax.experimental.pallas import tpu as pltpu
from jax.sharding import PartitionSpec as P

ROPE = 64
NOPE = 128
SCALE2 = (NOPE + ROPE) ** (-0.5) * math.log2(math.e)
HIDDEN = -1e30
LANES = 128
F32 = jnp.float32
BF16 = jnp.bfloat16
NT = (((1,), (1,)), ((), ()))

VMEM = pl.BlockSpec(memory_space=pltpu.VMEM)
SMEM = pl.BlockSpec(memory_space=pltpu.SMEM)
ANY = pl.BlockSpec(memory_space=pl.ANY)
HBM = pl.BlockSpec(memory_space=pltpu.HBM)
PARAMS = pltpu.CompilerParams(vmem_limit_bytes=40 * 1024 * 1024)
NO_COST = pl.CostEstimate(flops=0, bytes_accessed=0, transcendentals=0)
PACK = 8_000_000_000
PROJECT = 8_000_000_000


def shape(dims, dtype=BF16):
    return jax.ShapeDtypeStruct(dims, dtype)


def pack_kernel(rank, cache_ref, out_ref):
    local, span, _ = cache_ref.shape
    some = span // 2
    for p in range(local):
        part = pl.ds(p * some, some)
        first, second = cache_ref[p, :some], cache_ref[p, some:]
        out_ref[part, :rank] = first[:, :rank]
        out_ref[part, rank : 2 * rank] = second[:, :rank]
        out_ref[part, 2 * rank :] = jnp.concatenate([first[:, rank:], second[:, rank:]], axis=1)


def project_kernel(local, nope_ref, rope_ref, w_ref, own_ref):
    heads, _, rank = w_ref.shape
    nope = nope_ref[...].astype(F32)
    width = nope.shape[1]
    first = lax.broadcasted_iota(jnp.int32, (2 * local, width), 0) < local

    def pair(h):
        two = nope[h * local : (h + 2) * local]
        left = jnp.concatenate([jnp.where(first, two, 0.0), jnp.where(first, 0.0, two)], axis=1)
        weights = w_ref[pl.ds(h, 2)].reshape(2 * width, rank)
        return jnp.dot(left.astype(BF16), weights, preferred_element_type=F32)

    own_ref[:, rank:] = rope_ref[...]
    for h in range(0, heads, 4):
        own_ref[pl.ds(h * local, 4 * local), :rank] = jnp.concatenate(
            [pair(i) for i in (h, h + 2)], axis=0
        ).astype(BF16)


def prefix_kernel(count, tiles, *refs):
    query_refs = refs[:count]
    keys_ref, out_ref, max_ref, sum_ref, *give_ref, acc_ref = refs[count:]
    rank = acc_ref.shape[1]
    tile = keys_ref.shape[1] // tiles
    parts = [pl.ds(i * tile, tile) for i in range(tiles)]
    queries = jnp.concatenate([ref[...] for ref in query_refs], axis=0)

    def score(i):
        return jnp.dot(queries, keys_ref[:, parts[i]], preferred_element_type=F32) * SCALE2

    ahead = score(0)
    for i in range(tiles):
        scores = ahead
        if i + 1 < tiles:
            ahead = score(i + 1)
        top = jnp.max(scores, axis=1, keepdims=True)
        if i > 0:
            top = jnp.maximum(top, largest)
        weights = jnp.exp2(scores - top)
        total = jnp.sum(weights, axis=1, keepdims=True)
        acc = lax.dot_general(
            weights.astype(BF16), keys_ref[:rank, parts[i]], NT, preferred_element_type=F32
        )
        if i > 0:
            factor = jnp.exp2(largest - top)
            total = total + running * factor
            acc = acc + acc_ref[...] * factor
        largest, running = top, total
        if i < tiles - 1:
            acc_ref[...] = acc
    kept = out_ref.shape[0]
    out_ref[...] = acc[:kept]
    max_ref[...] = jnp.broadcast_to(largest[:kept], max_ref.shape)
    sum_ref[...] = jnp.broadcast_to(running[:kept], sum_ref.shape)
    if give_ref:
        level = largest[kept:] + jnp.log2(running[kept:])
        give_ref[0][...] = packed(acc[kept:] * (1.0 / running[kept:]), level)


def prefix_attention(queries, keys, rank, give, tiles=4):
    rows = sum(q.shape[0] for q in queries)
    kept = queries[0].shape[0] if give else rows
    width, length = keys.shape
    out = [shape((kept, rank), F32)] + [shape((kept, LANES), F32)] * 2
    if give:
        out.append(shape((rows - kept, rank + LANES)))
    return pl.pallas_call(
        functools.partial(prefix_kernel, len(queries), tiles),
        out_shape=out,
        in_specs=[VMEM] * (len(queries) + 1),
        out_specs=[VMEM] * len(out),
        scratch_shapes=[pltpu.VMEM((rows, rank), F32)],
        compiler_params=PARAMS,
        cost_estimate=pl.CostEstimate(
            flops=0 if give else 2 * rows * length * (width + rank),
            bytes_accessed=0 if give else 2 * width * length,
            transcendentals=0 if give else rows * length,
        ),
        name="prefix_attention",
    )(*queries, keys)


def packed(values, level):
    rows = values.shape[0]
    lane = lax.broadcasted_iota(jnp.int32, (rows, LANES), 1)
    high = level.astype(BF16).astype(F32)
    middle = (level - high).astype(BF16).astype(F32)
    low = level - high - middle
    stats = jnp.where(lane == 0, high, jnp.where(lane == 1, middle, jnp.where(lane == 2, low, 0.0)))
    return jnp.concatenate([values.astype(BF16), stats.astype(BF16)], axis=1)


def unpacked(part):
    rank = part.shape[1] - LANES
    return part[:, :rank].astype(F32), jnp.sum(part[:, rank:].astype(F32), axis=1, keepdims=True)


def merged(parts):
    levels = [level for _, level in parts]
    top = functools.reduce(jnp.maximum, levels)
    shares = [jnp.exp2(level - top) for level in levels]
    whole = functools.reduce(jnp.add, shares)
    acc = functools.reduce(jnp.add, [share * values for share, (values, _) in zip(shares, parts)])
    return acc * (1.0 / whole), top + jnp.log2(whole)


def column(stat):
    return jnp.max(stat, axis=1, keepdims=True)


def diagonal(rows, lanes):
    row = lax.broadcasted_iota(jnp.int32, (rows, lanes), 0)
    return row == lax.broadcasted_iota(jnp.int32, (rows, lanes), 1)


def visible(rows, ends, starts, span):
    local = len(ends)
    cols = len(starts) * local * span
    col = lax.broadcasted_iota(jnp.int32, (1, cols), 1)
    col_of = jnp.zeros_like(col)
    limit = jnp.full_like(col, ends[0] - starts[0])
    for at in range(1, len(starts) * local):
        begin, p = at * span, at % local
        later = col >= begin
        col_of = jnp.where(later, p, col_of)
        limit = jnp.where(later, ends[p] - starts[at // local] + begin, limit)
    col_of = jnp.where(col < limit, col_of, -1)
    row_of = lax.rem(lax.broadcasted_iota(jnp.int32, (rows, 1), 0), local)
    return row_of == col_of


def attend(queries, keys, seen, rank, known):
    scores = lax.dot_general(queries, keys, NT, preferred_element_type=F32)
    scores = jnp.where(seen, scores * SCALE2, HIDDEN)
    top = jnp.max(scores, axis=1, keepdims=True)
    for level, _, _ in known:
        top = jnp.maximum(top, level)
    weights = jnp.where(seen, jnp.exp2(scores - top), 0.0)
    total = jnp.sum(weights, axis=1, keepdims=True)
    acc = jnp.dot(weights.astype(BF16), keys[:, :rank], preferred_element_type=F32)
    for level, mass, part in known:
        factor = jnp.exp2(level - top)
        total = total + mass * factor
        acc = acc + part * factor
    return acc * (1.0 / total), top + jnp.log2(total)


def at_end(dom):
    return (dom == 0) | (dom == 3)


def gather_kernel(line, chosen, names, *refs):
    block_refs, out_ref = refs[:-1], refs[-1]
    if chosen:
        block_refs = block_refs[:-1]
    dom = lax.axis_index("dom")
    local = names.shape[0]
    some = out_ref.shape[0] // local
    for p in range(local):
        owner, slot = lax.div(names[p], local), lax.rem(names[p], local)
        if line:
            apart = jnp.bitwise_xor(owner, dom)
            which = jnp.where(at_end(dom), 0, jnp.maximum(apart - 1, 0))
            if chosen:
                slot = jnp.where(at_end(dom), p, slot)
        else:
            which = lax.rem(dom - owner + len(block_refs), len(block_refs))
        rows = pl.ds(pl.multiple_of(slot * some, some), some)
        for k, block_ref in enumerate(block_refs):

            @pl.when(which == k)
            def _():
                out_ref[pl.ds(p * some, some)] = block_ref[rows]


def gathered(names, blocks, line, token=None):
    token = [] if token is None else [token]
    return pl.pallas_call(
        functools.partial(gather_kernel, line, bool(token)),
        out_shape=shape(blocks[0].shape),
        in_specs=[SMEM] + [VMEM] * len(blocks) + [ANY] * len(token),
        out_specs=VMEM,
        compiler_params=PARAMS,
        cost_estimate=NO_COST,
        name="gather",
    )(names, *blocks, *token)


def far_part(anc, lens, query_ref, stage_refs, part, keys):
    acc_ref, max_ref, sum_ref = stage_refs
    local = anc.shape[0]
    span, rank = keys.shape[0] // local, acc_ref.shape[1]
    ends = [lens[anc[p]] for p in range(local)]
    seen = visible(query_ref.shape[0], ends, [lax.axis_index("seq") * span], span)
    known = [(column(max_ref[part]), column(sum_ref[part]), acc_ref[part])]
    return packed(*attend(query_ref[...], keys, seen, rank, known))


def give_kernel(stages, line, anc, lens, *refs):
    stage_refs, refs = refs[: 4 * stages], refs[4 * stages :]
    early_ref, late_ref, moved_ref, give_refs = refs[0], refs[1], refs[2], refs[3:]
    dom = lax.axis_index("dom")
    local = anc.shape[0]
    some = early_ref.shape[0] // local
    span, width = 2 * some, moved_ref.shape[1]
    rank = stage_refs[1].shape[1]

    def place(p, value):
        for h in range(2):
            rows, rope = pl.ds(p * span + h * some, some), 2 * rank + h * (width - rank)
            moved_ref[rows, :rank] = value[:, h * rank : (h + 1) * rank]
            moved_ref[rows, rank:] = value[:, rope : rope + width - rank]

    for p in range(local):
        if line:
            owner, slot = lax.div(anc[p], local), lax.rem(anc[p], local)
            apart = jnp.bitwise_xor(owner, dom)
            late = jnp.where(at_end(dom), apart != 0, apart == 1)
            slot = jnp.where(at_end(dom), p, slot)
            rows = pl.ds(pl.multiple_of(slot * some, some), some)

            @pl.when(late)
            def _():
                place(p, late_ref[rows])

            @pl.when(jnp.logical_not(late))
            def _():
                place(p, early_ref[pl.ds(p * some, some)])

        else:
            place(p, early_ref[pl.ds(p * some, some)])

    for k in range(stages):
        query_ref, *partial = stage_refs[4 * k : 4 * k + 4]
        rows = query_ref.shape[0]
        give_refs[k][...] = far_part(anc, lens, query_ref, partial, pl.ds(rows, rows), moved_ref[...])


def keep_kernel(stages, anc, lens, *refs):
    stage_refs, refs = refs[: 4 * stages], refs[4 * stages :]
    moved_ref, keep_refs = refs[0], refs[1:]
    for k in range(stages):
        query_ref, *partial = stage_refs[4 * k : 4 * k + 4]
        rows = query_ref.shape[0]
        keep_refs[k][...] = far_part(anc, lens, query_ref, partial, pl.ds(0, rows), moved_ref[...])


def near_kernel(anc, lens, fresh_ref, *refs):
    seq = lax.axis_index("seq")
    query_ref, acc_ref, max_ref, sum_ref, got_ref, moved_ref, other_ref, cache_ref, value_ref, level_ref = refs
    local, span, width = cache_ref.shape
    rank = acc_ref.shape[1]
    start, other = seq * span, jnp.bitwise_xor(seq, 1) * span
    ends = [lens[anc[p]] for p in range(local)]
    keys = jnp.concatenate([moved_ref[...], other_ref[...]], axis=0)
    seen = visible(query_ref.shape[0], ends, [start, other], span)
    level = jnp.sum(got_ref[:, rank:].astype(F32), axis=1, keepdims=True)
    known = [
        (column(max_ref[...]), column(sum_ref[...]), acc_ref[...]),
        (level, 1.0, got_ref[:, :rank].astype(F32)),
    ]
    values, level = attend(query_ref[...], keys, seen, rank, known)
    value_ref[...] = values.astype(BF16)
    level_ref[...] = jnp.broadcast_to(level, level_ref.shape)
    for p in range(local):
        at = start + lax.broadcasted_iota(jnp.int32, (span, 1), 0) == ends[p]
        cache_ref[p] = jnp.where(at, fresh_ref[pl.ds(p, 1), :], moved_ref[pl.ds(p * span, span)])


def chip_kernel(count, *refs):
    for k in range(count):
        value_ref, level_ref = refs[2 * count + 2 * k : 2 * count + 2 * k + 2]
        values, level = merged([unpacked(refs[k][...]), unpacked(refs[count + k][...])])
        value_ref[...] = values.astype(BF16)
        kept = jnp.where(diagonal(values.shape[0], level_ref.shape[1]), level, 0.0)
        level_ref[...] = jnp.broadcast_to(jnp.sum(kept, axis=0, keepdims=True), level_ref.shape)


def chip_merge(keep, got):
    rows, rank = keep[0].shape[0], keep[0].shape[1] - LANES
    return pl.pallas_call(
        functools.partial(chip_kernel, len(keep)),
        out_shape=[shape((rows, rank)), shape((8, max(rows, LANES)), F32)] * len(keep),
        in_specs=[VMEM] * (2 * len(keep)),
        out_specs=[VMEM] * (2 * len(keep)),
        compiler_params=PARAMS,
        name="chip_merge",
    )(*keep, *got)


def final_kernel(count, *refs):
    part_refs, (value_ref, level_ref, w_ref, out_ref, values) = refs[: 2 * count], refs[2 * count :]
    heads, rank, reach = w_ref.shape
    local = out_ref.shape[0]
    parts = [(value_ref[...].astype(F32), column(level_ref[...]))]
    for k in range(count):
        row = part_refs[2 * k + 1][0:1]
        kept = jnp.where(diagonal(value_ref.shape[0], row.shape[1]), row, 0.0)
        parts.append((part_refs[2 * k][...].astype(F32), jnp.sum(kept, axis=1, keepdims=True)))
    latent = merged(parts)[0].astype(BF16)
    first = lax.broadcasted_iota(jnp.int32, (2 * local, reach), 0) < local
    for h in range(0, heads, 2):
        two = latent[h * local : (h + 2) * local]
        weights = jnp.concatenate([w_ref[h], w_ref[h + 1]], axis=1)
        both = jnp.dot(two, weights, preferred_element_type=F32)
        values[pl.ds(h * local, 2 * local), :] = jnp.where(first, both[:, :reach], both[:, reach:])
    for p in range(local):
        out_ref[p] = values[pl.ds(p, heads, stride=local), :].astype(BF16)


def on_device(q_nope, q_rope, w_uk, w_uv, prefix, private_caches, new_latent, ancestors, lengths):
    local, heads, nope = q_nope.shape
    span, width = private_caches.shape[1:]
    rank, reach = w_uv.shape[1:]
    rows = local * heads
    seq_size, dom_size = lax.axis_size("seq"), lax.axis_size("dom")
    cores = 2
    chips = seq_size // cores
    block = pl.pallas_call(
        functools.partial(pack_kernel, rank),
        out_shape=shape((local * span // 2, 2 * width)),
        in_specs=[VMEM],
        out_specs=VMEM,
        compiler_params=PARAMS,
        cost_estimate=pl.CostEstimate(flops=PACK, bytes_accessed=0, transcendentals=0),
        name="pack",
    )(private_caches)
    nope_rows, rope_rows = (jnp.swapaxes(q, 0, 1).reshape(rows, -1) for q in (q_nope, q_rope))
    line = dom_size == 4
    if line:
        swap = [(0, 1), (1, 0), (2, 3), (3, 2)]
        middle = lax.ppermute(block, "dom", [(0, 2), (3, 1)])
        far = lax.ppermute(block, "dom", [(1, 2), (2, 1)])
        theirs = lax.ppermute(ancestors, "dom", [(0, 1), (3, 2)])
    else:
        blocks = [block] + [
            lax.ppermute(block, "dom", [(i, (i + k) % dom_size) for i in range(dom_size)])
            for k in range(1, dom_size)
        ]

    own = pl.pallas_call(
        functools.partial(project_kernel, local),
        out_shape=shape((rows, width)),
        in_specs=[VMEM] * 3,
        out_specs=VMEM,
        compiler_params=PARAMS,
        cost_estimate=pl.CostEstimate(flops=PROJECT, bytes_accessed=0, transcendentals=0),
        name="project",
    )(nope_rows, rope_rows, w_uk)
    keys = prefix.T

    def pairs(turn, flip):
        return [
            (x * cores + c, (x + turn) % chips * cores + (c ^ flip))
            for x in range(chips)
            for c in range(cores)
        ]

    def back(turn, flip):
        return [(b, a) for a, b in pairs(turn, flip)]

    routes = [(t, f) for t in range(chips) for f in range(cores)]
    queries = [own if r == (0, 0) else lax.ppermute(own, "seq", pairs(*r)) for r in routes]
    stages = []
    for t in range(chips):
        asked = queries[2 * t : 2 * t + 2]
        stage = [*asked, *prefix_attention(asked, keys, rank, t == 0)]
        stages.append(stage)
        if t == 0:
            given = lax.ppermute(stage.pop(), "seq", pairs(0, 1))
        if line and t == 0:
            chosen = gathered(theirs, [block, middle, far], line, stage[3])
            late = lax.ppermute(chosen, "dom", swap)
            early = gathered(ancestors, [block, middle, far], line)
    if not line:
        early = late = gathered(ancestors, blocks, line)

    part = shape((rows, rank + LANES))
    others = chips - 1
    giving = [a for stage in stages[1:] for a in stage[1:]]
    keeping = [a for stage in stages[1:] for a in (stage[0], *stage[2:])]
    moved, *give = pl.pallas_call(
        functools.partial(give_kernel, others, line),
        out_shape=[shape((local * span, width))] + [part] * others,
        in_specs=[SMEM] * 2 + [VMEM] * (len(giving) + 2),
        out_specs=[VMEM] * (1 + others),
        compiler_params=PARAMS,
        name="suffix_give",
    )(ancestors, lengths, *giving, early, late)
    keep = pl.pallas_call(
        functools.partial(keep_kernel, others),
        out_shape=[part] * others,
        in_specs=[SMEM] * 2 + [VMEM] * (len(keeping) + 1),
        out_specs=[VMEM] * others,
        compiler_params=PARAMS,
        name="suffix_keep",
    )(ancestors, lengths, *keeping, moved)
    sums = chip_merge(keep, [lax.ppermute(g, "seq", pairs(0, 1)) for g in give])
    parts = [lax.ppermute(s, "seq", back(1 + i // 2, 0)) for i, s in enumerate(sums)]
    other = lax.ppermute(moved, "seq", pairs(0, 1))

    moved, _ = lax.optimization_barrier((moved, sums[0]))
    query, _, acc, level, mass = stages[0]
    new_caches, *own_part = pl.pallas_call(
        near_kernel,
        out_shape=[shape(private_caches.shape), shape((rows, rank)), shape((rows, LANES), F32)],
        in_specs=[SMEM] * 2 + [VMEM] * 8,
        out_specs=[VMEM] * 3,
        compiler_params=PARAMS,
        name="suffix_near",
    )(ancestors, lengths, new_latent, query, acc, level, mass, given, moved, other)
    parts += own_part

    head_values = pl.pallas_call(
        functools.partial(final_kernel, others),
        out_shape=shape((local, heads, reach)),
        in_specs=[VMEM] * (2 * chips + 1),
        out_specs=VMEM,
        scratch_shapes=[pltpu.VMEM((rows, reach), F32)],
        compiler_params=PARAMS,
        name="final",
    )(*parts, w_uv)
    return (head_values, new_caches)


def solution(mesh):
    placed = (
        P(("group", "dom"), "seq", None),
        P(("group", "dom"), "seq", None),
        P("seq", None, None),
        P("seq", None, None),
        P(("group", "seq"), None),
        P(("group", "dom"), "seq", None),
        P(("group", "dom"), None),
        P(("group", "dom")),
        P("group"),
    )
    return jax.shard_map(
        on_device,
        mesh=mesh,
        in_specs=placed,
        out_specs=(P(("group", "dom"), "seq", None), P(("group", "dom"), "seq", None)),
        check_vma=False,
    )
```

```python
import functools
import math

import jax
import jax.numpy as jnp
from jax import lax
from jax.experimental import pallas as pl
from jax.experimental.pallas import tpu as pltpu
from jax.sharding import PartitionSpec as P

ROPE = 64
NOPE = 128
SCALE2 = (NOPE + ROPE) ** (-0.5) * math.log2(math.e)
HIDDEN = -1e30
LANES = 128
F32 = jnp.float32
BF16 = jnp.bfloat16
NT = (((1,), (1,)), ((), ()))

VMEM = pl.BlockSpec(memory_space=pltpu.VMEM)
SMEM = pl.BlockSpec(memory_space=pltpu.SMEM)
ANY = pl.BlockSpec(memory_space=pl.ANY)
HBM = pl.BlockSpec(memory_space=pltpu.HBM)
PARAMS = pltpu.CompilerParams(vmem_limit_bytes=40 * 1024 * 1024)
NO_COST = pl.CostEstimate(flops=0, bytes_accessed=0, transcendentals=0)
FOLD = 4
PAD = 32
PACK = 8_000_000_000
PROJECT = 8_000_000_000


def shape(dims, dtype=BF16):
    return jax.ShapeDtypeStruct(dims, dtype)


def pack_kernel(rank, cache_ref, out_ref, *part_refs):
    local, span, _ = cache_ref.shape
    piece = span // FOLD
    for p in range(local):
        part = pl.ds(p * piece, piece)
        pieces = [cache_ref[p, q * piece : (q + 1) * piece] for q in range(FOLD)]
        row = jnp.concatenate([x[:, :rank] for x in pieces] + [x[:, rank:] for x in pieces], axis=1)
        out_ref[part] = row
        begin = 0
        for part_ref in part_refs:
            end = begin + part_ref.shape[1]
            part_ref[part] = row[:, begin:end]
            begin = end


def project_kernel(local, nope_ref, rope_ref, w_ref, own_ref, wide_ref):
    heads, _, rank = w_ref.shape
    nope = nope_ref[...].astype(F32)
    width = nope.shape[1]
    first = lax.broadcasted_iota(jnp.int32, (2 * local, width), 0) < local

    def pair(h):
        two = nope[h * local : (h + 2) * local]
        left = jnp.concatenate([jnp.where(first, two, 0.0), jnp.where(first, 0.0, two)], axis=1)
        weights = w_ref[pl.ds(h, 2)].reshape(2 * width, rank)
        return jnp.dot(left.astype(BF16), weights, preferred_element_type=F32)

    own_ref[:, rank:] = rope_ref[...]
    for h in range(0, heads, 4):
        own_ref[pl.ds(h * local, 4 * local), :rank] = jnp.concatenate(
            [pair(i) for i in (h, h + 2)], axis=0
        ).astype(BF16)
    rows = own_ref.shape[0]
    wide_ref[pl.ds(0, rows)] = own_ref[...]
    wide_ref[pl.ds(rows, PAD)] = jnp.zeros((PAD, own_ref.shape[1]), BF16)


def prefix_kernel(count, tiles, *refs):
    query_refs = refs[:count]
    keys_ref, out_ref, max_ref, sum_ref, *give_ref, acc_ref = refs[count:]
    rank = acc_ref.shape[1]
    tile = keys_ref.shape[1] // tiles
    parts = [pl.ds(i * tile, tile) for i in range(tiles)]
    rows = acc_ref.shape[0] // count
    queries = jnp.concatenate([ref[pl.ds(0, rows)] for ref in query_refs], axis=0)

    def score(i):
        return jnp.dot(queries, keys_ref[:, parts[i]], preferred_element_type=F32) * SCALE2

    ahead = score(0)
    for i in range(tiles):
        scores = ahead
        if i + 1 < tiles:
            ahead = score(i + 1)
        top = jnp.max(scores, axis=1, keepdims=True)
        if i > 0:
            top = jnp.maximum(top, largest)
        weights = jnp.exp2(scores - top)
        total = jnp.sum(weights, axis=1, keepdims=True)
        acc = lax.dot_general(
            weights.astype(BF16), keys_ref[:rank, parts[i]], NT, preferred_element_type=F32
        )
        if i > 0:
            factor = jnp.exp2(largest - top)
            total = total + running * factor
            acc = acc + acc_ref[...] * factor
        largest, running = top, total
        if i < tiles - 1:
            acc_ref[...] = acc
    kept = out_ref.shape[0]
    out_ref[...] = acc[:kept]
    max_ref[...] = jnp.broadcast_to(largest[:kept], max_ref.shape)
    sum_ref[...] = jnp.broadcast_to(running[:kept], sum_ref.shape)
    if give_ref:
        level = largest[kept:] + jnp.log2(running[kept:])
        give_ref[0][...] = packed(acc[kept:] * (1.0 / running[kept:]), level)


def prefix_attention(queries, keys, rank, give, each, tiles=4):
    kept = queries[0].shape[0] if give else len(queries) * each
    rows = len(queries) * each
    width, length = keys.shape
    out = [shape((kept, rank), F32)] + [shape((kept, LANES), F32)] * 2
    if give:
        out.append(shape((rows - kept, rank + LANES)))
    return pl.pallas_call(
        functools.partial(prefix_kernel, len(queries), tiles),
        out_shape=out,
        in_specs=[VMEM] * (len(queries) + 1),
        out_specs=[VMEM] * len(out),
        scratch_shapes=[pltpu.VMEM((rows, rank), F32)],
        compiler_params=PARAMS,
        cost_estimate=pl.CostEstimate(
            flops=0 if give else 2 * rows * length * (width + rank),
            bytes_accessed=0 if give else 2 * width * length,
            transcendentals=0 if give else rows * length,
        ),
        name="prefix_attention",
    )(*queries, keys)


def packed(values, level):
    rows = values.shape[0]
    lane = lax.broadcasted_iota(jnp.int32, (rows, LANES), 1)
    high = level.astype(BF16).astype(F32)
    middle = (level - high).astype(BF16).astype(F32)
    low = level - high - middle
    stats = jnp.where(lane == 0, high, jnp.where(lane == 1, middle, jnp.where(lane == 2, low, 0.0)))
    return jnp.concatenate([values.astype(BF16), stats.astype(BF16)], axis=1)


def unpacked(part):
    rank = part.shape[1] - LANES
    return part[:, :rank].astype(F32), jnp.sum(part[:, rank:].astype(F32), axis=1, keepdims=True)


def merged(parts):
    levels = [level for _, level in parts]
    top = functools.reduce(jnp.maximum, levels)
    shares = [jnp.exp2(level - top) for level in levels]
    whole = functools.reduce(jnp.add, shares)
    acc = functools.reduce(jnp.add, [share * values for share, (values, _) in zip(shares, parts)])
    return acc * (1.0 / whole), top + jnp.log2(whole)


def column(stat):
    return jnp.max(stat, axis=1, keepdims=True)


def diagonal(rows, lanes):
    row = lax.broadcasted_iota(jnp.int32, (rows, lanes), 0)
    return row == lax.broadcasted_iota(jnp.int32, (rows, lanes), 1)


def visible(rows, ends, starts, span):
    local = len(ends)
    cols = len(starts) * local * span
    col = lax.broadcasted_iota(jnp.int32, (1, cols), 1)
    col_of = jnp.zeros_like(col)
    limit = jnp.full_like(col, ends[0] - starts[0])
    for at in range(1, len(starts) * local):
        begin, p = at * span, at % local
        later = col >= begin
        col_of = jnp.where(later, p, col_of)
        limit = jnp.where(later, ends[p] - starts[at // local] + begin, limit)
    col_of = jnp.where(col < limit, col_of, -1)
    row_of = lax.rem(lax.broadcasted_iota(jnp.int32, (rows, 1), 0), local)
    return row_of == col_of


def attend(queries, keys, seen, rank, known):
    scores = lax.dot_general(queries, keys, NT, preferred_element_type=F32)
    scores = jnp.where(seen, scores * SCALE2, HIDDEN)
    top = jnp.max(scores, axis=1, keepdims=True)
    for level, _, _ in known:
        top = jnp.maximum(top, level)
    weights = jnp.where(seen, jnp.exp2(scores - top), 0.0)
    total = jnp.sum(weights, axis=1, keepdims=True)
    acc = jnp.dot(weights.astype(BF16), keys[:, :rank], preferred_element_type=F32)
    for level, mass, part in known:
        factor = jnp.exp2(level - top)
        total = total + mass * factor
        acc = acc + part * factor
    return acc * (1.0 / total), top + jnp.log2(total)


def at_end(dom):
    return (dom == 0) | (dom == 3)


def gather_kernel(line, chosen, names, *refs):
    block_refs, out_ref = refs[:-1], refs[-1]
    block_refs = block_refs[: len(chosen) or None]
    dom = lax.axis_index("dom")
    local = names.shape[0]
    piece = out_ref.shape[0] // local
    for p in range(local):
        owner, slot = lax.div(names[p], local), lax.rem(names[p], local)
        if line:
            apart = jnp.bitwise_xor(owner, dom)
            which = jnp.where(at_end(dom), 0, jnp.maximum(apart - 1, 0))
            if chosen:
                slot = jnp.where(at_end(dom), p, slot)
        else:
            which = lax.rem(dom - owner + len(block_refs), len(block_refs))
        rows = pl.ds(pl.multiple_of(slot * piece, piece), piece)
        for k, (block_ref, begin) in enumerate(zip(block_refs, chosen or [0] * len(block_refs))):

            @pl.when(which == k)
            def _():
                out_ref[pl.ds(p * piece, piece)] = block_ref[rows, pl.ds(begin, out_ref.shape[1])]


def gathered(names, blocks, line, begins=(), token=None):
    token = [] if token is None else [token]
    return pl.pallas_call(
        functools.partial(gather_kernel, line, begins),
        out_shape=shape(blocks[0].shape),
        in_specs=[SMEM] + [VMEM] * len(blocks) + [ANY] * len(token),
        out_specs=VMEM,
        compiler_params=PARAMS,
        cost_estimate=NO_COST,
        name="gather",
    )(names, *blocks, *token)


def far_part(anc, lens, query_ref, stage_refs, part, keys):
    acc_ref, max_ref, sum_ref = stage_refs
    local = anc.shape[0]
    span, rank = keys.shape[0] // local, acc_ref.shape[1]
    ends = [lens[anc[p]] for p in range(local)]
    rows = acc_ref.shape[0] // 2
    seen = visible(rows, ends, [lax.axis_index("seq") * span], span)
    known = [(column(max_ref[part]), column(sum_ref[part]), acc_ref[part])]
    return packed(*attend(query_ref[pl.ds(0, rows)], keys, seen, rank, known))


def give_kernel(stages, line, anc, lens, *refs):
    stage_refs, refs = refs[: 4 * stages], refs[4 * stages :]
    give_refs = refs[len(refs) - stages :]
    source_refs, moved_ref = refs[: len(refs) - stages - 1], refs[len(refs) - stages - 1]
    dom = lax.axis_index("dom")
    local = anc.shape[0]
    piece = source_refs[0].shape[0] // local
    span, width = FOLD * piece, moved_ref.shape[1]
    rank = stage_refs[1].shape[1]

    def place(p, value):
        for q in range(FOLD):
            rows, rope = pl.ds(p * span + q * piece, piece), FOLD * rank + q * (width - rank)
            moved_ref[rows, :rank] = value[:, q * rank : (q + 1) * rank]
            moved_ref[rows, rank:] = value[:, rope : rope + width - rank]

    for p in range(local):
        own_rows = pl.ds(p * piece, piece)
        if line:
            near_ref, middle_refs, late_refs = source_refs[0], source_refs[1:3], source_refs[3:5]
            owner, slot = lax.div(anc[p], local), lax.rem(anc[p], local)
            apart = jnp.bitwise_xor(owner, dom)
            late = jnp.where(at_end(dom), apart != 0, apart == 1)
            middle = jnp.logical_not(at_end(dom)) & (apart == 2)
            slot = jnp.where(at_end(dom), p, slot)
            rows = pl.ds(pl.multiple_of(slot * piece, piece), piece)

            @pl.when(late)
            def _():
                place(p, jnp.concatenate([ref[rows] for ref in late_refs], axis=1))

            @pl.when(middle)
            def _():
                place(p, jnp.concatenate([ref[rows] for ref in middle_refs], axis=1))

            @pl.when(jnp.logical_not(late | middle))
            def _():
                place(p, near_ref[own_rows])

        else:
            place(p, source_refs[0][own_rows])

    for k in range(stages):
        query_ref, *partial = stage_refs[4 * k : 4 * k + 4]
        rows = partial[0].shape[0] // 2
        give_refs[k][...] = far_part(anc, lens, query_ref, partial, pl.ds(rows, rows), moved_ref[...])


def keep_kernel(stages, anc, lens, *refs):
    stage_refs, refs = refs[: 4 * stages], refs[4 * stages :]
    moved_ref, keep_refs = refs[0], refs[1:]
    for k in range(stages):
        query_ref, *partial = stage_refs[4 * k : 4 * k + 4]
        rows = partial[0].shape[0] // 2
        keep_refs[k][...] = far_part(anc, lens, query_ref, partial, pl.ds(0, rows), moved_ref[...])


def near_kernel(anc, lens, fresh_ref, *refs):
    seq = lax.axis_index("seq")
    query_ref, acc_ref, max_ref, sum_ref, got_ref, moved_ref, other_ref, cache_ref, value_ref, level_ref = refs
    local, span, width = cache_ref.shape
    rank = acc_ref.shape[1]
    start, other = seq * span, jnp.bitwise_xor(seq, 1) * span
    ends = [lens[anc[p]] for p in range(local)]
    keys = jnp.concatenate([moved_ref[...], other_ref[...]], axis=0)
    seen = visible(query_ref.shape[0], ends, [start, other], span)
    level = jnp.sum(got_ref[:, rank:].astype(F32), axis=1, keepdims=True)
    known = [
        (column(max_ref[...]), column(sum_ref[...]), acc_ref[...]),
        (level, 1.0, got_ref[:, :rank].astype(F32)),
    ]
    values, level = attend(query_ref[...], keys, seen, rank, known)
    value_ref[...] = values.astype(BF16)
    level_ref[...] = jnp.broadcast_to(level, level_ref.shape)
    for p in range(local):
        at = start + lax.broadcasted_iota(jnp.int32, (span, 1), 0) == ends[p]
        cache_ref[p] = jnp.where(at, fresh_ref[pl.ds(p, 1), :], moved_ref[pl.ds(p * span, span)])


def chip_kernel(count, *refs):
    for k in range(count):
        value_ref, level_ref = refs[2 * count + 2 * k : 2 * count + 2 * k + 2]
        values, level = merged([unpacked(refs[k][...]), unpacked(refs[count + k][...])])
        value_ref[...] = values.astype(BF16)
        kept = jnp.where(diagonal(values.shape[0], level_ref.shape[1]), level, 0.0)
        level_ref[...] = jnp.broadcast_to(jnp.sum(kept, axis=0, keepdims=True), level_ref.shape)


def chip_merge(keep, got):
    rows, rank = keep[0].shape[0], keep[0].shape[1] - LANES
    return pl.pallas_call(
        functools.partial(chip_kernel, len(keep)),
        out_shape=[shape((rows, rank)), shape((8, max(rows, LANES)), F32)] * len(keep),
        in_specs=[VMEM] * (2 * len(keep)),
        out_specs=[VMEM] * (2 * len(keep)),
        compiler_params=PARAMS,
        name="chip_merge",
    )(*keep, *got)


def final_kernel(count, *refs):
    part_refs, (value_ref, level_ref, w_ref, out_ref, values) = refs[: 2 * count], refs[2 * count :]
    heads, rank, reach = w_ref.shape
    local = out_ref.shape[0]
    parts = [(value_ref[...].astype(F32), column(level_ref[...]))]
    for k in range(count):
        row = part_refs[2 * k + 1][0:1]
        kept = jnp.where(diagonal(value_ref.shape[0], row.shape[1]), row, 0.0)
        parts.append((part_refs[2 * k][...].astype(F32), jnp.sum(kept, axis=1, keepdims=True)))
    latent = merged(parts)[0].astype(BF16)
    first = lax.broadcasted_iota(jnp.int32, (2 * local, reach), 0) < local
    for h in range(0, heads, 2):
        two = latent[h * local : (h + 2) * local]
        weights = jnp.concatenate([w_ref[h], w_ref[h + 1]], axis=1)
        both = jnp.dot(two, weights, preferred_element_type=F32)
        values[pl.ds(h * local, 2 * local), :] = jnp.where(first, both[:, :reach], both[:, reach:])
    for p in range(local):
        out_ref[p] = values[pl.ds(p, heads, stride=local), :].astype(BF16)


def on_device(q_nope, q_rope, w_uk, w_uv, prefix, private_caches, new_latent, ancestors, lengths):
    local, heads, nope = q_nope.shape
    span, width = private_caches.shape[1:]
    rank, reach = w_uv.shape[1:]
    rows = local * heads
    seq_size, dom_size = lax.axis_size("seq"), lax.axis_size("dom")
    cores = 2
    chips = seq_size // cores
    pack_rows, lanes = local * span // FOLD, FOLD * width
    cut = (lanes // LANES // 2 + 1) * LANES
    block, *halves = pl.pallas_call(
        functools.partial(pack_kernel, rank),
        out_shape=[shape((pack_rows, wide)) for wide in (lanes, cut, lanes - cut)],
        in_specs=[VMEM],
        out_specs=[VMEM] * 3,
        compiler_params=PARAMS,
        cost_estimate=pl.CostEstimate(flops=PACK, bytes_accessed=0, transcendentals=0),
        name="pack",
    )(private_caches)
    block, q_nope, q_rope = lax.optimization_barrier((block, q_nope, q_rope))
    if dom_size == 4:
        theirs = lax.ppermute(ancestors, "dom", [(0, 1), (1, 0), (2, 3), (3, 2)])
        theirs, q_nope = lax.optimization_barrier((theirs, q_nope))
    nope_rows, rope_rows = (jnp.swapaxes(q, 0, 1).reshape(rows, -1) for q in (q_nope, q_rope))
    line = dom_size == 4
    if line:
        swap = [(0, 1), (1, 0), (2, 3), (3, 2)]
        middle = [lax.ppermute(halves[0], "dom", [(0, 2), (3, 1)])]
        far = lax.ppermute(block, "dom", [(1, 2), (2, 1)])
    else:
        blocks = [block] + [
            lax.ppermute(block, "dom", [(i, (i + k) % dom_size) for i in range(dom_size)])
            for k in range(1, dom_size)
        ]

    own, wide = pl.pallas_call(
        functools.partial(project_kernel, local),
        out_shape=(shape((rows, width)), shape((rows + PAD, width))),
        in_specs=[VMEM] * 3,
        out_specs=[VMEM] * 2,
        compiler_params=PARAMS,
        cost_estimate=pl.CostEstimate(flops=PROJECT, bytes_accessed=0, transcendentals=0),
        name="project",
    )(nope_rows, rope_rows, w_uk)
    keys = prefix.T

    def pairs(turn, flip):
        return [
            (x * cores + c, (x + turn) % chips * cores + (c ^ flip))
            for x in range(chips)
            for c in range(cores)
        ]

    def back(turn, flip):
        return [(b, a) for a, b in pairs(turn, flip)]

    routes = [(t, f) for t in range(chips) for f in range(cores)]
    queries = [own, lax.ppermute(own, "seq", pairs(0, 1))]
    queries += [lax.ppermute(wide, "seq", pairs(*r)) for r in routes[2:]]
    stages = []
    for t in range(chips):
        asked = queries[2 * t : 2 * t + 2]
        stage = [*asked, *prefix_attention(asked, keys, rank, t == 0, rows)]
        stages.append(stage)
        if t == 0:
            given = lax.ppermute(stage.pop(), "seq", pairs(0, 1))
        if line and t == 0:
            rest, stage[3] = lax.optimization_barrier((halves[1], stage[3]))
            middle.append(lax.ppermute(rest, "dom", [(0, 2), (3, 1)]))
            token, sent = stage[3], []
            for h, begin in enumerate((0, cut)):
                sources = [halves[h], middle[h], far]
                token = gathered(theirs, sources, line, (0, 0, begin), token)
                sent.append(lax.ppermute(token, "dom", swap))
    if line:
        early = gathered(ancestors, [block, block, far], line)
        sources = [early, *middle, *sent]
    else:
        sources = [gathered(ancestors, blocks, line)]

    part = shape((rows, rank + LANES))
    others = chips - 1
    giving = [a for stage in stages[1:] for a in stage[1:]]
    keeping = [a for stage in stages[1:] for a in (stage[0], *stage[2:])]
    moved, *give = pl.pallas_call(
        functools.partial(give_kernel, others, line),
        out_shape=[shape((local * span, width))] + [part] * others,
        in_specs=[SMEM] * 2 + [VMEM] * (len(giving) + len(sources)),
        out_specs=[VMEM] * (1 + others),
        compiler_params=PARAMS,
        name="suffix_give",
    )(ancestors, lengths, *giving, *sources)
    keep = pl.pallas_call(
        functools.partial(keep_kernel, others),
        out_shape=[part] * others,
        in_specs=[SMEM] * 2 + [VMEM] * (len(keeping) + 1),
        out_specs=[VMEM] * others,
        compiler_params=PARAMS,
        name="suffix_keep",
    )(ancestors, lengths, *keeping, moved)
    sums = chip_merge(keep, [lax.ppermute(g, "seq", pairs(0, 1)) for g in give])
    parts = [lax.ppermute(s, "seq", back(1 + i // 2, 0)) for i, s in enumerate(sums)]
    other = lax.ppermute(moved, "seq", pairs(0, 1))

    moved, _ = lax.optimization_barrier((moved, sums[0]))
    query, _, acc, level, mass = stages[0]
    new_caches, *own_part = pl.pallas_call(
        near_kernel,
        out_shape=[shape(private_caches.shape), shape((rows, rank)), shape((rows, LANES), F32)],
        in_specs=[SMEM] * 2 + [VMEM] * 8,
        out_specs=[VMEM] * 3,
        compiler_params=PARAMS,
        name="suffix_near",
    )(ancestors, lengths, new_latent, query, acc, level, mass, given, moved, other)
    parts += own_part

    head_values = pl.pallas_call(
        functools.partial(final_kernel, others),
        out_shape=shape((local, heads, reach)),
        in_specs=[VMEM] * (2 * chips + 1),
        out_specs=VMEM,
        scratch_shapes=[pltpu.VMEM((rows, reach), F32)],
        compiler_params=PARAMS,
        name="final",
    )(*parts, w_uv)
    return (head_values, new_caches)


def solution(mesh):
    placed = (
        P(("group", "dom"), "seq", None),
        P(("group", "dom"), "seq", None),
        P("seq", None, None),
        P("seq", None, None),
        P(("group", "seq"), None),
        P(("group", "dom"), "seq", None),
        P(("group", "dom"), None),
        P(("group", "dom")),
        P("group"),
    )
    return jax.shard_map(
        on_device,
        mesh=mesh,
        in_specs=placed,
        out_specs=(P(("group", "dom"), "seq", None), P(("group", "dom"), "seq", None)),
        check_vma=False,
    )
```

```python
import functools
import math

import jax
import jax.numpy as jnp
from jax import lax
from jax.experimental import pallas as pl
from jax.experimental.pallas import tpu as pltpu
from jax.sharding import PartitionSpec as P

ROPE = 64
NOPE = 128
SCALE2 = (NOPE + ROPE) ** (-0.5) * math.log2(math.e)
HIDDEN = -1e30
LANES = 128
F32 = jnp.float32
BF16 = jnp.bfloat16
NT = (((1,), (1,)), ((), ()))

VMEM = pl.BlockSpec(memory_space=pltpu.VMEM)
SMEM = pl.BlockSpec(memory_space=pltpu.SMEM)
ANY = pl.BlockSpec(memory_space=pl.ANY)
HBM = pl.BlockSpec(memory_space=pltpu.HBM)
PARAMS = pltpu.CompilerParams(vmem_limit_bytes=40 * 1024 * 1024)
NO_COST = pl.CostEstimate(flops=0, bytes_accessed=0, transcendentals=0)
PACK = 8_000_000_000
PROJECT = 8_000_000_000


def shape(dims, dtype=BF16):
    return jax.ShapeDtypeStruct(dims, dtype)


def pack_kernel(rank, cache_ref, out_ref):
    local, span, _ = cache_ref.shape
    some = span // 2
    for p in range(local):
        part = pl.ds(p * some, some)
        first, second = cache_ref[p, :some], cache_ref[p, some:]
        out_ref[part, :rank] = first[:, :rank]
        out_ref[part, rank : 2 * rank] = second[:, :rank]
        out_ref[part, 2 * rank :] = jnp.concatenate([first[:, rank:], second[:, rank:]], axis=1)


def project_kernel(local, nope_ref, rope_ref, w_ref, own_ref):
    heads, _, rank = w_ref.shape
    nope = nope_ref[...].astype(F32)
    width = nope.shape[1]
    first = lax.broadcasted_iota(jnp.int32, (2 * local, width), 0) < local

    def pair(h):
        two = nope[h * local : (h + 2) * local]
        left = jnp.concatenate([jnp.where(first, two, 0.0), jnp.where(first, 0.0, two)], axis=1)
        weights = w_ref[pl.ds(h, 2)].reshape(2 * width, rank)
        return jnp.dot(left.astype(BF16), weights, preferred_element_type=F32)

    own_ref[:, rank:] = rope_ref[...]
    for h in range(0, heads, 4):
        own_ref[pl.ds(h * local, 4 * local), :rank] = jnp.concatenate(
            [pair(i) for i in (h, h + 2)], axis=0
        ).astype(BF16)


def prefix_kernel(count, tiles, *refs):
    query_refs = refs[:count]
    keys_ref, out_ref, max_ref, sum_ref, *give_ref, acc_ref = refs[count:]
    rank = acc_ref.shape[1]
    tile = keys_ref.shape[1] // tiles
    parts = [pl.ds(i * tile, tile) for i in range(tiles)]
    queries = jnp.concatenate([ref[...] for ref in query_refs], axis=0)

    def score(i):
        return jnp.dot(queries, keys_ref[:, parts[i]], preferred_element_type=F32) * SCALE2

    ahead = score(0)
    for i in range(tiles):
        scores = ahead
        if i + 1 < tiles:
            ahead = score(i + 1)
        top = jnp.max(scores, axis=1, keepdims=True)
        if i > 0:
            top = jnp.maximum(top, largest)
        weights = jnp.exp2(scores - top)
        total = jnp.sum(weights, axis=1, keepdims=True)
        acc = lax.dot_general(
            weights.astype(BF16), keys_ref[:rank, parts[i]], NT, preferred_element_type=F32
        )
        if i > 0:
            factor = jnp.exp2(largest - top)
            total = total + running * factor
            acc = acc + acc_ref[...] * factor
        largest, running = top, total
        if i < tiles - 1:
            acc_ref[...] = acc
    kept = out_ref.shape[0]
    out_ref[...] = acc[:kept]
    max_ref[...] = jnp.broadcast_to(largest[:kept], max_ref.shape)
    sum_ref[...] = jnp.broadcast_to(running[:kept], sum_ref.shape)
    if give_ref:
        level = largest[kept:] + jnp.log2(running[kept:])
        give_ref[0][...] = packed(acc[kept:] * (1.0 / running[kept:]), level)


def prefix_attention(queries, keys, rank, give, tiles=4):
    rows = sum(q.shape[0] for q in queries)
    kept = queries[0].shape[0] if give else rows
    width, length = keys.shape
    out = [shape((kept, rank), F32)] + [shape((kept, LANES), F32)] * 2
    if give:
        out.append(shape((rows - kept, rank + LANES)))
    return pl.pallas_call(
        functools.partial(prefix_kernel, len(queries), tiles),
        out_shape=out,
        in_specs=[VMEM] * (len(queries) + 1),
        out_specs=[VMEM] * len(out),
        scratch_shapes=[pltpu.VMEM((rows, rank), F32)],
        compiler_params=PARAMS,
        cost_estimate=pl.CostEstimate(
            flops=0 if give else 2 * rows * length * (width + rank),
            bytes_accessed=0 if give else 2 * width * length,
            transcendentals=0 if give else rows * length,
        ),
        name="prefix_attention",
    )(*queries, keys)


def packed(values, level):
    rows = values.shape[0]
    lane = lax.broadcasted_iota(jnp.int32, (rows, LANES), 1)
    high = level.astype(BF16).astype(F32)
    middle = (level - high).astype(BF16).astype(F32)
    low = level - high - middle
    stats = jnp.where(lane == 0, high, jnp.where(lane == 1, middle, jnp.where(lane == 2, low, 0.0)))
    return jnp.concatenate([values.astype(BF16), stats.astype(BF16)], axis=1)


def unpacked(part):
    rank = part.shape[1] - LANES
    return part[:, :rank].astype(F32), jnp.sum(part[:, rank:].astype(F32), axis=1, keepdims=True)


def merged(parts):
    levels = [level for _, level in parts]
    top = functools.reduce(jnp.maximum, levels)
    shares = [jnp.exp2(level - top) for level in levels]
    whole = functools.reduce(jnp.add, shares)
    acc = functools.reduce(jnp.add, [share * values for share, (values, _) in zip(shares, parts)])
    return acc * (1.0 / whole), top + jnp.log2(whole)


def column(stat):
    return jnp.max(stat, axis=1, keepdims=True)


def diagonal(rows, lanes):
    row = lax.broadcasted_iota(jnp.int32, (rows, lanes), 0)
    return row == lax.broadcasted_iota(jnp.int32, (rows, lanes), 1)


def visible(rows, ends, starts, span):
    local = len(ends)
    cols = len(starts) * local * span
    col = lax.broadcasted_iota(jnp.int32, (1, cols), 1)
    col_of = jnp.zeros_like(col)
    limit = jnp.full_like(col, ends[0] - starts[0])
    for at in range(1, len(starts) * local):
        begin, p = at * span, at % local
        later = col >= begin
        col_of = jnp.where(later, p, col_of)
        limit = jnp.where(later, ends[p] - starts[at // local] + begin, limit)
    col_of = jnp.where(col < limit, col_of, -1)
    row_of = lax.rem(lax.broadcasted_iota(jnp.int32, (rows, 1), 0), local)
    return row_of == col_of


def attend(queries, keys, seen, rank, known):
    scores = lax.dot_general(queries, keys, NT, preferred_element_type=F32)
    scores = jnp.where(seen, scores * SCALE2, HIDDEN)
    top = jnp.max(scores, axis=1, keepdims=True)
    for level, _, _ in known:
        top = jnp.maximum(top, level)
    weights = jnp.where(seen, jnp.exp2(scores - top), 0.0)
    total = jnp.sum(weights, axis=1, keepdims=True)
    acc = jnp.dot(weights.astype(BF16), keys[:, :rank], preferred_element_type=F32)
    for level, mass, part in known:
        factor = jnp.exp2(level - top)
        total = total + mass * factor
        acc = acc + part * factor
    return acc * (1.0 / total), top + jnp.log2(total)


def at_end(dom):
    return (dom == 0) | (dom == 3)


def gather_kernel(line, chosen, names, *refs):
    block_refs, out_ref = refs[:-1], refs[-1]
    if chosen:
        block_refs = block_refs[:-1]
    dom = lax.axis_index("dom")
    local = names.shape[0]
    some = out_ref.shape[0] // local
    for p in range(local):
        owner, slot = lax.div(names[p], local), lax.rem(names[p], local)
        if line:
            apart = jnp.bitwise_xor(owner, dom)
            which = jnp.where(at_end(dom), 0, jnp.maximum(apart - 1, 0))
            if chosen:
                slot = jnp.where(at_end(dom), p, slot)
        else:
            which = lax.rem(dom - owner + len(block_refs), len(block_refs))
        rows = pl.ds(pl.multiple_of(slot * some, some), some)
        for k, block_ref in enumerate(block_refs):

            @pl.when(which == k)
            def _():
                out_ref[pl.ds(p * some, some)] = block_ref[rows]


def gathered(names, blocks, line, token=None):
    token = [] if token is None else [token]
    return pl.pallas_call(
        functools.partial(gather_kernel, line, bool(token)),
        out_shape=shape(blocks[0].shape),
        in_specs=[SMEM] + [VMEM] * len(blocks) + [ANY] * len(token),
        out_specs=VMEM,
        compiler_params=PARAMS,
        cost_estimate=NO_COST,
        name="gather",
    )(names, *blocks, *token)


def far_part(anc, lens, query_ref, stage_refs, part, keys):
    acc_ref, max_ref, sum_ref = stage_refs
    local = anc.shape[0]
    span, rank = keys.shape[0] // local, acc_ref.shape[1]
    ends = [lens[anc[p]] for p in range(local)]
    seen = visible(query_ref.shape[0], ends, [lax.axis_index("seq") * span], span)
    known = [(column(max_ref[part]), column(sum_ref[part]), acc_ref[part])]
    return packed(*attend(query_ref[...], keys, seen, rank, known))


def give_kernel(stages, line, anc, lens, *refs):
    stage_refs, refs = refs[: 4 * stages], refs[4 * stages :]
    early_ref, late_ref, moved_ref, give_refs = refs[0], refs[1], refs[2], refs[3:]
    dom = lax.axis_index("dom")
    local = anc.shape[0]
    some = early_ref.shape[0] // local
    span, width = 2 * some, moved_ref.shape[1]
    rank = stage_refs[1].shape[1]

    def place(p, value):
        for h in range(2):
            rows, rope = pl.ds(p * span + h * some, some), 2 * rank + h * (width - rank)
            moved_ref[rows, :rank] = value[:, h * rank : (h + 1) * rank]
            moved_ref[rows, rank:] = value[:, rope : rope + width - rank]

    for p in range(local):
        if line:
            owner, slot = lax.div(anc[p], local), lax.rem(anc[p], local)
            apart = jnp.bitwise_xor(owner, dom)
            late = jnp.where(at_end(dom), apart != 0, apart == 1)
            slot = jnp.where(at_end(dom), p, slot)
            rows = pl.ds(pl.multiple_of(slot * some, some), some)

            @pl.when(late)
            def _():
                place(p, late_ref[rows])

            @pl.when(jnp.logical_not(late))
            def _():
                place(p, early_ref[pl.ds(p * some, some)])

        else:
            place(p, early_ref[pl.ds(p * some, some)])

    for k in range(stages):
        query_ref, *partial = stage_refs[4 * k : 4 * k + 4]
        rows = query_ref.shape[0]
        give_refs[k][...] = far_part(anc, lens, query_ref, partial, pl.ds(rows, rows), moved_ref[...])


def keep_kernel(stages, anc, lens, *refs):
    stage_refs, refs = refs[: 4 * stages], refs[4 * stages :]
    moved_ref, keep_refs, piece_refs = refs[0], refs[1 : 1 + stages], refs[1 + stages :]
    begin = 0
    for piece_ref in piece_refs:
        piece_ref[...] = moved_ref[pl.ds(begin, piece_ref.shape[0])]
        begin += piece_ref.shape[0]
    for k in range(stages):
        query_ref, *partial = stage_refs[4 * k : 4 * k + 4]
        rows = query_ref.shape[0]
        keep_refs[k][...] = far_part(anc, lens, query_ref, partial, pl.ds(0, rows), moved_ref[...])


def near_kernel(anc, lens, fresh_ref, *refs):
    seq = lax.axis_index("seq")
    query_ref, acc_ref, max_ref, sum_ref, got_ref, moved_ref, *other_refs = refs[:-3]
    cache_ref, value_ref, level_ref = refs[-3:]
    local, span, width = cache_ref.shape
    rank = acc_ref.shape[1]
    start, other = seq * span, jnp.bitwise_xor(seq, 1) * span
    ends = [lens[anc[p]] for p in range(local)]
    keys = jnp.concatenate([ref[...] for ref in (moved_ref, *other_refs)], axis=0)
    seen = visible(query_ref.shape[0], ends, [start, other], span)
    level = jnp.sum(got_ref[:, rank:].astype(F32), axis=1, keepdims=True)
    known = [
        (column(max_ref[...]), column(sum_ref[...]), acc_ref[...]),
        (level, 1.0, got_ref[:, :rank].astype(F32)),
    ]
    values, level = attend(query_ref[...], keys, seen, rank, known)
    value_ref[...] = values.astype(BF16)
    level_ref[...] = jnp.broadcast_to(level, level_ref.shape)
    for p in range(local):
        at = start + lax.broadcasted_iota(jnp.int32, (span, 1), 0) == ends[p]
        cache_ref[p] = jnp.where(at, fresh_ref[pl.ds(p, 1), :], moved_ref[pl.ds(p * span, span)])


def chip_kernel(count, *refs):
    for k in range(count):
        value_ref, level_ref = refs[2 * count + 2 * k : 2 * count + 2 * k + 2]
        values, level = merged([unpacked(refs[k][...]), unpacked(refs[count + k][...])])
        value_ref[...] = values.astype(BF16)
        kept = jnp.where(diagonal(values.shape[0], level_ref.shape[1]), level, 0.0)
        level_ref[...] = jnp.broadcast_to(jnp.sum(kept, axis=0, keepdims=True), level_ref.shape)


def chip_merge(keep, got):
    rows, rank = keep[0].shape[0], keep[0].shape[1] - LANES
    return pl.pallas_call(
        functools.partial(chip_kernel, len(keep)),
        out_shape=[shape((rows, rank)), shape((8, max(rows, LANES)), F32)] * len(keep),
        in_specs=[VMEM] * (2 * len(keep)),
        out_specs=[VMEM] * (2 * len(keep)),
        compiler_params=PARAMS,
        name="chip_merge",
    )(*keep, *got)


def final_kernel(count, *refs):
    part_refs, (value_ref, level_ref, w_ref, out_ref, values) = refs[: 2 * count], refs[2 * count :]
    heads, rank, reach = w_ref.shape
    local = out_ref.shape[0]
    parts = [(value_ref[...].astype(F32), column(level_ref[...]))]
    for k in range(count):
        row = part_refs[2 * k + 1][0:1]
        kept = jnp.where(diagonal(value_ref.shape[0], row.shape[1]), row, 0.0)
        parts.append((part_refs[2 * k][...].astype(F32), jnp.sum(kept, axis=1, keepdims=True)))
    latent = merged(parts)[0].astype(BF16)
    first = lax.broadcasted_iota(jnp.int32, (2 * local, reach), 0) < local
    for h in range(0, heads, 2):
        two = latent[h * local : (h + 2) * local]
        weights = jnp.concatenate([w_ref[h], w_ref[h + 1]], axis=1)
        both = jnp.dot(two, weights, preferred_element_type=F32)
        values[pl.ds(h * local, 2 * local), :] = jnp.where(first, both[:, :reach], both[:, reach:])
    for p in range(local):
        out_ref[p] = values[pl.ds(p, heads, stride=local), :].astype(BF16)


def on_device(q_nope, q_rope, w_uk, w_uv, prefix, private_caches, new_latent, ancestors, lengths):
    local, heads, nope = q_nope.shape
    span, width = private_caches.shape[1:]
    rank, reach = w_uv.shape[1:]
    rows = local * heads
    seq_size, dom_size = lax.axis_size("seq"), lax.axis_size("dom")
    cores = 2
    chips = seq_size // cores
    block = pl.pallas_call(
        functools.partial(pack_kernel, rank),
        out_shape=shape((local * span // 2, 2 * width)),
        in_specs=[VMEM],
        out_specs=VMEM,
        compiler_params=PARAMS,
        cost_estimate=pl.CostEstimate(flops=PACK, bytes_accessed=0, transcendentals=0),
        name="pack",
    )(private_caches)
    nope_rows, rope_rows = (jnp.swapaxes(q, 0, 1).reshape(rows, -1) for q in (q_nope, q_rope))
    line = dom_size == 4
    if line:
        swap = [(0, 1), (1, 0), (2, 3), (3, 2)]
        middle = lax.ppermute(block, "dom", [(0, 2), (3, 1)])
        far = lax.ppermute(block, "dom", [(1, 2), (2, 1)])
        theirs = lax.ppermute(ancestors, "dom", [(0, 1), (3, 2)])
    else:
        blocks = [block] + [
            lax.ppermute(block, "dom", [(i, (i + k) % dom_size) for i in range(dom_size)])
            for k in range(1, dom_size)
        ]

    own = pl.pallas_call(
        functools.partial(project_kernel, local),
        out_shape=shape((rows, width)),
        in_specs=[VMEM] * 3,
        out_specs=VMEM,
        compiler_params=PARAMS,
        cost_estimate=pl.CostEstimate(flops=PROJECT, bytes_accessed=0, transcendentals=0),
        name="project",
    )(nope_rows, rope_rows, w_uk)
    keys = prefix.T

    def pairs(turn, flip):
        return [
            (x * cores + c, (x + turn) % chips * cores + (c ^ flip))
            for x in range(chips)
            for c in range(cores)
        ]

    def back(turn, flip):
        return [(b, a) for a, b in pairs(turn, flip)]

    routes = [(t, f) for t in range(chips) for f in range(cores)]
    queries = [own if r == (0, 0) else lax.ppermute(own, "seq", pairs(*r)) for r in routes]
    stages = []
    for t in range(chips):
        asked = queries[2 * t : 2 * t + 2]
        stage = [*asked, *prefix_attention(asked, keys, rank, t == 0)]
        stages.append(stage)
        if t == 0:
            given = lax.ppermute(stage.pop(), "seq", pairs(0, 1))
        if line and t == 0:
            chosen = gathered(theirs, [block, middle, far], line, stage[3])
            late = lax.ppermute(chosen, "dom", swap)
            early = gathered(ancestors, [block, middle, far], line)
    if not line:
        early = late = gathered(ancestors, blocks, line)

    part = shape((rows, rank + LANES))
    others = chips - 1
    given, early = lax.optimization_barrier((given, early))
    giving = [a for stage in stages[1:] for a in stage[1:]]
    keeping = [a for stage in stages[1:] for a in (stage[0], *stage[2:])]
    moved, *give = pl.pallas_call(
        functools.partial(give_kernel, others, line),
        out_shape=[shape((local * span, width))] + [part] * others,
        in_specs=[SMEM] * 2 + [VMEM] * (len(giving) + 2),
        out_specs=[VMEM] * (1 + others),
        compiler_params=PARAMS,
        name="suffix_give",
    )(ancestors, lengths, *giving, early, late)
    small = local * span // 48 * 16
    cuts = (local * span - 2 * small, small, small)
    keep_and_pieces = pl.pallas_call(
        functools.partial(keep_kernel, others),
        out_shape=[part] * others + [shape((cut, width)) for cut in cuts],
        in_specs=[SMEM] * 2 + [VMEM] * (len(keeping) + 1),
        out_specs=[VMEM] * (others + len(cuts)),
        compiler_params=PARAMS,
        name="suffix_keep",
    )(ancestors, lengths, *keeping, moved)
    keep, pieces = keep_and_pieces[:others], keep_and_pieces[others:]
    sums = chip_merge(keep, [lax.ppermute(g, "seq", pairs(0, 1)) for g in give])
    parts = [lax.ppermute(s, "seq", back(1 + i // 2, 0)) for i, s in enumerate(sums)]
    other = [lax.ppermute(piece, "seq", pairs(0, 1)) for piece in pieces]

    moved, _ = lax.optimization_barrier((moved, sums[0]))
    query, _, acc, level, mass = stages[0]
    new_caches, *own_part = pl.pallas_call(
        near_kernel,
        out_shape=[shape(private_caches.shape), shape((rows, rank)), shape((rows, LANES), F32)],
        in_specs=[SMEM] * 2 + [VMEM] * (7 + len(other)),
        out_specs=[VMEM] * 3,
        compiler_params=PARAMS,
        cost_estimate=NO_COST,
        name="suffix_near",
    )(ancestors, lengths, new_latent, query, acc, level, mass, given, moved, *other)
    parts += own_part

    head_values = pl.pallas_call(
        functools.partial(final_kernel, others),
        out_shape=shape((local, heads, reach)),
        in_specs=[VMEM] * (2 * chips + 1),
        out_specs=VMEM,
        scratch_shapes=[pltpu.VMEM((rows, reach), F32)],
        compiler_params=PARAMS,
        name="final",
    )(*parts, w_uv)
    return (head_values, new_caches)


def solution(mesh):
    placed = (
        P(("group", "dom"), "seq", None),
        P(("group", "dom"), "seq", None),
        P("seq", None, None),
        P("seq", None, None),
        P(("group", "seq"), None),
        P(("group", "dom"), "seq", None),
        P(("group", "dom"), None),
        P(("group", "dom")),
        P("group"),
    )
    return jax.shard_map(
        on_device,
        mesh=mesh,
        in_specs=placed,
        out_specs=(P(("group", "dom"), "seq", None), P(("group", "dom"), "seq", None)),
        check_vma=False,
    )
```

```python
import functools
import math

import jax
import jax.numpy as jnp
from jax import lax
from jax.experimental import pallas as pl
from jax.experimental.pallas import tpu as pltpu
from jax.sharding import PartitionSpec as P

ROPE = 64
NOPE = 128
SCALE2 = (NOPE + ROPE) ** (-0.5) * math.log2(math.e)
HIDDEN = -1e30
LANES = 128
F32 = jnp.float32
BF16 = jnp.bfloat16
NT = (((1,), (1,)), ((), ()))

VMEM = pl.BlockSpec(memory_space=pltpu.VMEM)
SMEM = pl.BlockSpec(memory_space=pltpu.SMEM)
ANY = pl.BlockSpec(memory_space=pl.ANY)
HBM = pl.BlockSpec(memory_space=pltpu.HBM)
PARAMS = pltpu.CompilerParams(vmem_limit_bytes=40 * 1024 * 1024)
NO_COST = pl.CostEstimate(flops=0, bytes_accessed=0, transcendentals=0)
EXTRA = 16
PACK = 8_000_000_000
PROJECT = 8_000_000_000


def shape(dims, dtype=BF16):
    return jax.ShapeDtypeStruct(dims, dtype)


def pack_kernel(rank, cache_ref, out_ref):
    local, span, _ = cache_ref.shape
    some = span // 2
    for p in range(local):
        part = pl.ds(p * some, some)
        first, second = cache_ref[p, :some], cache_ref[p, some:]
        out_ref[part, :rank] = first[:, :rank]
        out_ref[part, rank : 2 * rank] = second[:, :rank]
        out_ref[part, 2 * rank :] = jnp.concatenate([first[:, rank:], second[:, rank:]], axis=1)


def project_kernel(local, nope_ref, rope_ref, w_ref, own_ref):
    heads, _, rank = w_ref.shape
    nope = nope_ref[...].astype(F32)
    width = nope.shape[1]
    first = lax.broadcasted_iota(jnp.int32, (2 * local, width), 0) < local

    def pair(h):
        two = nope[h * local : (h + 2) * local]
        left = jnp.concatenate([jnp.where(first, two, 0.0), jnp.where(first, 0.0, two)], axis=1)
        weights = w_ref[pl.ds(h, 2)].reshape(2 * width, rank)
        return jnp.dot(left.astype(BF16), weights, preferred_element_type=F32)

    own_ref[:, rank:] = rope_ref[...]
    for h in range(0, heads, 4):
        own_ref[pl.ds(h * local, 4 * local), :rank] = jnp.concatenate(
            [pair(i) for i in (h, h + 2)], axis=0
        ).astype(BF16)


def prefix_kernel(count, tiles, *refs):
    query_refs = refs[:count]
    keys_ref, out_ref, max_ref, sum_ref, *give_ref, acc_ref = refs[count:]
    rank = acc_ref.shape[1]
    tile = keys_ref.shape[1] // tiles
    parts = [pl.ds(i * tile, tile) for i in range(tiles)]
    queries = jnp.concatenate([ref[...] for ref in query_refs], axis=0)

    def score(i):
        return jnp.dot(queries, keys_ref[:, parts[i]], preferred_element_type=F32) * SCALE2

    ahead = score(0)
    for i in range(tiles):
        scores = ahead
        if i + 1 < tiles:
            ahead = score(i + 1)
        top = jnp.max(scores, axis=1, keepdims=True)
        if i > 0:
            top = jnp.maximum(top, largest)
        weights = jnp.exp2(scores - top)
        total = jnp.sum(weights, axis=1, keepdims=True)
        acc = lax.dot_general(
            weights.astype(BF16), keys_ref[:rank, parts[i]], NT, preferred_element_type=F32
        )
        if i > 0:
            factor = jnp.exp2(largest - top)
            total = total + running * factor
            acc = acc + acc_ref[...] * factor
        largest, running = top, total
        if i < tiles - 1:
            acc_ref[...] = acc
    kept = out_ref.shape[0]
    out_ref[...] = acc[:kept]
    max_ref[...] = jnp.broadcast_to(largest[:kept], max_ref.shape)
    sum_ref[...] = jnp.broadcast_to(running[:kept], sum_ref.shape)
    if give_ref:
        level = largest[kept:] + jnp.log2(running[kept:])
        give_ref[0][...] = packed(acc[kept:] * (1.0 / running[kept:]), level)


def prefix_attention(queries, keys, rank, give, tiles=4):
    rows = sum(q.shape[0] for q in queries)
    kept = queries[0].shape[0] if give else rows
    width, length = keys.shape
    out = [shape((kept, rank), F32)] + [shape((kept, LANES), F32)] * 2
    if give:
        out.append(shape((rows - kept, rank + LANES)))
    return pl.pallas_call(
        functools.partial(prefix_kernel, len(queries), tiles),
        out_shape=out,
        in_specs=[VMEM] * (len(queries) + 1),
        out_specs=[VMEM] * len(out),
        scratch_shapes=[pltpu.VMEM((rows, rank), F32)],
        compiler_params=PARAMS,
        cost_estimate=pl.CostEstimate(
            flops=0 if give else 2 * rows * length * (width + rank),
            bytes_accessed=0 if give else 2 * width * length,
            transcendentals=0 if give else rows * length,
        ),
        name="prefix_attention",
    )(*queries, keys)


def packed(values, level):
    rows = values.shape[0]
    lane = lax.broadcasted_iota(jnp.int32, (rows, LANES), 1)
    high = level.astype(BF16).astype(F32)
    middle = (level - high).astype(BF16).astype(F32)
    low = level - high - middle
    stats = jnp.where(lane == 0, high, jnp.where(lane == 1, middle, jnp.where(lane == 2, low, 0.0)))
    return jnp.concatenate([values.astype(BF16), stats.astype(BF16)], axis=1)


def unpacked(part):
    rank = part.shape[1] - LANES
    return part[:, :rank].astype(F32), jnp.sum(part[:, rank:].astype(F32), axis=1, keepdims=True)


def merged(parts):
    levels = [level for _, level in parts]
    top = functools.reduce(jnp.maximum, levels)
    shares = [jnp.exp2(level - top) for level in levels]
    whole = functools.reduce(jnp.add, shares)
    acc = functools.reduce(jnp.add, [share * values for share, (values, _) in zip(shares, parts)])
    return acc * (1.0 / whole), top + jnp.log2(whole)


def column(stat):
    return jnp.max(stat, axis=1, keepdims=True)


def diagonal(rows, lanes):
    row = lax.broadcasted_iota(jnp.int32, (rows, lanes), 0)
    return row == lax.broadcasted_iota(jnp.int32, (rows, lanes), 1)


def visible(rows, ends, starts, span):
    local = len(ends)
    cols = len(starts) * local * span
    col = lax.broadcasted_iota(jnp.int32, (1, cols), 1)
    col_of = jnp.zeros_like(col)
    limit = jnp.full_like(col, ends[0] - starts[0])
    for at in range(1, len(starts) * local):
        begin, p = at * span, at % local
        later = col >= begin
        col_of = jnp.where(later, p, col_of)
        limit = jnp.where(later, ends[p] - starts[at // local] + begin, limit)
    col_of = jnp.where(col < limit, col_of, -1)
    row_of = lax.rem(lax.broadcasted_iota(jnp.int32, (rows, 1), 0), local)
    return row_of == col_of


def attend(queries, keys, seen, rank, known):
    scores = lax.dot_general(queries, keys, NT, preferred_element_type=F32)
    scores = jnp.where(seen, scores * SCALE2, HIDDEN)
    top = jnp.max(scores, axis=1, keepdims=True)
    for level, _, _ in known:
        top = jnp.maximum(top, level)
    weights = jnp.where(seen, jnp.exp2(scores - top), 0.0)
    total = jnp.sum(weights, axis=1, keepdims=True)
    acc = jnp.dot(weights.astype(BF16), keys[:, :rank], preferred_element_type=F32)
    for level, mass, part in known:
        factor = jnp.exp2(level - top)
        total = total + mass * factor
        acc = acc + part * factor
    return acc * (1.0 / total), top + jnp.log2(total)


def at_end(dom):
    return (dom == 0) | (dom == 3)


def gather_kernel(line, chosen, names, *refs):
    block_refs, out_ref = refs[:-1], refs[-1]
    if chosen:
        block_refs = block_refs[:-1]
    dom = lax.axis_index("dom")
    local = names.shape[0]
    some = out_ref.shape[0] // local
    for p in range(local):
        owner, slot = lax.div(names[p], local), lax.rem(names[p], local)
        if line:
            apart = jnp.bitwise_xor(owner, dom)
            which = jnp.where(at_end(dom), 0, jnp.maximum(apart - 1, 0))
            if chosen:
                slot = jnp.where(at_end(dom), p, slot)
        else:
            which = lax.rem(dom - owner + len(block_refs), len(block_refs))
        rows = pl.ds(pl.multiple_of(slot * some, some), some)
        for k, block_ref in enumerate(block_refs):

            @pl.when(which == k)
            def _():
                out_ref[pl.ds(p * some, some)] = block_ref[rows]


def gathered(names, blocks, line, token=None):
    token = [] if token is None else [token]
    return pl.pallas_call(
        functools.partial(gather_kernel, line, bool(token)),
        out_shape=shape(blocks[0].shape),
        in_specs=[SMEM] + [VMEM] * len(blocks) + [ANY] * len(token),
        out_specs=VMEM,
        compiler_params=PARAMS,
        cost_estimate=NO_COST,
        name="gather",
    )(names, *blocks, *token)


def far_part(anc, lens, query_ref, stage_refs, part, keys):
    acc_ref, max_ref, sum_ref = stage_refs
    local = anc.shape[0]
    span, rank = keys.shape[0] // local, acc_ref.shape[1]
    ends = [lens[anc[p]] for p in range(local)]
    seen = visible(query_ref.shape[0], ends, [lax.axis_index("seq") * span], span)
    known = [(column(max_ref[part]), column(sum_ref[part]), acc_ref[part])]
    return packed(*attend(query_ref[...], keys, seen, rank, known))


def give_kernel(stages, line, anc, lens, *refs):
    stage_refs, refs = refs[: 4 * stages], refs[4 * stages :]
    early_ref, late_ref, moved_ref, give_refs = refs[0], refs[1], refs[2], refs[3:]
    dom = lax.axis_index("dom")
    local = anc.shape[0]
    some = early_ref.shape[0] // local
    span, width = 2 * some, moved_ref.shape[1]
    rank = stage_refs[1].shape[1]

    def place(p, value):
        for h in range(2):
            rows, rope = pl.ds(p * span + h * some, some), 2 * rank + h * (width - rank)
            moved_ref[rows, :rank] = value[:, h * rank : (h + 1) * rank]
            moved_ref[rows, rank:] = value[:, rope : rope + width - rank]

    for p in range(local):
        if line:
            owner, slot = lax.div(anc[p], local), lax.rem(anc[p], local)
            apart = jnp.bitwise_xor(owner, dom)
            late = jnp.where(at_end(dom), apart != 0, apart == 1)
            slot = jnp.where(at_end(dom), p, slot)
            rows = pl.ds(pl.multiple_of(slot * some, some), some)

            @pl.when(late)
            def _():
                place(p, late_ref[rows])

            @pl.when(jnp.logical_not(late))
            def _():
                place(p, early_ref[pl.ds(p * some, some)])

        else:
            place(p, early_ref[pl.ds(p * some, some)])

    for k in range(stages):
        query_ref, *partial = stage_refs[4 * k : 4 * k + 4]
        rows = query_ref.shape[0]
        give_refs[k][...] = far_part(anc, lens, query_ref, partial, pl.ds(rows, rows), moved_ref[...])


def keep_kernel(stages, anc, lens, *refs):
    stage_refs, refs = refs[: 4 * stages], refs[4 * stages :]
    moved_ref, keep_refs, piece_refs = refs[0], refs[1 : 1 + stages], refs[1 + stages :]
    begin = 0
    for piece_ref in piece_refs:
        piece_ref[...] = moved_ref[pl.ds(begin, piece_ref.shape[0])]
        begin += piece_ref.shape[0]
    for k in range(stages):
        query_ref, *partial = stage_refs[4 * k : 4 * k + 4]
        rows = query_ref.shape[0]
        keep_refs[k][...] = far_part(anc, lens, query_ref, partial, pl.ds(0, rows), moved_ref[...])


def near_kernel(anc, lens, fresh_ref, *refs):
    seq = lax.axis_index("seq")
    query_ref, acc_ref, max_ref, sum_ref, got_ref, moved_ref, *other_refs = refs[:-3]
    cache_ref, value_ref, level_ref = refs[-3:]
    local, span, width = cache_ref.shape
    rank = acc_ref.shape[1]
    start, other = seq * span, jnp.bitwise_xor(seq, 1) * span
    ends = [lens[anc[p]] for p in range(local)]
    keys = jnp.concatenate([ref[...] for ref in (moved_ref, *other_refs)], axis=0)
    seen = visible(query_ref.shape[0], ends, [start, other], span)
    level = jnp.sum(got_ref[:, rank:].astype(F32), axis=1, keepdims=True)
    known = [
        (column(max_ref[...]), column(sum_ref[...]), acc_ref[...]),
        (level, 1.0, got_ref[:, :rank].astype(F32)),
    ]
    values, level = attend(query_ref[...], keys, seen, rank, known)
    value_ref[...] = values.astype(BF16)
    level_ref[...] = jnp.broadcast_to(level, level_ref.shape)
    for p in range(local):
        at = start + lax.broadcasted_iota(jnp.int32, (span, 1), 0) == ends[p]
        cache_ref[p] = jnp.where(at, fresh_ref[pl.ds(p, 1), :], moved_ref[pl.ds(p * span, span)])


def chip_kernel(count, *refs):
    for k in range(count):
        out_ref = refs[2 * count + k]
        values, level = merged([unpacked(refs[k][...]), unpacked(refs[count + k][...])])
        rows, rank = values.shape
        lanes = max(rows, LANES)
        level = jnp.sum(jnp.where(diagonal(rows, lanes), level, 0.0), axis=0, keepdims=True)
        high = level.astype(BF16).astype(F32)
        middle = (level - high).astype(BF16).astype(F32)
        low = level - high - middle
        row = lax.broadcasted_iota(jnp.int32, (EXTRA, lanes), 0)
        stats = jnp.where(row == 0, high, jnp.where(row == 1, middle, jnp.where(row == 2, low, 0.0)))
        out_ref[pl.ds(0, rows)] = values.astype(BF16)
        out_ref[pl.ds(rows, EXTRA), :lanes] = stats.astype(BF16)
        out_ref[pl.ds(rows, EXTRA), lanes:] = jnp.zeros((EXTRA, rank - lanes), BF16)


def chip_merge(keep, got):
    rows, rank = keep[0].shape[0], keep[0].shape[1] - LANES
    return pl.pallas_call(
        functools.partial(chip_kernel, len(keep)),
        out_shape=[shape((rows + EXTRA, rank))] * len(keep),
        in_specs=[VMEM] * (2 * len(keep)),
        out_specs=[VMEM] * len(keep),
        compiler_params=PARAMS,
        name="chip_merge",
    )(*keep, *got)


def final_kernel(count, *refs):
    part_refs, (value_ref, level_ref, w_ref, out_ref, values) = refs[:count], refs[count:]
    heads, rank, reach = w_ref.shape
    local = out_ref.shape[0]
    rows = value_ref.shape[0]
    lanes = max(rows, LANES)
    parts = [(value_ref[...].astype(F32), column(level_ref[...]))]
    for part_ref in part_refs:
        stats = part_ref[pl.ds(rows, EXTRA), :lanes].astype(F32)
        level = jnp.sum(stats, axis=0, keepdims=True)
        level = jnp.sum(jnp.where(diagonal(rows, lanes), level, 0.0), axis=1, keepdims=True)
        parts.append((part_ref[pl.ds(0, rows)].astype(F32), level))
    latent = merged(parts)[0].astype(BF16)
    first = lax.broadcasted_iota(jnp.int32, (2 * local, reach), 0) < local
    for h in range(0, heads, 2):
        two = latent[h * local : (h + 2) * local]
        weights = jnp.concatenate([w_ref[h], w_ref[h + 1]], axis=1)
        both = jnp.dot(two, weights, preferred_element_type=F32)
        values[pl.ds(h * local, 2 * local), :] = jnp.where(first, both[:, :reach], both[:, reach:])
    for p in range(local):
        out_ref[p] = values[pl.ds(p, heads, stride=local), :].astype(BF16)


def on_device(q_nope, q_rope, w_uk, w_uv, prefix, private_caches, new_latent, ancestors, lengths):
    local, heads, nope = q_nope.shape
    span, width = private_caches.shape[1:]
    rank, reach = w_uv.shape[1:]
    rows = local * heads
    seq_size, dom_size = lax.axis_size("seq"), lax.axis_size("dom")
    cores = 2
    chips = seq_size // cores
    block = pl.pallas_call(
        functools.partial(pack_kernel, rank),
        out_shape=shape((local * span // 2, 2 * width)),
        in_specs=[VMEM],
        out_specs=VMEM,
        compiler_params=PARAMS,
        cost_estimate=pl.CostEstimate(flops=PACK, bytes_accessed=0, transcendentals=0),
        name="pack",
    )(private_caches)
    nope_rows, rope_rows = (jnp.swapaxes(q, 0, 1).reshape(rows, -1) for q in (q_nope, q_rope))
    line = dom_size == 4
    if line:
        swap = [(0, 1), (1, 0), (2, 3), (3, 2)]
        middle = lax.ppermute(block, "dom", [(0, 2), (3, 1)])
        far = lax.ppermute(block, "dom", [(1, 2), (2, 1)])
        theirs = lax.ppermute(ancestors, "dom", [(0, 1), (3, 2)])
    else:
        blocks = [block] + [
            lax.ppermute(block, "dom", [(i, (i + k) % dom_size) for i in range(dom_size)])
            for k in range(1, dom_size)
        ]

    own = pl.pallas_call(
        functools.partial(project_kernel, local),
        out_shape=shape((rows, width)),
        in_specs=[VMEM] * 3,
        out_specs=VMEM,
        compiler_params=PARAMS,
        cost_estimate=pl.CostEstimate(flops=PROJECT, bytes_accessed=0, transcendentals=0),
        name="project",
    )(nope_rows, rope_rows, w_uk)
    keys = prefix.T

    def pairs(turn, flip):
        return [
            (x * cores + c, (x + turn) % chips * cores + (c ^ flip))
            for x in range(chips)
            for c in range(cores)
        ]

    def back(turn, flip):
        return [(b, a) for a, b in pairs(turn, flip)]

    routes = [(t, f) for t in range(chips) for f in range(cores)]
    queries = [own if r == (0, 0) else lax.ppermute(own, "seq", pairs(*r)) for r in routes]
    stages = []
    for t in range(chips):
        asked = queries[2 * t : 2 * t + 2]
        stage = [*asked, *prefix_attention(asked, keys, rank, t == 0)]
        stages.append(stage)
        if t == 0:
            given = lax.ppermute(stage.pop(), "seq", pairs(0, 1))
        if line and t == 0:
            chosen = gathered(theirs, [block, middle, far], line, stage[3])
            late = lax.ppermute(chosen, "dom", swap)
            early = gathered(ancestors, [block, middle, far], line)
    if not line:
        early = late = gathered(ancestors, blocks, line)

    part = shape((rows, rank + LANES))
    others = chips - 1
    given, early = lax.optimization_barrier((given, early))
    giving = [a for stage in stages[1:] for a in stage[1:]]
    keeping = [a for stage in stages[1:] for a in (stage[0], *stage[2:])]
    moved, *give = pl.pallas_call(
        functools.partial(give_kernel, others, line),
        out_shape=[shape((local * span, width))] + [part] * others,
        in_specs=[SMEM] * 2 + [VMEM] * (len(giving) + 2),
        out_specs=[VMEM] * (1 + others),
        compiler_params=PARAMS,
        name="suffix_give",
    )(ancestors, lengths, *giving, early, late)
    small = local * span // 48 * 16
    cuts = (local * span - 2 * small, small, small)
    keep_and_pieces = pl.pallas_call(
        functools.partial(keep_kernel, others),
        out_shape=[part] * others + [shape((cut, width)) for cut in cuts],
        in_specs=[SMEM] * 2 + [VMEM] * (len(keeping) + 1),
        out_specs=[VMEM] * (others + len(cuts)),
        compiler_params=PARAMS,
        name="suffix_keep",
    )(ancestors, lengths, *keeping, moved)
    keep, pieces = keep_and_pieces[:others], keep_and_pieces[others:]
    sums = chip_merge(keep, [lax.ppermute(g, "seq", pairs(0, 1)) for g in give])
    parts = [lax.ppermute(s, "seq", back(t, 0)) for t, s in enumerate(sums, 1)]
    other = [lax.ppermute(piece, "seq", pairs(0, 1)) for piece in pieces]

    moved, _ = lax.optimization_barrier((moved, sums[0]))
    query, _, acc, level, mass = stages[0]
    new_caches, *own_part = pl.pallas_call(
        near_kernel,
        out_shape=[shape(private_caches.shape), shape((rows, rank)), shape((rows, LANES), F32)],
        in_specs=[SMEM] * 2 + [VMEM] * (7 + len(other)),
        out_specs=[VMEM] * 3,
        compiler_params=PARAMS,
        cost_estimate=NO_COST,
        name="suffix_near",
    )(ancestors, lengths, new_latent, query, acc, level, mass, given, moved, *other)
    parts += own_part

    head_values = pl.pallas_call(
        functools.partial(final_kernel, others),
        out_shape=shape((local, heads, reach)),
        in_specs=[VMEM] * (chips + 2),
        out_specs=VMEM,
        scratch_shapes=[pltpu.VMEM((rows, reach), F32)],
        compiler_params=PARAMS,
        name="final",
    )(*parts, w_uv)
    return (head_values, new_caches)


def solution(mesh):
    placed = (
        P(("group", "dom"), "seq", None),
        P(("group", "dom"), "seq", None),
        P("seq", None, None),
        P("seq", None, None),
        P(("group", "seq"), None),
        P(("group", "dom"), "seq", None),
        P(("group", "dom"), None),
        P(("group", "dom")),
        P("group"),
    )
    return jax.shard_map(
        on_device,
        mesh=mesh,
        in_specs=placed,
        out_specs=(P(("group", "dom"), "seq", None), P(("group", "dom"), "seq", None)),
        check_vma=False,
    )
```

```python
import functools
import math

import jax
import jax.numpy as jnp
from jax import lax
from jax.experimental import pallas as pl
from jax.experimental.pallas import tpu as pltpu
from jax.sharding import PartitionSpec as P

ROPE = 64
NOPE = 128
SCALE2 = (NOPE + ROPE) ** (-0.5) * math.log2(math.e)
HIDDEN = -1e30
LANES = 128
F32 = jnp.float32
BF16 = jnp.bfloat16
NT = (((1,), (1,)), ((), ()))

VMEM = pl.BlockSpec(memory_space=pltpu.VMEM)
SMEM = pl.BlockSpec(memory_space=pltpu.SMEM)
ANY = pl.BlockSpec(memory_space=pl.ANY)
HBM = pl.BlockSpec(memory_space=pltpu.HBM)
PARAMS = pltpu.CompilerParams(vmem_limit_bytes=40 * 1024 * 1024)
NO_COST = pl.CostEstimate(flops=0, bytes_accessed=0, transcendentals=0)
PACK = 8_000_000_000
PROJECT = 8_000_000_000


def shape(dims, dtype=BF16):
    return jax.ShapeDtypeStruct(dims, dtype)


def pack_slot(rows, out_ref, part):
    some, width = rows.shape[0] // 2, rows.shape[1]
    rank = width - ROPE
    first, second = rows[:some], rows[some:]
    out_ref[part, :rank] = first[:, :rank]
    out_ref[part, rank : 2 * rank] = second[:, :rank]
    out_ref[part, 2 * rank :] = jnp.concatenate([first[:, rank:], second[:, rank:]], axis=1)


def pack_kernel(cache_ref, out_ref):
    local, span, _ = cache_ref.shape
    for p in range(local):
        pack_slot(cache_ref[p], out_ref, pl.ds(p * span // 2, span // 2))


def project_kernel(local, nope_ref, rope_ref, w_ref, own_ref):
    heads, _, rank = w_ref.shape
    nope = nope_ref[...].astype(F32)
    width = nope.shape[1]
    first = lax.broadcasted_iota(jnp.int32, (2 * local, width), 0) < local

    def pair(h):
        two = nope[h * local : (h + 2) * local]
        left = jnp.concatenate([jnp.where(first, two, 0.0), jnp.where(first, 0.0, two)], axis=1)
        weights = w_ref[pl.ds(h, 2)].reshape(2 * width, rank)
        return jnp.dot(left.astype(BF16), weights, preferred_element_type=F32)

    own_ref[:, rank:] = rope_ref[...]
    for h in range(0, heads, 4):
        own_ref[pl.ds(h * local, 4 * local), :rank] = jnp.concatenate(
            [pair(i) for i in (h, h + 2)], axis=0
        ).astype(BF16)


def prefix_kernel(count, tiles, *refs):
    query_refs = refs[:count]
    keys_ref, out_ref, max_ref, sum_ref, *give_ref, acc_ref = refs[count:]
    rank = acc_ref.shape[1]
    tile = keys_ref.shape[1] // tiles
    parts = [pl.ds(i * tile, tile) for i in range(tiles)]
    queries = jnp.concatenate([ref[...] for ref in query_refs], axis=0)

    def score(i):
        return jnp.dot(queries, keys_ref[:, parts[i]], preferred_element_type=F32) * SCALE2

    ahead = score(0)
    for i in range(tiles):
        scores = ahead
        if i + 1 < tiles:
            ahead = score(i + 1)
        top = jnp.max(scores, axis=1, keepdims=True)
        if i > 0:
            top = jnp.maximum(top, largest)
        weights = jnp.exp2(scores - top)
        total = jnp.sum(weights, axis=1, keepdims=True)
        acc = lax.dot_general(
            weights.astype(BF16), keys_ref[:rank, parts[i]], NT, preferred_element_type=F32
        )
        if i > 0:
            factor = jnp.exp2(largest - top)
            total = total + running * factor
            acc = acc + acc_ref[...] * factor
        largest, running = top, total
        if i < tiles - 1:
            acc_ref[...] = acc
    kept = out_ref.shape[0]
    out_ref[...] = acc[:kept]
    max_ref[...] = jnp.broadcast_to(largest[:kept], max_ref.shape)
    sum_ref[...] = jnp.broadcast_to(running[:kept], sum_ref.shape)
    if give_ref:
        level = largest[kept:] + jnp.log2(running[kept:])
        give_ref[0][...] = packed(acc[kept:] * (1.0 / running[kept:]), level)


def prefix_attention(queries, keys, rank, give, tiles=4):
    rows = sum(q.shape[0] for q in queries)
    kept = queries[0].shape[0] if give else rows
    width, length = keys.shape
    out = [shape((kept, rank), F32)] + [shape((kept, LANES), F32)] * 2
    if give:
        out.append(shape((rows - kept, rank + LANES)))
    return pl.pallas_call(
        functools.partial(prefix_kernel, len(queries), tiles),
        out_shape=out,
        in_specs=[VMEM] * (len(queries) + 1),
        out_specs=[VMEM] * len(out),
        scratch_shapes=[pltpu.VMEM((rows, rank), F32)],
        compiler_params=PARAMS,
        cost_estimate=pl.CostEstimate(
            flops=0 if give else 2 * rows * length * (width + rank),
            bytes_accessed=0 if give else 2 * width * length,
            transcendentals=0 if give else rows * length,
        ),
        name="prefix_attention",
    )(*queries, keys)


def packed(values, level):
    rows = values.shape[0]
    lane = lax.broadcasted_iota(jnp.int32, (rows, LANES), 1)
    high = level.astype(BF16).astype(F32)
    middle = (level - high).astype(BF16).astype(F32)
    low = level - high - middle
    stats = jnp.where(lane == 0, high, jnp.where(lane == 1, middle, jnp.where(lane == 2, low, 0.0)))
    return jnp.concatenate([values.astype(BF16), stats.astype(BF16)], axis=1)


def unpacked(part):
    rank = part.shape[1] - LANES
    return part[:, :rank].astype(F32), jnp.sum(part[:, rank:].astype(F32), axis=1, keepdims=True)


def merged(parts):
    levels = [level for _, level in parts]
    top = functools.reduce(jnp.maximum, levels)
    shares = [jnp.exp2(level - top) for level in levels]
    whole = functools.reduce(jnp.add, shares)
    acc = functools.reduce(jnp.add, [share * values for share, (values, _) in zip(shares, parts)])
    return acc * (1.0 / whole), top + jnp.log2(whole)


def column(stat):
    return jnp.max(stat, axis=1, keepdims=True)


def diagonal(rows, lanes):
    row = lax.broadcasted_iota(jnp.int32, (rows, lanes), 0)
    return row == lax.broadcasted_iota(jnp.int32, (rows, lanes), 1)


def visible(rows, ends, starts, span):
    local = len(ends)
    cols = len(starts) * local * span
    col = lax.broadcasted_iota(jnp.int32, (1, cols), 1)
    col_of = jnp.zeros_like(col)
    limit = jnp.full_like(col, ends[0] - starts[0])
    for at in range(1, len(starts) * local):
        begin, p = at * span, at % local
        later = col >= begin
        col_of = jnp.where(later, p, col_of)
        limit = jnp.where(later, ends[p] - starts[at // local] + begin, limit)
    col_of = jnp.where(col < limit, col_of, -1)
    row_of = lax.rem(lax.broadcasted_iota(jnp.int32, (rows, 1), 0), local)
    return row_of == col_of


def attend(queries, keys, seen, rank, known):
    scores = lax.dot_general(queries, keys, NT, preferred_element_type=F32)
    scores = jnp.where(seen, scores * SCALE2, HIDDEN)
    top = jnp.max(scores, axis=1, keepdims=True)
    for level, _, _ in known:
        top = jnp.maximum(top, level)
    weights = jnp.where(seen, jnp.exp2(scores - top), 0.0)
    total = jnp.sum(weights, axis=1, keepdims=True)
    acc = jnp.dot(weights.astype(BF16), keys[:, :rank], preferred_element_type=F32)
    for level, mass, part in known:
        factor = jnp.exp2(level - top)
        total = total + mass * factor
        acc = acc + part * factor
    return acc * (1.0 / total), top + jnp.log2(total)


def at_end(dom):
    return (dom == 0) | (dom == 3)


def gather_kernel(line, chosen, names, *refs):
    block_refs, out_ref = refs[:-1], refs[-1]
    if chosen:
        block_refs = block_refs[:-1]
    dom = lax.axis_index("dom")
    local = names.shape[0]
    some = out_ref.shape[0] // local
    for p in range(local):
        owner, slot = lax.div(names[p], local), lax.rem(names[p], local)
        if line:
            apart = jnp.bitwise_xor(owner, dom)
            which = jnp.where(at_end(dom), 0, jnp.maximum(apart - 1, 0))
            if chosen:
                slot = jnp.where(at_end(dom), p, slot)
        else:
            which = lax.rem(dom - owner + len(block_refs), len(block_refs))
        rows = pl.ds(pl.multiple_of(slot * some, some), some)
        for k, block_ref in enumerate(block_refs):

            @pl.when(which == k)
            def _():
                part = pl.ds(p * some, some)
                if len(block_ref.shape) == 2:
                    out_ref[part] = block_ref[rows]
                else:
                    pack_slot(block_ref[slot], out_ref, part)


def gathered(names, blocks, line, token=None):
    token = [] if token is None else [token]
    return pl.pallas_call(
        functools.partial(gather_kernel, line, bool(token)),
        out_shape=shape(blocks[0].shape),
        in_specs=[SMEM] + [VMEM] * len(blocks) + [ANY] * len(token),
        out_specs=VMEM,
        compiler_params=PARAMS,
        cost_estimate=NO_COST,
        name="gather",
    )(names, *blocks, *token)


def far_part(anc, lens, query_ref, stage_refs, part, keys):
    acc_ref, max_ref, sum_ref = stage_refs
    local = anc.shape[0]
    span, rank = keys.shape[0] // local, acc_ref.shape[1]
    ends = [lens[anc[p]] for p in range(local)]
    seen = visible(query_ref.shape[0], ends, [lax.axis_index("seq") * span], span)
    known = [(column(max_ref[part]), column(sum_ref[part]), acc_ref[part])]
    return packed(*attend(query_ref[...], keys, seen, rank, known))


def give_kernel(stages, line, anc, lens, *refs):
    stage_refs, refs = refs[: 4 * stages], refs[4 * stages :]
    early_ref, late_ref, moved_ref, give_refs = refs[0], refs[1], refs[2], refs[3:]
    dom = lax.axis_index("dom")
    local = anc.shape[0]
    some = early_ref.shape[0] // local
    span, width = 2 * some, moved_ref.shape[1]
    rank = stage_refs[1].shape[1]

    def place(p, value):
        for h in range(2):
            rows, rope = pl.ds(p * span + h * some, some), 2 * rank + h * (width - rank)
            moved_ref[rows, :rank] = value[:, h * rank : (h + 1) * rank]
            moved_ref[rows, rank:] = value[:, rope : rope + width - rank]

    for p in range(local):
        if line:
            owner, slot = lax.div(anc[p], local), lax.rem(anc[p], local)
            apart = jnp.bitwise_xor(owner, dom)
            late = jnp.where(at_end(dom), apart != 0, apart == 1)
            slot = jnp.where(at_end(dom), p, slot)
            rows = pl.ds(pl.multiple_of(slot * some, some), some)

            @pl.when(late)
            def _():
                place(p, late_ref[rows])

            @pl.when(jnp.logical_not(late))
            def _():
                place(p, early_ref[pl.ds(p * some, some)])

        else:
            place(p, early_ref[pl.ds(p * some, some)])

    for k in range(stages):
        query_ref, *partial = stage_refs[4 * k : 4 * k + 4]
        rows = query_ref.shape[0]
        give_refs[k][...] = far_part(anc, lens, query_ref, partial, pl.ds(rows, rows), moved_ref[...])


def keep_kernel(stages, anc, lens, *refs):
    stage_refs, refs = refs[: 4 * stages], refs[4 * stages :]
    moved_ref, keep_refs, piece_refs = refs[0], refs[1 : 1 + stages], refs[1 + stages :]
    begin = 0
    for piece_ref in piece_refs:
        piece_ref[...] = moved_ref[pl.ds(begin, piece_ref.shape[0])]
        begin += piece_ref.shape[0]
    for k in range(stages):
        query_ref, *partial = stage_refs[4 * k : 4 * k + 4]
        rows = query_ref.shape[0]
        keep_refs[k][...] = far_part(anc, lens, query_ref, partial, pl.ds(0, rows), moved_ref[...])


def near_kernel(anc, lens, fresh_ref, *refs):
    seq = lax.axis_index("seq")
    query_ref, acc_ref, max_ref, sum_ref, got_ref, moved_ref, *other_refs = refs[:-3]
    cache_ref, value_ref, level_ref = refs[-3:]
    local, span, width = cache_ref.shape
    rank = acc_ref.shape[1]
    start, other = seq * span, jnp.bitwise_xor(seq, 1) * span
    ends = [lens[anc[p]] for p in range(local)]
    keys = jnp.concatenate([ref[...] for ref in (moved_ref, *other_refs)], axis=0)
    seen = visible(query_ref.shape[0], ends, [start, other], span)
    level = jnp.sum(got_ref[:, rank:].astype(F32), axis=1, keepdims=True)
    known = [
        (column(max_ref[...]), column(sum_ref[...]), acc_ref[...]),
        (level, 1.0, got_ref[:, :rank].astype(F32)),
    ]
    values, level = attend(query_ref[...], keys, seen, rank, known)
    value_ref[...] = values.astype(BF16)
    level_ref[...] = jnp.broadcast_to(level, level_ref.shape)
    for p in range(local):
        at = start + lax.broadcasted_iota(jnp.int32, (span, 1), 0) == ends[p]
        cache_ref[p] = jnp.where(at, fresh_ref[pl.ds(p, 1), :], moved_ref[pl.ds(p * span, span)])


def chip_kernel(count, *refs):
    for k in range(count):
        value_ref, level_ref = refs[2 * count + 2 * k : 2 * count + 2 * k + 2]
        values, level = merged([unpacked(refs[k][...]), unpacked(refs[count + k][...])])
        value_ref[...] = values.astype(BF16)
        kept = jnp.where(diagonal(values.shape[0], level_ref.shape[1]), level, 0.0)
        level_ref[...] = jnp.broadcast_to(jnp.sum(kept, axis=0, keepdims=True), level_ref.shape)


def chip_merge(keep, got):
    rows, rank = keep[0].shape[0], keep[0].shape[1] - LANES
    return pl.pallas_call(
        functools.partial(chip_kernel, len(keep)),
        out_shape=[shape((rows, rank)), shape((8, max(rows, LANES)), F32)] * len(keep),
        in_specs=[VMEM] * (2 * len(keep)),
        out_specs=[VMEM] * (2 * len(keep)),
        compiler_params=PARAMS,
        name="chip_merge",
    )(*keep, *got)


def final_kernel(count, *refs):
    part_refs, (value_ref, level_ref, w_ref, out_ref, values) = refs[: 2 * count], refs[2 * count :]
    heads, rank, reach = w_ref.shape
    local = out_ref.shape[0]
    parts = [(value_ref[...].astype(F32), column(level_ref[...]))]
    for k in range(count):
        row = part_refs[2 * k + 1][0:1]
        kept = jnp.where(diagonal(value_ref.shape[0], row.shape[1]), row, 0.0)
        parts.append((part_refs[2 * k][...].astype(F32), jnp.sum(kept, axis=1, keepdims=True)))
    latent = merged(parts)[0].astype(BF16)
    first = lax.broadcasted_iota(jnp.int32, (2 * local, reach), 0) < local
    for h in range(0, heads, 2):
        two = latent[h * local : (h + 2) * local]
        weights = jnp.concatenate([w_ref[h], w_ref[h + 1]], axis=1)
        both = jnp.dot(two, weights, preferred_element_type=F32)
        values[pl.ds(h * local, 2 * local), :] = jnp.where(first, both[:, :reach], both[:, reach:])
    for p in range(local):
        out_ref[p] = values[pl.ds(p, heads, stride=local), :].astype(BF16)


def on_device(q_nope, q_rope, w_uk, w_uv, prefix, private_caches, new_latent, ancestors, lengths):
    local, heads, nope = q_nope.shape
    span, width = private_caches.shape[1:]
    rank, reach = w_uv.shape[1:]
    rows = local * heads
    seq_size, dom_size = lax.axis_size("seq"), lax.axis_size("dom")
    cores = 2
    chips = seq_size // cores
    block = pl.pallas_call(
        pack_kernel,
        out_shape=shape((local * span // 2, 2 * width)),
        in_specs=[VMEM],
        out_specs=VMEM,
        compiler_params=PARAMS,
        cost_estimate=pl.CostEstimate(flops=PACK, bytes_accessed=0, transcendentals=0),
        name="pack",
    )(private_caches)
    nope_rows, rope_rows = (jnp.swapaxes(q, 0, 1).reshape(rows, -1) for q in (q_nope, q_rope))
    line = dom_size == 4
    if line:
        swap = [(0, 1), (1, 0), (2, 3), (3, 2)]
        middle = lax.ppermute(block, "dom", [(0, 2), (3, 1)])
        far = lax.ppermute(private_caches, "dom", [(1, 2), (2, 1)])
        theirs = lax.ppermute(ancestors, "dom", [(0, 1), (3, 2)])
    else:
        blocks = [block] + [
            lax.ppermute(block, "dom", [(i, (i + k) % dom_size) for i in range(dom_size)])
            for k in range(1, dom_size)
        ]

    own = pl.pallas_call(
        functools.partial(project_kernel, local),
        out_shape=shape((rows, width)),
        in_specs=[VMEM] * 3,
        out_specs=VMEM,
        compiler_params=PARAMS,
        cost_estimate=pl.CostEstimate(flops=PROJECT, bytes_accessed=0, transcendentals=0),
        name="project",
    )(nope_rows, rope_rows, w_uk)
    keys = prefix.T

    def pairs(turn, flip):
        return [
            (x * cores + c, (x + turn) % chips * cores + (c ^ flip))
            for x in range(chips)
            for c in range(cores)
        ]

    def back(turn, flip):
        return [(b, a) for a, b in pairs(turn, flip)]

    routes = [(t, f) for t in range(chips) for f in range(cores)]
    queries = [own if r == (0, 0) else lax.ppermute(own, "seq", pairs(*r)) for r in routes]
    stages = []
    for t in range(chips):
        asked = queries[2 * t : 2 * t + 2]
        stage = [*asked, *prefix_attention(asked, keys, rank, t == 0)]
        stages.append(stage)
        if t == 0:
            given = lax.ppermute(stage.pop(), "seq", pairs(0, 1))
        if line and t == 0:
            chosen = gathered(theirs, [block, middle, far], line, stage[3])
            late = lax.ppermute(chosen, "dom", swap)
            early = gathered(ancestors, [block, middle, far], line)
    if not line:
        early = late = gathered(ancestors, blocks, line)

    part = shape((rows, rank + LANES))
    others = chips - 1
    given, early = lax.optimization_barrier((given, early))
    giving = [a for stage in stages[1:] for a in stage[1:]]
    keeping = [a for stage in stages[1:] for a in (stage[0], *stage[2:])]
    moved, *give = pl.pallas_call(
        functools.partial(give_kernel, others, line),
        out_shape=[shape((local * span, width))] + [part] * others,
        in_specs=[SMEM] * 2 + [VMEM] * (len(giving) + 2),
        out_specs=[VMEM] * (1 + others),
        compiler_params=PARAMS,
        name="suffix_give",
    )(ancestors, lengths, *giving, early, late)
    small = local * span // 48 * 16
    cuts = (local * span - 2 * small, small, small)
    keep_and_pieces = pl.pallas_call(
        functools.partial(keep_kernel, others),
        out_shape=[part] * others + [shape((cut, width)) for cut in cuts],
        in_specs=[SMEM] * 2 + [VMEM] * (len(keeping) + 1),
        out_specs=[VMEM] * (others + len(cuts)),
        compiler_params=PARAMS,
        name="suffix_keep",
    )(ancestors, lengths, *keeping, moved)
    keep, pieces = keep_and_pieces[:others], keep_and_pieces[others:]
    sums = chip_merge(keep, [lax.ppermute(g, "seq", pairs(0, 1)) for g in give])
    parts = [lax.ppermute(s, "seq", back(1 + i // 2, 0)) for i, s in enumerate(sums)]
    other = [lax.ppermute(piece, "seq", pairs(0, 1)) for piece in pieces]

    moved, _ = lax.optimization_barrier((moved, sums[0]))
    query, _, acc, level, mass = stages[0]
    new_caches, *own_part = pl.pallas_call(
        near_kernel,
        out_shape=[shape(private_caches.shape), shape((rows, rank)), shape((rows, LANES), F32)],
        in_specs=[SMEM] * 2 + [VMEM] * (7 + len(other)),
        out_specs=[VMEM] * 3,
        compiler_params=PARAMS,
        cost_estimate=NO_COST,
        name="suffix_near",
    )(ancestors, lengths, new_latent, query, acc, level, mass, given, moved, *other)
    parts += own_part

    head_values = pl.pallas_call(
        functools.partial(final_kernel, others),
        out_shape=shape((local, heads, reach)),
        in_specs=[VMEM] * (2 * chips + 1),
        out_specs=VMEM,
        scratch_shapes=[pltpu.VMEM((rows, reach), F32)],
        compiler_params=PARAMS,
        name="final",
    )(*parts, w_uv)
    return (head_values, new_caches)


def solution(mesh):
    placed = (
        P(("group", "dom"), "seq", None),
        P(("group", "dom"), "seq", None),
        P("seq", None, None),
        P("seq", None, None),
        P(("group", "seq"), None),
        P(("group", "dom"), "seq", None),
        P(("group", "dom"), None),
        P(("group", "dom")),
        P("group"),
    )
    return jax.shard_map(
        on_device,
        mesh=mesh,
        in_specs=placed,
        out_specs=(P(("group", "dom"), "seq", None), P(("group", "dom"), "seq", None)),
        check_vma=False,
    )
```

```python
import functools
import math

import jax
import jax.numpy as jnp
from jax import lax
from jax.experimental import pallas as pl
from jax.experimental.pallas import tpu as pltpu
from jax.sharding import PartitionSpec as P

ROPE = 64
NOPE = 128
SCALE2 = (NOPE + ROPE) ** (-0.5) * math.log2(math.e)
HIDDEN = -1e30
LANES = 128
F32 = jnp.float32
BF16 = jnp.bfloat16
NT = (((1,), (1,)), ((), ()))

VMEM = pl.BlockSpec(memory_space=pltpu.VMEM)
SMEM = pl.BlockSpec(memory_space=pltpu.SMEM)
ANY = pl.BlockSpec(memory_space=pl.ANY)
HBM = pl.BlockSpec(memory_space=pltpu.HBM)
PARAMS = pltpu.CompilerParams(vmem_limit_bytes=40 * 1024 * 1024)
NO_COST = pl.CostEstimate(flops=0, bytes_accessed=0, transcendentals=0)
PACK = 8_000_000_000
PROJECT = 8_000_000_000


def shape(dims, dtype=BF16):
    return jax.ShapeDtypeStruct(dims, dtype)


def pack_slot(rows, out_ref, part):
    some, width = rows.shape[0] // 2, rows.shape[1]
    rank = width - ROPE
    first, second = rows[:some], rows[some:]
    out_ref[part, :rank] = first[:, :rank]
    out_ref[part, rank : 2 * rank] = second[:, :rank]
    out_ref[part, 2 * rank :] = jnp.concatenate([first[:, rank:], second[:, rank:]], axis=1)


def pack_kernel(cache_ref, out_ref):
    local, span, _ = cache_ref.shape
    for p in range(local):
        pack_slot(cache_ref[p], out_ref, pl.ds(p * span // 2, span // 2))


def project_kernel(local, nope_ref, rope_ref, w_ref, own_ref):
    heads, _, rank = w_ref.shape
    nope = nope_ref[...].astype(F32)
    width = nope.shape[1]
    first = lax.broadcasted_iota(jnp.int32, (2 * local, width), 0) < local

    def pair(h):
        two = nope[h * local : (h + 2) * local]
        left = jnp.concatenate([jnp.where(first, two, 0.0), jnp.where(first, 0.0, two)], axis=1)
        weights = w_ref[pl.ds(h, 2)].reshape(2 * width, rank)
        return jnp.dot(left.astype(BF16), weights, preferred_element_type=F32)

    own_ref[:, rank:] = rope_ref[...]
    for h in range(0, heads, 4):
        own_ref[pl.ds(h * local, 4 * local), :rank] = jnp.concatenate(
            [pair(i) for i in (h, h + 2)], axis=0
        ).astype(BF16)


def prefix_kernel(count, tiles, *refs):
    query_refs = refs[:count]
    keys_ref, out_ref, max_ref, sum_ref, *give_ref, acc_ref = refs[count:]
    rank = acc_ref.shape[1]
    tile = keys_ref.shape[1] // tiles
    parts = [pl.ds(i * tile, tile) for i in range(tiles)]
    queries = jnp.concatenate([ref[...] for ref in query_refs], axis=0)

    def score(i):
        return jnp.dot(queries, keys_ref[:, parts[i]], preferred_element_type=F32) * SCALE2

    ahead = score(0)
    for i in range(tiles):
        scores = ahead
        if i + 1 < tiles:
            ahead = score(i + 1)
        top = jnp.max(scores, axis=1, keepdims=True)
        if i > 0:
            top = jnp.maximum(top, largest)
        weights = jnp.exp2(scores - top)
        total = jnp.sum(weights, axis=1, keepdims=True)
        acc = lax.dot_general(
            weights.astype(BF16), keys_ref[:rank, parts[i]], NT, preferred_element_type=F32
        )
        if i > 0:
            factor = jnp.exp2(largest - top)
            total = total + running * factor
            acc = acc + acc_ref[...] * factor
        largest, running = top, total
        if i < tiles - 1:
            acc_ref[...] = acc
    kept = out_ref.shape[0]
    out_ref[...] = acc[:kept]
    max_ref[...] = jnp.broadcast_to(largest[:kept], max_ref.shape)
    sum_ref[...] = jnp.broadcast_to(running[:kept], sum_ref.shape)
    if give_ref:
        level = largest[kept:] + jnp.log2(running[kept:])
        give_ref[0][...] = packed(acc[kept:] * (1.0 / running[kept:]), level)


def prefix_attention(queries, keys, rank, give, tiles=4):
    rows = sum(q.shape[0] for q in queries)
    kept = queries[0].shape[0] if give else rows
    width, length = keys.shape
    out = [shape((kept, rank), F32)] + [shape((kept, LANES), F32)] * 2
    if give:
        out.append(shape((rows - kept, rank + LANES)))
    return pl.pallas_call(
        functools.partial(prefix_kernel, len(queries), tiles),
        out_shape=out,
        in_specs=[VMEM] * (len(queries) + 1),
        out_specs=[VMEM] * len(out),
        scratch_shapes=[pltpu.VMEM((rows, rank), F32)],
        compiler_params=PARAMS,
        cost_estimate=pl.CostEstimate(
            flops=0 if give else 2 * rows * length * (width + rank),
            bytes_accessed=0 if give else 2 * width * length,
            transcendentals=0 if give else rows * length,
        ),
        name="prefix_attention",
    )(*queries, keys)


def packed(values, level):
    rows = values.shape[0]
    lane = lax.broadcasted_iota(jnp.int32, (rows, LANES), 1)
    high = level.astype(BF16).astype(F32)
    middle = (level - high).astype(BF16).astype(F32)
    low = level - high - middle
    stats = jnp.where(lane == 0, high, jnp.where(lane == 1, middle, jnp.where(lane == 2, low, 0.0)))
    return jnp.concatenate([values.astype(BF16), stats.astype(BF16)], axis=1)


def unpacked(part):
    rank = part.shape[1] - LANES
    return part[:, :rank].astype(F32), jnp.sum(part[:, rank:].astype(F32), axis=1, keepdims=True)


def merged(parts):
    levels = [level for _, level in parts]
    top = functools.reduce(jnp.maximum, levels)
    shares = [jnp.exp2(level - top) for level in levels]
    whole = functools.reduce(jnp.add, shares)
    acc = functools.reduce(jnp.add, [share * values for share, (values, _) in zip(shares, parts)])
    return acc * (1.0 / whole), top + jnp.log2(whole)


def column(stat):
    return jnp.max(stat, axis=1, keepdims=True)


def diagonal(rows, lanes):
    row = lax.broadcasted_iota(jnp.int32, (rows, lanes), 0)
    return row == lax.broadcasted_iota(jnp.int32, (rows, lanes), 1)


def visible(rows, ends, starts, span):
    local = len(ends)
    cols = len(starts) * local * span
    col = lax.broadcasted_iota(jnp.int32, (1, cols), 1)
    col_of = jnp.zeros_like(col)
    limit = jnp.full_like(col, ends[0] - starts[0])
    for at in range(1, len(starts) * local):
        begin, p = at * span, at % local
        later = col >= begin
        col_of = jnp.where(later, p, col_of)
        limit = jnp.where(later, ends[p] - starts[at // local] + begin, limit)
    col_of = jnp.where(col < limit, col_of, -1)
    row_of = lax.rem(lax.broadcasted_iota(jnp.int32, (rows, 1), 0), local)
    return row_of == col_of


def attend(queries, keys, seen, rank, known):
    scores = lax.dot_general(queries, keys, NT, preferred_element_type=F32)
    scores = jnp.where(seen, scores * SCALE2, HIDDEN)
    top = jnp.max(scores, axis=1, keepdims=True)
    for level, _, _ in known:
        top = jnp.maximum(top, level)
    weights = jnp.where(seen, jnp.exp2(scores - top), 0.0)
    total = jnp.sum(weights, axis=1, keepdims=True)
    acc = jnp.dot(weights.astype(BF16), keys[:, :rank], preferred_element_type=F32)
    for level, mass, part in known:
        factor = jnp.exp2(level - top)
        total = total + mass * factor
        acc = acc + part * factor
    return acc * (1.0 / total), top + jnp.log2(total)


def at_end(dom):
    return (dom == 0) | (dom == 3)


def gather_kernel(line, chosen, names, *refs):
    block_refs, out_ref = refs[:-1], refs[-1]
    if chosen:
        block_refs = block_refs[:-1]
    dom = lax.axis_index("dom")
    local = names.shape[0]
    some = out_ref.shape[0] // local
    for p in range(local):
        owner, slot = lax.div(names[p], local), lax.rem(names[p], local)
        if line:
            apart = jnp.bitwise_xor(owner, dom)
            which = jnp.where(at_end(dom), 0, jnp.maximum(apart - 1, 0))
            if chosen:
                slot = jnp.where(at_end(dom), p, slot)
        else:
            which = lax.rem(dom - owner + len(block_refs), len(block_refs))
        rows = pl.ds(pl.multiple_of(slot * some, some), some)
        for k, block_ref in enumerate(block_refs):

            @pl.when(which == k)
            def _():
                part = pl.ds(p * some, some)
                if len(block_ref.shape) == 2:
                    out_ref[part] = block_ref[rows]
                else:
                    pack_slot(block_ref[slot], out_ref, part)


def gathered(names, blocks, line, token=None):
    token = [] if token is None else [token]
    return pl.pallas_call(
        functools.partial(gather_kernel, line, bool(token)),
        out_shape=shape(blocks[0].shape),
        in_specs=[SMEM] + [VMEM] * len(blocks) + [ANY] * len(token),
        out_specs=VMEM,
        compiler_params=PARAMS,
        cost_estimate=NO_COST,
        name="gather",
    )(names, *blocks, *token)


def far_part(anc, lens, query_ref, stage_refs, part, keys):
    acc_ref, max_ref, sum_ref = stage_refs
    local = anc.shape[0]
    span, rank = keys.shape[0] // local, acc_ref.shape[1]
    ends = [lens[anc[p]] for p in range(local)]
    seen = visible(query_ref.shape[0], ends, [lax.axis_index("seq") * span], span)
    known = [(column(max_ref[part]), column(sum_ref[part]), acc_ref[part])]
    return packed(*attend(query_ref[...], keys, seen, rank, known))


def give_kernel(stages, line, anc, lens, *refs):
    stage_refs, refs = refs[: 4 * stages], refs[4 * stages :]
    early_ref, late_ref, moved_ref, give_refs = refs[0], refs[1], refs[2], refs[3:]
    dom = lax.axis_index("dom")
    local = anc.shape[0]
    some = early_ref.shape[0] // local
    span, width = 2 * some, moved_ref.shape[1]
    rank = stage_refs[1].shape[1]

    def place(p, value):
        for h in range(2):
            rows, rope = pl.ds(p * span + h * some, some), 2 * rank + h * (width - rank)
            moved_ref[rows, :rank] = value[:, h * rank : (h + 1) * rank]
            moved_ref[rows, rank:] = value[:, rope : rope + width - rank]

    for p in range(local):
        if line:
            owner, slot = lax.div(anc[p], local), lax.rem(anc[p], local)
            apart = jnp.bitwise_xor(owner, dom)
            late = jnp.where(at_end(dom), apart != 0, apart == 1)
            slot = jnp.where(at_end(dom), p, slot)
            rows = pl.ds(pl.multiple_of(slot * some, some), some)

            @pl.when(late)
            def _():
                place(p, late_ref[rows])

            @pl.when(jnp.logical_not(late))
            def _():
                place(p, early_ref[pl.ds(p * some, some)])

        else:
            place(p, early_ref[pl.ds(p * some, some)])

    for k in range(stages):
        query_ref, *partial = stage_refs[4 * k : 4 * k + 4]
        rows = query_ref.shape[0]
        give_refs[k][...] = far_part(anc, lens, query_ref, partial, pl.ds(rows, rows), moved_ref[...])


def keep_kernel(stages, anc, lens, *refs):
    stage_refs, refs = refs[: 4 * stages], refs[4 * stages :]
    moved_ref, keep_refs, piece_refs = refs[0], refs[1 : 1 + stages], refs[1 + stages :]
    begin = 0
    for piece_ref in piece_refs:
        piece_ref[...] = moved_ref[pl.ds(begin, piece_ref.shape[0])]
        begin += piece_ref.shape[0]
    for k in range(stages):
        query_ref, *partial = stage_refs[4 * k : 4 * k + 4]
        rows = query_ref.shape[0]
        keep_refs[k][...] = far_part(anc, lens, query_ref, partial, pl.ds(0, rows), moved_ref[...])


def head_products(latent, w_ref, local):
    heads, _, reach = w_ref.shape
    first = lax.broadcasted_iota(jnp.int32, (2 * local, reach), 0) < local
    products = []
    for h in range(0, heads, 2):
        weights = jnp.concatenate([w_ref[h], w_ref[h + 1]], axis=1)
        both = jnp.dot(latent[h * local : (h + 2) * local], weights, preferred_element_type=F32)
        products.append(jnp.where(first, both[:, :reach], both[:, reach:]))
    return jnp.concatenate(products, axis=0)


def near_kernel(anc, lens, fresh_ref, w_ref, *refs):
    seq = lax.axis_index("seq")
    query_ref, acc_ref, max_ref, sum_ref, got_ref, moved_ref, *other_refs = refs[:-3]
    cache_ref, value_ref, level_ref = refs[-3:]
    local, span, width = cache_ref.shape
    rank = acc_ref.shape[1]
    start, other = seq * span, jnp.bitwise_xor(seq, 1) * span
    ends = [lens[anc[p]] for p in range(local)]
    keys = jnp.concatenate([ref[...] for ref in (moved_ref, *other_refs)], axis=0)
    seen = visible(query_ref.shape[0], ends, [start, other], span)
    level = jnp.sum(got_ref[:, rank:].astype(F32), axis=1, keepdims=True)
    known = [
        (column(max_ref[...]), column(sum_ref[...]), acc_ref[...]),
        (level, 1.0, got_ref[:, :rank].astype(F32)),
    ]
    values, level = attend(query_ref[...], keys, seen, rank, known)
    value_ref[...] = head_products(values.astype(BF16), w_ref, local)
    level_ref[...] = jnp.broadcast_to(level, level_ref.shape)
    for p in range(local):
        at = start + lax.broadcasted_iota(jnp.int32, (span, 1), 0) == ends[p]
        cache_ref[p] = jnp.where(at, fresh_ref[pl.ds(p, 1), :], moved_ref[pl.ds(p * span, span)])


def chip_kernel(count, *refs):
    for k in range(count):
        value_ref, level_ref = refs[2 * count + 2 * k : 2 * count + 2 * k + 2]
        values, level = merged([unpacked(refs[k][...]), unpacked(refs[count + k][...])])
        value_ref[...] = values.astype(BF16)
        kept = jnp.where(diagonal(values.shape[0], level_ref.shape[1]), level, 0.0)
        level_ref[...] = jnp.broadcast_to(jnp.sum(kept, axis=0, keepdims=True), level_ref.shape)


def chip_merge(keep, got):
    rows, rank = keep[0].shape[0], keep[0].shape[1] - LANES
    return pl.pallas_call(
        functools.partial(chip_kernel, len(keep)),
        out_shape=[shape((rows, rank)), shape((8, max(rows, LANES)), F32)] * len(keep),
        in_specs=[VMEM] * (2 * len(keep)),
        out_specs=[VMEM] * (2 * len(keep)),
        compiler_params=PARAMS,
        name="chip_merge",
    )(*keep, *got)


def final_kernel(count, *refs):
    part_refs, (value_ref, level_ref, w_ref, out_ref, values) = refs[: 2 * count], refs[2 * count :]
    heads, rank, reach = w_ref.shape
    local = out_ref.shape[0]
    parts = [(value_ref[...], column(level_ref[...]))]
    for k in range(count):
        row = part_refs[2 * k + 1][0:1]
        kept = jnp.where(diagonal(value_ref.shape[0], row.shape[1]), row, 0.0)
        products = head_products(part_refs[2 * k][...], w_ref, local)
        parts.append((products, jnp.sum(kept, axis=1, keepdims=True)))
    values[...] = merged(parts)[0]
    for p in range(local):
        out_ref[p] = values[pl.ds(p, heads, stride=local), :].astype(BF16)


def on_device(q_nope, q_rope, w_uk, w_uv, prefix, private_caches, new_latent, ancestors, lengths):
    local, heads, nope = q_nope.shape
    span, width = private_caches.shape[1:]
    rank, reach = w_uv.shape[1:]
    rows = local * heads
    seq_size, dom_size = lax.axis_size("seq"), lax.axis_size("dom")
    cores = 2
    chips = seq_size // cores
    block = pl.pallas_call(
        pack_kernel,
        out_shape=shape((local * span // 2, 2 * width)),
        in_specs=[VMEM],
        out_specs=VMEM,
        compiler_params=PARAMS,
        cost_estimate=pl.CostEstimate(flops=PACK, bytes_accessed=0, transcendentals=0),
        name="pack",
    )(private_caches)
    nope_rows, rope_rows = (jnp.swapaxes(q, 0, 1).reshape(rows, -1) for q in (q_nope, q_rope))
    line = dom_size == 4
    if line:
        swap = [(0, 1), (1, 0), (2, 3), (3, 2)]
        middle = lax.ppermute(block, "dom", [(0, 2), (3, 1)])
        far = lax.ppermute(private_caches, "dom", [(1, 2), (2, 1)])
        theirs = lax.ppermute(ancestors, "dom", [(0, 1), (3, 2)])
    else:
        blocks = [block] + [
            lax.ppermute(block, "dom", [(i, (i + k) % dom_size) for i in range(dom_size)])
            for k in range(1, dom_size)
        ]

    own = pl.pallas_call(
        functools.partial(project_kernel, local),
        out_shape=shape((rows, width)),
        in_specs=[VMEM] * 3,
        out_specs=VMEM,
        compiler_params=PARAMS,
        cost_estimate=pl.CostEstimate(flops=PROJECT, bytes_accessed=0, transcendentals=0),
        name="project",
    )(nope_rows, rope_rows, w_uk)
    keys = prefix.T

    def pairs(turn, flip):
        return [
            (x * cores + c, (x + turn) % chips * cores + (c ^ flip))
            for x in range(chips)
            for c in range(cores)
        ]

    def back(turn, flip):
        return [(b, a) for a, b in pairs(turn, flip)]

    routes = [(t, f) for t in range(chips) for f in range(cores)]
    queries = [own if r == (0, 0) else lax.ppermute(own, "seq", pairs(*r)) for r in routes]
    stages = []
    for t in range(chips):
        asked = queries[2 * t : 2 * t + 2]
        stage = [*asked, *prefix_attention(asked, keys, rank, t == 0)]
        stages.append(stage)
        if t == 0:
            given = lax.ppermute(stage.pop(), "seq", pairs(0, 1))
        if line and t == 0:
            chosen = gathered(theirs, [block, middle, far], line, stage[3])
            late = lax.ppermute(chosen, "dom", swap)
            early = gathered(ancestors, [block, middle, far], line)
    if not line:
        early = late = gathered(ancestors, blocks, line)

    part = shape((rows, rank + LANES))
    others = chips - 1
    given, early = lax.optimization_barrier((given, early))
    giving = [a for stage in stages[1:] for a in stage[1:]]
    keeping = [a for stage in stages[1:] for a in (stage[0], *stage[2:])]
    moved, *give = pl.pallas_call(
        functools.partial(give_kernel, others, line),
        out_shape=[shape((local * span, width))] + [part] * others,
        in_specs=[SMEM] * 2 + [VMEM] * (len(giving) + 2),
        out_specs=[VMEM] * (1 + others),
        compiler_params=PARAMS,
        name="suffix_give",
    )(ancestors, lengths, *giving, early, late)
    small = local * span // 48 * 16
    cuts = (local * span - 2 * small, small, small)
    keep_and_pieces = pl.pallas_call(
        functools.partial(keep_kernel, others),
        out_shape=[part] * others + [shape((cut, width)) for cut in cuts],
        in_specs=[SMEM] * 2 + [VMEM] * (len(keeping) + 1),
        out_specs=[VMEM] * (others + len(cuts)),
        compiler_params=PARAMS,
        name="suffix_keep",
    )(ancestors, lengths, *keeping, moved)
    keep, pieces = keep_and_pieces[:others], keep_and_pieces[others:]
    sums = chip_merge(keep, [lax.ppermute(g, "seq", pairs(0, 1)) for g in give])
    parts = [lax.ppermute(s, "seq", back(1 + i // 2, 0)) for i, s in enumerate(sums)]
    other = [lax.ppermute(piece, "seq", pairs(0, 1)) for piece in pieces]

    moved, _ = lax.optimization_barrier((moved, sums[0]))
    query, _, acc, level, mass = stages[0]
    new_caches, *own_part = pl.pallas_call(
        near_kernel,
        out_shape=[shape(private_caches.shape), shape((rows, reach), F32), shape((rows, LANES), F32)],
        in_specs=[SMEM] * 2 + [VMEM] * (8 + len(other)),
        out_specs=[VMEM] * 3,
        compiler_params=PARAMS,
        cost_estimate=NO_COST,
        name="suffix_near",
    )(ancestors, lengths, new_latent, w_uv, query, acc, level, mass, given, moved, *other)
    parts += own_part

    head_values = pl.pallas_call(
        functools.partial(final_kernel, others),
        out_shape=shape((local, heads, reach)),
        in_specs=[VMEM] * (2 * chips + 1),
        out_specs=VMEM,
        scratch_shapes=[pltpu.VMEM((rows, reach), F32)],
        compiler_params=PARAMS,
        name="final",
    )(*parts, w_uv)
    return (head_values, new_caches)


def solution(mesh):
    placed = (
        P(("group", "dom"), "seq", None),
        P(("group", "dom"), "seq", None),
        P("seq", None, None),
        P("seq", None, None),
        P(("group", "seq"), None),
        P(("group", "dom"), "seq", None),
        P(("group", "dom"), None),
        P(("group", "dom")),
        P("group"),
    )
    return jax.shard_map(
        on_device,
        mesh=mesh,
        in_specs=placed,
        out_specs=(P(("group", "dom"), "seq", None), P(("group", "dom"), "seq", None)),
        check_vma=False,
    )
```

```python
import functools
import math

import jax
import jax.numpy as jnp
from jax import lax
from jax.experimental import pallas as pl
from jax.experimental.pallas import tpu as pltpu
from jax.sharding import PartitionSpec as P

ROPE = 64
NOPE = 128
SCALE2 = (NOPE + ROPE) ** (-0.5) * math.log2(math.e)
HIDDEN = -1e30
LANES = 128
F32 = jnp.float32
BF16 = jnp.bfloat16
NT = (((1,), (1,)), ((), ()))

VMEM = pl.BlockSpec(memory_space=pltpu.VMEM)
SMEM = pl.BlockSpec(memory_space=pltpu.SMEM)
ANY = pl.BlockSpec(memory_space=pl.ANY)
HBM = pl.BlockSpec(memory_space=pltpu.HBM)
PARAMS = pltpu.CompilerParams(vmem_limit_bytes=40 * 1024 * 1024)
NO_COST = pl.CostEstimate(flops=0, bytes_accessed=0, transcendentals=0)
PACK = 8_000_000_000
PROJECT = 8_000_000_000


def shape(dims, dtype=BF16):
    return jax.ShapeDtypeStruct(dims, dtype)


def pack_slot(rows, out_ref, part):
    some, width = rows.shape[0] // 2, rows.shape[1]
    rank = width - ROPE
    first, second = rows[:some], rows[some:]
    out_ref[part, :rank] = first[:, :rank]
    out_ref[part, rank : 2 * rank] = second[:, :rank]
    out_ref[part, 2 * rank :] = jnp.concatenate([first[:, rank:], second[:, rank:]], axis=1)


def pack_kernel(cache_ref, out_ref):
    local, span, _ = cache_ref.shape
    for p in range(local):
        pack_slot(cache_ref[p], out_ref, pl.ds(p * span // 2, span // 2))


def project_kernel(local, nope_ref, rope_ref, w_ref, own_ref):
    heads, _, rank = w_ref.shape
    nope = nope_ref[...].astype(F32)
    width = nope.shape[1]
    first = lax.broadcasted_iota(jnp.int32, (2 * local, width), 0) < local

    def pair(h):
        two = nope[h * local : (h + 2) * local]
        left = jnp.concatenate([jnp.where(first, two, 0.0), jnp.where(first, 0.0, two)], axis=1)
        weights = w_ref[pl.ds(h, 2)].reshape(2 * width, rank)
        return jnp.dot(left.astype(BF16), weights, preferred_element_type=F32)

    own_ref[:, rank:] = rope_ref[...]
    for h in range(0, heads, 4):
        own_ref[pl.ds(h * local, 4 * local), :rank] = jnp.concatenate(
            [pair(i) for i in (h, h + 2)], axis=0
        ).astype(BF16)


def prefix_kernel(count, tiles, *refs):
    query_refs = refs[:count]
    keys_ref, out_ref, max_ref, sum_ref, *give_ref, acc_ref = refs[count:]
    rank = acc_ref.shape[1]
    tile = keys_ref.shape[1] // tiles
    parts = [pl.ds(i * tile, tile) for i in range(tiles)]
    queries = jnp.concatenate([ref[...] for ref in query_refs], axis=0)

    def score(i):
        return jnp.dot(queries, keys_ref[:, parts[i]], preferred_element_type=F32) * SCALE2

    ahead = score(0)
    for i in range(tiles):
        scores = ahead
        if i + 1 < tiles:
            ahead = score(i + 1)
        top = jnp.max(scores, axis=1, keepdims=True)
        if i > 0:
            top = jnp.maximum(top, largest)
        weights = jnp.exp2(scores - top)
        total = jnp.sum(weights, axis=1, keepdims=True)
        acc = lax.dot_general(
            weights.astype(BF16), keys_ref[:rank, parts[i]], NT, preferred_element_type=F32
        )
        if i > 0:
            factor = jnp.exp2(largest - top)
            total = total + running * factor
            acc = acc + acc_ref[...] * factor
        largest, running = top, total
        if i < tiles - 1:
            acc_ref[...] = acc
    kept = out_ref.shape[0]
    out_ref[...] = acc[:kept]
    max_ref[...] = jnp.broadcast_to(largest[:kept], max_ref.shape)
    sum_ref[...] = jnp.broadcast_to(running[:kept], sum_ref.shape)
    if give_ref:
        level = largest[kept:] + jnp.log2(running[kept:])
        give_ref[0][...] = packed(acc[kept:] * (1.0 / running[kept:]), level)


def prefix_attention(queries, keys, rank, give, tiles=4):
    rows = sum(q.shape[0] for q in queries)
    kept = queries[0].shape[0] if give else rows
    width, length = keys.shape
    out = [shape((kept, rank), F32)] + [shape((kept, LANES), F32)] * 2
    if give:
        out.append(shape((rows - kept, rank + LANES)))
    return pl.pallas_call(
        functools.partial(prefix_kernel, len(queries), tiles),
        out_shape=out,
        in_specs=[VMEM] * (len(queries) + 1),
        out_specs=[VMEM] * len(out),
        scratch_shapes=[pltpu.VMEM((rows, rank), F32)],
        compiler_params=PARAMS,
        cost_estimate=pl.CostEstimate(
            flops=0 if give else 2 * rows * length * (width + rank),
            bytes_accessed=0 if give else 2 * width * length,
            transcendentals=0 if give else rows * length,
        ),
        name="prefix_attention",
    )(*queries, keys)


def packed(values, level):
    rows = values.shape[0]
    lane = lax.broadcasted_iota(jnp.int32, (rows, LANES), 1)
    high = level.astype(BF16).astype(F32)
    middle = (level - high).astype(BF16).astype(F32)
    low = level - high - middle
    stats = jnp.where(lane == 0, high, jnp.where(lane == 1, middle, jnp.where(lane == 2, low, 0.0)))
    return jnp.concatenate([values.astype(BF16), stats.astype(BF16)], axis=1)


def unpacked(part):
    rank = part.shape[1] - LANES
    return part[:, :rank].astype(F32), jnp.sum(part[:, rank:].astype(F32), axis=1, keepdims=True)


def merged(parts):
    levels = [level for _, level in parts]
    top = functools.reduce(jnp.maximum, levels)
    shares = [jnp.exp2(level - top) for level in levels]
    whole = functools.reduce(jnp.add, shares)
    acc = functools.reduce(jnp.add, [share * values for share, (values, _) in zip(shares, parts)])
    return acc * (1.0 / whole), top + jnp.log2(whole)


def column(stat):
    return jnp.max(stat, axis=1, keepdims=True)


def diagonal(rows, lanes):
    row = lax.broadcasted_iota(jnp.int32, (rows, lanes), 0)
    return row == lax.broadcasted_iota(jnp.int32, (rows, lanes), 1)


def visible(rows, ends, starts, span):
    local = len(ends)
    cols = len(starts) * local * span
    col = lax.broadcasted_iota(jnp.int32, (1, cols), 1)
    col_of = jnp.zeros_like(col)
    limit = jnp.full_like(col, ends[0] - starts[0])
    for at in range(1, len(starts) * local):
        begin, p = at * span, at % local
        later = col >= begin
        col_of = jnp.where(later, p, col_of)
        limit = jnp.where(later, ends[p] - starts[at // local] + begin, limit)
    col_of = jnp.where(col < limit, col_of, -1)
    row_of = lax.rem(lax.broadcasted_iota(jnp.int32, (rows, 1), 0), local)
    return row_of == col_of


def attend(queries, keys, seen, rank, known):
    scores = lax.dot_general(queries, keys, NT, preferred_element_type=F32)
    scores = jnp.where(seen, scores * SCALE2, HIDDEN)
    top = jnp.max(scores, axis=1, keepdims=True)
    for level, _, _ in known:
        top = jnp.maximum(top, level)
    weights = jnp.where(seen, jnp.exp2(scores - top), 0.0)
    total = jnp.sum(weights, axis=1, keepdims=True)
    acc = jnp.dot(weights.astype(BF16), keys[:, :rank], preferred_element_type=F32)
    for level, mass, part in known:
        factor = jnp.exp2(level - top)
        total = total + mass * factor
        acc = acc + part * factor
    return acc * (1.0 / total), top + jnp.log2(total)


def at_end(dom):
    return (dom == 0) | (dom == 3)


def picked(row, at):
    lane = lax.broadcasted_iota(jnp.int32, row.shape, 1)
    return jnp.sum(jnp.where(lane == at, row.astype(F32), 0.0)).astype(jnp.int32)


def gather_kernel(line, chosen, local, names_ref, *refs):
    block_refs, out_ref = refs[:-1], refs[-1]
    if chosen:
        block_refs = block_refs[:-1]
    dom = lax.axis_index("dom")
    names = [picked(names_ref[...], p) for p in range(local)]
    some = out_ref.shape[0] // local
    for p in range(local):
        owner, slot = lax.div(names[p], local), lax.rem(names[p], local)
        if line:
            apart = jnp.bitwise_xor(owner, dom)
            which = jnp.where(at_end(dom), 0, jnp.maximum(apart - 1, 0))
            if chosen:
                slot = jnp.where(at_end(dom), p, slot)
        else:
            which = lax.rem(dom - owner + len(block_refs), len(block_refs))
        rows = pl.ds(pl.multiple_of(slot * some, some), some)
        for k, block_ref in enumerate(block_refs):

            @pl.when(which == k)
            def _():
                part = pl.ds(p * some, some)
                if len(block_ref.shape) == 2:
                    out_ref[part] = block_ref[rows]
                else:
                    pack_slot(block_ref[slot], out_ref, part)


def gathered(names, blocks, line, local, token=None):
    token = [] if token is None else [token]
    return pl.pallas_call(
        functools.partial(gather_kernel, line, bool(token), local),
        out_shape=shape(blocks[0].shape),
        in_specs=[VMEM] * (1 + len(blocks)) + [ANY] * len(token),
        out_specs=VMEM,
        compiler_params=PARAMS,
        cost_estimate=NO_COST,
        name="gather",
    )(names, *blocks, *token)


def far_part(ends, query_ref, stage_refs, part, keys):
    acc_ref, max_ref, sum_ref = stage_refs
    span, rank = keys.shape[0] // len(ends), acc_ref.shape[1]
    seen = visible(query_ref.shape[0], ends, [lax.axis_index("seq") * span], span)
    known = [(column(max_ref[part]), column(sum_ref[part]), acc_ref[part])]
    return packed(*attend(query_ref[...], keys, seen, rank, known))


def give_kernel(stages, line, local, names_ref, lens_ref, *refs):
    stage_refs, refs = refs[: 4 * stages], refs[4 * stages :]
    early_ref, late_ref, moved_ref, give_refs = refs[0], refs[1], refs[2], refs[3:]
    dom = lax.axis_index("dom")
    anc = [picked(names_ref[...], p) for p in range(local)]
    some = early_ref.shape[0] // local
    span, width = 2 * some, moved_ref.shape[1]
    rank = stage_refs[1].shape[1]

    def place(p, value):
        for h in range(2):
            rows, rope = pl.ds(p * span + h * some, some), 2 * rank + h * (width - rank)
            moved_ref[rows, :rank] = value[:, h * rank : (h + 1) * rank]
            moved_ref[rows, rank:] = value[:, rope : rope + width - rank]

    for p in range(local):
        if line:
            owner, slot = lax.div(anc[p], local), lax.rem(anc[p], local)
            apart = jnp.bitwise_xor(owner, dom)
            late = jnp.where(at_end(dom), apart != 0, apart == 1)
            slot = jnp.where(at_end(dom), p, slot)
            rows = pl.ds(pl.multiple_of(slot * some, some), some)

            @pl.when(late)
            def _():
                place(p, late_ref[rows])

            @pl.when(jnp.logical_not(late))
            def _():
                place(p, early_ref[pl.ds(p * some, some)])

        else:
            place(p, early_ref[pl.ds(p * some, some)])

    for k in range(stages):
        query_ref, *partial = stage_refs[4 * k : 4 * k + 4]
        rows = query_ref.shape[0]
        ends = [picked(lens_ref[...], anc[p]) for p in range(local)]
        give_refs[k][...] = far_part(ends, query_ref, partial, pl.ds(rows, rows), moved_ref[...])


def keep_kernel(stages, anc, lens, *refs):
    stage_refs, refs = refs[: 4 * stages], refs[4 * stages :]
    moved_ref, keep_refs, piece_refs = refs[0], refs[1 : 1 + stages], refs[1 + stages :]
    begin = 0
    for piece_ref in piece_refs:
        piece_ref[...] = moved_ref[pl.ds(begin, piece_ref.shape[0])]
        begin += piece_ref.shape[0]
    for k in range(stages):
        query_ref, *partial = stage_refs[4 * k : 4 * k + 4]
        rows = query_ref.shape[0]
        ends = [lens[anc[p]] for p in range(anc.shape[0])]
        keep_refs[k][...] = far_part(ends, query_ref, partial, pl.ds(0, rows), moved_ref[...])


def head_products(latent, w_ref, local):
    heads, _, reach = w_ref.shape
    first = lax.broadcasted_iota(jnp.int32, (2 * local, reach), 0) < local
    products = []
    for h in range(0, heads, 2):
        weights = jnp.concatenate([w_ref[h], w_ref[h + 1]], axis=1)
        both = jnp.dot(latent[h * local : (h + 2) * local], weights, preferred_element_type=F32)
        products.append(jnp.where(first, both[:, :reach], both[:, reach:]))
    return jnp.concatenate(products, axis=0)


def near_kernel(anc, lens, fresh_ref, w_ref, *refs):
    seq = lax.axis_index("seq")
    query_ref, acc_ref, max_ref, sum_ref, got_ref, moved_ref, *other_refs = refs[:-3]
    cache_ref, value_ref, level_ref = refs[-3:]
    local, span, width = cache_ref.shape
    rank = acc_ref.shape[1]
    start, other = seq * span, jnp.bitwise_xor(seq, 1) * span
    ends = [lens[anc[p]] for p in range(local)]
    keys = jnp.concatenate([ref[...] for ref in (moved_ref, *other_refs)], axis=0)
    seen = visible(query_ref.shape[0], ends, [start, other], span)
    level = jnp.sum(got_ref[:, rank:].astype(F32), axis=1, keepdims=True)
    known = [
        (column(max_ref[...]), column(sum_ref[...]), acc_ref[...]),
        (level, 1.0, got_ref[:, :rank].astype(F32)),
    ]
    values, level = attend(query_ref[...], keys, seen, rank, known)
    value_ref[...] = head_products(values.astype(BF16), w_ref, local)
    level_ref[...] = jnp.broadcast_to(level, level_ref.shape)
    for p in range(local):
        at = start + lax.broadcasted_iota(jnp.int32, (span, 1), 0) == ends[p]
        cache_ref[p] = jnp.where(at, fresh_ref[pl.ds(p, 1), :], moved_ref[pl.ds(p * span, span)])


def chip_kernel(count, *refs):
    for k in range(count):
        value_ref, level_ref = refs[2 * count + 2 * k : 2 * count + 2 * k + 2]
        values, level = merged([unpacked(refs[k][...]), unpacked(refs[count + k][...])])
        value_ref[...] = values.astype(BF16)
        kept = jnp.where(diagonal(values.shape[0], level_ref.shape[1]), level, 0.0)
        level_ref[...] = jnp.broadcast_to(jnp.sum(kept, axis=0, keepdims=True), level_ref.shape)


def chip_merge(keep, got):
    rows, rank = keep[0].shape[0], keep[0].shape[1] - LANES
    return pl.pallas_call(
        functools.partial(chip_kernel, len(keep)),
        out_shape=[shape((rows, rank)), shape((8, max(rows, LANES)), F32)] * len(keep),
        in_specs=[VMEM] * (2 * len(keep)),
        out_specs=[VMEM] * (2 * len(keep)),
        compiler_params=PARAMS,
        name="chip_merge",
    )(*keep, *got)


def final_kernel(count, *refs):
    part_refs, (value_ref, level_ref, w_ref, out_ref, values) = refs[: 2 * count], refs[2 * count :]
    heads, rank, reach = w_ref.shape
    local = out_ref.shape[0]
    parts = [(value_ref[...], column(level_ref[...]))]
    for k in range(count):
        row = part_refs[2 * k + 1][0:1]
        kept = jnp.where(diagonal(value_ref.shape[0], row.shape[1]), row, 0.0)
        products = head_products(part_refs[2 * k][...], w_ref, local)
        parts.append((products, jnp.sum(kept, axis=1, keepdims=True)))
    values[...] = merged(parts)[0]
    for p in range(local):
        out_ref[p] = values[pl.ds(p, heads, stride=local), :].astype(BF16)


def on_device(q_nope, q_rope, w_uk, w_uv, prefix, private_caches, new_latent, ancestors, lengths):
    local, heads, nope = q_nope.shape
    span, width = private_caches.shape[1:]
    rank, reach = w_uv.shape[1:]
    rows = local * heads
    seq_size, dom_size = lax.axis_size("seq"), lax.axis_size("dom")
    cores = 2
    chips = seq_size // cores
    block = pl.pallas_call(
        pack_kernel,
        out_shape=shape((local * span // 2, 2 * width)),
        in_specs=[VMEM],
        out_specs=VMEM,
        compiler_params=PARAMS,
        cost_estimate=pl.CostEstimate(flops=PACK, bytes_accessed=0, transcendentals=0),
        name="pack",
    )(private_caches)
    nope_rows, rope_rows = (jnp.swapaxes(q, 0, 1).reshape(rows, -1) for q in (q_nope, q_rope))
    names = jnp.pad(ancestors, (0, LANES - local))[None]
    line = dom_size == 4
    if line:
        swap = [(0, 1), (1, 0), (2, 3), (3, 2)]
        middle = lax.ppermute(block, "dom", [(0, 2), (3, 1)])
        far = lax.ppermute(private_caches, "dom", [(1, 2), (2, 1)])
        theirs = lax.ppermute(names, "dom", [(0, 1), (3, 2)])
    else:
        blocks = [block] + [
            lax.ppermute(block, "dom", [(i, (i + k) % dom_size) for i in range(dom_size)])
            for k in range(1, dom_size)
        ]

    own = pl.pallas_call(
        functools.partial(project_kernel, local),
        out_shape=shape((rows, width)),
        in_specs=[VMEM] * 3,
        out_specs=VMEM,
        compiler_params=PARAMS,
        cost_estimate=pl.CostEstimate(flops=PROJECT, bytes_accessed=0, transcendentals=0),
        name="project",
    )(nope_rows, rope_rows, w_uk)
    keys = prefix.T

    def pairs(turn, flip):
        return [
            (x * cores + c, (x + turn) % chips * cores + (c ^ flip))
            for x in range(chips)
            for c in range(cores)
        ]

    def back(turn, flip):
        return [(b, a) for a, b in pairs(turn, flip)]

    routes = [(t, f) for t in range(chips) for f in range(cores)]
    queries = [own if r == (0, 0) else lax.ppermute(own, "seq", pairs(*r)) for r in routes]
    stages = []
    for t in range(chips):
        asked = queries[2 * t : 2 * t + 2]
        stage = [*asked, *prefix_attention(asked, keys, rank, t == 0)]
        stages.append(stage)
        if t == 0:
            given = lax.ppermute(stage.pop(), "seq", pairs(0, 1))
        if line and t == 0:
            chosen = gathered(theirs, [block, middle, far], line, local, stage[3])
            late = lax.ppermute(chosen, "dom", swap)
            early = gathered(names, [block, middle, far], line, local)
    if not line:
        early = late = gathered(names, blocks, line, local)

    part = shape((rows, rank + LANES))
    others = chips - 1
    given, early = lax.optimization_barrier((given, early))
    giving = [a for stage in stages[1:] for a in stage[1:]]
    keeping = [a for stage in stages[1:] for a in (stage[0], *stage[2:])]
    moved, *give = pl.pallas_call(
        functools.partial(give_kernel, others, line, local),
        out_shape=[shape((local * span, width))] + [part] * others,
        in_specs=[VMEM] * (len(giving) + 4),
        out_specs=[VMEM] * (1 + others),
        compiler_params=PARAMS,
        name="suffix_give",
    )(names, jnp.pad(lengths, (0, max(0, LANES - lengths.shape[0])))[None], *giving, early, late)
    small = local * span // 48 * 16
    cuts = (local * span - 2 * small, small, small)
    keep_and_pieces = pl.pallas_call(
        functools.partial(keep_kernel, others),
        out_shape=[part] * others + [shape((cut, width)) for cut in cuts],
        in_specs=[SMEM] * 2 + [VMEM] * (len(keeping) + 1),
        out_specs=[VMEM] * (others + len(cuts)),
        compiler_params=PARAMS,
        name="suffix_keep",
    )(ancestors, lengths, *keeping, moved)
    keep, pieces = keep_and_pieces[:others], keep_and_pieces[others:]
    sums = chip_merge(keep, [lax.ppermute(g, "seq", pairs(0, 1)) for g in give])
    parts = [lax.ppermute(s, "seq", back(1 + i // 2, 0)) for i, s in enumerate(sums)]
    other = [lax.ppermute(piece, "seq", pairs(0, 1)) for piece in pieces]

    moved, _ = lax.optimization_barrier((moved, sums[0]))
    query, _, acc, level, mass = stages[0]
    new_caches, *own_part = pl.pallas_call(
        near_kernel,
        out_shape=[shape(private_caches.shape), shape((rows, reach), F32), shape((rows, LANES), F32)],
        in_specs=[SMEM] * 2 + [VMEM] * (8 + len(other)),
        out_specs=[VMEM] * 3,
        compiler_params=PARAMS,
        cost_estimate=NO_COST,
        name="suffix_near",
    )(ancestors, lengths, new_latent, w_uv, query, acc, level, mass, given, moved, *other)
    parts += own_part

    head_values = pl.pallas_call(
        functools.partial(final_kernel, others),
        out_shape=shape((local, heads, reach)),
        in_specs=[VMEM] * (2 * chips + 1),
        out_specs=VMEM,
        scratch_shapes=[pltpu.VMEM((rows, reach), F32)],
        compiler_params=PARAMS,
        name="final",
    )(*parts, w_uv)
    return (head_values, new_caches)


def solution(mesh):
    placed = (
        P(("group", "dom"), "seq", None),
        P(("group", "dom"), "seq", None),
        P("seq", None, None),
        P("seq", None, None),
        P(("group", "seq"), None),
        P(("group", "dom"), "seq", None),
        P(("group", "dom"), None),
        P(("group", "dom")),
        P("group"),
    )
    return jax.shard_map(
        on_device,
        mesh=mesh,
        in_specs=placed,
        out_specs=(P(("group", "dom"), "seq", None), P(("group", "dom"), "seq", None)),
        check_vma=False,
    )
```

```python
import functools
import math

import jax
import jax.numpy as jnp
from jax import lax
from jax.experimental import pallas as pl
from jax.experimental.pallas import tpu as pltpu
from jax.sharding import PartitionSpec as P

ROPE = 64
NOPE = 128
SCALE2 = (NOPE + ROPE) ** (-0.5) * math.log2(math.e)
HIDDEN = -1e30
LANES = 128
F32 = jnp.float32
BF16 = jnp.bfloat16
NT = (((1,), (1,)), ((), ()))

VMEM = pl.BlockSpec(memory_space=pltpu.VMEM)
SMEM = pl.BlockSpec(memory_space=pltpu.SMEM)
ANY = pl.BlockSpec(memory_space=pl.ANY)
HBM = pl.BlockSpec(memory_space=pltpu.HBM)
PARAMS = pltpu.CompilerParams(vmem_limit_bytes=40 * 1024 * 1024)
NO_COST = pl.CostEstimate(flops=0, bytes_accessed=0, transcendentals=0)
PACK = 8_000_000_000
PROJECT = 8_000_000_000


def shape(dims, dtype=BF16):
    return jax.ShapeDtypeStruct(dims, dtype)


def pack_slot(rows, out_ref, part):
    some, width = rows.shape[0] // 2, rows.shape[1]
    rank = width - ROPE
    first, second = rows[:some], rows[some:]
    out_ref[part, :rank] = first[:, :rank]
    out_ref[part, rank : 2 * rank] = second[:, :rank]
    out_ref[part, 2 * rank :] = jnp.concatenate([first[:, rank:], second[:, rank:]], axis=1)


def pack_kernel(cache_ref, out_ref):
    local, span, _ = cache_ref.shape
    for p in range(local):
        pack_slot(cache_ref[p], out_ref, pl.ds(p * span // 2, span // 2))


def project_kernel(local, nope_ref, rope_ref, w_ref, own_ref):
    heads, _, rank = w_ref.shape
    nope = nope_ref[...].astype(F32)
    width = nope.shape[1]
    first = lax.broadcasted_iota(jnp.int32, (2 * local, width), 0) < local

    def pair(h):
        two = nope[h * local : (h + 2) * local]
        left = jnp.concatenate([jnp.where(first, two, 0.0), jnp.where(first, 0.0, two)], axis=1)
        weights = w_ref[pl.ds(h, 2)].reshape(2 * width, rank)
        return jnp.dot(left.astype(BF16), weights, preferred_element_type=F32)

    own_ref[:, rank:] = rope_ref[...]
    for h in range(0, heads, 4):
        own_ref[pl.ds(h * local, 4 * local), :rank] = jnp.concatenate(
            [pair(i) for i in (h, h + 2)], axis=0
        ).astype(BF16)


def prefix_kernel(count, tiles, *refs):
    query_refs = refs[:count]
    keys_ref, out_ref, max_ref, sum_ref, *give_ref, acc_ref = refs[count:]
    rank = acc_ref.shape[1]
    tile = keys_ref.shape[1] // tiles
    parts = [pl.ds(i * tile, tile) for i in range(tiles)]
    queries = jnp.concatenate([ref[...] for ref in query_refs], axis=0)

    def score(i):
        return jnp.dot(queries, keys_ref[:, parts[i]], preferred_element_type=F32) * SCALE2

    ahead = score(0)
    for i in range(tiles):
        scores = ahead
        if i + 1 < tiles:
            ahead = score(i + 1)
        top = jnp.max(scores, axis=1, keepdims=True)
        if i > 0:
            top = jnp.maximum(top, largest)
        weights = jnp.exp2(scores - top)
        total = jnp.sum(weights, axis=1, keepdims=True)
        acc = lax.dot_general(
            weights.astype(BF16), keys_ref[:rank, parts[i]], NT, preferred_element_type=F32
        )
        if i > 0:
            factor = jnp.exp2(largest - top)
            total = total + running * factor
            acc = acc + acc_ref[...] * factor
        largest, running = top, total
        if i < tiles - 1:
            acc_ref[...] = acc
    kept = out_ref.shape[0]
    out_ref[...] = acc[:kept]
    max_ref[...] = jnp.broadcast_to(largest[:kept], max_ref.shape)
    sum_ref[...] = jnp.broadcast_to(running[:kept], sum_ref.shape)
    if give_ref:
        level = largest[kept:] + jnp.log2(running[kept:])
        give_ref[0][...] = packed(acc[kept:] * (1.0 / running[kept:]), level)


def prefix_attention(queries, keys, rank, give, tiles=4):
    rows = sum(q.shape[0] for q in queries)
    kept = queries[0].shape[0] if give else rows
    width, length = keys.shape
    out = [shape((kept, rank), F32)] + [shape((kept, LANES), F32)] * 2
    if give:
        out.append(shape((rows - kept, rank + LANES)))
    return pl.pallas_call(
        functools.partial(prefix_kernel, len(queries), tiles),
        out_shape=out,
        in_specs=[VMEM] * (len(queries) + 1),
        out_specs=[VMEM] * len(out),
        scratch_shapes=[pltpu.VMEM((rows, rank), F32)],
        compiler_params=PARAMS,
        cost_estimate=pl.CostEstimate(
            flops=0 if give else 2 * rows * length * (width + rank),
            bytes_accessed=0 if give else 2 * width * length,
            transcendentals=0 if give else rows * length,
        ),
        name="prefix_attention",
    )(*queries, keys)


def packed(values, level):
    rows = values.shape[0]
    lane = lax.broadcasted_iota(jnp.int32, (rows, LANES), 1)
    high = level.astype(BF16).astype(F32)
    middle = (level - high).astype(BF16).astype(F32)
    low = level - high - middle
    stats = jnp.where(lane == 0, high, jnp.where(lane == 1, middle, jnp.where(lane == 2, low, 0.0)))
    return jnp.concatenate([values.astype(BF16), stats.astype(BF16)], axis=1)


def unpacked(part):
    rank = part.shape[1] - LANES
    return part[:, :rank].astype(F32), jnp.sum(part[:, rank:].astype(F32), axis=1, keepdims=True)


def merged(parts):
    levels = [level for _, level in parts]
    top = functools.reduce(jnp.maximum, levels)
    shares = [jnp.exp2(level - top) for level in levels]
    whole = functools.reduce(jnp.add, shares)
    acc = functools.reduce(jnp.add, [share * values for share, (values, _) in zip(shares, parts)])
    return acc * (1.0 / whole), top + jnp.log2(whole)


def column(stat):
    return jnp.max(stat, axis=1, keepdims=True)


def diagonal(rows, lanes):
    row = lax.broadcasted_iota(jnp.int32, (rows, lanes), 0)
    return row == lax.broadcasted_iota(jnp.int32, (rows, lanes), 1)


def visible(rows, ends, starts, span):
    local = len(ends)
    cols = len(starts) * local * span
    col = lax.broadcasted_iota(jnp.int32, (1, cols), 1)
    col_of = jnp.zeros_like(col)
    limit = jnp.full_like(col, ends[0] - starts[0])
    for at in range(1, len(starts) * local):
        begin, p = at * span, at % local
        later = col >= begin
        col_of = jnp.where(later, p, col_of)
        limit = jnp.where(later, ends[p] - starts[at // local] + begin, limit)
    col_of = jnp.where(col < limit, col_of, -1)
    row_of = lax.rem(lax.broadcasted_iota(jnp.int32, (rows, 1), 0), local)
    return row_of == col_of


def attend(queries, keys, seen, rank, known):
    scores = lax.dot_general(queries, keys, NT, preferred_element_type=F32)
    scores = jnp.where(seen, scores * SCALE2, HIDDEN)
    top = jnp.max(scores, axis=1, keepdims=True)
    for level, _, _ in known:
        top = jnp.maximum(top, level)
    weights = jnp.where(seen, jnp.exp2(scores - top), 0.0)
    total = jnp.sum(weights, axis=1, keepdims=True)
    acc = jnp.dot(weights.astype(BF16), keys[:, :rank], preferred_element_type=F32)
    for level, mass, part in known:
        factor = jnp.exp2(level - top)
        total = total + mass * factor
        acc = acc + part * factor
    return acc * (1.0 / total), top + jnp.log2(total)


def at_end(dom):
    return (dom == 0) | (dom == 3)


def picked(row, at):
    lane = lax.broadcasted_iota(jnp.int32, row.shape, 1)
    return jnp.sum(jnp.where(lane == at, row.astype(F32), 0.0)).astype(jnp.int32)


def gather_kernel(line, chosen, local, names_ref, *refs):
    block_refs, out_ref = refs[:-1], refs[-1]
    if chosen:
        block_refs = block_refs[:-1]
    dom = lax.axis_index("dom")
    names = [picked(names_ref[...], p) for p in range(local)]
    some = out_ref.shape[0] // local
    for p in range(local):
        owner, slot = lax.div(names[p], local), lax.rem(names[p], local)
        if line:
            apart = jnp.bitwise_xor(owner, dom)
            which = jnp.where(at_end(dom), 0, jnp.maximum(apart - 1, 0))
            if chosen:
                slot = jnp.where(at_end(dom), p, slot)
        else:
            which = lax.rem(dom - owner + len(block_refs), len(block_refs))
        rows = pl.ds(pl.multiple_of(slot * some, some), some)
        for k, block_ref in enumerate(block_refs):

            @pl.when(which == k)
            def _():
                part = pl.ds(p * some, some)
                if len(block_ref.shape) == 2:
                    out_ref[part] = block_ref[rows]
                else:
                    pack_slot(block_ref[slot], out_ref, part)


def gathered(names, blocks, line, local, token=None):
    token = [] if token is None else [token]
    return pl.pallas_call(
        functools.partial(gather_kernel, line, bool(token), local),
        out_shape=shape(blocks[0].shape),
        in_specs=[VMEM] * (1 + len(blocks)) + [ANY] * len(token),
        out_specs=VMEM,
        compiler_params=PARAMS,
        cost_estimate=NO_COST,
        name="gather",
    )(names, *blocks, *token)


def far_part(ends, query_ref, stage_refs, part, keys):
    acc_ref, max_ref, sum_ref = stage_refs
    span, rank = keys.shape[0] // len(ends), acc_ref.shape[1]
    seen = visible(query_ref.shape[0], ends, [lax.axis_index("seq") * span], span)
    known = [(column(max_ref[part]), column(sum_ref[part]), acc_ref[part])]
    return packed(*attend(query_ref[...], keys, seen, rank, known))


def give_kernel(stages, line, local, names_ref, lens_ref, *refs):
    stage_refs, refs = refs[: 4 * stages], refs[4 * stages :]
    early_ref, late_ref, moved_ref, give_refs = refs[0], refs[1], refs[2], refs[3:]
    dom = lax.axis_index("dom")
    anc = [picked(names_ref[...], p) for p in range(local)]
    some = early_ref.shape[0] // local
    span, width = 2 * some, moved_ref.shape[1]
    rank = stage_refs[1].shape[1]

    def place(p, value):
        for h in range(2):
            rows, rope = pl.ds(p * span + h * some, some), 2 * rank + h * (width - rank)
            moved_ref[rows, :rank] = value[:, h * rank : (h + 1) * rank]
            moved_ref[rows, rank:] = value[:, rope : rope + width - rank]

    for p in range(local):
        if line:
            owner, slot = lax.div(anc[p], local), lax.rem(anc[p], local)
            apart = jnp.bitwise_xor(owner, dom)
            late = jnp.where(at_end(dom), apart != 0, apart == 1)
            slot = jnp.where(at_end(dom), p, slot)
            rows = pl.ds(pl.multiple_of(slot * some, some), some)

            @pl.when(late)
            def _():
                place(p, late_ref[rows])

            @pl.when(jnp.logical_not(late))
            def _():
                place(p, early_ref[pl.ds(p * some, some)])

        else:
            place(p, early_ref[pl.ds(p * some, some)])

    for k in range(stages):
        query_ref, *partial = stage_refs[4 * k : 4 * k + 4]
        rows = query_ref.shape[0]
        ends = [picked(lens_ref[...], anc[p]) for p in range(local)]
        give_refs[k][...] = far_part(ends, query_ref, partial, pl.ds(rows, rows), moved_ref[...])


def keep_kernel(stages, local, names_ref, lens_ref, *refs):
    anc = [picked(names_ref[...], p) for p in range(local)]
    ends = [picked(lens_ref[...], at) for at in anc]
    stage_refs, refs = refs[: 4 * stages], refs[4 * stages :]
    moved_ref, keep_refs, piece_refs = refs[0], refs[1 : 1 + stages], refs[1 + stages :]
    begin = 0
    for piece_ref in piece_refs:
        piece_ref[...] = moved_ref[pl.ds(begin, piece_ref.shape[0])]
        begin += piece_ref.shape[0]
    for k in range(stages):
        query_ref, *partial = stage_refs[4 * k : 4 * k + 4]
        rows = query_ref.shape[0]
        keep_refs[k][...] = far_part(ends, query_ref, partial, pl.ds(0, rows), moved_ref[...])


def head_products(latent, w_ref, local):
    heads, _, reach = w_ref.shape
    first = lax.broadcasted_iota(jnp.int32, (2 * local, reach), 0) < local
    products = []
    for h in range(0, heads, 2):
        weights = jnp.concatenate([w_ref[h], w_ref[h + 1]], axis=1)
        both = jnp.dot(latent[h * local : (h + 2) * local], weights, preferred_element_type=F32)
        products.append(jnp.where(first, both[:, :reach], both[:, reach:]))
    return jnp.concatenate(products, axis=0)


def near_kernel(names_ref, lens_ref, fresh_ref, w_ref, *refs):
    seq = lax.axis_index("seq")
    query_ref, acc_ref, max_ref, sum_ref, got_ref, moved_ref, *other_refs = refs[:-3]
    cache_ref, value_ref, level_ref = refs[-3:]
    local, span, width = cache_ref.shape
    rank = acc_ref.shape[1]
    start, other = seq * span, jnp.bitwise_xor(seq, 1) * span
    ends = [picked(lens_ref[...], picked(names_ref[...], p)) for p in range(local)]
    keys = jnp.concatenate([ref[...] for ref in (moved_ref, *other_refs)], axis=0)
    seen = visible(query_ref.shape[0], ends, [start, other], span)
    level = jnp.sum(got_ref[:, rank:].astype(F32), axis=1, keepdims=True)
    known = [
        (column(max_ref[...]), column(sum_ref[...]), acc_ref[...]),
        (level, 1.0, got_ref[:, :rank].astype(F32)),
    ]
    values, level = attend(query_ref[...], keys, seen, rank, known)
    value_ref[...] = head_products(values.astype(BF16), w_ref, local)
    level_ref[...] = jnp.broadcast_to(level, level_ref.shape)
    for p in range(local):
        at = start + lax.broadcasted_iota(jnp.int32, (span, 1), 0) == ends[p]
        cache_ref[p] = jnp.where(at, fresh_ref[pl.ds(p, 1), :], moved_ref[pl.ds(p * span, span)])


def chip_kernel(count, *refs):
    for k in range(count):
        value_ref, level_ref = refs[2 * count + 2 * k : 2 * count + 2 * k + 2]
        values, level = merged([unpacked(refs[k][...]), unpacked(refs[count + k][...])])
        value_ref[...] = values.astype(BF16)
        kept = jnp.where(diagonal(values.shape[0], level_ref.shape[1]), level, 0.0)
        level_ref[...] = jnp.broadcast_to(jnp.sum(kept, axis=0, keepdims=True), level_ref.shape)


def chip_merge(keep, got):
    rows, rank = keep[0].shape[0], keep[0].shape[1] - LANES
    return pl.pallas_call(
        functools.partial(chip_kernel, len(keep)),
        out_shape=[shape((rows, rank)), shape((8, max(rows, LANES)), F32)] * len(keep),
        in_specs=[VMEM] * (2 * len(keep)),
        out_specs=[VMEM] * (2 * len(keep)),
        compiler_params=PARAMS,
        name="chip_merge",
    )(*keep, *got)


def final_kernel(count, *refs):
    part_refs, (value_ref, level_ref, w_ref, out_ref, values) = refs[: 2 * count], refs[2 * count :]
    heads, rank, reach = w_ref.shape
    local = out_ref.shape[0]
    parts = [(value_ref[...], column(level_ref[...]))]
    for k in range(count):
        row = part_refs[2 * k + 1][0:1]
        kept = jnp.where(diagonal(value_ref.shape[0], row.shape[1]), row, 0.0)
        products = head_products(part_refs[2 * k][...], w_ref, local)
        parts.append((products, jnp.sum(kept, axis=1, keepdims=True)))
    values[...] = merged(parts)[0]
    for p in range(local):
        out_ref[p] = values[pl.ds(p, heads, stride=local), :].astype(BF16)


def on_device(q_nope, q_rope, w_uk, w_uv, prefix, private_caches, new_latent, ancestors, lengths):
    local, heads, nope = q_nope.shape
    span, width = private_caches.shape[1:]
    rank, reach = w_uv.shape[1:]
    rows = local * heads
    seq_size, dom_size = lax.axis_size("seq"), lax.axis_size("dom")
    cores = 2
    chips = seq_size // cores
    block = pl.pallas_call(
        pack_kernel,
        out_shape=shape((local * span // 2, 2 * width)),
        in_specs=[VMEM],
        out_specs=VMEM,
        compiler_params=PARAMS,
        cost_estimate=pl.CostEstimate(flops=PACK, bytes_accessed=0, transcendentals=0),
        name="pack",
    )(private_caches)
    nope_rows, rope_rows = (jnp.swapaxes(q, 0, 1).reshape(rows, -1) for q in (q_nope, q_rope))
    names = jnp.pad(ancestors, (0, LANES - local))[None]
    limits = jnp.pad(lengths, (0, max(0, LANES - lengths.shape[0])))[None]
    line = dom_size == 4
    if line:
        swap = [(0, 1), (1, 0), (2, 3), (3, 2)]
        middle = lax.ppermute(block, "dom", [(0, 2), (3, 1)])
        far = lax.ppermute(private_caches, "dom", [(1, 2), (2, 1)])
        theirs = lax.ppermute(names, "dom", [(0, 1), (3, 2)])
    else:
        blocks = [block] + [
            lax.ppermute(block, "dom", [(i, (i + k) % dom_size) for i in range(dom_size)])
            for k in range(1, dom_size)
        ]

    own = pl.pallas_call(
        functools.partial(project_kernel, local),
        out_shape=shape((rows, width)),
        in_specs=[VMEM] * 3,
        out_specs=VMEM,
        compiler_params=PARAMS,
        cost_estimate=pl.CostEstimate(flops=PROJECT, bytes_accessed=0, transcendentals=0),
        name="project",
    )(nope_rows, rope_rows, w_uk)
    keys = prefix.T

    def pairs(turn, flip):
        return [
            (x * cores + c, (x + turn) % chips * cores + (c ^ flip))
            for x in range(chips)
            for c in range(cores)
        ]

    def back(turn, flip):
        return [(b, a) for a, b in pairs(turn, flip)]

    routes = [(t, f) for t in range(chips) for f in range(cores)]
    queries = [own if r == (0, 0) else lax.ppermute(own, "seq", pairs(*r)) for r in routes]
    stages = []
    for t in range(chips):
        asked = queries[2 * t : 2 * t + 2]
        stage = [*asked, *prefix_attention(asked, keys, rank, t == 0)]
        stages.append(stage)
        if t == 0:
            given = lax.ppermute(stage.pop(), "seq", pairs(0, 1))
        if line and t == 0:
            chosen = gathered(theirs, [block, middle, far], line, local, stage[3])
            late = lax.ppermute(chosen, "dom", swap)
            early = gathered(names, [block, middle, far], line, local)
    if not line:
        early = late = gathered(names, blocks, line, local)

    part = shape((rows, rank + LANES))
    others = chips - 1
    given, early = lax.optimization_barrier((given, early))
    giving = [a for stage in stages[1:] for a in stage[1:]]
    keeping = [a for stage in stages[1:] for a in (stage[0], *stage[2:])]
    moved, *give = pl.pallas_call(
        functools.partial(give_kernel, others, line, local),
        out_shape=[shape((local * span, width))] + [part] * others,
        in_specs=[VMEM] * (len(giving) + 4),
        out_specs=[VMEM] * (1 + others),
        compiler_params=PARAMS,
        name="suffix_give",
    )(names, limits, *giving, early, late)
    cuts = (local * span // 2,) * 2
    keep_and_pieces = pl.pallas_call(
        functools.partial(keep_kernel, others, local),
        out_shape=[part] * others + [shape((cut, width)) for cut in cuts],
        in_specs=[VMEM] * (len(keeping) + 3),
        out_specs=[VMEM] * (others + len(cuts)),
        compiler_params=PARAMS,
        name="suffix_keep",
    )(names, limits, *keeping, moved)
    keep, pieces = keep_and_pieces[:others], keep_and_pieces[others:]
    sums = chip_merge(keep, [lax.ppermute(g, "seq", pairs(0, 1)) for g in give])
    parts = [lax.ppermute(s, "seq", back(1 + i // 2, 0)) for i, s in enumerate(sums)]
    other = [lax.ppermute(piece, "seq", pairs(0, 1)) for piece in pieces]

    moved, _ = lax.optimization_barrier((moved, sums[0]))
    query, _, acc, level, mass = stages[0]
    new_caches, *own_part = pl.pallas_call(
        near_kernel,
        out_shape=[shape(private_caches.shape), shape((rows, reach), F32), shape((rows, LANES), F32)],
        in_specs=[VMEM] * (10 + len(other)),
        out_specs=[VMEM] * 3,
        compiler_params=PARAMS,
        cost_estimate=NO_COST,
        name="suffix_near",
    )(names, limits, new_latent, w_uv, query, acc, level, mass, given, moved, *other)
    parts += own_part

    head_values = pl.pallas_call(
        functools.partial(final_kernel, others),
        out_shape=shape((local, heads, reach)),
        in_specs=[VMEM] * (2 * chips + 1),
        out_specs=VMEM,
        scratch_shapes=[pltpu.VMEM((rows, reach), F32)],
        compiler_params=PARAMS,
        name="final",
    )(*parts, w_uv)
    return (head_values, new_caches)


def solution(mesh):
    placed = (
        P(("group", "dom"), "seq", None),
        P(("group", "dom"), "seq", None),
        P("seq", None, None),
        P("seq", None, None),
        P(("group", "seq"), None),
        P(("group", "dom"), "seq", None),
        P(("group", "dom"), None),
        P(("group", "dom")),
        P("group"),
    )
    return jax.shard_map(
        on_device,
        mesh=mesh,
        in_specs=placed,
        out_specs=(P(("group", "dom"), "seq", None), P(("group", "dom"), "seq", None)),
        check_vma=False,
    )
```

```python
import functools
import math

import jax
import jax.numpy as jnp
from jax import lax
from jax.experimental import pallas as pl
from jax.experimental.pallas import tpu as pltpu
from jax.sharding import PartitionSpec as P

ROPE = 64
NOPE = 128
SCALE2 = (NOPE + ROPE) ** (-0.5) * math.log2(math.e)
HIDDEN = -1e30
LANES = 128
F32 = jnp.float32
BF16 = jnp.bfloat16
NT = (((1,), (1,)), ((), ()))

VMEM = pl.BlockSpec(memory_space=pltpu.VMEM)
SMEM = pl.BlockSpec(memory_space=pltpu.SMEM)
ANY = pl.BlockSpec(memory_space=pl.ANY)
HBM = pl.BlockSpec(memory_space=pltpu.HBM)
PARAMS = pltpu.CompilerParams(vmem_limit_bytes=40 * 1024 * 1024)
NO_COST = pl.CostEstimate(flops=0, bytes_accessed=0, transcendentals=0)
PACK = 8_000_000_000
PROJECT = 8_000_000_000


def shape(dims, dtype=BF16):
    return jax.ShapeDtypeStruct(dims, dtype)


def pack_slot(rows, out_ref, part):
    some, width = rows.shape[0] // 2, rows.shape[1]
    rank = width - ROPE
    first, second = rows[:some], rows[some:]
    out_ref[part, :rank] = first[:, :rank]
    out_ref[part, rank : 2 * rank] = second[:, :rank]
    out_ref[part, 2 * rank :] = jnp.concatenate([first[:, rank:], second[:, rank:]], axis=1)


def pack_kernel(cache_ref, out_ref):
    local, span, _ = cache_ref.shape
    for p in range(local):
        pack_slot(cache_ref[p], out_ref, pl.ds(p * span // 2, span // 2))


def project_kernel(local, nope_ref, rope_ref, w_ref, own_ref):
    heads, _, rank = w_ref.shape
    nope = nope_ref[...].astype(F32)
    width = nope.shape[1]
    first = lax.broadcasted_iota(jnp.int32, (2 * local, width), 0) < local

    def pair(h):
        two = nope[h * local : (h + 2) * local]
        left = jnp.concatenate([jnp.where(first, two, 0.0), jnp.where(first, 0.0, two)], axis=1)
        weights = w_ref[pl.ds(h, 2)].reshape(2 * width, rank)
        return jnp.dot(left.astype(BF16), weights, preferred_element_type=F32)

    own_ref[:, rank:] = rope_ref[...]
    for h in range(0, heads, 4):
        own_ref[pl.ds(h * local, 4 * local), :rank] = jnp.concatenate(
            [pair(i) for i in (h, h + 2)], axis=0
        ).astype(BF16)


def prefix_kernel(count, tiles, *refs):
    query_refs = refs[:count]
    keys_ref, out_ref, max_ref, sum_ref, *give_ref, acc_ref = refs[count:]
    rank = acc_ref.shape[1]
    tile = keys_ref.shape[1] // tiles
    parts = [pl.ds(i * tile, tile) for i in range(tiles)]
    queries = jnp.concatenate([ref[...] for ref in query_refs], axis=0)

    def score(i):
        return jnp.dot(queries, keys_ref[:, parts[i]], preferred_element_type=F32) * SCALE2

    ahead = score(0)
    for i in range(tiles):
        scores = ahead
        if i + 1 < tiles:
            ahead = score(i + 1)
        top = jnp.max(scores, axis=1, keepdims=True)
        if i > 0:
            top = jnp.maximum(top, largest)
        weights = jnp.exp2(scores - top)
        total = jnp.sum(weights, axis=1, keepdims=True)
        acc = lax.dot_general(
            weights.astype(BF16), keys_ref[:rank, parts[i]], NT, preferred_element_type=F32
        )
        if i > 0:
            factor = jnp.exp2(largest - top)
            total = total + running * factor
            acc = acc + acc_ref[...] * factor
        largest, running = top, total
        if i < tiles - 1:
            acc_ref[...] = acc
    kept = out_ref.shape[0]
    out_ref[...] = acc[:kept]
    max_ref[...] = jnp.broadcast_to(largest[:kept], max_ref.shape)
    sum_ref[...] = jnp.broadcast_to(running[:kept], sum_ref.shape)
    if give_ref:
        level = largest[kept:] + jnp.log2(running[kept:])
        give_ref[0][...] = packed(acc[kept:] * (1.0 / running[kept:]), level)


def prefix_attention(queries, keys, rank, give, tiles=4):
    rows = sum(q.shape[0] for q in queries)
    kept = queries[0].shape[0] if give else rows
    width, length = keys.shape
    out = [shape((kept, rank), F32)] + [shape((kept, LANES), F32)] * 2
    if give:
        out.append(shape((rows - kept, rank + LANES)))
    return pl.pallas_call(
        functools.partial(prefix_kernel, len(queries), tiles),
        out_shape=out,
        in_specs=[VMEM] * (len(queries) + 1),
        out_specs=[VMEM] * len(out),
        scratch_shapes=[pltpu.VMEM((rows, rank), F32)],
        compiler_params=PARAMS,
        cost_estimate=pl.CostEstimate(
            flops=0 if give else 2 * rows * length * (width + rank),
            bytes_accessed=0 if give else 2 * width * length,
            transcendentals=0 if give else rows * length,
        ),
        name="prefix_attention",
    )(*queries, keys)


def packed(values, level):
    rows = values.shape[0]
    lane = lax.broadcasted_iota(jnp.int32, (rows, LANES), 1)
    high = level.astype(BF16).astype(F32)
    middle = (level - high).astype(BF16).astype(F32)
    low = level - high - middle
    stats = jnp.where(lane == 0, high, jnp.where(lane == 1, middle, jnp.where(lane == 2, low, 0.0)))
    return jnp.concatenate([values.astype(BF16), stats.astype(BF16)], axis=1)


def unpacked(part):
    rank = part.shape[1] - LANES
    return part[:, :rank].astype(F32), jnp.sum(part[:, rank:].astype(F32), axis=1, keepdims=True)


def merged(parts):
    levels = [level for _, level in parts]
    top = functools.reduce(jnp.maximum, levels)
    shares = [jnp.exp2(level - top) for level in levels]
    whole = functools.reduce(jnp.add, shares)
    acc = functools.reduce(jnp.add, [share * values for share, (values, _) in zip(shares, parts)])
    return acc * (1.0 / whole), top + jnp.log2(whole)


def column(stat):
    return jnp.max(stat, axis=1, keepdims=True)


def diagonal(rows, lanes):
    row = lax.broadcasted_iota(jnp.int32, (rows, lanes), 0)
    return row == lax.broadcasted_iota(jnp.int32, (rows, lanes), 1)


def visible(rows, ends, starts, span):
    local = len(ends)
    cols = len(starts) * local * span
    col = lax.broadcasted_iota(jnp.int32, (1, cols), 1)
    col_of = jnp.zeros_like(col)
    limit = jnp.full_like(col, ends[0] - starts[0])
    for at in range(1, len(starts) * local):
        begin, p = at * span, at % local
        later = col >= begin
        col_of = jnp.where(later, p, col_of)
        limit = jnp.where(later, ends[p] - starts[at // local] + begin, limit)
    col_of = jnp.where(col < limit, col_of, -1)
    row_of = lax.rem(lax.broadcasted_iota(jnp.int32, (rows, 1), 0), local)
    return row_of == col_of


def attend(queries, keys, seen, rank, known):
    scores = lax.dot_general(queries, keys, NT, preferred_element_type=F32)
    scores = jnp.where(seen, scores * SCALE2, HIDDEN)
    top = jnp.max(scores, axis=1, keepdims=True)
    for level, _, _ in known:
        top = jnp.maximum(top, level)
    weights = jnp.where(seen, jnp.exp2(scores - top), 0.0)
    total = jnp.sum(weights, axis=1, keepdims=True)
    acc = jnp.dot(weights.astype(BF16), keys[:, :rank], preferred_element_type=F32)
    for level, mass, part in known:
        factor = jnp.exp2(level - top)
        total = total + mass * factor
        acc = acc + part * factor
    return acc * (1.0 / total), top + jnp.log2(total)


def at_end(dom):
    return (dom == 0) | (dom == 3)


def picked(row, at):
    lane = lax.broadcasted_iota(jnp.int32, row.shape, 1)
    return jnp.sum(jnp.where(lane == at, row.astype(F32), 0.0)).astype(jnp.int32)


def gather_kernel(line, chosen, local, names_ref, *refs):
    block_refs, out_ref = refs[:-1], refs[-1]
    if chosen:
        block_refs = block_refs[:-1]
    dom = lax.axis_index("dom")
    names = [picked(names_ref[...], p) for p in range(local)]
    some = out_ref.shape[0] // local
    for p in range(local):
        owner, slot = lax.div(names[p], local), lax.rem(names[p], local)
        if line:
            apart = jnp.bitwise_xor(owner, dom)
            which = jnp.where(at_end(dom), 0, jnp.maximum(apart - 1, 0))
            if chosen:
                slot = jnp.where(at_end(dom), p, slot)
        else:
            which = lax.rem(dom - owner + len(block_refs), len(block_refs))
        rows = pl.ds(pl.multiple_of(slot * some, some), some)
        for k, block_ref in enumerate(block_refs):

            @pl.when(which == k)
            def _():
                part = pl.ds(p * some, some)
                if len(block_ref.shape) == 2:
                    out_ref[part] = block_ref[rows]
                else:
                    pack_slot(block_ref[slot], out_ref, part)


def gathered(names, blocks, line, local, token=None):
    token = [] if token is None else [token]
    return pl.pallas_call(
        functools.partial(gather_kernel, line, bool(token), local),
        out_shape=shape(blocks[0].shape),
        in_specs=[VMEM] * (1 + len(blocks)) + [ANY] * len(token),
        out_specs=VMEM,
        compiler_params=PARAMS,
        cost_estimate=NO_COST,
        name="gather",
    )(names, *blocks, *token)


def far_part(ends, query_ref, stage_refs, part, keys):
    acc_ref, max_ref, sum_ref = stage_refs
    span, rank = keys.shape[0] // len(ends), acc_ref.shape[1]
    seen = visible(query_ref.shape[0], ends, [lax.axis_index("seq") * span], span)
    known = [(column(max_ref[part]), column(sum_ref[part]), acc_ref[part])]
    return packed(*attend(query_ref[...], keys, seen, rank, known))


def give_kernel(stages, line, local, names_ref, lens_ref, *refs):
    stage_refs, refs = refs[: 4 * stages], refs[4 * stages :]
    early_ref, late_ref, moved_ref, give_refs = refs[0], refs[1], refs[2], refs[3:]
    dom = lax.axis_index("dom")
    anc = [picked(names_ref[...], p) for p in range(local)]
    some = early_ref.shape[0] // local
    span, width = 2 * some, moved_ref.shape[1]
    rank = stage_refs[1].shape[1]

    def place(p, value):
        for h in range(2):
            rows, rope = pl.ds(p * span + h * some, some), 2 * rank + h * (width - rank)
            moved_ref[rows, :rank] = value[:, h * rank : (h + 1) * rank]
            moved_ref[rows, rank:] = value[:, rope : rope + width - rank]

    for p in range(local):
        if line:
            owner, slot = lax.div(anc[p], local), lax.rem(anc[p], local)
            apart = jnp.bitwise_xor(owner, dom)
            late = jnp.where(at_end(dom), apart != 0, apart == 1)
            slot = jnp.where(at_end(dom), p, slot)
            rows = pl.ds(pl.multiple_of(slot * some, some), some)

            @pl.when(late)
            def _():
                place(p, late_ref[rows])

            @pl.when(jnp.logical_not(late))
            def _():
                place(p, early_ref[pl.ds(p * some, some)])

        else:
            place(p, early_ref[pl.ds(p * some, some)])

    for k in range(stages):
        query_ref, *partial = stage_refs[4 * k : 4 * k + 4]
        rows = query_ref.shape[0]
        ends = [picked(lens_ref[...], anc[p]) for p in range(local)]
        give_refs[k][...] = far_part(ends, query_ref, partial, pl.ds(rows, rows), moved_ref[...])


def keep_kernel(stages, local, names_ref, lens_ref, *refs):
    anc = [picked(names_ref[...], p) for p in range(local)]
    ends = [picked(lens_ref[...], at) for at in anc]
    stage_refs, refs = refs[: 4 * stages], refs[4 * stages :]
    moved_ref, keep_refs, piece_refs = refs[0], refs[1 : 1 + stages], refs[1 + stages :]
    begin = 0
    for piece_ref in piece_refs:
        piece_ref[...] = moved_ref[pl.ds(begin, piece_ref.shape[0])]
        begin += piece_ref.shape[0]
    for k in range(stages):
        query_ref, *partial = stage_refs[4 * k : 4 * k + 4]
        rows = query_ref.shape[0]
        keep_refs[k][...] = far_part(ends, query_ref, partial, pl.ds(0, rows), moved_ref[...])


def head_products(latent, w_ref, local, begin=0):
    heads, reach = latent.shape[0] // local, w_ref.shape[2]
    first = lax.broadcasted_iota(jnp.int32, (2 * local, reach), 0) < local
    products = []
    for h in range(0, heads, 2):
        weights = jnp.concatenate([w_ref[begin + h], w_ref[begin + h + 1]], axis=1)
        both = jnp.dot(latent[h * local : (h + 2) * local], weights, preferred_element_type=F32)
        products.append(jnp.where(first, both[:, :reach], both[:, reach:]))
    return jnp.concatenate(products, axis=0)


def near_kernel(names_ref, lens_ref, fresh_ref, w_ref, *refs):
    seq = lax.axis_index("seq")
    query_ref, acc_ref, max_ref, sum_ref, got_ref, moved_ref, *other_refs = refs[:-3]
    cache_ref, value_ref, level_ref = refs[-3:]
    local, span, width = cache_ref.shape
    rank = acc_ref.shape[1]
    start, other = seq * span, jnp.bitwise_xor(seq, 1) * span
    ends = [picked(lens_ref[...], picked(names_ref[...], p)) for p in range(local)]
    keys = jnp.concatenate([ref[...] for ref in (moved_ref, *other_refs)], axis=0)
    seen = visible(query_ref.shape[0], ends, [start, other], span)
    level = jnp.sum(got_ref[:, rank:].astype(F32), axis=1, keepdims=True)
    known = [
        (column(max_ref[...]), column(sum_ref[...]), acc_ref[...]),
        (level, 1.0, got_ref[:, :rank].astype(F32)),
    ]
    values, level = attend(query_ref[...], keys, seen, rank, known)
    value_ref[...] = head_products(values.astype(BF16), w_ref, local)
    level_ref[...] = jnp.broadcast_to(level, level_ref.shape)
    for p in range(local):
        at = start + lax.broadcasted_iota(jnp.int32, (span, 1), 0) == ends[p]
        cache_ref[p] = jnp.where(at, fresh_ref[pl.ds(p, 1), :], moved_ref[pl.ds(p * span, span)])


def chip_kernel(count, *refs):
    for k in range(count):
        first_ref, second_ref, level_ref = refs[2 * count + 3 * k : 2 * count + 3 * k + 3]
        values, level = merged([unpacked(refs[k][...]), unpacked(refs[count + k][...])])
        half = first_ref.shape[0]
        first_ref[...] = values[:half].astype(BF16)
        second_ref[...] = values[half:].astype(BF16)
        kept = jnp.where(diagonal(values.shape[0], level_ref.shape[1]), level, 0.0)
        level_ref[...] = jnp.broadcast_to(jnp.sum(kept, axis=0, keepdims=True), level_ref.shape)


def chip_merge(keep, got):
    rows, rank = keep[0].shape[0], keep[0].shape[1] - LANES
    half = shape((rows // 2, rank))
    return pl.pallas_call(
        functools.partial(chip_kernel, len(keep)),
        out_shape=[half, half, shape((8, max(rows, LANES)), F32)] * len(keep),
        in_specs=[VMEM] * (2 * len(keep)),
        out_specs=[VMEM] * (3 * len(keep)),
        compiler_params=PARAMS,
        name="chip_merge",
    )(*keep, *got)


def half_kernel(local, part_ref, w_ref, out_ref):
    out_ref[...] = head_products(part_ref[...], w_ref, local)


def half_products(part, w_uv, local):
    return pl.pallas_call(
        functools.partial(half_kernel, local),
        out_shape=shape((part.shape[0], w_uv.shape[2]), F32),
        in_specs=[VMEM] * 2,
        out_specs=VMEM,
        compiler_params=PARAMS,
        cost_estimate=NO_COST,
        name="half",
    )(part, w_uv)


def final_kernel(count, *refs):
    part_refs, (value_ref, level_ref, w_ref, out_ref, values) = refs[: 3 * count], refs[3 * count :]
    heads, rank, reach = w_ref.shape
    local = out_ref.shape[0]
    parts = [(value_ref[...], column(level_ref[...]))]
    for k in range(count):
        row = part_refs[3 * k + 2][0:1]
        kept = jnp.where(diagonal(value_ref.shape[0], row.shape[1]), row, 0.0)
        rest = head_products(part_refs[3 * k + 1][...], w_ref, local, heads // 2)
        products = jnp.concatenate([part_refs[3 * k][...], rest], axis=0)
        parts.append((products, jnp.sum(kept, axis=1, keepdims=True)))
    values[...] = merged(parts)[0]
    for p in range(local):
        out_ref[p] = values[pl.ds(p, heads, stride=local), :].astype(BF16)


def on_device(q_nope, q_rope, w_uk, w_uv, prefix, private_caches, new_latent, ancestors, lengths):
    local, heads, nope = q_nope.shape
    span, width = private_caches.shape[1:]
    rank, reach = w_uv.shape[1:]
    rows = local * heads
    seq_size, dom_size = lax.axis_size("seq"), lax.axis_size("dom")
    cores = 2
    chips = seq_size // cores
    block = pl.pallas_call(
        pack_kernel,
        out_shape=shape((local * span // 2, 2 * width)),
        in_specs=[VMEM],
        out_specs=VMEM,
        compiler_params=PARAMS,
        cost_estimate=pl.CostEstimate(flops=PACK, bytes_accessed=0, transcendentals=0),
        name="pack",
    )(private_caches)
    nope_rows, rope_rows = (jnp.swapaxes(q, 0, 1).reshape(rows, -1) for q in (q_nope, q_rope))
    names = jnp.pad(ancestors, (0, LANES - local))[None]
    limits = jnp.pad(lengths, (0, max(0, LANES - lengths.shape[0])))[None]
    line = dom_size == 4
    if line:
        swap = [(0, 1), (1, 0), (2, 3), (3, 2)]
        middle = lax.ppermute(block, "dom", [(0, 2), (3, 1)])
        far = lax.ppermute(private_caches, "dom", [(1, 2), (2, 1)])
        theirs = lax.ppermute(names, "dom", [(0, 1), (3, 2)])
    else:
        blocks = [block] + [
            lax.ppermute(block, "dom", [(i, (i + k) % dom_size) for i in range(dom_size)])
            for k in range(1, dom_size)
        ]

    own = pl.pallas_call(
        functools.partial(project_kernel, local),
        out_shape=shape((rows, width)),
        in_specs=[VMEM] * 3,
        out_specs=VMEM,
        compiler_params=PARAMS,
        cost_estimate=pl.CostEstimate(flops=PROJECT, bytes_accessed=0, transcendentals=0),
        name="project",
    )(nope_rows, rope_rows, w_uk)
    keys = prefix.T

    def pairs(turn, flip):
        return [
            (x * cores + c, (x + turn) % chips * cores + (c ^ flip))
            for x in range(chips)
            for c in range(cores)
        ]

    def back(turn, flip):
        return [(b, a) for a, b in pairs(turn, flip)]

    routes = [(t, f) for t in range(chips) for f in range(cores)]
    queries = [own if r == (0, 0) else lax.ppermute(own, "seq", pairs(*r)) for r in routes]
    stages = []
    for t in range(chips):
        asked = queries[2 * t : 2 * t + 2]
        stage = [*asked, *prefix_attention(asked, keys, rank, t == 0)]
        stages.append(stage)
        if t == 0:
            given = lax.ppermute(stage.pop(), "seq", pairs(0, 1))
        if line and t == 0:
            chosen = gathered(theirs, [block, middle, far], line, local, stage[3])
            late = lax.ppermute(chosen, "dom", swap)
            early = gathered(names, [block, middle, far], line, local)
    if not line:
        early = late = gathered(names, blocks, line, local)

    part = shape((rows, rank + LANES))
    others = chips - 1
    given, early = lax.optimization_barrier((given, early))
    giving = [a for stage in stages[1:] for a in stage[1:]]
    keeping = [a for stage in stages[1:] for a in (stage[0], *stage[2:])]
    moved, *give = pl.pallas_call(
        functools.partial(give_kernel, others, line, local),
        out_shape=[shape((local * span, width))] + [part] * others,
        in_specs=[VMEM] * (len(giving) + 4),
        out_specs=[VMEM] * (1 + others),
        compiler_params=PARAMS,
        name="suffix_give",
    )(names, limits, *giving, early, late)
    cuts = (local * span // 2,) * 2
    keep_and_pieces = pl.pallas_call(
        functools.partial(keep_kernel, others, local),
        out_shape=[part] * others + [shape((cut, width)) for cut in cuts],
        in_specs=[VMEM] * (len(keeping) + 3),
        out_specs=[VMEM] * (others + len(cuts)),
        compiler_params=PARAMS,
        name="suffix_keep",
    )(names, limits, *keeping, moved)
    keep, pieces = keep_and_pieces[:others], keep_and_pieces[others:]
    sums = chip_merge(keep, [lax.ppermute(g, "seq", pairs(0, 1)) for g in give])
    parts = [lax.ppermute(s, "seq", back(1 + i // 3, 0)) for i, s in enumerate(sums)]
    parts[::3] = [half_products(part, w_uv, local) for part in parts[::3]]
    other = [lax.ppermute(piece, "seq", pairs(0, 1)) for piece in pieces]

    moved, _ = lax.optimization_barrier((moved, sums[0]))
    query, _, acc, level, mass = stages[0]
    new_caches, *own_part = pl.pallas_call(
        near_kernel,
        out_shape=[shape(private_caches.shape), shape((rows, reach), F32), shape((rows, LANES), F32)],
        in_specs=[VMEM] * (10 + len(other)),
        out_specs=[VMEM] * 3,
        compiler_params=PARAMS,
        cost_estimate=NO_COST,
        name="suffix_near",
    )(names, limits, new_latent, w_uv, query, acc, level, mass, given, moved, *other)
    parts += own_part

    head_values = pl.pallas_call(
        functools.partial(final_kernel, others),
        out_shape=shape((local, heads, reach)),
        in_specs=[VMEM] * (3 * others + 3),
        out_specs=VMEM,
        scratch_shapes=[pltpu.VMEM((rows, reach), F32)],
        compiler_params=PARAMS,
        name="final",
    )(*parts, w_uv)
    return (head_values, new_caches)


def solution(mesh):
    placed = (
        P(("group", "dom"), "seq", None),
        P(("group", "dom"), "seq", None),
        P("seq", None, None),
        P("seq", None, None),
        P(("group", "seq"), None),
        P(("group", "dom"), "seq", None),
        P(("group", "dom"), None),
        P(("group", "dom")),
        P("group"),
    )
    return jax.shard_map(
        on_device,
        mesh=mesh,
        in_specs=placed,
        out_specs=(P(("group", "dom"), "seq", None), P(("group", "dom"), "seq", None)),
        check_vma=False,
    )
```

```python
import functools
import math

import jax
import jax.numpy as jnp
from jax import lax
from jax.experimental import pallas as pl
from jax.experimental.pallas import tpu as pltpu
from jax.sharding import PartitionSpec as P

ROPE = 64
NOPE = 128
SCALE2 = (NOPE + ROPE) ** (-0.5) * math.log2(math.e)
HIDDEN = -1e30
LANES = 128
F32 = jnp.float32
BF16 = jnp.bfloat16
NT = (((1,), (1,)), ((), ()))

VMEM = pl.BlockSpec(memory_space=pltpu.VMEM)
SMEM = pl.BlockSpec(memory_space=pltpu.SMEM)
ANY = pl.BlockSpec(memory_space=pl.ANY)
HBM = pl.BlockSpec(memory_space=pltpu.HBM)
PARAMS = pltpu.CompilerParams(vmem_limit_bytes=40 * 1024 * 1024)
NO_COST = pl.CostEstimate(flops=0, bytes_accessed=0, transcendentals=0)
PACK = 8_000_000_000
PROJECT = 8_000_000_000


def shape(dims, dtype=BF16):
    return jax.ShapeDtypeStruct(dims, dtype)


def pack_slot(rows, out_ref, part):
    some, width = rows.shape[0] // 2, rows.shape[1]
    rank = width - ROPE
    first, second = rows[:some], rows[some:]
    out_ref[part, :rank] = first[:, :rank]
    out_ref[part, rank : 2 * rank] = second[:, :rank]
    out_ref[part, 2 * rank :] = jnp.concatenate([first[:, rank:], second[:, rank:]], axis=1)


def pack_kernel(cache_ref, out_ref):
    local, span, _ = cache_ref.shape
    for p in range(local):
        pack_slot(cache_ref[p], out_ref, pl.ds(p * span // 2, span // 2))


def project_kernel(local, nope_ref, rope_ref, w_ref, own_ref):
    heads, _, rank = w_ref.shape
    nope = nope_ref[...].astype(F32)
    width = nope.shape[1]
    first = lax.broadcasted_iota(jnp.int32, (2 * local, width), 0) < local

    def pair(h):
        two = nope[h * local : (h + 2) * local]
        left = jnp.concatenate([jnp.where(first, two, 0.0), jnp.where(first, 0.0, two)], axis=1)
        weights = w_ref[pl.ds(h, 2)].reshape(2 * width, rank)
        return jnp.dot(left.astype(BF16), weights, preferred_element_type=F32)

    own_ref[:, rank:] = rope_ref[...]
    for h in range(0, heads, 4):
        own_ref[pl.ds(h * local, 4 * local), :rank] = jnp.concatenate(
            [pair(i) for i in (h, h + 2)], axis=0
        ).astype(BF16)


def prefix_kernel(count, tiles, *refs):
    query_refs = refs[:count]
    keys_ref, out_ref, max_ref, sum_ref, *give_ref, acc_ref = refs[count:]
    rank = acc_ref.shape[1]
    tile = keys_ref.shape[1] // tiles
    parts = [pl.ds(i * tile, tile) for i in range(tiles)]
    queries = jnp.concatenate([ref[...] for ref in query_refs], axis=0)

    def score(i):
        return jnp.dot(queries, keys_ref[:, parts[i]], preferred_element_type=F32) * SCALE2

    ahead = score(0)
    for i in range(tiles):
        scores = ahead
        if i + 1 < tiles:
            ahead = score(i + 1)
        top = jnp.max(scores, axis=1, keepdims=True)
        if i > 0:
            top = jnp.maximum(top, largest)
        weights = jnp.exp2(scores - top)
        total = jnp.sum(weights, axis=1, keepdims=True)
        acc = lax.dot_general(
            weights.astype(BF16), keys_ref[:rank, parts[i]], NT, preferred_element_type=F32
        )
        if i > 0:
            factor = jnp.exp2(largest - top)
            total = total + running * factor
            acc = acc + acc_ref[...] * factor
        largest, running = top, total
        if i < tiles - 1:
            acc_ref[...] = acc
    kept = out_ref.shape[0]
    out_ref[...] = acc[:kept]
    max_ref[...] = jnp.broadcast_to(largest[:kept], max_ref.shape)
    sum_ref[...] = jnp.broadcast_to(running[:kept], sum_ref.shape)
    if give_ref:
        level = largest[kept:] + jnp.log2(running[kept:])
        give_ref[0][...] = packed(acc[kept:] * (1.0 / running[kept:]), level)


def prefix_attention(queries, keys, rank, give, tiles=4):
    rows = sum(q.shape[0] for q in queries)
    kept = queries[0].shape[0] if give else rows
    width, length = keys.shape
    out = [shape((kept, rank), F32)] + [shape((kept, LANES), F32)] * 2
    if give:
        out.append(shape((rows - kept, rank + LANES)))
    return pl.pallas_call(
        functools.partial(prefix_kernel, len(queries), tiles),
        out_shape=out,
        in_specs=[VMEM] * (len(queries) + 1),
        out_specs=[VMEM] * len(out),
        scratch_shapes=[pltpu.VMEM((rows, rank), F32)],
        compiler_params=PARAMS,
        cost_estimate=pl.CostEstimate(
            flops=0 if give else 2 * rows * length * (width + rank),
            bytes_accessed=0 if give else 2 * width * length,
            transcendentals=0 if give else rows * length,
        ),
        name="prefix_attention",
    )(*queries, keys)


def packed(values, level):
    rows = values.shape[0]
    lane = lax.broadcasted_iota(jnp.int32, (rows, LANES), 1)
    high = level.astype(BF16).astype(F32)
    middle = (level - high).astype(BF16).astype(F32)
    low = level - high - middle
    stats = jnp.where(lane == 0, high, jnp.where(lane == 1, middle, jnp.where(lane == 2, low, 0.0)))
    return jnp.concatenate([values.astype(BF16), stats.astype(BF16)], axis=1)


def unpacked(part):
    rank = part.shape[1] - LANES
    return part[:, :rank].astype(F32), jnp.sum(part[:, rank:].astype(F32), axis=1, keepdims=True)


def merged(parts):
    levels = [level for _, level in parts]
    top = functools.reduce(jnp.maximum, levels)
    shares = [jnp.exp2(level - top) for level in levels]
    whole = functools.reduce(jnp.add, shares)
    acc = functools.reduce(jnp.add, [share * values for share, (values, _) in zip(shares, parts)])
    return acc * (1.0 / whole), top + jnp.log2(whole)


def column(stat):
    return jnp.max(stat, axis=1, keepdims=True)


def diagonal(rows, lanes):
    row = lax.broadcasted_iota(jnp.int32, (rows, lanes), 0)
    return row == lax.broadcasted_iota(jnp.int32, (rows, lanes), 1)


def visible(rows, ends, starts, span):
    local = len(ends)
    cols = len(starts) * local * span
    col = lax.broadcasted_iota(jnp.int32, (1, cols), 1)
    col_of = jnp.zeros_like(col)
    limit = jnp.full_like(col, ends[0] - starts[0])
    for at in range(1, len(starts) * local):
        begin, p = at * span, at % local
        later = col >= begin
        col_of = jnp.where(later, p, col_of)
        limit = jnp.where(later, ends[p] - starts[at // local] + begin, limit)
    col_of = jnp.where(col < limit, col_of, -1)
    row_of = lax.rem(lax.broadcasted_iota(jnp.int32, (rows, 1), 0), local)
    return row_of == col_of


def attend(queries, keys, seen, rank, known):
    scores = lax.dot_general(queries, keys, NT, preferred_element_type=F32)
    scores = jnp.where(seen, scores * SCALE2, HIDDEN)
    top = jnp.max(scores, axis=1, keepdims=True)
    for level, _, _ in known:
        top = jnp.maximum(top, level)
    weights = jnp.where(seen, jnp.exp2(scores - top), 0.0)
    total = jnp.sum(weights, axis=1, keepdims=True)
    acc = jnp.dot(weights.astype(BF16), keys[:, :rank], preferred_element_type=F32)
    for level, mass, part in known:
        factor = jnp.exp2(level - top)
        total = total + mass * factor
        acc = acc + part * factor
    return acc * (1.0 / total), top + jnp.log2(total)


def at_end(dom):
    return (dom == 0) | (dom == 3)


def picked(row, at):
    lane = lax.broadcasted_iota(jnp.int32, row.shape, 1)
    return jnp.sum(jnp.where(lane == at, row.astype(F32), 0.0)).astype(jnp.int32)


def gather_kernel(line, chosen, local, names_ref, *refs):
    block_refs, out_ref = refs[:-1], refs[-1]
    if chosen:
        block_refs = block_refs[:-1]
    dom = lax.axis_index("dom")
    names = [picked(names_ref[...], p) for p in range(local)]
    some = out_ref.shape[0] // local
    for p in range(local):
        owner, slot = lax.div(names[p], local), lax.rem(names[p], local)
        if line:
            apart = jnp.bitwise_xor(owner, dom)
            which = jnp.where(at_end(dom), 0, jnp.maximum(apart - 1, 0))
            if chosen:
                slot = jnp.where(at_end(dom), p, slot)
        else:
            which = lax.rem(dom - owner + len(block_refs), len(block_refs))
        rows = pl.ds(pl.multiple_of(slot * some, some), some)
        for k, block_ref in enumerate(block_refs):

            @pl.when(which == k)
            def _():
                part = pl.ds(p * some, some)
                if len(block_ref.shape) == 2:
                    out_ref[part] = block_ref[rows]
                else:
                    pack_slot(block_ref[slot], out_ref, part)


def gathered(names, blocks, line, local, token=None):
    token = [] if token is None else [token]
    return pl.pallas_call(
        functools.partial(gather_kernel, line, bool(token), local),
        out_shape=shape(blocks[0].shape),
        in_specs=[VMEM] * (1 + len(blocks)) + [ANY] * len(token),
        out_specs=VMEM,
        compiler_params=PARAMS,
        cost_estimate=NO_COST,
        name="gather",
    )(names, *blocks, *token)


def far_part(ends, query_ref, stage_refs, part, keys):
    acc_ref, max_ref, sum_ref = stage_refs
    span, rank = keys.shape[0] // len(ends), acc_ref.shape[1]
    seen = visible(query_ref.shape[0], ends, [lax.axis_index("seq") * span], span)
    known = [(column(max_ref[part]), column(sum_ref[part]), acc_ref[part])]
    return packed(*attend(query_ref[...], keys, seen, rank, known))


def give_kernel(stages, line, local, names_ref, lens_ref, *refs):
    stage_refs, refs = refs[: 4 * stages], refs[4 * stages :]
    early_ref, late_ref, moved_ref, give_refs = refs[0], refs[1], refs[2], refs[3:]
    dom = lax.axis_index("dom")
    anc = [picked(names_ref[...], p) for p in range(local)]
    some = early_ref.shape[0] // local
    span, width = 2 * some, moved_ref.shape[1]
    rank = stage_refs[1].shape[1]

    def place(p, value):
        for h in range(2):
            rows, rope = pl.ds(p * span + h * some, some), 2 * rank + h * (width - rank)
            moved_ref[rows, :rank] = value[:, h * rank : (h + 1) * rank]
            moved_ref[rows, rank:] = value[:, rope : rope + width - rank]

    for p in range(local):
        if line:
            owner, slot = lax.div(anc[p], local), lax.rem(anc[p], local)
            apart = jnp.bitwise_xor(owner, dom)
            late = jnp.where(at_end(dom), apart != 0, apart == 1)
            slot = jnp.where(at_end(dom), p, slot)
            rows = pl.ds(pl.multiple_of(slot * some, some), some)

            @pl.when(late)
            def _():
                place(p, late_ref[rows])

            @pl.when(jnp.logical_not(late))
            def _():
                place(p, early_ref[pl.ds(p * some, some)])

        else:
            place(p, early_ref[pl.ds(p * some, some)])

    for k in range(stages):
        query_ref, *partial = stage_refs[4 * k : 4 * k + 4]
        rows = query_ref.shape[0]
        ends = [picked(lens_ref[...], anc[p]) for p in range(local)]
        give_refs[k][...] = far_part(ends, query_ref, partial, pl.ds(rows, rows), moved_ref[...])


def keep_kernel(stages, local, names_ref, lens_ref, *refs):
    anc = [picked(names_ref[...], p) for p in range(local)]
    ends = [picked(lens_ref[...], at) for at in anc]
    stage_refs, refs = refs[: 4 * stages], refs[4 * stages :]
    moved_ref, keep_refs, piece_refs = refs[0], refs[1 : 1 + stages], refs[1 + stages :]
    begin = 0
    for piece_ref in piece_refs:
        piece_ref[...] = moved_ref[pl.ds(begin, piece_ref.shape[0])]
        begin += piece_ref.shape[0]
    for k in range(stages):
        query_ref, *partial = stage_refs[4 * k : 4 * k + 4]
        rows = query_ref.shape[0]
        keep_refs[k][...] = far_part(ends, query_ref, partial, pl.ds(0, rows), moved_ref[...])


def head_products(latent, w_ref, local, begin=0):
    heads, reach = latent.shape[0] // local, w_ref.shape[2]
    first = lax.broadcasted_iota(jnp.int32, (2 * local, reach), 0) < local
    products = []
    for h in range(0, heads, 2):
        weights = jnp.concatenate([w_ref[begin + h], w_ref[begin + h + 1]], axis=1)
        both = jnp.dot(latent[h * local : (h + 2) * local], weights, preferred_element_type=F32)
        products.append(jnp.where(first, both[:, :reach], both[:, reach:]))
    return jnp.concatenate(products, axis=0)


def near_kernel(names_ref, lens_ref, fresh_ref, w_ref, *refs):
    seq = lax.axis_index("seq")
    query_ref, acc_ref, max_ref, sum_ref, got_ref, moved_ref, *other_refs = refs[:-3]
    cache_ref, value_ref, level_ref = refs[-3:]
    local, span, width = cache_ref.shape
    rank = acc_ref.shape[1]
    start, other = seq * span, jnp.bitwise_xor(seq, 1) * span
    ends = [picked(lens_ref[...], picked(names_ref[...], p)) for p in range(local)]
    keys = jnp.concatenate([ref[...] for ref in (moved_ref, *other_refs)], axis=0)
    seen = visible(query_ref.shape[0], ends, [start, other], span)
    level = jnp.sum(got_ref[:, rank:].astype(F32), axis=1, keepdims=True)
    known = [
        (column(max_ref[...]), column(sum_ref[...]), acc_ref[...]),
        (level, 1.0, got_ref[:, :rank].astype(F32)),
    ]
    values, level = attend(query_ref[...], keys, seen, rank, known)
    value_ref[...] = head_products(values.astype(BF16), w_ref, local)
    level_ref[...] = jnp.broadcast_to(level, level_ref.shape)
    for p in range(local):
        at = start + lax.broadcasted_iota(jnp.int32, (span, 1), 0) == ends[p]
        cache_ref[p] = jnp.where(at, fresh_ref[pl.ds(p, 1), :], moved_ref[pl.ds(p * span, span)])


def chip_kernel(count, *refs):
    for k in range(count):
        first_ref, second_ref, level_ref = refs[2 * count + 3 * k : 2 * count + 3 * k + 3]
        values, level = merged([unpacked(refs[k][...]), unpacked(refs[count + k][...])])
        half = first_ref.shape[0]
        first_ref[...] = values[:half].astype(BF16)
        second_ref[...] = values[half:].astype(BF16)
        kept = jnp.where(diagonal(values.shape[0], level_ref.shape[1]), level, 0.0)
        level_ref[...] = jnp.broadcast_to(jnp.sum(kept, axis=0, keepdims=True), level_ref.shape)


def chip_merge(keep, got):
    rows, rank = keep[0].shape[0], keep[0].shape[1] - LANES
    cut = rows * 3 // 64 * 16
    halves = [shape((cut, rank)), shape((rows - cut, rank))]
    return pl.pallas_call(
        functools.partial(chip_kernel, len(keep)),
        out_shape=[*halves, shape((8, max(rows, LANES)), F32)] * len(keep),
        in_specs=[VMEM] * (2 * len(keep)),
        out_specs=[VMEM] * (3 * len(keep)),
        compiler_params=PARAMS,
        name="chip_merge",
    )(*keep, *got)


def half_kernel(local, part_ref, w_ref, out_ref):
    out_ref[...] = head_products(part_ref[...], w_ref, local)


def half_products(part, w_uv, local):
    return pl.pallas_call(
        functools.partial(half_kernel, local),
        out_shape=shape((part.shape[0], w_uv.shape[2]), F32),
        in_specs=[VMEM] * 2,
        out_specs=VMEM,
        compiler_params=PARAMS,
        cost_estimate=NO_COST,
        name="half",
    )(part, w_uv)


def final_kernel(count, *refs):
    part_refs, (value_ref, level_ref, w_ref, out_ref, values) = refs[: 3 * count], refs[3 * count :]
    heads, rank, reach = w_ref.shape
    local = out_ref.shape[0]
    parts = [(value_ref[...], column(level_ref[...]))]
    for k in range(count):
        row = part_refs[3 * k + 2][0:1]
        kept = jnp.where(diagonal(value_ref.shape[0], row.shape[1]), row, 0.0)
        done = part_refs[3 * k].shape[0] // local
        rest = head_products(part_refs[3 * k + 1][...], w_ref, local, done)
        products = jnp.concatenate([part_refs[3 * k][...], rest], axis=0)
        parts.append((products, jnp.sum(kept, axis=1, keepdims=True)))
    values[...] = merged(parts)[0]
    for p in range(local):
        out_ref[p] = values[pl.ds(p, heads, stride=local), :].astype(BF16)


def on_device(q_nope, q_rope, w_uk, w_uv, prefix, private_caches, new_latent, ancestors, lengths):
    local, heads, nope = q_nope.shape
    span, width = private_caches.shape[1:]
    rank, reach = w_uv.shape[1:]
    rows = local * heads
    seq_size, dom_size = lax.axis_size("seq"), lax.axis_size("dom")
    cores = 2
    chips = seq_size // cores
    block = pl.pallas_call(
        pack_kernel,
        out_shape=shape((local * span // 2, 2 * width)),
        in_specs=[VMEM],
        out_specs=VMEM,
        compiler_params=PARAMS,
        cost_estimate=pl.CostEstimate(flops=PACK, bytes_accessed=0, transcendentals=0),
        name="pack",
    )(private_caches)
    nope_rows, rope_rows = (jnp.swapaxes(q, 0, 1).reshape(rows, -1) for q in (q_nope, q_rope))
    names = jnp.pad(ancestors, (0, LANES - local))[None]
    limits = jnp.pad(lengths, (0, max(0, LANES - lengths.shape[0])))[None]
    line = dom_size == 4
    if line:
        swap = [(0, 1), (1, 0), (2, 3), (3, 2)]
        middle = lax.ppermute(block, "dom", [(0, 2), (3, 1)])
        far = lax.ppermute(private_caches, "dom", [(1, 2), (2, 1)])
        theirs = lax.ppermute(names, "dom", [(0, 1), (3, 2)])
    else:
        blocks = [block] + [
            lax.ppermute(block, "dom", [(i, (i + k) % dom_size) for i in range(dom_size)])
            for k in range(1, dom_size)
        ]

    own = pl.pallas_call(
        functools.partial(project_kernel, local),
        out_shape=shape((rows, width)),
        in_specs=[VMEM] * 3,
        out_specs=VMEM,
        compiler_params=PARAMS,
        cost_estimate=pl.CostEstimate(flops=PROJECT, bytes_accessed=0, transcendentals=0),
        name="project",
    )(nope_rows, rope_rows, w_uk)
    keys = prefix.T

    def pairs(turn, flip):
        return [
            (x * cores + c, (x + turn) % chips * cores + (c ^ flip))
            for x in range(chips)
            for c in range(cores)
        ]

    def back(turn, flip):
        return [(b, a) for a, b in pairs(turn, flip)]

    routes = [(t, f) for t in range(chips) for f in range(cores)]
    queries = [own if r == (0, 0) else lax.ppermute(own, "seq", pairs(*r)) for r in routes]
    stages = []
    for t in range(chips):
        asked = queries[2 * t : 2 * t + 2]
        stage = [*asked, *prefix_attention(asked, keys, rank, t == 0)]
        stages.append(stage)
        if t == 0:
            given = lax.ppermute(stage.pop(), "seq", pairs(0, 1))
        if line and t == 0:
            chosen = gathered(theirs, [block, middle, far], line, local, stage[3])
            late = lax.ppermute(chosen, "dom", swap)
            early = gathered(names, [block, middle, far], line, local)
    if not line:
        early = late = gathered(names, blocks, line, local)

    part = shape((rows, rank + LANES))
    others = chips - 1
    given, early = lax.optimization_barrier((given, early))
    giving = [a for stage in stages[1:] for a in stage[1:]]
    keeping = [a for stage in stages[1:] for a in (stage[0], *stage[2:])]
    moved, *give = pl.pallas_call(
        functools.partial(give_kernel, others, line, local),
        out_shape=[shape((local * span, width))] + [part] * others,
        in_specs=[VMEM] * (len(giving) + 4),
        out_specs=[VMEM] * (1 + others),
        compiler_params=PARAMS,
        name="suffix_give",
    )(names, limits, *giving, early, late)
    cuts = (local * span // 2,) * 2
    keep_and_pieces = pl.pallas_call(
        functools.partial(keep_kernel, others, local),
        out_shape=[part] * others + [shape((cut, width)) for cut in cuts],
        in_specs=[VMEM] * (len(keeping) + 3),
        out_specs=[VMEM] * (others + len(cuts)),
        compiler_params=PARAMS,
        name="suffix_keep",
    )(names, limits, *keeping, moved)
    keep, pieces = keep_and_pieces[:others], keep_and_pieces[others:]
    sums = chip_merge(keep, [lax.ppermute(g, "seq", pairs(0, 1)) for g in give])
    parts = [lax.ppermute(s, "seq", back(1 + i // 3, 0)) for i, s in enumerate(sums)]
    parts[::3] = [half_products(part, w_uv, local) for part in parts[::3]]
    other = [lax.ppermute(piece, "seq", pairs(0, 1)) for piece in pieces]

    moved, _ = lax.optimization_barrier((moved, sums[0]))
    query, _, acc, level, mass = stages[0]
    new_caches, *own_part = pl.pallas_call(
        near_kernel,
        out_shape=[shape(private_caches.shape), shape((rows, reach), F32), shape((rows, LANES), F32)],
        in_specs=[VMEM] * (10 + len(other)),
        out_specs=[VMEM] * 3,
        compiler_params=PARAMS,
        cost_estimate=NO_COST,
        name="suffix_near",
    )(names, limits, new_latent, w_uv, query, acc, level, mass, given, moved, *other)
    parts += own_part

    head_values = pl.pallas_call(
        functools.partial(final_kernel, others),
        out_shape=shape((local, heads, reach)),
        in_specs=[VMEM] * (3 * others + 3),
        out_specs=VMEM,
        scratch_shapes=[pltpu.VMEM((rows, reach), F32)],
        compiler_params=PARAMS,
        name="final",
    )(*parts, w_uv)
    return (head_values, new_caches)


def solution(mesh):
    placed = (
        P(("group", "dom"), "seq", None),
        P(("group", "dom"), "seq", None),
        P("seq", None, None),
        P("seq", None, None),
        P(("group", "seq"), None),
        P(("group", "dom"), "seq", None),
        P(("group", "dom"), None),
        P(("group", "dom")),
        P("group"),
    )
    return jax.shard_map(
        on_device,
        mesh=mesh,
        in_specs=placed,
        out_specs=(P(("group", "dom"), "seq", None), P(("group", "dom"), "seq", None)),
        check_vma=False,
    )
```
